32 devices in a mesh: replica: 8 (over z, x), shard: 4 (over y, core).
Axes of the slice: x: 2, y: 2, z: 4, core: 2. Of those that a mesh axis runs over, the one named last changes fastest.
Arguments:
- hidden_in: bfloat16 [4096, 1024], P(('replica', 'shard'))
- cotangent: bfloat16 [4096, 1024], P(('replica', 'shard')), may hold values from -6 to 6
- doc_starts: int32 [8, 9], P('replica'), may hold values from 0 to 511, as said below
- valid_mask: int32 [4096], P(('replica', 'shard')), may hold values from 0 to 1, as said below
- norm_one: float32 [1024], replicated, may hold values from 0.5 to 1.5
- in_proj: bfloat16 [1024, 3352], P('shard'), may hold values from -0.1875 to 0.1875
- conv_weight: float32 [1792, 4], replicated, may hold values from -3 to 3
- conv_bias: float32 [1792], replicated, may hold values from -0.5 to 0.5
- dt_bias: float32 [24], replicated, may hold values from -7 to -2.5
- a_log: float32 [24], replicated, may hold values from -1 to 2.5
- skip_scale: float32 [24], replicated, may hold values from 0.5 to 2
- gated_gain: float32 [1536], replicated, may hold values from 0.5 to 1.5
- qkv_proj: bfloat16 [1024, 768], P('shard'), may hold values from -0.1875 to 0.1875
- ssm_out: bfloat16 [1536, 1024], P('shard'), may hold values from -0.15625 to 0.15625
- attn_out: bfloat16 [512, 1024], P('shard'), may hold values from -2 to 2
- norm_two: float32 [1024], replicated, may hold values from 0.5 to 1.5
- gate_up: bfloat16 [1024, 4096], P('shard'), may hold values from -0.1875 to 0.1875
- down_proj: bfloat16 [2048, 1024], P('shard'), may hold values from -0.125 to 0.125
Outputs:
- output: bfloat16 [4096, 1024], P(('replica', 'shard'))
- grad_input: float32 [4096, 1024], P(('replica', 'shard'))
- grad_norm_one: float32 [1024], replicated
- grad_in_proj: float32 [1024, 3352], P('shard')
- grad_conv_weight: float32 [1792, 4], replicated
- grad_conv_bias: float32 [1792], replicated
- grad_dt_bias: float32 [24], replicated
- grad_a_log: float32 [24], replicated
- grad_skip_scale: float32 [24], replicated
- grad_gated_gain: float32 [1536], replicated
- grad_qkv_proj: float32 [1024, 768], P('shard')
- grad_ssm_out: float32 [1536, 1024], P('shard')
- grad_attn_out: float32 [512, 1024], P('shard')
- grad_norm_two: float32 [1024], replicated
- grad_gate_up: float32 [1024, 4096], P('shard')
- grad_down_proj: float32 [2048, 1024], P('shard')
- rms_stats: float32 [3], replicated
The draws below stay inside these ranges and needn't reach their ends.
Inputs may be any that keep to these rules, and one draw needn't show every extreme that they name: `doc_starts`: row g lists the first positions of the 9 documents of sequence g in strictly increasing order; the first is 0 and the last document is the single token at position 511. `valid_mask`: in each sequence the tokens with 0 form a tail of 1 to 64 positions at its end; all others are 1.
All inputs are finite; a program needn't handle non-finite values.
Results may differ from the reference program's by a relative error of at most 0.0096.
Values may be sent and summed in bfloat16 or wider, within the bound.
No kernel may reach another device: no remote copies, remote signals or barrier semaphores. Data moves between devices by JAX's collectives and lax.ppermute only.
A program may use at most 192 MiB of HBM per device.

```python
import math
import jax
import jax.numpy as jnp
from jax import lax

D = 1024
NH = 24
HP = 64
NS = 128
KC = 4
QH = 8
KVH = 2
HD = 64
FF = 2048
TOK_DEV = 128
SPAN = 128
KBLK = 512
SIDE = 4
DS = 1536
QW = 512
KW = 128
CONV_CH = 1792
IN_W = 3352
SEQ = 512
GROUPS = 8
TOKENS = 4096


def draw_hidden_in(key, part):
    key = jax.random.fold_in(key, 11)
    ramp = 0.6 + 1.2 * jnp.arange(TOKENS, dtype=jnp.float32)[:, None] / (TOKENS - 1)
    base = jnp.clip(jax.random.normal(key, (TOKENS, D), jnp.float32), -6.0, 6.0)
    return (base * ramp).astype(jnp.bfloat16)


def draw_doc_starts(key, part):
    key = jax.random.fold_in(key, 23)
    head_key, tail_key = jax.random.split(key)
    head_lengths = jax.random.randint(head_key, (GROUPS, SIDE), 1, TOK_DEV // 4)
    tail_drawn = jax.random.randint(tail_key, (GROUPS, SIDE), 1, TOK_DEV // 4)
    tail_lengths = jnp.concatenate([tail_drawn[:, :SIDE - 1], jnp.ones((GROUPS, 1), jnp.int32)], axis=1)
    head_starts = jnp.cumsum(head_lengths, axis=1) - head_lengths
    long_start = jnp.sum(head_lengths, axis=1, keepdims=True)
    tail_starts = SEQ - jnp.flip(jnp.cumsum(jnp.flip(tail_lengths, axis=1), axis=1), axis=1)
    return jnp.concatenate([head_starts, long_start, tail_starts], axis=1).astype(jnp.int32)


def draw_valid_mask(key, part):
    key = jax.random.fold_in(key, 37)
    padding = jax.random.randint(key, (GROUPS, 1), 1, TOK_DEV // 2 + 1)
    places = jnp.arange(SEQ, dtype=jnp.int32)[None, :]
    return (places < SEQ - padding).astype(jnp.int32).reshape(TOKENS)


def steps_of(key, dims, cuts, least, high):
    def one(dim, shards_of):
        steps = jax.random.uniform(jax.random.fold_in(jax.random.fold_in(key, 6), dim), (shards_of,), jnp.float32, least / len(cuts), high / len(cuts))
        return jnp.repeat(jnp.exp(steps), dims[dim] // shards_of).reshape((-1,) + (1,) * (len(dims) - dim - 1))

    gain = one(*cuts[0])
    for cut in cuts[1:]:
        gain = gain * one(*cut)
    return gain


def centred(key, extent, width, most, shards=(), kind=jnp.bfloat16):
    result = width * jax.random.normal(key, extent, jnp.float32)
    if shards:
        result = result * steps_of(key, extent, shards, -0.22, 0.18)
    return jnp.clip(result, -most, most).astype(kind)


def setup_inputs(seed: int = 0) -> dict:
    key_of = jax.random.split(jax.random.key(seed), 19)
    hidden_in = draw_hidden_in(jax.random.fold_in(key_of[18], 71), 0)
    cotangent = centred(key_of[1], (TOKENS, D), 1.0, 6.0, ((0, 32),))
    doc_starts = draw_doc_starts(jax.random.fold_in(key_of[18], 71), 0)
    valid_mask = draw_valid_mask(jax.random.fold_in(key_of[18], 71), 0)
    norm_one = jnp.clip(1.0 + 0.1 * jax.random.normal(key_of[4], (D,), jnp.float32), 0.5, 1.5)
    in_proj = centred(key_of[5], (D, IN_W), D ** -0.5, 0.1875, ((0, 4),))
    conv_weight = centred(key_of[6], (CONV_CH, KC), KC ** -0.5, 3.0, (), jnp.float32)
    conv_bias = jnp.clip(jax.random.uniform(key_of[7], (CONV_CH,), jnp.float32, -0.5, 0.5), -0.5, 0.5)
    dt_bias = jnp.clip(jax.random.uniform(key_of[8], (NH,), jnp.float32, -7.0, -2.5), -7.0, -2.5)
    a_log = jnp.clip(jax.random.uniform(key_of[9], (NH,), jnp.float32, -1.0, 2.5), -1.0, 2.5)
    skip_scale = jnp.clip(jax.random.uniform(key_of[10], (NH,), jnp.float32, 0.5, 2.0), 0.5, 2.0)
    gated_gain = jnp.clip(1.0 + 0.1 * jax.random.normal(key_of[11], (DS,), jnp.float32), 0.5, 1.5)
    qkv_proj = centred(key_of[12], (D, QW + 2 * KW), D ** -0.5, 0.1875, ((0, 4),))
    ssm_out = centred(key_of[13], (DS, D), DS ** -0.5, 0.15625, ((0, 4),))
    attn_out = centred(key_of[14], (QW, D), (QW // 64) ** -0.5, 2.0, ((0, 4),))
    norm_two = jnp.clip(1.0 + 0.1 * jax.random.normal(key_of[15], (D,), jnp.float32), 0.5, 1.5)
    gate_up = centred(key_of[16], (D, 2 * FF), D ** -0.5, 0.1875, ((0, 4),))
    down_proj = centred(key_of[17], (FF, D), FF ** -0.5, 0.125, ((0, 4),))
    return {"hidden_in": hidden_in, "cotangent": cotangent, "doc_starts": doc_starts, "valid_mask": valid_mask, "norm_one": norm_one, "in_proj": in_proj, "conv_weight": conv_weight, "conv_bias": conv_bias, "dt_bias": dt_bias, "a_log": a_log, "skip_scale": skip_scale, "gated_gain": gated_gain, "qkv_proj": qkv_proj, "ssm_out": ssm_out, "attn_out": attn_out, "norm_two": norm_two, "gate_up": gate_up, "down_proj": down_proj}


EPS = 1e-05
ROPE_BASE = 100000000000.0
NEG = -1e+30
HIGH = lax.Precision.HIGHEST

@jax.custom_vjp
def low(v):
    return lax.optimization_barrier(v.astype(jnp.bfloat16)).astype(jnp.float32)

@jax.custom_vjp
def low_back(v):
    return v

def low_keep(v):
    return (low(v), None)

def low_pass(kept, grad):
    return (grad,)

def back_keep(v):
    return (v, None)

def back_low(kept, grad):
    return (low(grad),)
low.defvjp(low_keep, low_pass)
low_back.defvjp(back_keep, back_low)

def rms_scale(tensor):
    return lax.rsqrt(lax.optimization_barrier(jnp.mean(tensor * tensor, axis=-1, keepdims=True)) + EPS)

def rope_tables(positions):
    freqs = ROPE_BASE ** (-(jnp.arange(HD // 2).astype(jnp.float32) * 2.0) / HD)
    angles = positions.astype(jnp.float32)[:, None] * freqs[None, :]
    return (jnp.cos(angles), jnp.sin(angles))

def rotate(tensor, heads, cosines, sines):
    shaped = tensor.reshape(tensor.shape[0], heads, HD)
    first_half = shaped[:, :, :HD // 2]
    second_half = shaped[:, :, HD // 2:]
    cos_b = cosines[:, None, :]
    sin_b = sines[:, None, :]
    turned = jnp.concatenate([first_half * cos_b - second_half * sin_b, second_half * cos_b + first_half * sin_b], axis=-1)
    return turned.reshape(tensor.shape[0], heads * HD)

def ssd_spans(state, ssm_x, ssm_b, ssm_c, step_size, log_decay, skip_scale, seg_ids, before):
    count = ssm_x.shape[0] // SPAN
    prev_seg = jnp.concatenate([before.reshape(1), seg_ids[:-1]]).astype(jnp.int32)

    def by_span(tensor):
        return tensor.reshape((count, SPAN) + tensor.shape[1:])

    def span_step(state_acc, pieces):
        x_c, b_c, c_c, dt_c, la_c, s_c, p_c = pieces
        cum_decay = jnp.cumsum(la_c, axis=0)
        order = jnp.arange(SPAN)
        same_mask = (s_c[:, None] == s_c[None, :]) & (order[:, None] >= order[None, :])
        differ = cum_decay.T[:, :, None] - cum_decay.T[:, None, :]
        decay_mat = jnp.exp(jnp.where(same_mask[None], differ, NEG))
        inner = jnp.dot(c_c, b_c.T, precision=HIGH)
        mixing = decay_mat * inner[None] * dt_c.T[:, None, :]
        y_inner = jnp.einsum('hpq,qhd->phd', mixing, x_c, precision=HIGH)
        alive = (s_c == p_c[0]).astype(jnp.float32)
        carried = jnp.exp(cum_decay) * alive[:, None]
        y_state = jnp.einsum('hdn,pn->phd', state_acc, c_c, precision=HIGH) * carried[:, :, None]
        y_span = y_inner + y_state + skip_scale[None, :, None] * x_c
        tail_w = jnp.exp(cum_decay[-1][None, :] - cum_decay) * (s_c == s_c[-1]).astype(jnp.float32)[:, None] * dt_c
        new_state = state_acc * carried[-1][:, None, None] + jnp.einsum('qh,qhd,qn->hdn', tail_w, x_c, b_c, precision=HIGH)
        return (new_state, y_span)
    final_state, ys = lax.scan(jax.checkpoint(span_step), state, (by_span(ssm_x), by_span(ssm_b), by_span(ssm_c), by_span(step_size), by_span(log_decay), by_span(seg_ids), by_span(prev_seg)))
    return (ys.reshape(ssm_x.shape), final_state)

def sequence_forward(params, inputs):
    norm_one, in_proj, conv_weight, conv_bias, dt_bias, a_log, skip_scale, gated_gain, qkv_proj, ssm_out, attn_out, norm_two, gate_up, down_proj = params
    hidden, starts_row = inputs
    length = hidden.shape[0]
    score_scale = 1.0 / math.sqrt(HD)
    positions = jnp.arange(length, dtype=jnp.int32)
    seg_ids = (lax.optimization_barrier(jnp.sum((starts_row[None, :] <= positions[:, None]).astype(jnp.int32), axis=1)) - 1).astype(jnp.int32)
    normed_in = low(hidden * rms_scale(hidden) * norm_one)
    proj_out = low_back(jnp.dot(normed_in, in_proj, precision=HIGH))
    gate_z = proj_out[:, :DS]
    xbc = proj_out[:, DS:DS + CONV_CH]
    dt_raw = proj_out[:, DS + CONV_CH:]
    padded = jnp.concatenate([jnp.zeros((KC - 1, CONV_CH), hidden.dtype), xbc], axis=0)
    seg_pad = jnp.concatenate([jnp.full((KC - 1,), -1, jnp.int32), seg_ids]).astype(jnp.int32)
    conv_pre = jnp.zeros((length, CONV_CH), hidden.dtype) + conv_bias[None, :]
    for tap_index in range(KC):
        same_doc = (seg_pad[tap_index:tap_index + length] == seg_ids).astype(hidden.dtype)
        conv_pre = conv_pre + conv_weight[:, tap_index][None, :] * padded[tap_index:tap_index + length] * same_doc[:, None]
    conv_act = jax.nn.silu(conv_pre)
    ssm_x = conv_act[:, :DS].reshape(length, NH, HP)
    ssm_b = conv_act[:, DS:DS + NS]
    ssm_c = conv_act[:, DS + NS:]
    step_size = jax.nn.softplus(dt_raw + dt_bias)
    log_decay = -step_size * jnp.exp(a_log)
    ssm_y, final_state = ssd_spans(jnp.zeros((NH, HP, NS), hidden.dtype), ssm_x, ssm_b, ssm_c, step_size, log_decay, skip_scale, seg_ids, jnp.int32(-1))
    ssm_y = ssm_y.reshape(length, DS)
    gated = ssm_y * jax.nn.silu(gate_z)
    normed = low(gated * rms_scale(gated) * gated_gain)
    qkv = low_back(jnp.dot(normed_in, qkv_proj, precision=HIGH))
    cosines, sines = rope_tables(positions)
    queries = low(rotate(qkv[:, :QW], QH, cosines, sines)).reshape(length, KVH, QH // KVH, HD)
    keys = low(rotate(qkv[:, QW:QW + KW], KVH, cosines, sines)).reshape(length, KVH, HD)
    values = low(qkv[:, QW + KW:]).reshape(length, KVH, HD)

    def attend_block(pieces):
        q_blk, pos_blk, seg_blk = pieces
        raw_scores = jnp.einsum('tgqd,kgd->gqtk', q_blk, keys, precision=HIGH)
        scores = low_back(raw_scores) * score_scale
        key_mask = (positions[None, :] <= pos_blk[:, None]) & (seg_ids[None, :] == seg_blk[:, None])
        scores = jnp.where(key_mask[None, None], scores, NEG)
        probs = low(jnp.exp(scores - jax.nn.logsumexp(scores, axis=-1, keepdims=True)))
        return jnp.einsum('gqtk,kgd->tgqd', probs, values, precision=HIGH)
    block_count = length // KBLK
    attended = lax.map(jax.checkpoint(attend_block), (queries.reshape(block_count, KBLK, KVH, QH // KVH, HD), positions.reshape(block_count, KBLK), seg_ids.reshape(block_count, KBLK)))
    attn = low(low_back(attended.reshape(length, QW)))
    mixed = low_back(jnp.dot(normed, ssm_out, precision=HIGH) + jnp.dot(attn, attn_out, precision=HIGH))
    residual = hidden + mixed
    normed_two = low(residual * rms_scale(residual) * norm_two)
    gate_vals = low_back(jnp.dot(normed_two, gate_up, precision=HIGH))
    hid = low(jax.nn.silu(gate_vals[:, :FF]) * gate_vals[:, FF:])
    mlp_out = low_back(jnp.dot(hid, down_proj, precision=HIGH))
    return (residual + mlp_out, (mixed, mlp_out))

def reference(hidden_in, cotangent, doc_starts, valid_mask, norm_one, in_proj, conv_weight, conv_bias, dt_bias, a_log, skip_scale, gated_gain, qkv_proj, ssm_out, attn_out, norm_two, gate_up, down_proj):
    weights = tuple((w.astype(jnp.float32) for w in (norm_one, in_proj, conv_weight, conv_bias, dt_bias, a_log, skip_scale, gated_gain, qkv_proj, ssm_out, attn_out, norm_two, gate_up, down_proj)))
    x_groups = hidden_in.astype(jnp.float32).reshape(GROUPS, SEQ, D)

    def forward(x_all, *params):

        def one_group(inputs):
            return sequence_forward(params, inputs)
        out_all, extras = lax.map(jax.checkpoint(one_group), (x_all, doc_starts))
        return (out_all, extras)
    out_all, pull_back, extras = jax.vjp(forward, x_groups, *weights, has_aux=True)
    keep_rows = valid_mask.astype(jnp.float32).reshape(GROUPS, SEQ)
    grads = pull_back(cotangent.astype(jnp.float32).reshape(GROUPS, SEQ, D) * keep_rows[:, :, None])
    count = jnp.sum(keep_rows)

    def rms_of(tensor):
        return jnp.sqrt(jnp.sum(keep_rows * lax.optimization_barrier(jnp.sum(tensor * tensor, axis=-1))) / (count * D))
    rms_stats = jnp.stack([rms_of(out_all), rms_of(extras[0]), rms_of(extras[1])])
    return (out_all.reshape(TOKENS, D).astype(jnp.bfloat16), grads[0].reshape(TOKENS, D), grads[1], grads[2], grads[3], grads[4], grads[5], grads[6], grads[7], grads[8], grads[9], grads[10], grads[11], grads[12], grads[13], grads[14], rms_stats)
```

```python
import math

import jax
import jax.numpy as jnp
from jax import lax
from jax.experimental import pallas as pl
from jax.experimental.pallas import tpu as pltpu
from jax.sharding import PartitionSpec as P

D = 1024
NH = 24
HP = 64
NS = 128
KC = 4
QH = 8
KVH = 2
HD = 64
FF = 2048
SPAN = 128
KBLK = 512
DS = 1536
QW = 512
KW = 128
CONV_CH = 1792


EPS = 1e-05
ROPE_BASE = 100000000000.0
NEG = -1e30
HIGH = lax.Precision.HIGHEST


def from_behind(block, axis, distance):
    devices = range(lax.axis_size(axis))
    route = [(i - distance, i) for i in devices if i - distance in devices]
    return lax.ppermute(block, axis, route)


def carried_in(part, axis, combine, identity):
    place = lax.axis_index(axis)
    gathered = jax.tree.map(lambda a: lax.all_gather(a, axis), part)
    state = jax.tree.map(lambda a, e: jnp.zeros_like(a) + jnp.asarray(e, a.dtype), part, identity)

    def one(step, state):
        return combine(
            state, jax.tree.map(lambda a: lax.dynamic_index_in_dim(a, step, 0, False), gathered)
        )

    return lax.fori_loop(0, place, one, state)


def entering(value, axis, combine, identity):
    size, mine = (lax.axis_size(axis), lax.axis_index(axis))
    everything = jax.tree.map(
        lambda part, kind: lax.all_gather(part.astype(kind), axis),
        value,
        jax.tree.map(lambda a: jnp.bfloat16 if a.dtype == jnp.float32 else a.dtype, value),
    )
    start = jax.tree.map(
        lambda part, zero: jnp.broadcast_to(jnp.asarray(zero, part.dtype), part.shape),
        value,
        identity,
    )

    def step(k, before):
        at = size - 1 - k
        reached = at > mine
        new = combine(
            before, jax.tree.map(lambda part, own: part[at].astype(own.dtype), everything, value)
        )
        return jax.tree.map(lambda a, b: jnp.where(reached, a, b), new, before)

    return lax.fori_loop(0, size, step, start)


def rms_scale(tensor):
    return lax.rsqrt(jnp.mean(tensor * tensor, axis=-1, keepdims=True) + EPS)


def rope_tables(positions):
    freqs = ROPE_BASE ** (-(jnp.arange(HD // 2).astype(jnp.float32) * 2.0) / HD)
    angles = positions.astype(jnp.float32)[:, None] * freqs[None, :]
    return (jnp.cos(angles), jnp.sin(angles))


def rotate(tensor, heads, cosines, sines):
    shaped = tensor.reshape(tensor.shape[0], heads, HD)
    first_half = shaped[:, :, : HD // 2]
    second_half = shaped[:, :, HD // 2 :]
    cos_b = cosines[:, None, :]
    sin_b = sines[:, None, :]
    turned = jnp.concatenate(
        [first_half * cos_b - second_half * sin_b, second_half * cos_b + first_half * sin_b],
        axis=-1,
    )
    return turned.reshape(tensor.shape[0], heads * HD)


def segment_of(positions, starts_row):
    return jnp.sum((starts_row[None, :] <= positions[:, None]).astype(jnp.int32), axis=1) - 1


def norm_back(grad_out, tensor, scale_rows, gain):
    scaled = grad_out * gain
    grad_in = scale_rows * scaled - tensor * scale_rows**3 * jnp.mean(
        scaled * tensor, axis=-1, keepdims=True
    )
    return (grad_in, jnp.sum(grad_out * tensor * scale_rows, axis=0))


def dsilu(tensor):
    sig_part = jax.nn.sigmoid(tensor)
    return sig_part * (1.0 + tensor * (1.0 - sig_part))


def combine_states(earlier, later):
    return (earlier[0] * later[1][:, None, None] + later[0], earlier[1] * later[1])


def ssd_spans(state, ssm_x, ssm_b, ssm_c, step_size, log_decay, skip_scale, seg_ids, before):
    count = ssm_x.shape[0] // SPAN
    prev_seg = jnp.concatenate([before.reshape(1), seg_ids[:-1]])

    def by_span(tensor):
        return tensor.reshape((count, SPAN) + tensor.shape[1:])

    def span_step(state_acc, pieces):
        x_c, b_c, c_c, dt_c, la_c, s_c, p_c = pieces
        cum_decay = jnp.cumsum(la_c, axis=0)
        order = jnp.arange(SPAN)
        same_mask = (s_c[:, None] == s_c[None, :]) & (order[:, None] >= order[None, :])
        differ = cum_decay.T[:, :, None] - cum_decay.T[:, None, :]
        decay_mat = jnp.exp(jnp.where(same_mask[None], differ, NEG))
        inner = jnp.dot(c_c, b_c.T, precision=HIGH)
        mixing = decay_mat * inner[None] * dt_c.T[:, None, :]
        y_inner = jnp.einsum("hpq,qhd->phd", mixing, x_c, precision=HIGH)
        alive = (s_c == p_c[0]).astype(jnp.float32)
        carried = jnp.exp(cum_decay) * alive[:, None]
        y_state = jnp.einsum("hdn,pn->phd", state_acc, c_c, precision=HIGH) * carried[:, :, None]
        y_span = y_inner + y_state + skip_scale[None, :, None] * x_c
        tail_w = (
            jnp.exp(cum_decay[-1][None, :] - cum_decay)
            * (s_c == s_c[-1]).astype(jnp.float32)[:, None]
            * dt_c
        )
        new_state = state_acc * carried[-1][:, None, None] + jnp.einsum(
            "qh,qhd,qn->hdn", tail_w, x_c, b_c, precision=HIGH
        )
        return (new_state, y_span)

    final_state, ys = lax.scan(
        span_step,
        state,
        (
            by_span(ssm_x),
            by_span(ssm_b),
            by_span(ssm_c),
            by_span(step_size),
            by_span(log_decay),
            by_span(seg_ids),
            by_span(prev_seg),
        ),
    )
    return (ys.reshape(ssm_x.shape), final_state)


def on_device(
    hidden_in,
    cotangent,
    doc_starts,
    valid_mask,
    norm_one,
    in_proj,
    conv_weight,
    conv_bias,
    dt_bias,
    a_log,
    skip_scale,
    gated_gain,
    qkv_proj,
    ssm_out,
    attn_out,
    norm_two,
    gate_up,
    down_proj,
):
    tok_rows = hidden_in.shape[0]
    shard_count = lax.axis_size("shard")
    offset = lax.axis_index("shard") * tok_rows
    seq_len = tok_rows * shard_count
    score_scale = 1.0 / math.sqrt(HD)
    q_per_kv = QH // KVH
    starts_row = doc_starts[0]
    positions = offset + jnp.arange(tok_rows, dtype=jnp.int32)
    seg_ids = segment_of(positions, starts_row)
    before = segment_of(positions[:1] - 1, starts_row)[0]
    first_start = jnp.max(jnp.where(starts_row <= positions[0], starts_row, 0))
    last_pos = positions[-1]
    full_weights = (
        lax.all_gather(in_proj, "shard", axis=0, tiled=True),
        lax.all_gather(qkv_proj, "shard", axis=0, tiled=True),
        lax.all_gather(ssm_out, "shard", axis=0, tiled=True),
        lax.all_gather(attn_out, "shard", axis=0, tiled=True),
        lax.all_gather(gate_up, "shard", axis=0, tiled=True),
        lax.all_gather(down_proj, "shard", axis=0, tiled=True),
    )
    f_in, f_attn, f_mo, f_ao, f_gu, f_down = full_weights
    x_full = hidden_in.astype(jnp.float32)
    r_one = rms_scale(x_full)
    h_low = (x_full * r_one * norm_one).astype(jnp.bfloat16)
    proj_out = jnp.dot(h_low, f_in, preferred_element_type=jnp.float32)
    gate_z = proj_out[:, :DS]
    xbc = proj_out[:, DS : DS + CONV_CH]
    dt_raw = proj_out[:, DS + CONV_CH :]
    edge_rows = from_behind(xbc[tok_rows - (KC - 1) :], "shard", 1)
    padded = jnp.concatenate([edge_rows, xbc], axis=0)
    pad_pos = positions[0] - (KC - 1) + jnp.arange(tok_rows + KC - 1, dtype=jnp.int32)
    pad_seg = segment_of(pad_pos, starts_row)
    tap_masks = [
        (pad_seg[tap_index : tap_index + tok_rows] == seg_ids).astype(jnp.float32)[:, None]
        for tap_index in range(KC)
    ]
    conv_pre = jnp.zeros((tok_rows, CONV_CH), jnp.float32) + conv_bias[None, :]
    for tap_index in range(KC):
        conv_pre = (
            conv_pre
            + conv_weight[:, tap_index][None, :]
            * padded[tap_index : tap_index + tok_rows]
            * tap_masks[tap_index]
        )
    conv_act = jax.nn.silu(conv_pre)
    ssm_x = conv_act[:, :DS].reshape(tok_rows, NH, HP)
    ssm_b = conv_act[:, DS : DS + NS]
    ssm_c = conv_act[:, DS + NS :]
    soft_in = dt_raw + dt_bias
    step_size = jax.nn.softplus(soft_in)
    decay_rate = jnp.exp(a_log)
    log_decay = -step_size * decay_rate
    empty_state = jnp.zeros((NH, HP, NS), jnp.float32)

    def carry_factor(log_vals):
        return (
            jnp.exp(jnp.cumsum(log_vals, axis=0)) * (seg_ids == before).astype(jnp.float32)[:, None]
        )

    def carry_term(state_in, c_vals, factor):
        return jnp.einsum("hdn,pn->phd", state_in, c_vals, precision=HIGH) * factor[:, :, None]

    ssm_zero, local_state = ssd_spans(
        empty_state, ssm_x, ssm_b, ssm_c, step_size, log_decay, skip_scale, seg_ids, before
    )
    factor = carry_factor(log_decay)
    dev_decay = factor[-1]
    state_in, unused_decay = carried_in(
        (local_state, dev_decay),
        "shard",
        combine_states,
        (jnp.zeros_like(local_state), jnp.ones_like(dev_decay)),
    )
    ssm_y = (ssm_zero + carry_term(state_in, ssm_c, factor)).reshape(tok_rows, DS)
    silu_z = jax.nn.silu(gate_z)
    gated = ssm_y * silu_z
    r_gate = rms_scale(gated)
    normed_low = (gated * r_gate * gated_gain).astype(jnp.bfloat16)
    qkv = jnp.dot(h_low, f_attn, preferred_element_type=jnp.float32)
    cosines, sines = rope_tables(positions)
    q_low = (
        rotate(qkv[:, :QW], QH, cosines, sines)
        .astype(jnp.bfloat16)
        .reshape(tok_rows, KVH, q_per_kv, HD)
    )
    k_low = rotate(qkv[:, QW : QW + KW], KVH, cosines, sines).astype(jnp.bfloat16)
    v_low = qkv[:, QW + KW :].astype(jnp.bfloat16)
    key_all, value_all = (
        lax.all_gather(k_low, "shard", axis=0, tiled=True),
        lax.all_gather(v_low, "shard", axis=0, tiled=True),
    )
    key_all = key_all.reshape(seq_len, KVH, HD)
    value_all = value_all.reshape(seq_len, KVH, HD)
    key_pos = jnp.arange(seq_len, dtype=jnp.int32)
    key_seg = segment_of(key_pos, starts_row)
    block_count = seq_len // KBLK
    row_shape = (KVH, q_per_kv, tok_rows)

    def needed(blk_index):
        low_edge = blk_index * KBLK
        return (low_edge <= last_pos) & (low_edge + KBLK > first_start)

    def block_keys(blk_index):
        return (
            lax.dynamic_slice_in_dim(key_all, blk_index * KBLK, KBLK, 0),
            lax.dynamic_slice_in_dim(value_all, blk_index * KBLK, KBLK, 0),
        )

    def block_scores(blk_index, k_blk):
        pos_blk = lax.dynamic_slice_in_dim(key_pos, blk_index * KBLK, KBLK, 0)
        seg_blk = lax.dynamic_slice_in_dim(key_seg, blk_index * KBLK, KBLK, 0)
        raw_scores = (
            jnp.einsum("tgqd,kgd->gqtk", q_low, k_blk, preferred_element_type=jnp.float32)
            * score_scale
        )
        key_mask = (pos_blk[None, :] <= positions[:, None]) & (seg_blk[None, :] == seg_ids[:, None])
        return (raw_scores, key_mask[None, None])

    def unchanged(passed):
        return passed

    def lse_step(blk_index, state_acc):

        def lse_do_block(state_acc):
            row_top, row_total = state_acc
            k_blk, v_blk = block_keys(blk_index)
            raw_scores, key_mask = block_scores(blk_index, k_blk)
            new_top = jnp.maximum(row_top, jnp.max(jnp.where(key_mask, raw_scores, NEG), axis=-1))
            row_total = row_total * jnp.exp(row_top - new_top) + jnp.sum(
                jnp.where(key_mask, jnp.exp(raw_scores - new_top[..., None]), 0.0), axis=-1
            )
            return (new_top, row_total)

        return lax.cond(needed(blk_index), lse_do_block, unchanged, state_acc)

    row_top, row_total = lax.fori_loop(
        0,
        block_count,
        lse_step,
        (jnp.full(row_shape, NEG, jnp.float32), jnp.zeros(row_shape, jnp.float32)),
    )
    log_total = row_top + jnp.log(row_total)

    def probs_of(blk_index, k_blk):
        raw_scores, key_mask = block_scores(blk_index, k_blk)
        return jnp.where(key_mask, jnp.exp(raw_scores - log_total[..., None]), 0.0)

    def out_step(blk_index, acc_out):

        def out_do_block(acc_out):
            k_blk, v_blk = block_keys(blk_index)
            prob_blk = probs_of(blk_index, k_blk).astype(jnp.bfloat16)
            return acc_out + jnp.einsum(
                "gqtk,kgd->tgqd", prob_blk, v_blk, preferred_element_type=jnp.float32
            )

        return lax.cond(needed(blk_index), out_do_block, unchanged, acc_out)

    attended = lax.fori_loop(
        0, block_count, out_step, jnp.zeros((tok_rows, KVH, q_per_kv, HD), jnp.float32)
    )
    attn_low = attended.reshape(tok_rows, QW).astype(jnp.bfloat16)
    mixed = jnp.dot(normed_low, f_mo, preferred_element_type=jnp.float32) + jnp.dot(
        attn_low, f_ao, preferred_element_type=jnp.float32
    )
    residual = x_full + mixed
    r_two = rms_scale(residual)
    h2_low = (residual * r_two * norm_two).astype(jnp.bfloat16)
    gate_vals = jnp.dot(h2_low, f_gu, preferred_element_type=jnp.float32)
    gate_part = gate_vals[:, :FF]
    up_part = gate_vals[:, FF:]
    hid_low = (jax.nn.silu(gate_part) * up_part).astype(jnp.bfloat16)
    mlp_out = jnp.dot(hid_low, f_down, preferred_element_type=jnp.float32)
    out_full = residual + mlp_out
    keep_rows = valid_mask.astype(jnp.float32)
    stat_local = jnp.stack(
        [
            jnp.sum(keep_rows * jnp.sum(out_full * out_full, axis=1)),
            jnp.sum(keep_rows * jnp.sum(mixed * mixed, axis=1)),
            jnp.sum(keep_rows * jnp.sum(mlp_out * mlp_out, axis=1)),
            jnp.sum(keep_rows),
        ]
    )
    back_weights = (
        lax.all_gather(in_proj, "shard", axis=0, tiled=True),
        lax.all_gather(qkv_proj, "shard", axis=0, tiled=True),
        lax.all_gather(ssm_out, "shard", axis=0, tiled=True),
        lax.all_gather(attn_out, "shard", axis=0, tiled=True),
        lax.all_gather(gate_up, "shard", axis=0, tiled=True),
        lax.all_gather(down_proj, "shard", axis=0, tiled=True),
    )
    b_in, b_attn, b_mo, b_ao, b_gu, b_down = back_weights
    grad_out = cotangent.astype(jnp.float32) * keep_rows[:, None]
    grad_mlp = grad_out.astype(jnp.bfloat16)
    g_down = jnp.dot(hid_low.T, grad_mlp, preferred_element_type=jnp.float32)
    grad_hid = jnp.dot(grad_mlp, b_down.T, preferred_element_type=jnp.float32)
    grad_gu = jnp.concatenate(
        [grad_hid * up_part * dsilu(gate_part), grad_hid * jax.nn.silu(gate_part)], axis=1
    ).astype(jnp.bfloat16)
    g_gu = jnp.dot(h2_low.T, grad_gu, preferred_element_type=jnp.float32)
    grad_h2 = jnp.dot(grad_gu, b_gu.T, preferred_element_type=jnp.float32)
    grad_res_n, g_norm_two = norm_back(grad_h2, residual, r_two, norm_two)
    grad_res = grad_out + grad_res_n
    grad_mix = grad_res.astype(jnp.bfloat16)
    g_mo = jnp.dot(normed_low.T, grad_mix, preferred_element_type=jnp.float32)
    g_ao = jnp.dot(attn_low.T, grad_mix, preferred_element_type=jnp.float32)
    grad_normed = jnp.dot(grad_mix, b_mo.T, preferred_element_type=jnp.float32)
    grad_attn = (
        jnp.dot(grad_mix, b_ao.T, preferred_element_type=jnp.float32)
        .astype(jnp.bfloat16)
        .reshape(tok_rows, KVH, q_per_kv, HD)
    )

    def delta_step(blk_index, acc_out):

        def delta_do_block(acc_out):
            k_blk, v_blk = block_keys(blk_index)
            prob_blk = probs_of(blk_index, k_blk)
            grad_prob = jnp.einsum(
                "tgqd,kgd->gqtk", grad_attn, v_blk, preferred_element_type=jnp.float32
            )
            return acc_out + jnp.sum(prob_blk * grad_prob, axis=-1)

        return lax.cond(needed(blk_index), delta_do_block, unchanged, acc_out)

    delta_row = lax.fori_loop(0, block_count, delta_step, jnp.zeros(row_shape, jnp.float32))

    def grad_step(blk_index, state_acc):

        def grad_do_block(state_acc):
            grad_query, grad_kv = state_acc
            k_blk, v_blk = block_keys(blk_index)
            prob_blk = probs_of(blk_index, k_blk)
            grad_prob = jnp.einsum(
                "tgqd,kgd->gqtk", grad_attn, v_blk, preferred_element_type=jnp.float32
            )
            grad_raw = (prob_blk * (grad_prob - delta_row[..., None]) * score_scale).astype(
                jnp.bfloat16
            )
            grad_query = grad_query + jnp.einsum(
                "gqtk,kgd->tgqd", grad_raw, k_blk, preferred_element_type=jnp.float32
            )
            grad_key = jnp.einsum(
                "gqtk,tgqd->kgd", grad_raw, q_low, preferred_element_type=jnp.float32
            )
            grad_value = jnp.einsum(
                "gqtk,tgqd->kgd",
                prob_blk.astype(jnp.bfloat16),
                grad_attn,
                preferred_element_type=jnp.float32,
            )
            kv_piece = jnp.concatenate(
                [grad_key.reshape(KBLK, KW), grad_value.reshape(KBLK, KW)], axis=1
            )
            grad_kv = lax.dynamic_update_slice_in_dim(grad_kv, kv_piece, blk_index * KBLK, 0)
            return (grad_query, grad_kv)

        return lax.cond(needed(blk_index), grad_do_block, unchanged, state_acc)

    grad_query, grad_kv = lax.fori_loop(
        0,
        block_count,
        grad_step,
        (
            jnp.zeros((tok_rows, KVH, q_per_kv, HD), jnp.float32),
            jnp.zeros((seq_len, 2 * KW), jnp.float32),
        ),
    )
    own_kv = lax.psum_scatter(grad_kv, "shard", scatter_dimension=0, tiled=True)
    neg_sines = -sines
    grad_q_raw = rotate(grad_query.reshape(tok_rows, QW), QH, cosines, neg_sines)
    grad_k_raw = rotate(own_kv[:, :KW], KVH, cosines, neg_sines)
    grad_qkv = jnp.concatenate([grad_q_raw, grad_k_raw, own_kv[:, KW:]], axis=1).astype(
        jnp.bfloat16
    )
    g_attn = jnp.dot(h_low.T, grad_qkv, preferred_element_type=jnp.float32)
    grad_h_attn = jnp.dot(grad_qkv, b_attn.T, preferred_element_type=jnp.float32)
    grad_gated, g_gated_gain = norm_back(grad_normed, gated, r_gate, gated_gain)
    grad_y = (grad_gated * silu_z).reshape(tok_rows, NH, HP)
    grad_z = grad_gated * ssm_y * dsilu(gate_z)

    def mamba_out(state_start, x_vals, b_vals, c_vals, dt_vals, la_vals, skip_vals):
        y_zero, state_local = ssd_spans(
            empty_state, x_vals, b_vals, c_vals, dt_vals, la_vals, skip_vals, seg_ids, before
        )
        fac_vals = carry_factor(la_vals)
        return (
            y_zero + carry_term(state_start, c_vals, fac_vals),
            state_local + state_start * fac_vals[-1][:, None, None],
        )

    unused_out, pull_back = jax.vjp(
        mamba_out, state_in, ssm_x, ssm_b, ssm_c, step_size, log_decay, skip_scale
    )
    first_pull = pull_back((grad_y, jnp.zeros_like(state_in)))
    later_state, unused_later = entering(
        (first_pull[0], dev_decay),
        "shard",
        combine_states,
        (jnp.zeros_like(state_in), jnp.ones_like(dev_decay)),
    )
    second = pull_back((jnp.zeros_like(grad_y), later_state))
    grad_x = first_pull[1] + second[1]
    grad_b = first_pull[2] + second[2]
    grad_c = first_pull[3] + second[3]
    grad_dt = first_pull[4] + second[4]
    grad_la = first_pull[5] + second[5]
    g_skip = first_pull[6] + second[6]
    g_a_log = jnp.sum(-grad_la * step_size * decay_rate, axis=0)
    grad_soft = (grad_dt - grad_la * decay_rate) * jax.nn.sigmoid(soft_in)
    g_dt_bias = jnp.sum(grad_soft, axis=0)
    grad_act = jnp.concatenate([grad_x.reshape(tok_rows, DS), grad_b, grad_c], axis=1)
    grad_conv = grad_act * dsilu(conv_pre)
    g_conv_bias = jnp.sum(grad_conv, axis=0)
    grad_padded = jnp.zeros((tok_rows + KC - 1, CONV_CH), jnp.float32)
    weight_cols = []
    for tap_index in range(KC):
        term_vals = grad_conv * tap_masks[tap_index]
        grad_padded = grad_padded + jnp.pad(
            term_vals * conv_weight[:, tap_index][None, :],
            ((tap_index, KC - 1 - tap_index), (0, 0)),
        )
        weight_cols.append(jnp.sum(term_vals * padded[tap_index : tap_index + tok_rows], axis=0))
    g_conv_weight = jnp.stack(weight_cols, axis=1)
    back_edge = from_behind(grad_padded[: KC - 1], "shard", -1)
    grad_xbc = grad_padded[KC - 1 :] + jnp.concatenate(
        [jnp.zeros((tok_rows - (KC - 1), CONV_CH), jnp.float32), back_edge], axis=0
    )
    grad_proj = jnp.concatenate([grad_z, grad_xbc, grad_soft], axis=1).astype(jnp.bfloat16)
    g_in = jnp.dot(h_low.T, grad_proj, preferred_element_type=jnp.float32)
    grad_h = jnp.dot(grad_proj, b_in.T, preferred_element_type=jnp.float32) + grad_h_attn
    grad_x_n, g_norm_one = norm_back(grad_h, x_full, r_one, norm_one)
    grad_input = grad_res + grad_x_n
    owned_grads = (
        lax.psum_scatter(g_in, "shard", scatter_dimension=0, tiled=True),
        lax.psum_scatter(g_attn, "shard", scatter_dimension=0, tiled=True),
        lax.psum_scatter(g_mo, "shard", scatter_dimension=0, tiled=True),
        lax.psum_scatter(g_ao, "shard", scatter_dimension=0, tiled=True),
        lax.psum_scatter(g_gu, "shard", scatter_dimension=0, tiled=True),
        lax.psum_scatter(g_down, "shard", scatter_dimension=0, tiled=True),
    )
    summed = lax.psum(
        (
            owned_grads[0],
            owned_grads[1],
            owned_grads[2],
            owned_grads[3],
            owned_grads[4],
            owned_grads[5],
        ),
        "replica",
    )
    small_sums = lax.psum(
        (
            g_norm_one,
            g_conv_weight,
            g_conv_bias,
            g_dt_bias,
            g_a_log,
            g_skip,
            g_gated_gain,
            g_norm_two,
            stat_local,
        ),
        ("replica", "shard"),
    )
    stat_sums = small_sums[8]
    rms_stats = jnp.sqrt(stat_sums[:3] / (stat_sums[3] * D))
    return (
        out_full.astype(jnp.bfloat16),
        grad_input,
        small_sums[0],
        summed[0],
        small_sums[1],
        small_sums[2],
        small_sums[3],
        small_sums[4],
        small_sums[5],
        small_sums[6],
        summed[1],
        summed[2],
        summed[3],
        small_sums[7],
        summed[4],
        summed[5],
        rms_stats,
    )


HEADS_AT = 6
XW = HEADS_AT * HP
LANES = 128
VMEM_BYTES = 48 * 1024 * 1024


def swap(block, bit):
    size = lax.axis_size("shard")
    return lax.ppermute(block, "shard", [(i, i ^ bit) for i in range(size)])


def swap_far(block, bit):
    size = lax.axis_size("replica")
    return lax.ppermute(block, "replica", [(i, i ^ bit) for i in range(size)])


def in_order(own, other, mine, axis):
    first = jnp.where(mine == 0, own, other)
    second = jnp.where(mine == 0, other, own)
    return jnp.stack([first, second], axis=axis)


def dot32(a, b):
    return jnp.dot(a, b, preferred_element_type=jnp.float32)


def dot_t(a, b):
    return lax.dot_general(a, b, (((1,), (1,)), ((), ())), preferred_element_type=jnp.float32)


def t_dot(a, b):
    return lax.dot_general(a, b, (((0,), (0,)), ((), ())), preferred_element_type=jnp.float32)


def exact(a, b, dims=((1,), (0,))):
    return lax.dot_general(
        a, b, (dims, ((), ())), precision=HIGH, preferred_element_type=jnp.float32
    )


def count_starts(starts_ref, where):
    total = (starts_ref[0] <= where).astype(jnp.int32)
    for k in range(1, starts_ref.shape[0]):
        total = total + (starts_ref[k] <= where).astype(jnp.int32)
    return total


def iota(shape, axis):
    return lax.broadcasted_iota(jnp.int32, shape, axis)


def head_spread():
    row, col = iota((LANES, XW), 0), iota((LANES, XW), 1)
    return ((col >= row * HP) & (col < (row + 1) * HP)).astype(jnp.float32)


def span_parts(starts_ref, first, dt, la):
    shape = (SPAN, SPAN)
    row, col = iota(shape, 0), iota(shape, 1)
    seg_row = count_starts(starts_ref, row + first)
    seg_col = count_starts(starts_ref, col + first)
    seen = (seg_row == seg_col) & (row >= col)
    before = count_starts(starts_ref, first - 1)
    last = count_starts(starts_ref, first + SPAN - 1)
    total = exact((row >= col).astype(jnp.float32), la)
    alive = (seg_row == before).astype(jnp.float32)
    carried = jnp.exp(total) * alive
    tail = jnp.exp(total[SPAN - 1 :] - total) * (seg_row == last).astype(jnp.float32)
    return seen, total, total.T, dt.T, carried, tail


def decay_of(seen, total, total_t, h):
    return jnp.exp(jnp.where(seen, total[:, h : h + 1] - total_t[h : h + 1, :], NEG))


def scan_forward_kernel(starts_ref, act_ref, dt_ref, la_ref, skip_ref, y_ref, states_ref):
    spread = head_spread()
    state = jnp.zeros((NS, XW), jnp.float32)
    for k in range(act_ref.shape[0] // SPAN):
        rows = pl.ds(k * SPAN, SPAN)
        x = act_ref[rows, :XW]
        b = act_ref[rows, XW : XW + NS]
        c = act_ref[rows, XW + NS :]
        dt = dt_ref[rows, :]
        seen, total, total_t, dt_t, carried, tail = span_parts(
            starts_ref, k * SPAN, dt, la_ref[rows, :]
        )
        states_ref[k] = state
        inner = exact(c, b, ((1,), (1,)))
        wide = exact(carried, spread)
        y = exact(c, state) * wide + x * skip_ref[...]
        parts = []
        for h in range(HEADS_AT):
            mixing = decay_of(seen, total, total_t, h) * inner * dt_t[h : h + 1, :]
            parts.append(exact(mixing, x[:, h * HP : (h + 1) * HP]))
        y_ref[rows, :] = y + jnp.concatenate(parts, axis=1)
        weighted = x * exact(tail * dt, spread)
        state = state * wide[SPAN - 1 :] + exact(b, weighted, ((0,), (0,)))


def scan_backward_kernel(
    starts_ref, act_ref, dt_ref, la_ref, skip_ref, states_ref, gy_ref,
    gact_ref, gdt_ref, gla_ref, gskip_ref,
):
    spread = head_spread()
    shape = (SPAN, SPAN)
    row, col = iota(shape, 0), iota(shape, 1)
    upper = (col >= row).astype(jnp.float32)
    later = jnp.zeros((NS, XW), jnp.float32)
    skip_sum = jnp.zeros((1, XW), jnp.float32)
    for k in reversed(range(act_ref.shape[0] // SPAN)):
        rows = pl.ds(k * SPAN, SPAN)
        x = act_ref[rows, :XW]
        b = act_ref[rows, XW : XW + NS]
        c = act_ref[rows, XW + NS :]
        dt = dt_ref[rows, :]
        gy = gy_ref[rows, :]
        state = states_ref[k]
        seen, total, total_t, dt_t, carried, tail = span_parts(
            starts_ref, k * SPAN, dt, la_ref[rows, :]
        )
        inner = exact(c, b, ((1,), (1,)))
        wide = exact(carried, spread)
        tail_dt = tail * dt
        wide_tail = exact(tail_dt, spread)
        gy_wide = gy * wide
        ginner = jnp.zeros(shape, jnp.float32)
        out_sum = jnp.zeros(shape, jnp.float32)
        in_sum = jnp.zeros(shape, jnp.float32)
        parts = []
        for h in range(HEADS_AT):
            own = slice(h * HP, (h + 1) * HP)
            decay = decay_of(seen, total, total_t, h)
            product = exact(gy[:, own], x[:, own], ((1,), (1,))) * decay
            scaled = product * dt_t[h : h + 1, :]
            ginner = ginner + scaled
            both = product * inner
            out_sum = out_sum + jnp.where(
                col == h, jnp.sum(scaled * inner, axis=1, keepdims=True), 0.0
            )
            in_sum = in_sum + jnp.where(row == h, jnp.sum(both, axis=0, keepdims=True), 0.0)
            mixing = decay * inner * dt_t[h : h + 1, :]
            parts.append(exact(mixing, gy[:, own], ((0,), (0,))))
        from_later = exact(b, later)
        gx = jnp.concatenate(parts, axis=1) + from_later * wide_tail + gy * skip_ref[...]
        gact_ref[rows, :XW] = gx
        gact_ref[rows, XW : XW + NS] = exact(ginner, c, ((0,), (0,))) + exact(
            x * wide_tail, later, ((1,), (1,))
        )
        gact_ref[rows, XW + NS :] = exact(ginner, b) + exact(gy_wide, state, ((1,), (1,)))
        tail_in = exact(x * from_later, spread, ((1,), (1,)))
        state_out = exact(exact(c, state) * gy_wide, spread, ((1,), (1,)))
        in_col = in_sum.T
        gdt_ref[rows, :] = in_col + tail_in * tail
        moved = tail_in * tail_dt
        kept = exact(
            jnp.sum(state * later, axis=0, keepdims=True) * wide[SPAN - 1 :],
            spread,
            ((1,), (1,)),
        )
        at_end = jnp.sum(moved, axis=0, keepdims=True) + kept
        change = out_sum - in_col * dt + state_out - moved
        gla_ref[rows, :] = exact(upper, change) + at_end
        skip_sum = skip_sum + jnp.sum(gy * x, axis=0, keepdims=True)
        later = later * wide[SPAN - 1 :] + exact(c, gy_wide, ((0,), (0,)))
    gskip_ref[...] = skip_sum


def scores_of(starts_ref, q, keys, first, scale):
    shape = (q.shape[0], keys.shape[0])
    row, col = iota(shape, 0) + first, iota(shape, 1)
    counted = (col <= row) & (
        count_starts(starts_ref, row) == count_starts(starts_ref, col)
    )
    return counted, scale


def attend_forward_kernel(starts_ref, q_ref, kv_ref, out_ref, lse_ref):
    scale = 1.0 / math.sqrt(HD)
    heads = q_ref.shape[1] // HD
    for k in range(q_ref.shape[0] // SPAN):
        rows, reach = pl.ds(k * SPAN, SPAN), (k + 1) * SPAN
        keys, values = kv_ref[:reach, :HD], kv_ref[:reach, HD:]
        counted, _ = scores_of(starts_ref, q_ref[rows, :HD], keys, k * SPAN, scale)
        outs, tops = [], []
        for h in range(heads):
            s = dot_t(q_ref[rows, h * HD : (h + 1) * HD], keys) * scale
            s = jnp.where(counted, s, NEG)
            top = jnp.max(s, axis=1, keepdims=True)
            lse = top + jnp.log(jnp.sum(jnp.exp(s - top), axis=1, keepdims=True))
            prob = jnp.exp(s - lse).astype(jnp.bfloat16)
            outs.append(dot32(prob, values))
            tops.append(lse)
        out_ref[rows, :] = jnp.concatenate(outs, axis=1).astype(jnp.bfloat16)
        lane = iota((SPAN, LANES), 1)
        lse_ref[rows, :] = sum(jnp.where(lane == h, t, 0.0) for h, t in enumerate(tops))


def attend_backward_kernel(starts_ref, q_ref, kv_ref, lse_ref, gout_ref, gq_ref, gkv_ref):
    scale = 1.0 / math.sqrt(HD)
    heads = q_ref.shape[1] // HD
    gkv_ref[...] = jnp.zeros_like(gkv_ref)
    for k in range(q_ref.shape[0] // SPAN):
        rows, reach = pl.ds(k * SPAN, SPAN), (k + 1) * SPAN
        keys, values = kv_ref[:reach, :HD], kv_ref[:reach, HD:]
        counted, _ = scores_of(starts_ref, q_ref[rows, :HD], keys, k * SPAN, scale)
        outs, gkeys, gvalues = [], 0.0, 0.0
        for h in range(heads):
            own = slice(h * HD, (h + 1) * HD)
            q, gout = q_ref[rows, own], gout_ref[rows, own]
            s = dot_t(q, keys) * scale
            pe = jnp.exp(jnp.where(counted, s - lse_ref[rows, h : h + 1], NEG))
            gprob = dot_t(gout, values)
            delta = jnp.sum(pe * gprob, axis=1, keepdims=True)
            gs = (pe * (gprob - delta) * scale).astype(jnp.bfloat16)
            outs.append(dot32(gs, keys))
            gkeys = gkeys + t_dot(gs, q)
            gvalues = gvalues + t_dot(pe.astype(jnp.bfloat16), gout)
        gq_ref[rows, :] = jnp.concatenate(outs, axis=1)
        gkv_ref[:reach, :] += jnp.concatenate([gkeys, gvalues], axis=1)


def local_call(kernel, outs, *operands):
    whole = pl.BlockSpec(memory_space=pltpu.VMEM)
    return pl.pallas_call(
        kernel,
        out_shape=outs,
        in_specs=[pl.BlockSpec(memory_space=pltpu.SMEM)] + [whole] * (len(operands) - 1),
        out_specs=jax.tree.map(lambda _: whole, outs),
        compiler_params=pltpu.CompilerParams(vmem_limit_bytes=VMEM_BYTES),
    )(*operands)


def f32_of(*shape):
    return jax.ShapeDtypeStruct(shape, jnp.float32)


def low_of(*shape):
    return jax.ShapeDtypeStruct(shape, jnp.bfloat16)


def sum_scatter(parts, order):
    place = lax.axis_index("replica")
    left = [4, 2, 1]
    for bit in order:
        axis = left.index(bit)
        left.remove(bit)
        mine = (place // bit) % 2
        kept = lax.dynamic_index_in_dim(parts, mine, axis, False)
        given = lax.dynamic_index_in_dim(parts, 1 - mine, axis, False)
        parts = kept + swap_far(given.astype(jnp.bfloat16), bit).astype(jnp.float32)
    return parts


def gather_far(part, order):
    place = lax.axis_index("replica")
    left = []
    for bit in order[::-1]:
        other = swap_far(part, bit)
        axis = sum(1 for b in left if b > bit)
        left = sorted(left + [bit], reverse=True)
        part = in_order(part, other, (place // bit) % 2, axis)
    return part.reshape((8,) + part.shape[3:])


def sum_rows(grad, order):
    rows, width = grad.shape
    own = sum_scatter(grad.reshape(2, 2, 2, rows // 8, width), order)
    return gather_far(own.astype(jnp.bfloat16), order).reshape(rows, width)


def sum_columns(grad, order, y, c):
    rows, width = grad.shape
    parts = grad.reshape(4, 2, 2, 2, rows // 32, width).transpose(1, 2, 3, 0, 4, 5)
    own = sum_scatter(parts, order).astype(jnp.bfloat16)
    own = own.reshape(2, 2, rows // 32, width)
    kept = lax.dynamic_index_in_dim(own, y, 0, False)
    given = lax.dynamic_index_in_dim(own, 1 - y, 0, False)
    pair = in_order(kept, swap(given, 2), y, 0)
    kept = lax.dynamic_index_in_dim(pair, c, 1, False)
    given = lax.dynamic_index_in_dim(pair, 1 - c, 1, False)
    mine = in_order(kept, swap(given, 1), c, 1).reshape(4, rows // 32, width)
    return gather_far(mine, order).transpose(0, 2, 1, 3).reshape(rows // 4, 4, width)


def by_heads(
    hidden_in, cotangent, doc_starts, valid_mask, norm_one, in_proj, conv_weight, conv_bias,
    dt_bias, a_log, skip_scale, gated_gain, qkv_proj, ssm_out, attn_out, norm_two, gate_up,
    down_proj,
):
    place = lax.axis_index("shard")
    y, c = place // 2, place % 2
    rows = hidden_in.shape[0]
    seq = rows * 4
    starts = doc_starts[0]
    low = jnp.bfloat16

    def whole_tokens(block):
        pair = in_order(block, swap(block, 2), y, 0)
        return in_order(pair, swap(pair, 1), c, 1).reshape((seq,) + block.shape[1:])

    def other_core(pair):
        return in_order(pair, swap(pair, 1), c, 1).reshape((seq,) + pair.shape[2:])

    def pair_sum(partial):
        parts = partial.reshape(2, 2, rows, partial.shape[1])
        kept = lax.dynamic_index_in_dim(parts, c, 1, False)
        given = lax.dynamic_index_in_dim(parts, 1 - c, 1, False)
        chip = kept + swap(given, 1)
        return chip + swap(chip.astype(low), 2).astype(jnp.float32)

    def own_sum(partial):
        parts = partial.reshape(2, 2, rows, partial.shape[1])
        kept = lax.dynamic_index_in_dim(parts, c, 1, False)
        given = lax.dynamic_index_in_dim(parts, 1 - c, 1, False)
        chip = kept + swap(given, 1)
        kept = lax.dynamic_index_in_dim(chip, y, 0, False)
        given = lax.dynamic_index_in_dim(chip, 1 - y, 0, False)
        return kept + swap(given, 2)

    def mine_of(pair):
        return lax.dynamic_index_in_dim(pair, y, 0, False)

    hidden_all = whole_tokens(hidden_in)
    keep = valid_mask.astype(jnp.float32)
    gmlp_own = cotangent * valid_mask.astype(low)[:, None]

    def columns(array, start, chip, width):
        return lax.dynamic_slice_in_dim(array, start + chip * width, width, 1)

    def exchange(core_block, shared):
        def flat(chip):
            block = core_block(chip)
            return jnp.concatenate([block.reshape(block.shape[0], -1)] + shared(chip), axis=1)

        width = core_block(y).shape[2]
        pair = in_order(flat(y), swap(flat(1 - y), 2), y, 0)

        def of_core(core):
            part = lax.dynamic_slice_in_dim(pair, core * width, width, 2)
            return jnp.concatenate([part, pair[:, :, 2 * width :]], axis=2)

        full = in_order(of_core(c), swap(of_core(1 - c), 1), c, 1)
        return full.reshape(4 * pair.shape[1], full.shape[3])

    def cores(block):
        return block.reshape(block.shape[0], 2, -1)

    def first_block(chip):
        return jnp.concatenate(
            [
                cores(columns(in_proj, DS, chip, DS // 2)),
                cores(columns(qkv_proj, 0, chip, QW // 2)),
            ],
            axis=2,
        )

    def first_shared(chip):
        kv = [
            jnp.concatenate(
                [
                    qkv_proj[:, QW + g * HD : QW + (g + 1) * HD],
                    qkv_proj[:, QW + KW + g * HD : QW + KW + (g + 1) * HD],
                ],
                axis=1,
            )
            for g in range(KVH)
        ]
        return [
            jnp.where(chip == 0, kv[0], kv[1]),
            in_proj[:, 2 * DS : 2 * DS + 2 * NS],
            jnp.pad(in_proj[:, DS + CONV_CH :], ((0, 0), (0, LANES - NH))),
        ]

    w_first = exchange(first_block, first_shared)
    w_z = exchange(lambda chip: cores(columns(in_proj, 0, chip, DS // 2)), lambda chip: [])
    gmlp = whole_tokens(gmlp_own)
    w_gu = exchange(
        lambda chip: jnp.concatenate(
            [
                cores(columns(gate_up, 0, chip, FF // 2)),
                cores(columns(gate_up, FF, chip, FF // 2)),
            ],
            axis=2,
        ),
        lambda chip: [],
    )

    x_all = hidden_all.astype(jnp.float32)
    r_one = rms_scale(x_all)
    h_low = (x_all * r_one * norm_one).astype(low)
    proj = dot32(h_low, w_first)
    q_at, kv_at, bc_at, dt_at = XW, XW + QW // 4, XW + QW // 4 + LANES, XW + QW // 4 + 3 * LANES
    gate_z = dot32(h_low, w_z)

    xbc = jnp.concatenate([proj[:, :XW], proj[:, bc_at:dt_at]], axis=1)
    positions = jnp.arange(seq, dtype=jnp.int32)
    seg = segment_of(positions, starts)
    taps = jnp.concatenate(
        [
            lax.dynamic_slice_in_dim(conv_weight, place * XW, XW, 0),
            conv_weight[DS:],
        ],
        axis=0,
    ).T
    bias = jnp.concatenate([lax.dynamic_slice_in_dim(conv_bias, place * XW, XW, 0), conv_bias[DS:]])
    masks = [
        (segment_of(positions - (KC - 1 - j), starts) == seg).astype(jnp.float32)[:, None]
        for j in range(KC)
    ]
    padded = jnp.pad(xbc, ((KC - 1, 0), (0, 0)))
    conv_pre = bias[None, :]
    for j in range(KC):
        conv_pre = conv_pre + taps[j][None, :] * padded[j : j + seq] * masks[j]
    act = jax.nn.silu(conv_pre)

    own_head = (iota((LANES, LANES), 0) == iota((LANES, LANES), 1) + place * HEADS_AT) & (
        iota((LANES, LANES), 1) < HEADS_AT
    )
    pick = own_head.astype(jnp.float32)

    def own_heads(vector):
        return lax.dynamic_slice_in_dim(vector, place * HEADS_AT, HEADS_AT, 0)

    def on_lanes(vector):
        return jnp.pad(own_heads(vector), (0, LANES - HEADS_AT))

    real = (jnp.arange(LANES) < HEADS_AT).astype(jnp.float32)[None, :]
    soft_in = exact(proj[:, dt_at:], pick) + on_lanes(dt_bias)[None, :]
    step = jax.nn.softplus(soft_in) * real
    rate = jnp.exp(on_lanes(a_log))[None, :]
    log_decay = -step * rate
    skip_wide = jnp.repeat(own_heads(skip_scale), HP)[None, :]

    ssm_y, states = local_call(
        scan_forward_kernel,
        (f32_of(seq, XW), f32_of(seq // SPAN, NS, XW)),
        starts, act, step, log_decay, skip_wide,
    )
    silu_z = jax.nn.silu(gate_z)
    gated = ssm_y * silu_z

    def shard_sum(rows_of):
        chip = rows_of + swap(rows_of, 1)
        return chip + swap(chip, 2)

    square = shard_sum(jnp.sum(gated * gated, axis=1).reshape(seq // LANES, LANES))
    r_gate = lax.rsqrt(square.reshape(seq, 1) / DS + EPS)
    gain = lax.dynamic_slice_in_dim(gated_gain, place * XW, XW, 0)[None, :]
    normed = (gated * r_gate * gain).astype(low)

    freqs = ROPE_BASE ** (-(jnp.arange(HD // 2).astype(jnp.float32) * 2.0) / HD)
    angles = positions.astype(jnp.float32)[:, None] * jnp.tile(freqs, LANES // (HD // 2))[None, :]
    cosines, sines = jnp.cos(angles), jnp.sin(angles)
    row, col = iota((LANES, LANES), 0), iota((LANES, LANES), 1)
    half = HD // 2
    first_half = (col // half) % 2 == 0
    turn = jnp.where(
        first_half, -(row == col + half).astype(jnp.float32), (row == col - half).astype(jnp.float32)
    )
    is_key = (jnp.arange(LANES) < HD)[None, :]

    def turned(value, sign):
        return value * cosines + sign * exact(value, turn) * sines

    q_low = turned(proj[:, q_at:kv_at], 1.0).astype(low)
    kv_raw = proj[:, kv_at:bc_at]
    kv_low = jnp.where(is_key, turned(kv_raw, 1.0), kv_raw).astype(low)
    attn, lse = local_call(
        attend_forward_kernel,
        (low_of(seq, QW // 4), f32_of(seq, LANES)),
        starts, q_low, kv_low,
    )

    mixed = pair_sum(dot32(normed, ssm_out) + dot32(attn, attn_out))
    x_pair = lax.dynamic_index_in_dim(x_all.reshape(2, 2, rows, D), c, 1, False)
    residual = x_pair + mixed
    r_two = rms_scale(residual)
    h2_low = other_core((residual * r_two * norm_two).astype(low))
    gate_vals = dot32(h2_low, w_gu)
    gate_part, up_part = gate_vals[:, : FF // 4], gate_vals[:, FF // 4 :]
    hid = (jax.nn.silu(gate_part) * up_part).astype(low)
    mlp_partial = dot32(hid, down_proj)

    ghid = dot_t(gmlp, down_proj)
    ggu = jnp.concatenate(
        [ghid * up_part * dsilu(gate_part), ghid * jax.nn.silu(gate_part)], axis=1
    ).astype(low)
    g_down = t_dot(hid, gmlp)
    g_gu = t_dot(h2_low, ggu)
    gh2 = pair_sum(dot_t(ggu, w_gu))
    gout = lax.dynamic_index_in_dim(gmlp.reshape(2, 2, rows, D), c, 1, False).astype(jnp.float32)
    scaled = gh2 * norm_two
    gres = (
        gout
        + r_two * scaled
        - residual * r_two**3 * jnp.mean(scaled * residual, axis=-1, keepdims=True)
    )
    g_norm_two = jnp.sum(mine_of(gh2) * mine_of(residual) * mine_of(r_two), axis=0)
    gmix = other_core(gres.astype(low))

    mlp_out = own_sum(mlp_partial)
    mixed_own = mine_of(mixed)
    out_full = mine_of(residual) + mlp_out
    stats = jnp.stack(
        [
            jnp.sum(keep * jnp.sum(out_full * out_full, axis=1)),
            jnp.sum(keep * jnp.sum(mixed_own * mixed_own, axis=1)),
            jnp.sum(keep * jnp.sum(mlp_out * mlp_out, axis=1)),
            jnp.sum(keep),
        ]
    )

    g_mo = t_dot(normed, gmix)
    g_ao = t_dot(attn, gmix)
    gnormed = dot_t(gmix, ssm_out)
    gattn = dot_t(gmix, attn_out).astype(low)

    uu = gnormed * gain
    mean_uv = shard_sum(jnp.sum(uu * gated, axis=1).reshape(seq // LANES, LANES)) / DS
    ggz = r_gate * uu - gated * r_gate**3 * mean_uv.reshape(seq, 1)
    g_gain = jnp.sum(gnormed * gated * r_gate, axis=0)
    gy = ggz * silu_z
    gzz = (ggz * ssm_y * dsilu(gate_z)).astype(low)

    gq_rot, gkv_part = local_call(
        attend_backward_kernel,
        (f32_of(seq, QW // 4), f32_of(seq, LANES)),
        starts, q_low, kv_low, lse, gattn,
    )
    gkv_rot = gkv_part + swap(gkv_part, 1)
    gq = turned(gq_rot, -1.0).astype(low)
    mine_kv = is_key == (c == 0)
    gkv = jnp.where(is_key, turned(gkv_rot, -1.0), gkv_rot)
    gkv = jnp.where(mine_kv, gkv, 0.0).astype(low)

    gact, gdt, gla, gskip = local_call(
        scan_backward_kernel,
        (f32_of(seq, XW + 2 * NS), f32_of(seq, LANES), f32_of(seq, LANES), f32_of(1, XW)),
        starts, act, step, log_decay, skip_wide, states, gy,
    )
    g_skip = jnp.sum(gskip.reshape(HEADS_AT, HP), axis=1)
    g_a_log = jnp.sum(-gla * step * rate, axis=0)[:HEADS_AT]
    gsoft = (gdt - gla * rate) * jax.nn.sigmoid(soft_in) * real
    g_dt_bias = jnp.sum(gsoft, axis=0)[:HEADS_AT]
    gdr = exact(gsoft, pick, ((1,), (1,))).astype(low)

    gbc = gact[:, XW:].reshape(seq, 2, NS)
    kept = lax.dynamic_index_in_dim(gbc, c, 1, False)
    given = lax.dynamic_index_in_dim(gbc, 1 - c, 1, False)
    gbc = kept + swap(given, 1)
    gbc = gbc + swap(gbc, 2)

    def own_channels(array, axis):
        return jnp.concatenate(
            [
                lax.slice_in_dim(array, 0, XW, axis=axis),
                lax.dynamic_slice_in_dim(array, XW + c * NS, NS, axis),
            ],
            axis=axis,
        )

    taps_own = own_channels(taps, 1)
    gconv = jnp.concatenate([gact[:, :XW], gbc], axis=1) * dsilu(own_channels(conv_pre, 1))
    g_conv_bias = jnp.sum(gconv, axis=0)
    padded_own = own_channels(padded, 1)
    gxbc = jnp.zeros((seq + KC - 1, XW + NS), jnp.float32)
    weight_rows = []
    for j in range(KC):
        term = gconv * masks[j]
        gxbc = gxbc + jnp.pad(term * taps_own[j][None, :], ((j, KC - 1 - j), (0, 0)))
        weight_rows.append(jnp.sum(term * padded_own[j : j + seq], axis=0))
    g_taps = jnp.stack(weight_rows, axis=0)
    gxbc = gxbc[KC - 1 :].astype(low)

    once = jnp.where(y == 0, gxbc[:, XW:], 0.0).astype(low)
    gbc_wide = jnp.concatenate(
        [jnp.where(c == 0, once, 0).astype(low), jnp.where(c == 1, once, 0).astype(low)], axis=1
    )
    gfirst = jnp.concatenate([gxbc[:, :XW], gq, gkv, gbc_wide, gdr], axis=1)
    gh = own_sum(dot_t(gfirst, w_first) + dot_t(gzz, w_z))
    x_full = hidden_in.astype(jnp.float32)
    r_own = rms_scale(x_full)
    gx_n, g_norm_one = norm_back(gh, x_full, r_own, norm_one)
    grad_input = mine_of(gres) + gx_n

    up_first, out_first = (1, 2, 4), (2, 4, 1)
    s_gu = sum_columns(g_gu, up_first, y, c)
    s_down = sum_rows(g_down, out_first)
    s_mid = sum_rows(jnp.concatenate([g_mo, g_ao], axis=0).reshape(-1, D), up_first)
    early = t_dot(h_low, jnp.concatenate([gzz, gq, gkv], axis=1))
    late = t_dot(h_low, jnp.concatenate([gxbc, gdr], axis=1))
    s_early = sum_columns(early, out_first, y, c)
    s_late = sum_columns(late, up_first, y, c)

    def spread_out(block):
        return block.reshape(block.shape[0], -1)

    gate_grad = spread_out(s_gu[:, :, : FF // 4])
    up_grad = spread_out(s_gu[:, :, FF // 4 :])
    full_gu = jnp.concatenate([gate_grad, up_grad], axis=1).astype(jnp.float32)
    dt_grad = sum(s_late[:, k, XW + NS : XW + NS + NH].astype(jnp.float32) for k in range(4))
    full_in = jnp.concatenate(
        [
            spread_out(s_early[:, :, :XW]).astype(jnp.float32),
            spread_out(s_late[:, :, :XW]).astype(jnp.float32),
            s_late[:, 0, XW : XW + NS].astype(jnp.float32),
            s_late[:, 1, XW : XW + NS].astype(jnp.float32),
            dt_grad,
        ],
        axis=1,
    )
    kv_at = XW + QW // 4
    full_qkv = jnp.concatenate(
        [
            spread_out(s_early[:, :, XW:kv_at]),
            s_early[:, 0, kv_at : kv_at + HD],
            s_early[:, 2, kv_at : kv_at + HD],
            s_early[:, 1, kv_at + HD :],
            s_early[:, 3, kv_at + HD :],
        ],
        axis=1,
    ).astype(jnp.float32)
    s_down = s_down.astype(jnp.float32)
    s_mid = s_mid.astype(jnp.float32)

    def at_heads(vector, width):
        return lax.dynamic_update_slice_in_dim(
            jnp.zeros((width,), jnp.float32), vector, place * vector.shape[0], 0
        )

    def channels(own):
        full = jnp.zeros((own.shape[0], CONV_CH), jnp.float32)
        full = lax.dynamic_update_slice_in_dim(full, own[:, :XW], place * XW, 1)
        shared = jnp.where(y == 0, own[:, XW:], 0.0)
        return lax.dynamic_update_slice_in_dim(full, shared, DS + c * NS, 1)

    conv_grads = channels(jnp.concatenate([g_taps, g_conv_bias[None, :]], axis=0))
    small = lax.psum(
        (
            g_norm_one,
            conv_grads,
            at_heads(g_dt_bias, NH),
            at_heads(g_a_log, NH),
            at_heads(g_skip, NH),
            at_heads(g_gain, DS),
            g_norm_two,
            stats,
        ),
        ("replica", "shard"),
    )
    totals = small[7]
    return (
        out_full.astype(low),
        grad_input,
        small[0],
        full_in,
        small[1][:KC].T,
        small[1][KC],
        small[2],
        small[3],
        small[4],
        small[5],
        full_qkv,
        s_mid[: DS // 4],
        s_mid[DS // 4 :],
        small[6],
        full_gu,
        s_down,
        jnp.sqrt(totals[:3] / (totals[3] * D)),
    )


def fits_heads(mesh):
    return mesh.shape["shard"] == 4 and mesh.shape["replica"] == 8


def solution(mesh):
    return jax.shard_map(
        by_heads if fits_heads(mesh) else on_device,
        mesh=mesh,
        in_specs=(
            P(("replica", "shard"), None),
            P(("replica", "shard"), None),
            P("replica", None),
            P(("replica", "shard")),
            P(),
            P("shard", None),
            P(),
            P(),
            P(),
            P(),
            P(),
            P(),
            P("shard", None),
            P("shard", None),
            P("shard", None),
            P(),
            P("shard", None),
            P("shard", None),
        ),
        out_specs=(
            P(("replica", "shard"), None),
            P(("replica", "shard"), None),
            P(),
            P("shard", None),
            P(),
            P(),
            P(),
            P(),
            P(),
            P(),
            P("shard", None),
            P("shard", None),
            P("shard", None),
            P(),
            P("shard", None),
            P("shard", None),
            P(),
        ),
        check_vma=False,
    )
```

```python
import functools
import math

import jax
import jax.numpy as jnp
from jax import lax
from jax.experimental import pallas as pl
from jax.experimental.pallas import tpu as pltpu
from jax.sharding import PartitionSpec as P

D = 1024
NH = 24
HP = 64
NS = 128
KC = 4
QH = 8
KVH = 2
HD = 64
FF = 2048
SPAN = 128
KBLK = 512
DS = 1536
QW = 512
KW = 128
CONV_CH = 1792


EPS = 1e-05
ROPE_BASE = 100000000000.0
NEG = -1e30
HIGH = lax.Precision.HIGHEST


def from_behind(block, axis, distance):
    devices = range(lax.axis_size(axis))
    route = [(i - distance, i) for i in devices if i - distance in devices]
    return lax.ppermute(block, axis, route)


def carried_in(part, axis, combine, identity):
    place = lax.axis_index(axis)
    gathered = jax.tree.map(lambda a: lax.all_gather(a, axis), part)
    state = jax.tree.map(lambda a, e: jnp.zeros_like(a) + jnp.asarray(e, a.dtype), part, identity)

    def one(step, state):
        return combine(
            state, jax.tree.map(lambda a: lax.dynamic_index_in_dim(a, step, 0, False), gathered)
        )

    return lax.fori_loop(0, place, one, state)


def entering(value, axis, combine, identity):
    size, mine = (lax.axis_size(axis), lax.axis_index(axis))
    everything = jax.tree.map(
        lambda part, kind: lax.all_gather(part.astype(kind), axis),
        value,
        jax.tree.map(lambda a: jnp.bfloat16 if a.dtype == jnp.float32 else a.dtype, value),
    )
    start = jax.tree.map(
        lambda part, zero: jnp.broadcast_to(jnp.asarray(zero, part.dtype), part.shape),
        value,
        identity,
    )

    def step(k, before):
        at = size - 1 - k
        reached = at > mine
        new = combine(
            before, jax.tree.map(lambda part, own: part[at].astype(own.dtype), everything, value)
        )
        return jax.tree.map(lambda a, b: jnp.where(reached, a, b), new, before)

    return lax.fori_loop(0, size, step, start)


def rms_scale(tensor):
    return lax.rsqrt(jnp.mean(tensor * tensor, axis=-1, keepdims=True) + EPS)


def rope_tables(positions):
    freqs = ROPE_BASE ** (-(jnp.arange(HD // 2).astype(jnp.float32) * 2.0) / HD)
    angles = positions.astype(jnp.float32)[:, None] * freqs[None, :]
    return (jnp.cos(angles), jnp.sin(angles))


def rotate(tensor, heads, cosines, sines):
    shaped = tensor.reshape(tensor.shape[0], heads, HD)
    first_half = shaped[:, :, : HD // 2]
    second_half = shaped[:, :, HD // 2 :]
    cos_b = cosines[:, None, :]
    sin_b = sines[:, None, :]
    turned = jnp.concatenate(
        [first_half * cos_b - second_half * sin_b, second_half * cos_b + first_half * sin_b],
        axis=-1,
    )
    return turned.reshape(tensor.shape[0], heads * HD)


def segment_of(positions, starts_row):
    return jnp.sum((starts_row[None, :] <= positions[:, None]).astype(jnp.int32), axis=1) - 1


def norm_back(grad_out, tensor, scale_rows, gain):
    scaled = grad_out * gain
    grad_in = scale_rows * scaled - tensor * scale_rows**3 * jnp.mean(
        scaled * tensor, axis=-1, keepdims=True
    )
    return (grad_in, jnp.sum(grad_out * tensor * scale_rows, axis=0))


def dsilu(tensor):
    sig_part = jax.nn.sigmoid(tensor)
    return sig_part * (1.0 + tensor * (1.0 - sig_part))


def combine_states(earlier, later):
    return (earlier[0] * later[1][:, None, None] + later[0], earlier[1] * later[1])


def ssd_spans(state, ssm_x, ssm_b, ssm_c, step_size, log_decay, skip_scale, seg_ids, before):
    count = ssm_x.shape[0] // SPAN
    prev_seg = jnp.concatenate([before.reshape(1), seg_ids[:-1]])

    def by_span(tensor):
        return tensor.reshape((count, SPAN) + tensor.shape[1:])

    def span_step(state_acc, pieces):
        x_c, b_c, c_c, dt_c, la_c, s_c, p_c = pieces
        cum_decay = jnp.cumsum(la_c, axis=0)
        order = jnp.arange(SPAN)
        same_mask = (s_c[:, None] == s_c[None, :]) & (order[:, None] >= order[None, :])
        differ = cum_decay.T[:, :, None] - cum_decay.T[:, None, :]
        decay_mat = jnp.exp(jnp.where(same_mask[None], differ, NEG))
        inner = jnp.dot(c_c, b_c.T, precision=HIGH)
        mixing = decay_mat * inner[None] * dt_c.T[:, None, :]
        y_inner = jnp.einsum("hpq,qhd->phd", mixing, x_c, precision=HIGH)
        alive = (s_c == p_c[0]).astype(jnp.float32)
        carried = jnp.exp(cum_decay) * alive[:, None]
        y_state = jnp.einsum("hdn,pn->phd", state_acc, c_c, precision=HIGH) * carried[:, :, None]
        y_span = y_inner + y_state + skip_scale[None, :, None] * x_c
        tail_w = (
            jnp.exp(cum_decay[-1][None, :] - cum_decay)
            * (s_c == s_c[-1]).astype(jnp.float32)[:, None]
            * dt_c
        )
        new_state = state_acc * carried[-1][:, None, None] + jnp.einsum(
            "qh,qhd,qn->hdn", tail_w, x_c, b_c, precision=HIGH
        )
        return (new_state, y_span)

    final_state, ys = lax.scan(
        span_step,
        state,
        (
            by_span(ssm_x),
            by_span(ssm_b),
            by_span(ssm_c),
            by_span(step_size),
            by_span(log_decay),
            by_span(seg_ids),
            by_span(prev_seg),
        ),
    )
    return (ys.reshape(ssm_x.shape), final_state)


def on_device(
    hidden_in,
    cotangent,
    doc_starts,
    valid_mask,
    norm_one,
    in_proj,
    conv_weight,
    conv_bias,
    dt_bias,
    a_log,
    skip_scale,
    gated_gain,
    qkv_proj,
    ssm_out,
    attn_out,
    norm_two,
    gate_up,
    down_proj,
):
    tok_rows = hidden_in.shape[0]
    shard_count = lax.axis_size("shard")
    offset = lax.axis_index("shard") * tok_rows
    seq_len = tok_rows * shard_count
    score_scale = 1.0 / math.sqrt(HD)
    q_per_kv = QH // KVH
    starts_row = doc_starts[0]
    positions = offset + jnp.arange(tok_rows, dtype=jnp.int32)
    seg_ids = segment_of(positions, starts_row)
    before = segment_of(positions[:1] - 1, starts_row)[0]
    first_start = jnp.max(jnp.where(starts_row <= positions[0], starts_row, 0))
    last_pos = positions[-1]
    full_weights = (
        lax.all_gather(in_proj, "shard", axis=0, tiled=True),
        lax.all_gather(qkv_proj, "shard", axis=0, tiled=True),
        lax.all_gather(ssm_out, "shard", axis=0, tiled=True),
        lax.all_gather(attn_out, "shard", axis=0, tiled=True),
        lax.all_gather(gate_up, "shard", axis=0, tiled=True),
        lax.all_gather(down_proj, "shard", axis=0, tiled=True),
    )
    f_in, f_attn, f_mo, f_ao, f_gu, f_down = full_weights
    x_full = hidden_in.astype(jnp.float32)
    r_one = rms_scale(x_full)
    h_low = (x_full * r_one * norm_one).astype(jnp.bfloat16)
    proj_out = jnp.dot(h_low, f_in, preferred_element_type=jnp.float32)
    gate_z = proj_out[:, :DS]
    xbc = proj_out[:, DS : DS + CONV_CH]
    dt_raw = proj_out[:, DS + CONV_CH :]
    edge_rows = from_behind(xbc[tok_rows - (KC - 1) :], "shard", 1)
    padded = jnp.concatenate([edge_rows, xbc], axis=0)
    pad_pos = positions[0] - (KC - 1) + jnp.arange(tok_rows + KC - 1, dtype=jnp.int32)
    pad_seg = segment_of(pad_pos, starts_row)
    tap_masks = [
        (pad_seg[tap_index : tap_index + tok_rows] == seg_ids).astype(jnp.float32)[:, None]
        for tap_index in range(KC)
    ]
    conv_pre = jnp.zeros((tok_rows, CONV_CH), jnp.float32) + conv_bias[None, :]
    for tap_index in range(KC):
        conv_pre = (
            conv_pre
            + conv_weight[:, tap_index][None, :]
            * padded[tap_index : tap_index + tok_rows]
            * tap_masks[tap_index]
        )
    conv_act = jax.nn.silu(conv_pre)
    ssm_x = conv_act[:, :DS].reshape(tok_rows, NH, HP)
    ssm_b = conv_act[:, DS : DS + NS]
    ssm_c = conv_act[:, DS + NS :]
    soft_in = dt_raw + dt_bias
    step_size = jax.nn.softplus(soft_in)
    decay_rate = jnp.exp(a_log)
    log_decay = -step_size * decay_rate
    empty_state = jnp.zeros((NH, HP, NS), jnp.float32)

    def carry_factor(log_vals):
        return (
            jnp.exp(jnp.cumsum(log_vals, axis=0)) * (seg_ids == before).astype(jnp.float32)[:, None]
        )

    def carry_term(state_in, c_vals, factor):
        return jnp.einsum("hdn,pn->phd", state_in, c_vals, precision=HIGH) * factor[:, :, None]

    ssm_zero, local_state = ssd_spans(
        empty_state, ssm_x, ssm_b, ssm_c, step_size, log_decay, skip_scale, seg_ids, before
    )
    factor = carry_factor(log_decay)
    dev_decay = factor[-1]
    state_in, unused_decay = carried_in(
        (local_state, dev_decay),
        "shard",
        combine_states,
        (jnp.zeros_like(local_state), jnp.ones_like(dev_decay)),
    )
    ssm_y = (ssm_zero + carry_term(state_in, ssm_c, factor)).reshape(tok_rows, DS)
    silu_z = jax.nn.silu(gate_z)
    gated = ssm_y * silu_z
    r_gate = rms_scale(gated)
    normed_low = (gated * r_gate * gated_gain).astype(jnp.bfloat16)
    qkv = jnp.dot(h_low, f_attn, preferred_element_type=jnp.float32)
    cosines, sines = rope_tables(positions)
    q_low = (
        rotate(qkv[:, :QW], QH, cosines, sines)
        .astype(jnp.bfloat16)
        .reshape(tok_rows, KVH, q_per_kv, HD)
    )
    k_low = rotate(qkv[:, QW : QW + KW], KVH, cosines, sines).astype(jnp.bfloat16)
    v_low = qkv[:, QW + KW :].astype(jnp.bfloat16)
    key_all, value_all = (
        lax.all_gather(k_low, "shard", axis=0, tiled=True),
        lax.all_gather(v_low, "shard", axis=0, tiled=True),
    )
    key_all = key_all.reshape(seq_len, KVH, HD)
    value_all = value_all.reshape(seq_len, KVH, HD)
    key_pos = jnp.arange(seq_len, dtype=jnp.int32)
    key_seg = segment_of(key_pos, starts_row)
    block_count = seq_len // KBLK
    row_shape = (KVH, q_per_kv, tok_rows)

    def needed(blk_index):
        low_edge = blk_index * KBLK
        return (low_edge <= last_pos) & (low_edge + KBLK > first_start)

    def block_keys(blk_index):
        return (
            lax.dynamic_slice_in_dim(key_all, blk_index * KBLK, KBLK, 0),
            lax.dynamic_slice_in_dim(value_all, blk_index * KBLK, KBLK, 0),
        )

    def block_scores(blk_index, k_blk):
        pos_blk = lax.dynamic_slice_in_dim(key_pos, blk_index * KBLK, KBLK, 0)
        seg_blk = lax.dynamic_slice_in_dim(key_seg, blk_index * KBLK, KBLK, 0)
        raw_scores = (
            jnp.einsum("tgqd,kgd->gqtk", q_low, k_blk, preferred_element_type=jnp.float32)
            * score_scale
        )
        key_mask = (pos_blk[None, :] <= positions[:, None]) & (seg_blk[None, :] == seg_ids[:, None])
        return (raw_scores, key_mask[None, None])

    def unchanged(passed):
        return passed

    def lse_step(blk_index, state_acc):

        def lse_do_block(state_acc):
            row_top, row_total = state_acc
            k_blk, v_blk = block_keys(blk_index)
            raw_scores, key_mask = block_scores(blk_index, k_blk)
            new_top = jnp.maximum(row_top, jnp.max(jnp.where(key_mask, raw_scores, NEG), axis=-1))
            row_total = row_total * jnp.exp(row_top - new_top) + jnp.sum(
                jnp.where(key_mask, jnp.exp(raw_scores - new_top[..., None]), 0.0), axis=-1
            )
            return (new_top, row_total)

        return lax.cond(needed(blk_index), lse_do_block, unchanged, state_acc)

    row_top, row_total = lax.fori_loop(
        0,
        block_count,
        lse_step,
        (jnp.full(row_shape, NEG, jnp.float32), jnp.zeros(row_shape, jnp.float32)),
    )
    log_total = row_top + jnp.log(row_total)

    def probs_of(blk_index, k_blk):
        raw_scores, key_mask = block_scores(blk_index, k_blk)
        return jnp.where(key_mask, jnp.exp(raw_scores - log_total[..., None]), 0.0)

    def out_step(blk_index, acc_out):

        def out_do_block(acc_out):
            k_blk, v_blk = block_keys(blk_index)
            prob_blk = probs_of(blk_index, k_blk).astype(jnp.bfloat16)
            return acc_out + jnp.einsum(
                "gqtk,kgd->tgqd", prob_blk, v_blk, preferred_element_type=jnp.float32
            )

        return lax.cond(needed(blk_index), out_do_block, unchanged, acc_out)

    attended = lax.fori_loop(
        0, block_count, out_step, jnp.zeros((tok_rows, KVH, q_per_kv, HD), jnp.float32)
    )
    attn_low = attended.reshape(tok_rows, QW).astype(jnp.bfloat16)
    mixed = jnp.dot(normed_low, f_mo, preferred_element_type=jnp.float32) + jnp.dot(
        attn_low, f_ao, preferred_element_type=jnp.float32
    )
    residual = x_full + mixed
    r_two = rms_scale(residual)
    h2_low = (residual * r_two * norm_two).astype(jnp.bfloat16)
    gate_vals = jnp.dot(h2_low, f_gu, preferred_element_type=jnp.float32)
    gate_part = gate_vals[:, :FF]
    up_part = gate_vals[:, FF:]
    hid_low = (jax.nn.silu(gate_part) * up_part).astype(jnp.bfloat16)
    mlp_out = jnp.dot(hid_low, f_down, preferred_element_type=jnp.float32)
    out_full = residual + mlp_out
    keep_rows = valid_mask.astype(jnp.float32)
    stat_local = jnp.stack(
        [
            jnp.sum(keep_rows * jnp.sum(out_full * out_full, axis=1)),
            jnp.sum(keep_rows * jnp.sum(mixed * mixed, axis=1)),
            jnp.sum(keep_rows * jnp.sum(mlp_out * mlp_out, axis=1)),
            jnp.sum(keep_rows),
        ]
    )
    back_weights = (
        lax.all_gather(in_proj, "shard", axis=0, tiled=True),
        lax.all_gather(qkv_proj, "shard", axis=0, tiled=True),
        lax.all_gather(ssm_out, "shard", axis=0, tiled=True),
        lax.all_gather(attn_out, "shard", axis=0, tiled=True),
        lax.all_gather(gate_up, "shard", axis=0, tiled=True),
        lax.all_gather(down_proj, "shard", axis=0, tiled=True),
    )
    b_in, b_attn, b_mo, b_ao, b_gu, b_down = back_weights
    grad_out = cotangent.astype(jnp.float32) * keep_rows[:, None]
    grad_mlp = grad_out.astype(jnp.bfloat16)
    g_down = jnp.dot(hid_low.T, grad_mlp, preferred_element_type=jnp.float32)
    grad_hid = jnp.dot(grad_mlp, b_down.T, preferred_element_type=jnp.float32)
    grad_gu = jnp.concatenate(
        [grad_hid * up_part * dsilu(gate_part), grad_hid * jax.nn.silu(gate_part)], axis=1
    ).astype(jnp.bfloat16)
    g_gu = jnp.dot(h2_low.T, grad_gu, preferred_element_type=jnp.float32)
    grad_h2 = jnp.dot(grad_gu, b_gu.T, preferred_element_type=jnp.float32)
    grad_res_n, g_norm_two = norm_back(grad_h2, residual, r_two, norm_two)
    grad_res = grad_out + grad_res_n
    grad_mix = grad_res.astype(jnp.bfloat16)
    g_mo = jnp.dot(normed_low.T, grad_mix, preferred_element_type=jnp.float32)
    g_ao = jnp.dot(attn_low.T, grad_mix, preferred_element_type=jnp.float32)
    grad_normed = jnp.dot(grad_mix, b_mo.T, preferred_element_type=jnp.float32)
    grad_attn = (
        jnp.dot(grad_mix, b_ao.T, preferred_element_type=jnp.float32)
        .astype(jnp.bfloat16)
        .reshape(tok_rows, KVH, q_per_kv, HD)
    )

    def delta_step(blk_index, acc_out):

        def delta_do_block(acc_out):
            k_blk, v_blk = block_keys(blk_index)
            prob_blk = probs_of(blk_index, k_blk)
            grad_prob = jnp.einsum(
                "tgqd,kgd->gqtk", grad_attn, v_blk, preferred_element_type=jnp.float32
            )
            return acc_out + jnp.sum(prob_blk * grad_prob, axis=-1)

        return lax.cond(needed(blk_index), delta_do_block, unchanged, acc_out)

    delta_row = lax.fori_loop(0, block_count, delta_step, jnp.zeros(row_shape, jnp.float32))

    def grad_step(blk_index, state_acc):

        def grad_do_block(state_acc):
            grad_query, grad_kv = state_acc
            k_blk, v_blk = block_keys(blk_index)
            prob_blk = probs_of(blk_index, k_blk)
            grad_prob = jnp.einsum(
                "tgqd,kgd->gqtk", grad_attn, v_blk, preferred_element_type=jnp.float32
            )
            grad_raw = (prob_blk * (grad_prob - delta_row[..., None]) * score_scale).astype(
                jnp.bfloat16
            )
            grad_query = grad_query + jnp.einsum(
                "gqtk,kgd->tgqd", grad_raw, k_blk, preferred_element_type=jnp.float32
            )
            grad_key = jnp.einsum(
                "gqtk,tgqd->kgd", grad_raw, q_low, preferred_element_type=jnp.float32
            )
            grad_value = jnp.einsum(
                "gqtk,tgqd->kgd",
                prob_blk.astype(jnp.bfloat16),
                grad_attn,
                preferred_element_type=jnp.float32,
            )
            kv_piece = jnp.concatenate(
                [grad_key.reshape(KBLK, KW), grad_value.reshape(KBLK, KW)], axis=1
            )
            grad_kv = lax.dynamic_update_slice_in_dim(grad_kv, kv_piece, blk_index * KBLK, 0)
            return (grad_query, grad_kv)

        return lax.cond(needed(blk_index), grad_do_block, unchanged, state_acc)

    grad_query, grad_kv = lax.fori_loop(
        0,
        block_count,
        grad_step,
        (
            jnp.zeros((tok_rows, KVH, q_per_kv, HD), jnp.float32),
            jnp.zeros((seq_len, 2 * KW), jnp.float32),
        ),
    )
    own_kv = lax.psum_scatter(grad_kv, "shard", scatter_dimension=0, tiled=True)
    neg_sines = -sines
    grad_q_raw = rotate(grad_query.reshape(tok_rows, QW), QH, cosines, neg_sines)
    grad_k_raw = rotate(own_kv[:, :KW], KVH, cosines, neg_sines)
    grad_qkv = jnp.concatenate([grad_q_raw, grad_k_raw, own_kv[:, KW:]], axis=1).astype(
        jnp.bfloat16
    )
    g_attn = jnp.dot(h_low.T, grad_qkv, preferred_element_type=jnp.float32)
    grad_h_attn = jnp.dot(grad_qkv, b_attn.T, preferred_element_type=jnp.float32)
    grad_gated, g_gated_gain = norm_back(grad_normed, gated, r_gate, gated_gain)
    grad_y = (grad_gated * silu_z).reshape(tok_rows, NH, HP)
    grad_z = grad_gated * ssm_y * dsilu(gate_z)

    def mamba_out(state_start, x_vals, b_vals, c_vals, dt_vals, la_vals, skip_vals):
        y_zero, state_local = ssd_spans(
            empty_state, x_vals, b_vals, c_vals, dt_vals, la_vals, skip_vals, seg_ids, before
        )
        fac_vals = carry_factor(la_vals)
        return (
            y_zero + carry_term(state_start, c_vals, fac_vals),
            state_local + state_start * fac_vals[-1][:, None, None],
        )

    unused_out, pull_back = jax.vjp(
        mamba_out, state_in, ssm_x, ssm_b, ssm_c, step_size, log_decay, skip_scale
    )
    first_pull = pull_back((grad_y, jnp.zeros_like(state_in)))
    later_state, unused_later = entering(
        (first_pull[0], dev_decay),
        "shard",
        combine_states,
        (jnp.zeros_like(state_in), jnp.ones_like(dev_decay)),
    )
    second = pull_back((jnp.zeros_like(grad_y), later_state))
    grad_x = first_pull[1] + second[1]
    grad_b = first_pull[2] + second[2]
    grad_c = first_pull[3] + second[3]
    grad_dt = first_pull[4] + second[4]
    grad_la = first_pull[5] + second[5]
    g_skip = first_pull[6] + second[6]
    g_a_log = jnp.sum(-grad_la * step_size * decay_rate, axis=0)
    grad_soft = (grad_dt - grad_la * decay_rate) * jax.nn.sigmoid(soft_in)
    g_dt_bias = jnp.sum(grad_soft, axis=0)
    grad_act = jnp.concatenate([grad_x.reshape(tok_rows, DS), grad_b, grad_c], axis=1)
    grad_conv = grad_act * dsilu(conv_pre)
    g_conv_bias = jnp.sum(grad_conv, axis=0)
    grad_padded = jnp.zeros((tok_rows + KC - 1, CONV_CH), jnp.float32)
    weight_cols = []
    for tap_index in range(KC):
        term_vals = grad_conv * tap_masks[tap_index]
        grad_padded = grad_padded + jnp.pad(
            term_vals * conv_weight[:, tap_index][None, :],
            ((tap_index, KC - 1 - tap_index), (0, 0)),
        )
        weight_cols.append(jnp.sum(term_vals * padded[tap_index : tap_index + tok_rows], axis=0))
    g_conv_weight = jnp.stack(weight_cols, axis=1)
    back_edge = from_behind(grad_padded[: KC - 1], "shard", -1)
    grad_xbc = grad_padded[KC - 1 :] + jnp.concatenate(
        [jnp.zeros((tok_rows - (KC - 1), CONV_CH), jnp.float32), back_edge], axis=0
    )
    grad_proj = jnp.concatenate([grad_z, grad_xbc, grad_soft], axis=1).astype(jnp.bfloat16)
    g_in = jnp.dot(h_low.T, grad_proj, preferred_element_type=jnp.float32)
    grad_h = jnp.dot(grad_proj, b_in.T, preferred_element_type=jnp.float32) + grad_h_attn
    grad_x_n, g_norm_one = norm_back(grad_h, x_full, r_one, norm_one)
    grad_input = grad_res + grad_x_n
    owned_grads = (
        lax.psum_scatter(g_in, "shard", scatter_dimension=0, tiled=True),
        lax.psum_scatter(g_attn, "shard", scatter_dimension=0, tiled=True),
        lax.psum_scatter(g_mo, "shard", scatter_dimension=0, tiled=True),
        lax.psum_scatter(g_ao, "shard", scatter_dimension=0, tiled=True),
        lax.psum_scatter(g_gu, "shard", scatter_dimension=0, tiled=True),
        lax.psum_scatter(g_down, "shard", scatter_dimension=0, tiled=True),
    )
    summed = lax.psum(
        (
            owned_grads[0],
            owned_grads[1],
            owned_grads[2],
            owned_grads[3],
            owned_grads[4],
            owned_grads[5],
        ),
        "replica",
    )
    small_sums = lax.psum(
        (
            g_norm_one,
            g_conv_weight,
            g_conv_bias,
            g_dt_bias,
            g_a_log,
            g_skip,
            g_gated_gain,
            g_norm_two,
            stat_local,
        ),
        ("replica", "shard"),
    )
    stat_sums = small_sums[8]
    rms_stats = jnp.sqrt(stat_sums[:3] / (stat_sums[3] * D))
    return (
        out_full.astype(jnp.bfloat16),
        grad_input,
        small_sums[0],
        summed[0],
        small_sums[1],
        small_sums[2],
        small_sums[3],
        small_sums[4],
        small_sums[5],
        small_sums[6],
        summed[1],
        summed[2],
        summed[3],
        small_sums[7],
        summed[4],
        summed[5],
        rms_stats,
    )


HEADS_AT = 6
XW = HEADS_AT * HP
LANES = 128
TB = 128
VMEM_BYTES = 20 * 1024 * 1024
AT_Y, AT_CORE, AT_BIT, AT_STARTS = 0, 1, {1: 2, 2: 3, 4: 4}, 5
Q_AT = XW
KV_AT = Q_AT + QW // 4
BC_AT = KV_AT + LANES
DT_AT = BC_AT + 2 * NS
W_FIRST = DT_AT + LANES
LOW = jnp.bfloat16
F32 = jnp.float32


def swap(block, bits):
    return lax.ppermute(block, "shard", [(i, i ^ bits) for i in range(lax.axis_size("shard"))])


def swap_far(block, bit):
    return lax.ppermute(block, "replica", [(i, i ^ bit) for i in range(lax.axis_size("replica"))])


def after(value, other):
    return lax.optimization_barrier((value, other))[0]


def dot32(a, b):
    return jnp.dot(a, b, preferred_element_type=F32)


def dot_t(a, b):
    return lax.dot_general(a, b, (((1,), (1,)), ((), ())), preferred_element_type=F32)


def t_dot(a, b):
    return lax.dot_general(a, b, (((0,), (0,)), ((), ())), preferred_element_type=F32)


def rough(a, b, dims=((1,), (0,))):
    return lax.dot_general(
        a.astype(LOW), b.astype(LOW), (dims, ((), ())), preferred_element_type=F32
    )


def picked(a, b, dims=((1,), (0,)), terms=2):
    value, total = (b, 0.0) if a.dtype == LOW else (a, 0.0)
    for _ in range(terms):
        low = value.astype(LOW)
        pair = (a, low) if a.dtype == LOW else (low, b)
        total = total + lax.dot_general(*pair, (dims, ((), ())), preferred_element_type=F32)
        value = value - low.astype(F32)
    return total


def iota(shape, axis):
    return lax.broadcasted_iota(jnp.int32, shape, axis)


def count_starts(info, where):
    total = (info[AT_STARTS] <= where).astype(jnp.int32)
    for k in range(AT_STARTS + 1, info.shape[0]):
        total = total + (info[k] <= where).astype(jnp.int32)
    return total


def part(index, size):
    return pl.ds(pl.multiple_of(index * size, size), size)


def part_at(start, index, step, size):
    return pl.ds(pl.multiple_of(start + index * step, LANES), size)


def peers(info):
    y, c = info[AT_Y], info[AT_CORE]
    return (2 * y + c, 2 * y + 1 - c, 2 * (1 - y) + c, 2 * (1 - y) + 1 - c)


def f32_of(*shape):
    return jax.ShapeDtypeStruct(shape, F32)


def low_of(*shape):
    return jax.ShapeDtypeStruct(shape, LOW)


def call(kernel, outs, info, *operands, scratch=()):
    whole = pl.BlockSpec(memory_space=pltpu.VMEM)
    return pl.pallas_call(
        kernel,
        out_shape=outs,
        in_specs=[pl.BlockSpec(memory_space=pltpu.SMEM)] + [whole] * len(operands),
        out_specs=jax.tree.map(lambda _: whole, outs),
        scratch_shapes=scratch,
        compiler_params=pltpu.CompilerParams(vmem_limit_bytes=VMEM_BYTES),
    )(info, *operands)


def pack_in_kernel(
    info, w_in, w_qkv, own, core, far, far_core, z_own, z_core, z_far, z_far_core
):
    y = info[AT_Y]

    def shared(dst, chip):
        k, v = w_qkv[:, QW : QW + KW], w_qkv[:, QW + KW :]
        first = jnp.concatenate([k[:, :HD], v[:, :HD]], axis=1)
        second = jnp.concatenate([k[:, HD:], v[:, HD:]], axis=1)
        dst[KV_AT:BC_AT, :] = jnp.where(chip == 0, first, second).T
        dst[BC_AT:DT_AT, :] = w_in[2 * DS : 2 * DS + 2 * NS, :]
        dst[DT_AT:, :] = jnp.zeros((LANES, dst.shape[1]), LOW)
        dst[DT_AT : DT_AT + NH, :] = w_in[DS + CONV_CH :, :]

    for place, dst, z_dst in zip(
        peers(info), (own, core, far, far_core), (z_own, z_core, z_far, z_far_core)
    ):
        dst[:XW, :] = w_in[part_at(DS, place, XW, XW), :]
        dst[Q_AT:KV_AT, :] = w_qkv[:, part(place, QW // 4)].T
        z_dst[...] = w_in[part_at(0, place, XW, XW), :]
    shared(own, y)
    shared(core, y)
    shared(far_core, 1 - y)


def pack_up_kernel(info, w_up, own, core, far):
    quarter, half = FF // 4, w_up.shape[0] // 2
    places = peers(info)
    for place, dst in zip(places, (own, core)):
        dst[:, :quarter] = w_up[:, part_at(0, place, quarter, quarter)]
        dst[:, quarter:] = w_up[:, part_at(FF, place, quarter, quarter)]
    mine = part(info[AT_BIT[1]], half)
    for k, place in enumerate(places[2:]):
        rows = slice(k * half, (k + 1) * half)
        far[rows, :quarter] = w_up[mine, part_at(0, place, quarter, quarter)]
        far[rows, quarter:] = w_up[mine, part_at(FF, place, quarter, quarter)]


def head_spread():
    row, col = iota((LANES, XW), 0), iota((LANES, XW), 1)
    return ((col >= row * HP) & (col < (row + 1) * HP)).astype(LOW)


def own_heads_pick(info):
    row, col = iota((LANES, LANES), 0), iota((LANES, LANES), 1)
    return ((row == col + peers(info)[0] * HEADS_AT) & (col < HEADS_AT)).astype(LOW)


def step_sizes(soft):
    real = iota(soft.shape, 1) < HEADS_AT
    return jnp.where(real, jnp.maximum(soft, 0.0) + jnp.log1p(jnp.exp(-jnp.abs(soft))), 0.0)


def span_parts(info, first, dt, la):
    shape = (SPAN, SPAN)
    row, col = iota(shape, 0), iota(shape, 1)
    seg_row = count_starts(info, row + first)
    seg_col = count_starts(info, col + first)
    seen = (seg_row == seg_col) & (row >= col)
    before = count_starts(info, first - 1)
    last = count_starts(info, first + SPAN - 1)
    total = picked((row >= col).astype(LOW), la, terms=3)
    carried = jnp.exp(total) * (seg_row == before).astype(F32)
    tail = jnp.exp(total[SPAN - 1 :] - total) * (seg_row == last).astype(F32)
    return seen, total, total.T, dt.T, carried, tail


def decay_of(seen, total, total_t, h):
    return jnp.exp(jnp.where(seen, total[:, h : h + 1] - total_t[h : h + 1, :], NEG))


def tap_masks(info, seg):
    seq = seg.shape[0] - 8
    seg[:8, :] = jnp.full((8, LANES), -1, jnp.int32)
    seg[8:, :] = count_starts(info, iota((seq, LANES), 0))
    here = seg[8:, :]
    return [
        (seg[8 - back : 8 - back + seq, :] == here).astype(F32) for back in range(KC - 1, 0, -1)
    ]


def forward_kernel(
    info, h_own, h_core, h_far, h_far_core, w_own, w_core, w_far, w_far_shared, w_far_core,
    norm, taps, bias, dt_bias, rate, skip, cosines, sines, turn,
    h_low, w_full, xbc, conv_pre, soft, q_low, kv_low, y_out, states,
    padded, act, step, seg,
):
    seq = h_low.shape[0]
    places = peers(info)
    for place, ref in zip(places, (h_own, h_core, h_far, h_far_core)):
        x = ref[...].astype(F32)
        h_low[part(place, TB), :] = (x * rms_scale(x) * norm[...]).astype(LOW)
    depth = w_own.shape[1]
    for place, ref in zip(places, (w_own, w_core, w_far, w_far_core)):
        w_full[:KV_AT, part(place, depth)] = ref[:KV_AT, :]
    for place, ref in zip(places, (w_own, w_core, w_far_shared, w_far_core)):
        w_full[KV_AT:, part(place, depth)] = ref[KV_AT:, :]
    h = h_low[...]
    xbc[:, :XW] = dot_t(h, w_full[:XW, :])
    xbc[:, XW:] = dot_t(h, w_full[BC_AT:DT_AT, :])
    rest = dot_t(h, w_full[Q_AT:BC_AT, :])
    q, kv = rest[:, :LANES], rest[:, LANES:]
    soft[...] = picked(dot_t(h, w_full[DT_AT:, :]), own_heads_pick(info), terms=3) + dt_bias[...]

    def turned(value):
        return value * cosines[...] + picked(value, turn[...]) * sines[...]

    q_low[...] = turned(q).astype(LOW)
    kv_low[...] = jnp.where(iota(kv.shape, 1) < HD, turned(kv), kv).astype(LOW)

    width = xbc.shape[1]
    padded[:8, :] = jnp.zeros((8, width), F32)
    padded[8:, :] = xbc[...]
    masks = tap_masks(info, seg)
    for block in range(0, width, LANES):
        lanes = slice(block, block + LANES)
        total = bias[:, lanes] + taps[KC - 1 : KC, lanes] * padded[8:, lanes]
        for j in range(KC - 1):
            start = 8 - (KC - 1 - j)
            total = total + taps[j : j + 1, lanes] * padded[start : start + seq, lanes] * masks[j]
        conv_pre[:, lanes] = total
        act[:, lanes] = total * jax.nn.sigmoid(total)

    step[...] = step_sizes(soft[...])
    spread = head_spread()
    state = jnp.zeros((NS, XW), F32)
    for k in range(seq // SPAN):
        rows = pl.ds(k * SPAN, SPAN)
        x = act[rows, :XW]
        b = act[rows, XW : XW + NS]
        c = act[rows, XW + NS :]
        dt = step[rows, :]
        seen, total, total_t, dt_t, carried, tail = span_parts(
            info, k * SPAN, dt, -dt * rate[...]
        )
        states[k] = state
        inner = rough(c, b, ((1,), (1,)))
        wide = picked(carried, spread)
        y = rough(c, state) * wide + x * skip[...]
        parts = []
        for h in range(HEADS_AT):
            mixing = decay_of(seen, total, total_t, h) * inner * dt_t[h : h + 1, :]
            parts.append(rough(mixing, x[:, h * HP : (h + 1) * HP]))
        y_out[rows, :] = y + jnp.concatenate(parts, axis=1)
        weighted = x * picked(tail * dt, spread)
        state = state * wide[SPAN - 1 :] + rough(b, weighted, ((0,), (0,)))


def gate_kernel(info, h_low, z_own, z_core, z_far, z_far_core, y, z_full, gate_z, square):
    depth = z_own.shape[1]
    for place, ref in zip(peers(info), (z_own, z_core, z_far, z_far_core)):
        z_full[:, part(place, depth)] = ref[...]
    z = dot_t(h_low[...], z_full[...])
    gate_z[...] = z
    gated = y[...] * (z * jax.nn.sigmoid(z))
    square[...] = picked(jnp.ones((8, XW), LOW), gated * gated, ((1,), (1,)))


def column_of(row):
    return jnp.concatenate(
        [row[:, k : k + LANES].T[:, :1] for k in range(0, row.shape[1], LANES)], axis=0
    )


def output_kernel(
    info, sq_a, sq_b, y, gate_z, gain, attn, ssm_out, attn_out, given, kept, normed
):
    z = gate_z[...]
    scale = lax.rsqrt(column_of(sq_a[...] + sq_b[...]) / DS + EPS)
    normed[...] = (y[...] * (z * jax.nn.sigmoid(z)) * scale * gain[...]).astype(LOW)
    c = info[AT_CORE]
    for core, dst in ((1 - c, given), (c, kept)):
        for k in range(2):
            rows = part(2 * k + core, TB)
            dst[k] = dot32(normed[rows, :], ssm_out[...]) + dot32(attn[rows, :], attn_out[...])


def add_kernel(info, kept, moved, chip, low):
    total = kept[...] + moved[...]
    chip[...] = total
    low[...] = total.astype(LOW)


def add_split_kernel(info, kept, moved, mine, given):
    y = info[AT_Y]
    mine[...] = kept[y] + moved[y]
    given[...] = kept[1 - y] + moved[1 - y]


def pair_of(info, own, far, dst):
    y = info[AT_Y]
    dst[y] = own[...]
    dst[1 - y] = far[...]


def second_norm_kernel(
    info, chip, moved, h_own, h_far, norm, keep, residual, h2, mixed_sum, x_pair
):
    pair_of(info, h_own, h_far, x_pair)
    mixed = chip[...] + moved[...].astype(F32)
    total = x_pair[...].astype(F32) + mixed
    residual[...] = total
    h2[...] = (total * rms_scale(total) * norm[...]).astype(LOW)
    mine = (chip[info[AT_Y]] + moved[info[AT_Y]].astype(F32)) * keep[...]
    mixed_sum[...] = jnp.sum(mine * mine, axis=0, keepdims=True)


def mlp_kernel(
    info, h2, h2_core, u_own, u_core, u_y, u_x, u_y_core, u_x_core, g_own, g_core, g_far, g_far_core, w_down,
    given, kept, hid, ggu, h2_cat, gmlp, u_full,
):
    y, quarter = info[AT_Y], FF // 4
    half = 2 * TB
    for k in range(2):
        h2_cat[k * TB : (k + 1) * TB, :] = h2[k]
        h2_cat[half + k * TB : half + (k + 1) * TB, :] = h2_core[k]
    for at, ref in ((y, g_own), (1 - y, g_far), (2 + y, g_core), (3 - y, g_far_core)):
        gmlp[part(at, TB), :] = ref[...]
    depth = u_own.shape[0]
    places, x, piece = peers(info), info[AT_BIT[1]], depth // 2
    u_full[part(places[0], depth), :] = u_own[...]
    u_full[part(places[1], depth), :] = u_core[...]
    for at, ref, ref_core in ((x, u_y, u_y_core), (1 - x, u_x, u_x_core)):
        u_full[part(2 * places[2] + at, piece), :] = ref[:piece, :]
        u_full[part(2 * places[3] + at, piece), :] = ref_core[piece:, :]
    tile = quarter // 2
    for t in range(0, quarter, tile):
        ghid = dot_t(gmlp[...], w_down[t : t + tile, :])
        gate = dot32(h2_cat[...], u_full[:, t : t + tile])
        up = dot32(h2_cat[...], u_full[:, quarter + t : quarter + t + tile])
        sig = jax.nn.sigmoid(gate)
        silu = gate * sig
        hid[:, t : t + tile] = (silu * up).astype(LOW)
        ggu[:, t : t + tile] = (ghid * up * (sig * (1.0 + gate * (1.0 - sig)))).astype(LOW)
        ggu[:, quarter + t : quarter + t + tile] = (ghid * silu).astype(LOW)
    for t in range(0, D, 2 * tile):
        cols = slice(t, t + 2 * tile)
        part_sum = dot_t(ggu[half:, :], u_full[cols, :])
        given[0, :, cols] = part_sum[:TB]
        given[1, :, cols] = part_sum[TB:]
        part_sum = dot_t(ggu[:half, :], u_full[cols, :])
        kept[0, :, cols] = part_sum[:TB]
        kept[1, :, cols] = part_sum[TB:]


def down_kernel(info, hid, w_down, given, kept):
    half = 2 * TB
    for k in range(2):
        given[k] = dot32(hid[half + k * TB : half + (k + 1) * TB, :], w_down[...])
        kept[k] = dot32(hid[k * TB : (k + 1) * TB, :], w_down[...])


def grad_rows_kernel(bit, info, left, right, given, kept):
    mine = info[AT_BIT[bit]]
    half = left.shape[1] // 2
    given[...] = t_dot(left[:, part(1 - mine, half)], right[...]).astype(LOW)
    kept[...] = t_dot(left[:, part(mine, half)], right[...])


def grad_mid_kernel(bit, info, normed, attn, right, given, kept, left):
    left[:, :XW] = normed[...]
    left[:, XW:] = attn[...]
    grad_rows_kernel(bit, info, left, right, given, kept)


def grad_columns_kernel(bit, info, left, right, given, kept):
    mine = info[AT_BIT[bit]]
    step = left.shape[1] // 4
    for k in range(4):
        other = left[:, part_at(k * step, 1 - mine, step // 2, step // 2)]
        given[k] = t_dot(other, right[...]).astype(LOW)
    for k in range(4):
        own = left[:, part_at(k * step, mine, step // 2, step // 2)]
        kept[k] = t_dot(own, right[...])


def norm_back_pair_kernel(info, chip, moved, residual, norm, g_own, g_far, gres, gmix, g_norm, gout):
    pair_of(info, g_own, g_far, gout)
    gh2 = chip[...] + moved[...].astype(F32)
    value = residual[...]
    scale = rms_scale(value)
    uu = gh2 * norm[...]
    mean = jnp.mean(uu * value, axis=-1, keepdims=True)
    grad = gout[...].astype(F32) + scale * uu - value * scale**3 * mean
    gres[...] = grad
    gmix[...] = grad.astype(LOW)
    y = info[AT_Y]
    mine = residual[y]
    g_norm[...] = jnp.sum(
        (chip[y] + moved[y].astype(F32)) * mine * rms_scale(mine), axis=0, keepdims=True
    )


def output_back_kernel(
    info, gmix, gmix_core, y, gate_z, gain, ssm_out, attn_out, gmix_all, gnormed, gattn, uv
):
    c = info[AT_CORE]
    for core, src in ((c, gmix), (1 - c, gmix_core)):
        for k in range(2):
            gmix_all[part(2 * k + core, TB), :] = src[k]
    grad = dot_t(gmix_all[...], ssm_out[...])
    gnormed[...] = grad
    z = gate_z[...]
    product = grad * gain[...] * (y[...] * (z * jax.nn.sigmoid(z)))
    uv[...] = picked(jnp.ones((8, XW), LOW), product, ((1,), (1,)))
    gattn[...] = dot_t(gmix_all[...], attn_out[...]).astype(LOW)


def conv_back(masks, gconv, pre, taps, inputs, gpad):
    seq = gconv.shape[0]
    gconv = gconv * dsilu(pre)
    gpad[seq:, :] = jnp.zeros((8, LANES), F32)
    total = taps[KC - 1] * gconv
    rows = []
    for j in range(KC - 1):
        back = KC - 1 - j
        term = gconv * masks[j]
        rows.append(jnp.sum(term * inputs(j), axis=0, keepdims=True))
        gpad[:seq, :] = term * taps[j]
        total = total + gpad[back : back + seq, :]
    rows.append(jnp.sum(gconv * inputs(KC - 1), axis=0, keepdims=True))
    rows.append(jnp.sum(gconv, axis=0, keepdims=True))
    return total, rows


def gate_back_kernel(
    info, sq_a, sq_b, uv_a, uv_b, gnormed, y, gate_z, gain, gq, gkv, early, gy, g_gain
):
    z = gate_z[...]
    sig = jax.nn.sigmoid(z)
    gated = y[...] * (z * sig)
    scale = lax.rsqrt(column_of(sq_a[...] + sq_b[...]) / DS + EPS)
    mean = column_of(uv_a[...] + uv_b[...]) / DS
    grad = gnormed[...]
    ggz = scale * (grad * gain[...]) - gated * scale**3 * mean
    gy[...] = ggz * (z * sig)
    early[:, :XW] = (ggz * y[...] * (sig * (1.0 + z * (1.0 - sig)))).astype(LOW)
    early[:, XW : XW + LANES] = gq[...]
    half = (iota(gkv.shape, 1) < HD) == (info[AT_CORE] == 0)
    early[:, XW + LANES :] = jnp.where(half, gkv[...], 0.0).astype(LOW)
    g_gain[...] = jnp.sum(grad * gated * scale, axis=0, keepdims=True)


def scan_back_kernel(
    info, xbc, conv_pre, soft, rate, skip, states, taps, gy,
    gx_low, gbc_given, gbc_kept, gdr, gsoft_low, g_taps, g_skip, g_heads,
    act, step, gact, gdt, gla, padded, gpad, seg,
):
    seq = gy.shape[0]
    pre = conv_pre[...]
    act[...] = pre * jax.nn.sigmoid(pre)
    step[...] = step_sizes(soft[...])
    spread = head_spread()
    shape = (SPAN, SPAN)
    row, col = iota(shape, 0), iota(shape, 1)
    upper = (col >= row).astype(LOW)
    later = jnp.zeros((NS, XW), F32)
    skip_sum = jnp.zeros((1, XW), F32)
    for k in reversed(range(seq // SPAN)):
        rows = pl.ds(k * SPAN, SPAN)
        x = act[rows, :XW]
        b = act[rows, XW : XW + NS]
        c = act[rows, XW + NS :]
        dt = step[rows, :]
        g = gy[rows, :]
        state = states[k]
        seen, total, total_t, dt_t, carried, tail = span_parts(
            info, k * SPAN, dt, -dt * rate[...]
        )
        inner = rough(c, b, ((1,), (1,)))
        wide = picked(carried, spread)
        tail_dt = tail * dt
        wide_tail = picked(tail_dt, spread)
        g_carried = g * wide
        ginner = jnp.zeros(shape, F32)
        out_sum = jnp.zeros(shape, F32)
        in_sum = jnp.zeros(shape, F32)
        parts = []
        for h in range(HEADS_AT):
            own = slice(h * HP, (h + 1) * HP)
            decay = decay_of(seen, total, total_t, h)
            product = rough(g[:, own], x[:, own], ((1,), (1,))) * decay
            scaled = product * dt_t[h : h + 1, :]
            ginner = ginner + scaled
            out_sum = out_sum + jnp.where(
                col == h, jnp.sum(scaled * inner, axis=1, keepdims=True), 0.0
            )
            in_sum = in_sum + jnp.where(
                row == h, jnp.sum(product * inner, axis=0, keepdims=True), 0.0
            )
            mixing = decay * inner * dt_t[h : h + 1, :]
            parts.append(rough(mixing, g[:, own], ((0,), (0,))))
        from_later = rough(b, later)
        gact[rows, :XW] = (
            jnp.concatenate(parts, axis=1) + from_later * wide_tail + g * skip[...]
        )
        gact[rows, XW : XW + NS] = rough(ginner, c, ((0,), (0,))) + rough(
            x * wide_tail, later, ((1,), (1,))
        )
        gact[rows, XW + NS :] = rough(ginner, b) + rough(g_carried, state, ((1,), (1,)))
        tail_in = picked(x * from_later, spread, ((1,), (1,)))
        state_out = picked(rough(c, state) * g_carried, spread, ((1,), (1,)))
        in_col = in_sum.T
        gdt[rows, :] = in_col + tail_in * tail
        moved = tail_in * tail_dt
        kept = picked(
            jnp.sum(state * later, axis=0, keepdims=True) * wide[SPAN - 1 :],
            spread,
            ((1,), (1,)),
        )
        at_end = jnp.sum(moved, axis=0, keepdims=True) + kept
        change = out_sum - in_col * dt + state_out - moved
        gla[rows, :] = picked(upper, change, terms=3) + at_end
        skip_sum = skip_sum + jnp.sum(g * x, axis=0, keepdims=True)
        later = later * wide[SPAN - 1 :] + rough(c, g_carried, ((0,), (0,)))
    g_skip[...] = skip_sum

    core = info[AT_CORE]
    gbc_given[...] = gact[:, part_at(XW, 1 - core, NS, NS)]
    gbc_kept[...] = gact[:, part_at(XW, core, NS, NS)]

    gsoft = (gdt[...] - gla[...] * rate[...]) * jax.nn.sigmoid(soft[...])
    gsoft = jnp.where(iota(gsoft.shape, 1) < HEADS_AT, gsoft, 0.0)
    gsoft_low[...] = gsoft.astype(LOW)
    gdr[...] = dot_t(gsoft.astype(LOW), own_heads_pick(info)).astype(LOW)
    g_heads[0:1, :] = jnp.sum(-gla[...] * step[...] * rate[...], axis=0, keepdims=True)
    g_heads[1:2, :] = jnp.sum(gsoft, axis=0, keepdims=True)
    g_heads[2:, :] = jnp.zeros((6, LANES), F32)

    padded[:8, :] = jnp.zeros((8, LANES), F32)
    masks = tap_masks(info, seg)
    g_taps[...] = jnp.zeros_like(g_taps)
    for block in range(0, XW, LANES):
        lanes = slice(block, block + LANES)
        padded[8:, :] = xbc[:, lanes]
        total, sums = conv_back(
            masks, gact[:, lanes], conv_pre[:, lanes],
            [taps[j : j + 1, lanes] for j in range(KC)],
            lambda j: padded[8 - (KC - 1 - j) : 8 - (KC - 1 - j) + seq, :], gpad,
        )
        gx_low[:, lanes] = total.astype(LOW)
        for j, value in enumerate(sums):
            g_taps[j : j + 1, lanes] = value


def late_kernel(
    info, gbc_kept, gbc_moved, xbc, conv_pre, taps, gx_low, gsoft, h_low,
    given_a, kept_a, given_b, kept_b, g_dt, gbc_low, g_taps, left, padded, gpad, seg,
):
    seq = gx_low.shape[0]
    lanes = part_at(XW, info[AT_CORE], NS, NS)
    padded[:8, :] = jnp.zeros((8, LANES), F32)
    padded[8:, :] = xbc[:, lanes]
    total, sums = conv_back(
        tap_masks(info, seg), gbc_kept[...] + gbc_moved[...], conv_pre[:, lanes],
        [taps[j : j + 1, lanes] for j in range(KC)],
        lambda j: padded[8 - (KC - 1 - j) : 8 - (KC - 1 - j) + seq, :], gpad,
    )
    g_taps[...] = jnp.zeros_like(g_taps)
    for j, value in enumerate(sums):
        g_taps[j : j + 1, :] = value
    gbc_low[...] = total.astype(LOW)
    left[:, :XW] = gx_low[...]
    left[:, XW:] = gbc_low[...]
    half = left.shape[1] // 4
    for bit, first, given, kept in ((1, 0, given_a, kept_a), (2, 2 * half, given_b, kept_b)):
        mine = info[AT_BIT[bit]]
        other = left[:, part_at(first, 1 - mine, half, half)]
        given[0] = t_dot(other, h_low[...]).astype(LOW)
        kept[0] = t_dot(left[:, part_at(first, mine, half, half)], h_low[...])
    g_dt[...] = t_dot(gsoft[...], h_low[...])[:8]


def early_kernel(info, early, h_low, given, kept):
    mine = info[AT_BIT[1]]
    full = t_dot(early[...], h_low[...])
    half = full.shape[0] // 2
    first, second = full[:half], full[half:]
    given[0] = jnp.where(mine == 0, second, first).astype(LOW)
    kept[0] = jnp.where(mine == 0, first, second)


def inputs_back_kernel(
    info, gx_low, early, gbc_low, gdr, w_full, z_full, given, kept, back
):
    c = info[AT_CORE]
    gbc = gbc_low[...]
    nothing = jnp.zeros_like(gbc)
    back[:, :XW] = gx_low[...]
    back[:, Q_AT:BC_AT] = early[:, XW:]
    back[:, BC_AT : BC_AT + NS] = jnp.where(c == 0, gbc, nothing)
    back[:, BC_AT + NS : DT_AT] = jnp.where(c == 0, nothing, gbc)
    back[:, DT_AT:W_FIRST] = gdr[...]
    back[:, W_FIRST:] = early[:, :XW]
    for core, dst in ((1 - c, given), (c, kept)):
        for k in range(2):
            rows = part(2 * k + core, TB)
            dst[k] = dot32(back[rows, :W_FIRST], w_full[...]) + dot32(
                back[rows, W_FIRST:], z_full[...]
            )


def first_norm_back_kernel(info, mine, moved, hidden, norm, gres, out, g_norm):
    gh = mine[...] + moved[...]
    value = hidden[...].astype(F32)
    scale = rms_scale(value)
    uu = gh * norm[...]
    mean = jnp.mean(uu * value, axis=-1, keepdims=True)
    out[...] = gres[info[AT_Y]] + scale * uu - value * scale**3 * mean
    g_norm[...] = jnp.sum(gh * value * scale, axis=0, keepdims=True)


def result_kernel(info, mine, moved, residual, keep, out, sums):
    mlp = mine[...] + moved[...]
    full = residual[info[AT_Y]] + mlp
    out[...] = full.astype(LOW)
    full = full * keep[...]
    mlp = mlp * keep[...]
    sums[0:1, :] = jnp.sum(full * full, axis=0, keepdims=True)
    sums[1:2, :] = jnp.sum(mlp * mlp, axis=0, keepdims=True)
    sums[2:, :] = jnp.zeros((6, D), F32)


def attend_kernel(info, q_ref, kv_ref, out_ref, lse_ref):
    scale = 1.0 / math.sqrt(HD)
    heads = q_ref.shape[1] // HD
    for k in range(q_ref.shape[0] // SPAN):
        rows, reach = pl.ds(k * SPAN, SPAN), (k + 1) * SPAN
        keys, values = kv_ref[:reach, :HD], kv_ref[:reach, HD:]
        counted = counted_keys(info, k * SPAN, reach)
        outs, tops = [], []
        for h in range(heads):
            s = dot_t(q_ref[rows, h * HD : (h + 1) * HD], keys) * scale
            s = jnp.where(counted, s, NEG)
            top = jnp.max(s, axis=1, keepdims=True)
            lse = top + jnp.log(jnp.sum(jnp.exp(s - top), axis=1, keepdims=True))
            prob = jnp.exp(s - lse).astype(LOW)
            outs.append(dot32(prob, values))
            tops.append(lse)
        out_ref[rows, :] = jnp.concatenate(outs, axis=1).astype(LOW)
        lane = iota((SPAN, LANES), 1)
        lse_ref[rows, :] = sum(jnp.where(lane == h, t, 0.0) for h, t in enumerate(tops))


def counted_keys(info, first, reach):
    shape = (SPAN, reach)
    row, col = iota(shape, 0) + first, iota(shape, 1)
    return (col <= row) & (count_starts(info, row) == count_starts(info, col))


def attend_back_kernel(
    info, q_ref, kv_ref, lse_ref, gout_ref, cosines, sines, turn, gq_ref, gkv_ref, gq_rot
):
    scale = 1.0 / math.sqrt(HD)
    heads = q_ref.shape[1] // HD
    gkv_ref[...] = jnp.zeros_like(gkv_ref)
    for k in range(q_ref.shape[0] // SPAN):
        rows, reach = pl.ds(k * SPAN, SPAN), (k + 1) * SPAN
        keys, values = kv_ref[:reach, :HD], kv_ref[:reach, HD:]
        counted = counted_keys(info, k * SPAN, reach)
        outs, gkeys, gvalues = [], 0.0, 0.0
        for h in range(heads):
            own = slice(h * HD, (h + 1) * HD)
            q, gout = q_ref[rows, own], gout_ref[rows, own]
            s = dot_t(q, keys) * scale
            pe = jnp.exp(jnp.where(counted, s - lse_ref[rows, h : h + 1], NEG))
            gprob = dot_t(gout, values)
            delta = jnp.sum(pe * gprob, axis=1, keepdims=True)
            gs = (pe * (gprob - delta) * scale).astype(LOW)
            outs.append(dot32(gs, keys))
            gkeys = gkeys + t_dot(gs, q)
            gvalues = gvalues + t_dot(pe.astype(LOW), gout)
        gq_rot[rows, :] = jnp.concatenate(outs, axis=1)
        gkv_ref[:reach, :] += jnp.concatenate([gkeys, gvalues], axis=1)
    value = gq_rot[...]
    gq_ref[...] = (value * cosines[...] - picked(value, turn[...]) * sines[...]).astype(LOW)


def keys_back_kernel(info, own, moved, cosines, sines, turn, out):
    value = own[...] + moved[...]
    back = value * cosines[...] - picked(value, turn[...]) * sines[...]
    out[...] = jnp.where(iota(value.shape, 1) < HD, back, value)


def halve_kernel(bit, info, kept, moved, given_next, kept_next):
    mine = info[AT_BIT[bit]]
    half = kept.shape[1] // 2
    own, other = part(mine, half), part(1 - mine, half)
    given_next[...] = (kept[:, other, :] + moved[:, other, :].astype(F32)).astype(LOW)
    kept_next[...] = kept[:, own, :] + moved[:, own, :].astype(F32)


def settle_kernel(info, kept, moved, out):
    out[...] = (kept[...] + moved[...].astype(F32)).astype(LOW)


def settle_columns_kernel(info, kept, moved, own, core, far, far_core):
    for place, dst in zip(peers(info), (own, core, far, far_core)):
        dst[...] = (kept[place] + moved[place].astype(F32)).astype(LOW)


def settle_lanes_kernel(info, kept, moved, own, core, far, far_core):
    for place, dst in zip(peers(info), (own, core, far, far_core)):
        lanes = part(place, dst.shape[1])
        dst[...] = (kept[0, :, lanes] + moved[0, :, lanes].astype(F32)).astype(LOW)


def gather_columns_kernel(info, own, core, far, far_core, out):
    for place, ref in zip(peers(info), (own, core, far, far_core)):
        out[place] = ref[...]


def join_kernel(bit, info, own, moved, out):
    mine, size = info[AT_BIT[bit]], own.shape[1]
    out[:, part(mine, size), :] = own[...]
    out[:, part(1 - mine, size), :] = moved[...]


def sum_steps(info, given, kept, order, spread):
    moved = swap_far(given, order[0])
    for bit in order[1:]:
        moved = after(moved, (yield given))
        n, size, width = kept.shape
        given, kept = call(
            functools.partial(halve_kernel, bit),
            (low_of(n, size // 2, width), f32_of(n, size // 2, width)),
            info, kept, moved,
        )
        moved = swap_far(given, bit)
    moved = after(moved, (yield given))
    if spread:
        n, size, width = kept.shape
        if n == 4:
            kernel, block = settle_columns_kernel, (size, width)
        else:
            kernel, block = settle_lanes_kernel, (size, width // 4)
        blocks = call(kernel, (low_of(*block),) * 4, info, kept, moved)
        sent = [swap(blocks[bits], bits) for bits in (1, 2, 3)]
        sent = after(sent, (yield blocks))
        own = call(gather_columns_kernel, low_of(4, *block), info, blocks[0], *sent)
    else:
        own = call(settle_kernel, low_of(*kept.shape), info, kept, moved)
    for bit in order[:0:-1]:
        moved = swap_far(own, bit)
        moved = after(moved, (yield own))
        n, size, width = own.shape
        own = call(
            functools.partial(join_kernel, bit), low_of(n, 2 * size, width), info, own, moved
        )
    moved = swap_far(own, order[0])
    return own, after(moved, (yield own))


class Running:
    def __init__(self, *args):
        self.steps, self.result, self.done = sum_steps(*args), None, False
        self.sent = next(self.steps)

    def step(self, value):
        if not self.done:
            try:
                self.sent = self.steps.send(value)
            except StopIteration as end:
                self.result, self.done = end.value, True
        return self.sent


def each_part(bit, info, own, moved):
    mine = info[AT_BIT[bit]]
    return ((mine, own), (1 - mine, moved))


def finish_up_kernel(bit, info, own, moved, out):
    quarter = FF // 4
    size = own.shape[1]
    for at, ref in each_part(bit, info, own, moved):
        for k in range(4):
            block = ref[k].astype(F32)
            out[part(at, size), k * quarter : (k + 1) * quarter] = block[:, :quarter]
            out[part(at, size), FF + k * quarter : FF + (k + 1) * quarter] = block[:, quarter:]


def finish_in_kernel(
    info, early, early_moved, a, a_moved, b, b_moved, dt, out, out_qkv, early_full, late_full
):
    half = early.shape[1]
    for at, ref in each_part(1, info, early, early_moved):
        early_full[:, part(at, half), :] = ref[...]
    size = a.shape[1]
    for bit, first, pair in ((1, 0, (a, a_moved)), (2, 1, (b, b_moved))):
        for at, ref in each_part(bit, info, *pair):
            late_full[:, part(2 * first + at, size), :] = ref[...]
    for k in range(4):
        out[k * XW : (k + 1) * XW, :] = early_full[k, :XW, :].astype(F32)
        out[DS + k * XW : DS + (k + 1) * XW, :] = late_full[k, :XW, :].astype(F32)
        q = early_full[k, XW : XW + LANES, :].astype(F32)
        out_qkv[:, k * LANES : (k + 1) * LANES] = q.T
    for k in range(2):
        first = late_full[k, XW:, :].astype(F32)
        second = late_full[k + 2, XW:, :].astype(F32)
        out[2 * DS + k * NS : 2 * DS + (k + 1) * NS, :] = first + second
    out[DS + CONV_CH :, :] = dt[...]
    kv_at = XW + LANES
    for k in range(2):
        rows = slice(kv_at + k * HD, kv_at + (k + 1) * HD)
        pair = [early_full[k, rows, :], early_full[k + 2, rows, :]]
        both = jnp.concatenate(pair, axis=0).astype(F32)
        out_qkv[:, QW + k * KW : QW + (k + 1) * KW] = both.T


def finish_mid_kernel(bit, info, own, moved, out_a, out_b, full):
    size = own.shape[1]
    for at, ref in each_part(bit, info, own, moved):
        full[part(at, size), :] = ref[0].astype(F32)
    out_a[...] = full[:XW, :]
    out_b[...] = full[XW:, :]


def finish_rows_kernel(bit, info, own, moved, out):
    size = own.shape[1]
    for at, ref in each_part(bit, info, own, moved):
        out[part(at, size), :] = ref[0].astype(F32)


def sum_all(vector):
    for bits in (1, 2):
        vector = vector + swap(vector, bits)
    for bit in (1, 2, 4):
        vector = vector + swap_far(vector, bit)
    return vector


ROW_ONE, ROW_TWO, ROW_TAPS = 0, 8, 16
CONV_ROWS = CONV_CH // LANES
ROW_GAIN = ROW_TAPS + (KC + 1) * CONV_ROWS
ROW_SKIP = ROW_GAIN + DS // LANES
ROW_RATE = ROW_SKIP + DS // LANES
ROW_BIAS = ROW_RATE + 4
ROW_STATS = ROW_BIAS + 4
ROW_DT = 128
SMALL_ROWS = ROW_DT + NH * D // LANES


def small_kernel(
    info, one, two, taps_x, taps_bc, gain, skip, heads, dt, sums, mixed, keep, out
):
    out[...] = jnp.zeros_like(out)
    place, core = peers(info)[0], info[AT_CORE]
    for k in range(D // LANES):
        lanes = slice(k * LANES, (k + 1) * LANES)
        out[ROW_ONE + k : ROW_ONE + k + 1, :] = one[:, lanes]
        out[ROW_TWO + k : ROW_TWO + k + 1, :] = two[:, lanes]
    blocks = XW // LANES
    for k in range(blocks):
        lanes = slice(k * LANES, (k + 1) * LANES)
        at = place * blocks + k
        for j in range(KC + 1):
            out[pl.ds(ROW_TAPS + j * CONV_ROWS + at, 1), :] = taps_x[j : j + 1, lanes]
        out[pl.ds(ROW_GAIN + at, 1), :] = gain[:, lanes]
        out[pl.ds(ROW_SKIP + at, 1), :] = skip[:, lanes]
    for j in range(KC + 1):
        out[pl.ds(ROW_TAPS + j * CONV_ROWS + DS // LANES + core, 1), :] = taps_bc[j : j + 1, :]
    across = D // LANES
    for h in range(HEADS_AT):
        for k in range(across):
            at = ROW_DT + (place * HEADS_AT + h) * across + k
            out[pl.ds(at, 1), :] = dt[h : h + 1, k * LANES : (k + 1) * LANES]
    out[pl.ds(ROW_RATE + place, 1), :] = heads[0:1, :]
    out[pl.ds(ROW_BIAS + place, 1), :] = heads[1:2, :]
    for k, row in enumerate((sums[0:1, :], mixed[...], sums[1:2, :])):
        folded = row[:, :LANES]
        for j in range(1, D // LANES):
            folded = folded + row[:, j * LANES : (j + 1) * LANES]
        out[ROW_STATS + k : ROW_STATS + k + 1, :] = folded
    out[ROW_STATS + 3 : ROW_STATS + 4, :] = keep[...]


def by_heads(
    hidden_in, cotangent, doc_starts, valid_mask, norm_one, in_proj, conv_weight, conv_bias,
    dt_bias, a_log, skip_scale, gated_gain, qkv_proj, ssm_out, attn_out, norm_two, gate_up,
    down_proj,
):
    place, far_place = lax.axis_index("shard"), lax.axis_index("replica")
    y, c = place // 2, place % 2
    rows = hidden_in.shape[0]
    seq, depth = 4 * rows, in_proj.shape[0]
    bits = [y, c, far_place % 2, far_place // 2 % 2, far_place // 4]
    info = jnp.concatenate([jnp.stack(bits).astype(jnp.int32), doc_starts[0]])
    keep = valid_mask.astype(F32)
    pair = (2, rows, D)

    h_far = swap(hidden_in, 2)
    h_core = swap(hidden_in, 1)
    wide, narrow, z_wide = low_of(W_FIRST, depth), low_of(KV_AT, depth), low_of(XW, depth)
    w_own, w_core, w_far, w_far_core, z_own, z_core, z_far, z_far_core = call(
        pack_in_kernel, (wide, wide, narrow, wide) + (z_wide,) * 4, info, in_proj.T, qkv_proj
    )
    w_far, w_passed = swap(w_far, 2), swap(w_far_core, 2)
    w_core = swap(w_core, 1)
    u_own, u_core, u_far = call(
        pack_up_kernel, (low_of(depth, FF // 2),) * 3, info, after(gate_up, w_own)
    )
    g_own = cotangent * valid_mask.astype(LOW)[:, None]
    h_far_core = swap(h_far, 1)
    w_far_core = swap(w_passed, 1)
    z_far, z_far_core = after((z_far, z_far_core), (w_passed, u_own, g_own))
    z_far, z_passed = swap(z_far, 2), swap(z_far_core, 2)

    def own_channels(array):
        mine = lax.dynamic_slice_in_dim(array, place * XW, XW, 0)
        return jnp.concatenate([mine, array[DS:]], axis=0)

    def on_lanes(vector):
        mine = lax.dynamic_slice_in_dim(vector, place * HEADS_AT, HEADS_AT, 0)
        return jnp.pad(mine, (0, LANES - HEADS_AT))[None, :]

    taps = own_channels(conv_weight).T
    bias = own_channels(conv_bias)[None, :]
    rate = jnp.exp(on_lanes(a_log))
    skip = jnp.repeat(
        lax.dynamic_slice_in_dim(skip_scale, place * HEADS_AT, HEADS_AT, 0), HP
    )[None, :]
    gain = lax.dynamic_slice_in_dim(gated_gain, place * XW, XW, 0)[None, :]
    gain_one, gain_two = norm_one[None, :], norm_two[None, :]
    freqs = ROPE_BASE ** (-(jnp.arange(HD // 2).astype(F32) * 2.0) / HD)
    angles = jnp.arange(seq).astype(F32)[:, None] * jnp.tile(freqs, LANES // (HD // 2))[None, :]
    cosines, sines = jnp.cos(angles), jnp.sin(angles)
    row, col, half = iota((LANES, LANES), 0), iota((LANES, LANES), 1), HD // 2
    turn = jnp.where(
        (col // half) % 2 == 0, -(row == col + half).astype(F32), (row == col - half).astype(F32)
    ).astype(LOW)

    h_low, w_full, xbc, conv_pre, soft, q_low, kv_low, ssm_y, states = call(
        forward_kernel,
        (
            low_of(seq, D), low_of(W_FIRST, D), f32_of(seq, XW + 2 * NS), f32_of(seq, XW + 2 * NS),
            f32_of(seq, LANES), low_of(seq, LANES), low_of(seq, LANES), f32_of(seq, XW),
            f32_of(seq // SPAN, NS, XW),
        ),
        info, hidden_in, h_core, h_far, h_far_core, w_own, w_core, w_far, w_passed, w_far_core,
        gain_one, taps, bias, on_lanes(dt_bias), rate, skip, cosines, sines, turn,
        scratch=(
            pltpu.VMEM((seq + 8, XW + 2 * NS), F32), pltpu.VMEM((seq, XW + 2 * NS), F32),
            pltpu.VMEM((seq, LANES), F32), pltpu.VMEM((seq + 8, LANES), jnp.int32),
        ),
    )
    z_passed, z_core = after((z_passed, z_core), h_low)
    z_core, z_far_core = swap(z_core, 1), swap(z_passed, 1)
    u_far, u_core, g_out = after((u_far, u_core, g_own), z_passed)
    u_y, g_far = swap(u_far, 2), swap(g_out, 2)
    z_full, gate_z, square = call(
        gate_kernel, (low_of(XW, D), f32_of(seq, XW), f32_of(8, seq)),
        info, h_low, z_own, z_core, z_far, z_far_core, ssm_y,
    )
    square = square + swap(square, 1)
    square_far = swap(square, 2)
    attn, lse = call(
        attend_kernel, (low_of(seq, LANES), f32_of(seq, LANES)), info, after(q_low, square), kv_low
    )

    given, kept, normed = call(
        output_kernel, (f32_of(*pair), f32_of(*pair), low_of(seq, XW)),
        info, square, square_far, ssm_y, gate_z, gain, attn, ssm_out, attn_out,
    )
    kept = after(kept, u_y)
    u_x = swap_far(after(u_y, given), 1)
    u_y_core = swap(after(u_y, given), 1)
    chip, sent = call(add_kernel, (f32_of(*pair), low_of(*pair)), info, kept, swap(given, 1))
    u_core, g_core = swap(after(u_core, sent), 1), swap(after(g_out, sent), 1)
    g_far_core = swap(after(g_far, sent), 1)
    residual, h2, mixed_sum = call(
        second_norm_kernel, (f32_of(*pair), low_of(*pair), f32_of(1, D)),
        info, chip, swap(sent, 2), hidden_in, h_far, gain_two, keep[:, None],
        scratch=(pltpu.VMEM(pair, LOW),),
    )
    u_x_core = swap(u_x, 1)

    given, kept, hid, ggu, h2_cat, gmlp = call(
        mlp_kernel,
        (
            f32_of(*pair), f32_of(*pair), low_of(seq, FF // 4), low_of(seq, FF // 2),
            low_of(seq, D), low_of(seq, D),
        ),
        info, h2, swap(h2, 1), u_own, u_core, u_y, u_x, u_y_core, u_x_core,
        g_own, g_core, g_far, g_far_core, down_proj,
        scratch=(pltpu.VMEM((D, FF // 2), LOW),),
    )
    x_order, z_order = (1, 2, 4), (2, 4, 1)
    moved = swap(given, 1)
    up_given, up_kept = call(
        functools.partial(grad_columns_kernel, x_order[0]),
        (low_of(4, D // 8, FF // 2), f32_of(4, D // 8, FF // 2)), info, h2_cat, ggu,
    )
    s_up = Running(info, up_given, up_kept, x_order, True)
    down_given, down_kept = call(
        functools.partial(grad_rows_kernel, z_order[0]),
        (low_of(FF // 8, D), f32_of(FF // 8, D)), info, hid, after(gmlp, up_given),
    )
    s_down = Running(info, down_given[None], down_kept[None], z_order, False)
    kept = after(kept, (up_given, down_given))
    chip, sent = call(add_kernel, (f32_of(*pair), low_of(*pair)), info, kept, moved)
    mlp_given, mlp_kept = call(
        down_kernel, (f32_of(*pair), f32_of(*pair)), info, after(hid, sent), down_proj
    )
    mlp_mine, mlp_given = call(
        add_split_kernel, (f32_of(rows, D),) * 2, info, mlp_kept, swap(mlp_given, 1)
    )
    gres, gmix, g_norm_two = call(
        norm_back_pair_kernel, (f32_of(*pair), low_of(*pair), f32_of(1, D)),
        info, after(chip, mlp_given), swap(sent, 2), residual, gain_two, g_own, g_far,
        scratch=(pltpu.VMEM(pair, LOW),),
    )

    moved = after(swap(gmix, 1), s_down.step(gmix))
    gmix_all, gnormed, gattn, uv = call(
        output_back_kernel,
        (low_of(seq, D), f32_of(seq, XW), low_of(seq, LANES), f32_of(8, seq)),
        info, gmix, moved, ssm_y, gate_z, gain, ssm_out, attn_out,
    )
    uv = uv + swap(uv, 1)
    uv_far = swap(uv, 2)
    gq, gkv_part = call(
        attend_back_kernel, (low_of(seq, LANES), f32_of(seq, LANES)),
        info, q_low, kv_low, lse, after(gattn, uv), cosines, sines, turn,
        scratch=(pltpu.VMEM((seq, LANES), F32),),
    )
    moved = swap(gkv_part, 1)
    mid_given, mid_kept = call(
        functools.partial(grad_mid_kernel, x_order[0]),
        (low_of(XW - LANES, D), f32_of(XW - LANES, D)),
        info, normed, attn, after(gmix_all, gkv_part),
        scratch=(pltpu.VMEM((seq, XW + LANES), LOW),),
    )
    s_mid = Running(info, mid_given[None], mid_kept[None], x_order, False)
    gkv = call(
        keys_back_kernel, f32_of(seq, LANES),
        info, after(gkv_part, mid_given), moved, cosines, sines, turn,
    )
    early, gy, g_gain = call(
        gate_back_kernel, (low_of(seq, XW + 2 * LANES), f32_of(seq, XW), f32_of(1, XW)),
        info, square, square_far, uv, uv_far, gnormed, ssm_y, gate_z, gain, gq, gkv,
    )
    half = early.shape[1] // 2
    early_given, early_kept = call(
        early_kernel, (low_of(1, half, D), f32_of(1, half, D)), info, early, h_low
    )
    s_early = Running(info, early_given, early_kept, x_order, True)
    sent = [one.step(gy) for one in (s_up, s_down)]
    mlp_moved = swap(after(mlp_given, gy), 2)

    gx_low, gbc_given, gbc_kept, gdr, gsoft, taps_x, g_skip, g_heads = call(
        scan_back_kernel,
        (
            low_of(seq, XW), f32_of(seq, NS), f32_of(seq, NS), low_of(seq, LANES),
            low_of(seq, LANES), f32_of(8, XW), f32_of(1, XW), f32_of(8, LANES),
        ),
        info, xbc, conv_pre, soft, rate, skip, states, taps, after(gy, (early_given, sent)),
        scratch=(
            pltpu.VMEM((seq, XW + 2 * NS), F32), pltpu.VMEM((seq, LANES), F32),
            pltpu.VMEM((seq, XW + 2 * NS), F32),
            pltpu.VMEM((seq, LANES), F32), pltpu.VMEM((seq, LANES), F32),
            pltpu.VMEM((seq + 8, LANES), F32), pltpu.VMEM((seq + 8, LANES), F32),
            pltpu.VMEM((seq + 8, LANES), jnp.int32),
        ),
    )
    moved = swap(gbc_given, 1)
    sent = [one.step(gbc_given) for one in (s_up, s_mid, s_early, s_down)]
    quarter = (XW + NS) // 4
    a_given, a_kept, b_given, b_kept, g_dt, gbc_low, taps_bc = call(
        late_kernel,
        (
            low_of(1, quarter, D), f32_of(1, quarter, D), low_of(1, quarter, D),
            f32_of(1, quarter, D), f32_of(8, D), low_of(seq, NS), f32_of(8, LANES),
        ),
        info, after(gbc_kept, sent), moved, xbc, conv_pre, taps, gx_low, gsoft, h_low,
        scratch=(
            pltpu.VMEM((seq, XW + NS), LOW), pltpu.VMEM((seq + 8, LANES), F32),
            pltpu.VMEM((seq + 8, LANES), F32), pltpu.VMEM((seq + 8, LANES), jnp.int32),
        ),
    )
    s_a = Running(info, a_given, a_kept, x_order, True)
    s_b = Running(info, b_given, b_kept, z_order, True)

    given, kept = call(
        inputs_back_kernel, (f32_of(*pair), f32_of(*pair)),
        info, after(gx_low, a_given), early, gbc_low, gdr, w_full, z_full,
        scratch=(pltpu.VMEM((seq, W_FIRST + XW), LOW),),
    )
    mine, given = call(add_split_kernel, (f32_of(rows, D),) * 2, info, kept, swap(given, 1))
    moved = swap(given, 2)
    running = (s_a, s_b, s_early, s_up, s_mid, s_down)
    for one in running:
        one.step(given)
    grad_input, g_norm_one = call(
        first_norm_back_kernel, (f32_of(rows, D), f32_of(1, D)),
        info, mine, moved, hidden_in, gain_one, gres,
    )
    output, sums = call(
        result_kernel, (low_of(rows, D), f32_of(8, D)),
        info, mlp_mine, mlp_moved, residual, keep[:, None],
    )
    small = call(
        small_kernel, f32_of(SMALL_ROWS, LANES),
        info, g_norm_one, g_norm_two, taps_x, taps_bc, g_gain, g_skip, g_heads, g_dt, sums,
        mixed_sum, keep[None, :],
    )
    while not all(one.done for one in running):
        for one in running:
            one.step(grad_input)
    small = sum_all(small)

    def rows_of(first, count):
        return small[first : first + count]

    dt = lax.dynamic_slice_in_dim(
        rows_of(ROW_DT, NH * D // LANES).reshape(NH, D), place * depth, depth, 1
    )
    grad_in, grad_qkv = call(
        finish_in_kernel, (f32_of(in_proj.shape[1], depth), f32_of(*qkv_proj.shape)),
        info, *s_early.result, *s_a.result, *s_b.result, dt,
        scratch=(
            pltpu.VMEM((4, XW + 2 * LANES, depth), LOW), pltpu.VMEM((4, XW + NS, depth), LOW)
        ),
    )
    grad_up = call(
        functools.partial(finish_up_kernel, x_order[0]), f32_of(*gate_up.shape), info, *s_up.result
    )
    grad_down = call(
        functools.partial(finish_rows_kernel, z_order[0]), f32_of(*down_proj.shape),
        info, *s_down.result,
    )
    grad_ssm, grad_attn = call(
        functools.partial(finish_mid_kernel, x_order[0]),
        (f32_of(*ssm_out.shape), f32_of(*attn_out.shape)), info, *s_mid.result,
        scratch=(pltpu.VMEM((XW + LANES, D), F32),),
    )

    conv = rows_of(ROW_TAPS, (KC + 1) * CONV_ROWS).reshape(KC + 1, CONV_CH)
    heads = rows_of(ROW_RATE, 8)[:, :HEADS_AT].reshape(2, NH)
    stats = jnp.sum(rows_of(ROW_STATS, 4), axis=1)
    return (
        output,
        grad_input,
        rows_of(ROW_ONE, 8).reshape(D),
        grad_in.T,
        conv[:KC].T,
        conv[KC],
        heads[1],
        heads[0],
        jnp.sum(rows_of(ROW_SKIP, DS // LANES).reshape(NH, HP), axis=1),
        rows_of(ROW_GAIN, DS // LANES).reshape(DS),
        grad_qkv,
        grad_ssm,
        grad_attn,
        rows_of(ROW_TWO, 8).reshape(D),
        grad_up,
        grad_down,
        jnp.sqrt(stats[:3] / (stats[3] * D)),
    )


def on_any(*args):
    sizes = (lax.axis_size("replica"), lax.axis_size("shard"), args[0].shape[0])
    return (by_heads if sizes == (8, 4, TB) else on_device)(*args)


def solution(mesh):
    return jax.shard_map(
        on_any,
        mesh=mesh,
        in_specs=(
            P(("replica", "shard"), None),
            P(("replica", "shard"), None),
            P("replica", None),
            P(("replica", "shard")),
            P(),
            P("shard", None),
            P(),
            P(),
            P(),
            P(),
            P(),
            P(),
            P("shard", None),
            P("shard", None),
            P("shard", None),
            P(),
            P("shard", None),
            P("shard", None),
        ),
        out_specs=(
            P(("replica", "shard"), None),
            P(("replica", "shard"), None),
            P(),
            P("shard", None),
            P(),
            P(),
            P(),
            P(),
            P(),
            P(),
            P("shard", None),
            P("shard", None),
            P("shard", None),
            P(),
            P("shard", None),
            P("shard", None),
            P(),
        ),
        check_vma=False,
    )
```

```python
import functools
import math

import jax
import jax.numpy as jnp
from jax import lax
from jax.experimental import pallas as pl
from jax.experimental.pallas import tpu as pltpu
from jax.sharding import PartitionSpec as P

D = 1024
NH = 24
HP = 64
NS = 128
KC = 4
QH = 8
KVH = 2
HD = 64
FF = 2048
SPAN = 128
KBLK = 512
DS = 1536
QW = 512
KW = 128
CONV_CH = 1792


EPS = 1e-05
ROPE_BASE = 100000000000.0
NEG = -1e30
HIGH = lax.Precision.HIGHEST


def from_behind(block, axis, distance):
    devices = range(lax.axis_size(axis))
    route = [(i - distance, i) for i in devices if i - distance in devices]
    return lax.ppermute(block, axis, route)


def carried_in(part, axis, combine, identity):
    place = lax.axis_index(axis)
    gathered = jax.tree.map(lambda a: lax.all_gather(a, axis), part)
    state = jax.tree.map(lambda a, e: jnp.zeros_like(a) + jnp.asarray(e, a.dtype), part, identity)

    def one(step, state):
        return combine(
            state, jax.tree.map(lambda a: lax.dynamic_index_in_dim(a, step, 0, False), gathered)
        )

    return lax.fori_loop(0, place, one, state)


def entering(value, axis, combine, identity):
    size, mine = (lax.axis_size(axis), lax.axis_index(axis))
    everything = jax.tree.map(
        lambda part, kind: lax.all_gather(part.astype(kind), axis),
        value,
        jax.tree.map(lambda a: jnp.bfloat16 if a.dtype == jnp.float32 else a.dtype, value),
    )
    start = jax.tree.map(
        lambda part, zero: jnp.broadcast_to(jnp.asarray(zero, part.dtype), part.shape),
        value,
        identity,
    )

    def step(k, before):
        at = size - 1 - k
        reached = at > mine
        new = combine(
            before, jax.tree.map(lambda part, own: part[at].astype(own.dtype), everything, value)
        )
        return jax.tree.map(lambda a, b: jnp.where(reached, a, b), new, before)

    return lax.fori_loop(0, size, step, start)


def rms_scale(tensor):
    return lax.rsqrt(jnp.mean(tensor * tensor, axis=-1, keepdims=True) + EPS)


def rope_tables(positions):
    freqs = ROPE_BASE ** (-(jnp.arange(HD // 2).astype(jnp.float32) * 2.0) / HD)
    angles = positions.astype(jnp.float32)[:, None] * freqs[None, :]
    return (jnp.cos(angles), jnp.sin(angles))


def rotate(tensor, heads, cosines, sines):
    shaped = tensor.reshape(tensor.shape[0], heads, HD)
    first_half = shaped[:, :, : HD // 2]
    second_half = shaped[:, :, HD // 2 :]
    cos_b = cosines[:, None, :]
    sin_b = sines[:, None, :]
    turned = jnp.concatenate(
        [first_half * cos_b - second_half * sin_b, second_half * cos_b + first_half * sin_b],
        axis=-1,
    )
    return turned.reshape(tensor.shape[0], heads * HD)


def segment_of(positions, starts_row):
    return jnp.sum((starts_row[None, :] <= positions[:, None]).astype(jnp.int32), axis=1) - 1


def norm_back(grad_out, tensor, scale_rows, gain):
    scaled = grad_out * gain
    grad_in = scale_rows * scaled - tensor * scale_rows**3 * jnp.mean(
        scaled * tensor, axis=-1, keepdims=True
    )
    return (grad_in, jnp.sum(grad_out * tensor * scale_rows, axis=0))


def dsilu(tensor):
    sig_part = jax.nn.sigmoid(tensor)
    return sig_part * (1.0 + tensor * (1.0 - sig_part))


def combine_states(earlier, later):
    return (earlier[0] * later[1][:, None, None] + later[0], earlier[1] * later[1])


def ssd_spans(state, ssm_x, ssm_b, ssm_c, step_size, log_decay, skip_scale, seg_ids, before):
    count = ssm_x.shape[0] // SPAN
    prev_seg = jnp.concatenate([before.reshape(1), seg_ids[:-1]])

    def by_span(tensor):
        return tensor.reshape((count, SPAN) + tensor.shape[1:])

    def span_step(state_acc, pieces):
        x_c, b_c, c_c, dt_c, la_c, s_c, p_c = pieces
        cum_decay = jnp.cumsum(la_c, axis=0)
        order = jnp.arange(SPAN)
        same_mask = (s_c[:, None] == s_c[None, :]) & (order[:, None] >= order[None, :])
        differ = cum_decay.T[:, :, None] - cum_decay.T[:, None, :]
        decay_mat = jnp.exp(jnp.where(same_mask[None], differ, NEG))
        inner = jnp.dot(c_c, b_c.T, precision=HIGH)
        mixing = decay_mat * inner[None] * dt_c.T[:, None, :]
        y_inner = jnp.einsum("hpq,qhd->phd", mixing, x_c, precision=HIGH)
        alive = (s_c == p_c[0]).astype(jnp.float32)
        carried = jnp.exp(cum_decay) * alive[:, None]
        y_state = jnp.einsum("hdn,pn->phd", state_acc, c_c, precision=HIGH) * carried[:, :, None]
        y_span = y_inner + y_state + skip_scale[None, :, None] * x_c
        tail_w = (
            jnp.exp(cum_decay[-1][None, :] - cum_decay)
            * (s_c == s_c[-1]).astype(jnp.float32)[:, None]
            * dt_c
        )
        new_state = state_acc * carried[-1][:, None, None] + jnp.einsum(
            "qh,qhd,qn->hdn", tail_w, x_c, b_c, precision=HIGH
        )
        return (new_state, y_span)

    final_state, ys = lax.scan(
        span_step,
        state,
        (
            by_span(ssm_x),
            by_span(ssm_b),
            by_span(ssm_c),
            by_span(step_size),
            by_span(log_decay),
            by_span(seg_ids),
            by_span(prev_seg),
        ),
    )
    return (ys.reshape(ssm_x.shape), final_state)


def on_device(
    hidden_in,
    cotangent,
    doc_starts,
    valid_mask,
    norm_one,
    in_proj,
    conv_weight,
    conv_bias,
    dt_bias,
    a_log,
    skip_scale,
    gated_gain,
    qkv_proj,
    ssm_out,
    attn_out,
    norm_two,
    gate_up,
    down_proj,
):
    tok_rows = hidden_in.shape[0]
    shard_count = lax.axis_size("shard")
    offset = lax.axis_index("shard") * tok_rows
    seq_len = tok_rows * shard_count
    score_scale = 1.0 / math.sqrt(HD)
    q_per_kv = QH // KVH
    starts_row = doc_starts[0]
    positions = offset + jnp.arange(tok_rows, dtype=jnp.int32)
    seg_ids = segment_of(positions, starts_row)
    before = segment_of(positions[:1] - 1, starts_row)[0]
    first_start = jnp.max(jnp.where(starts_row <= positions[0], starts_row, 0))
    last_pos = positions[-1]
    full_weights = (
        lax.all_gather(in_proj, "shard", axis=0, tiled=True),
        lax.all_gather(qkv_proj, "shard", axis=0, tiled=True),
        lax.all_gather(ssm_out, "shard", axis=0, tiled=True),
        lax.all_gather(attn_out, "shard", axis=0, tiled=True),
        lax.all_gather(gate_up, "shard", axis=0, tiled=True),
        lax.all_gather(down_proj, "shard", axis=0, tiled=True),
    )
    f_in, f_attn, f_mo, f_ao, f_gu, f_down = full_weights
    x_full = hidden_in.astype(jnp.float32)
    r_one = rms_scale(x_full)
    h_low = (x_full * r_one * norm_one).astype(jnp.bfloat16)
    proj_out = jnp.dot(h_low, f_in, preferred_element_type=jnp.float32)
    gate_z = proj_out[:, :DS]
    xbc = proj_out[:, DS : DS + CONV_CH]
    dt_raw = proj_out[:, DS + CONV_CH :]
    edge_rows = from_behind(xbc[tok_rows - (KC - 1) :], "shard", 1)
    padded = jnp.concatenate([edge_rows, xbc], axis=0)
    pad_pos = positions[0] - (KC - 1) + jnp.arange(tok_rows + KC - 1, dtype=jnp.int32)
    pad_seg = segment_of(pad_pos, starts_row)
    tap_masks = [
        (pad_seg[tap_index : tap_index + tok_rows] == seg_ids).astype(jnp.float32)[:, None]
        for tap_index in range(KC)
    ]
    conv_pre = jnp.zeros((tok_rows, CONV_CH), jnp.float32) + conv_bias[None, :]
    for tap_index in range(KC):
        conv_pre = (
            conv_pre
            + conv_weight[:, tap_index][None, :]
            * padded[tap_index : tap_index + tok_rows]
            * tap_masks[tap_index]
        )
    conv_act = jax.nn.silu(conv_pre)
    ssm_x = conv_act[:, :DS].reshape(tok_rows, NH, HP)
    ssm_b = conv_act[:, DS : DS + NS]
    ssm_c = conv_act[:, DS + NS :]
    soft_in = dt_raw + dt_bias
    step_size = jax.nn.softplus(soft_in)
    decay_rate = jnp.exp(a_log)
    log_decay = -step_size * decay_rate
    empty_state = jnp.zeros((NH, HP, NS), jnp.float32)

    def carry_factor(log_vals):
        return (
            jnp.exp(jnp.cumsum(log_vals, axis=0)) * (seg_ids == before).astype(jnp.float32)[:, None]
        )

    def carry_term(state_in, c_vals, factor):
        return jnp.einsum("hdn,pn->phd", state_in, c_vals, precision=HIGH) * factor[:, :, None]

    ssm_zero, local_state = ssd_spans(
        empty_state, ssm_x, ssm_b, ssm_c, step_size, log_decay, skip_scale, seg_ids, before
    )
    factor = carry_factor(log_decay)
    dev_decay = factor[-1]
    state_in, unused_decay = carried_in(
        (local_state, dev_decay),
        "shard",
        combine_states,
        (jnp.zeros_like(local_state), jnp.ones_like(dev_decay)),
    )
    ssm_y = (ssm_zero + carry_term(state_in, ssm_c, factor)).reshape(tok_rows, DS)
    silu_z = jax.nn.silu(gate_z)
    gated = ssm_y * silu_z
    r_gate = rms_scale(gated)
    normed_low = (gated * r_gate * gated_gain).astype(jnp.bfloat16)
    qkv = jnp.dot(h_low, f_attn, preferred_element_type=jnp.float32)
    cosines, sines = rope_tables(positions)
    q_low = (
        rotate(qkv[:, :QW], QH, cosines, sines)
        .astype(jnp.bfloat16)
        .reshape(tok_rows, KVH, q_per_kv, HD)
    )
    k_low = rotate(qkv[:, QW : QW + KW], KVH, cosines, sines).astype(jnp.bfloat16)
    v_low = qkv[:, QW + KW :].astype(jnp.bfloat16)
    key_all, value_all = (
        lax.all_gather(k_low, "shard", axis=0, tiled=True),
        lax.all_gather(v_low, "shard", axis=0, tiled=True),
    )
    key_all = key_all.reshape(seq_len, KVH, HD)
    value_all = value_all.reshape(seq_len, KVH, HD)
    key_pos = jnp.arange(seq_len, dtype=jnp.int32)
    key_seg = segment_of(key_pos, starts_row)
    block_count = seq_len // KBLK
    row_shape = (KVH, q_per_kv, tok_rows)

    def needed(blk_index):
        low_edge = blk_index * KBLK
        return (low_edge <= last_pos) & (low_edge + KBLK > first_start)

    def block_keys(blk_index):
        return (
            lax.dynamic_slice_in_dim(key_all, blk_index * KBLK, KBLK, 0),
            lax.dynamic_slice_in_dim(value_all, blk_index * KBLK, KBLK, 0),
        )

    def block_scores(blk_index, k_blk):
        pos_blk = lax.dynamic_slice_in_dim(key_pos, blk_index * KBLK, KBLK, 0)
        seg_blk = lax.dynamic_slice_in_dim(key_seg, blk_index * KBLK, KBLK, 0)
        raw_scores = (
            jnp.einsum("tgqd,kgd->gqtk", q_low, k_blk, preferred_element_type=jnp.float32)
            * score_scale
        )
        key_mask = (pos_blk[None, :] <= positions[:, None]) & (seg_blk[None, :] == seg_ids[:, None])
        return (raw_scores, key_mask[None, None])

    def unchanged(passed):
        return passed

    def lse_step(blk_index, state_acc):

        def lse_do_block(state_acc):
            row_top, row_total = state_acc
            k_blk, v_blk = block_keys(blk_index)
            raw_scores, key_mask = block_scores(blk_index, k_blk)
            new_top = jnp.maximum(row_top, jnp.max(jnp.where(key_mask, raw_scores, NEG), axis=-1))
            row_total = row_total * jnp.exp(row_top - new_top) + jnp.sum(
                jnp.where(key_mask, jnp.exp(raw_scores - new_top[..., None]), 0.0), axis=-1
            )
            return (new_top, row_total)

        return lax.cond(needed(blk_index), lse_do_block, unchanged, state_acc)

    row_top, row_total = lax.fori_loop(
        0,
        block_count,
        lse_step,
        (jnp.full(row_shape, NEG, jnp.float32), jnp.zeros(row_shape, jnp.float32)),
    )
    log_total = row_top + jnp.log(row_total)

    def probs_of(blk_index, k_blk):
        raw_scores, key_mask = block_scores(blk_index, k_blk)
        return jnp.where(key_mask, jnp.exp(raw_scores - log_total[..., None]), 0.0)

    def out_step(blk_index, acc_out):

        def out_do_block(acc_out):
            k_blk, v_blk = block_keys(blk_index)
            prob_blk = probs_of(blk_index, k_blk).astype(jnp.bfloat16)
            return acc_out + jnp.einsum(
                "gqtk,kgd->tgqd", prob_blk, v_blk, preferred_element_type=jnp.float32
            )

        return lax.cond(needed(blk_index), out_do_block, unchanged, acc_out)

    attended = lax.fori_loop(
        0, block_count, out_step, jnp.zeros((tok_rows, KVH, q_per_kv, HD), jnp.float32)
    )
    attn_low = attended.reshape(tok_rows, QW).astype(jnp.bfloat16)
    mixed = jnp.dot(normed_low, f_mo, preferred_element_type=jnp.float32) + jnp.dot(
        attn_low, f_ao, preferred_element_type=jnp.float32
    )
    residual = x_full + mixed
    r_two = rms_scale(residual)
    h2_low = (residual * r_two * norm_two).astype(jnp.bfloat16)
    gate_vals = jnp.dot(h2_low, f_gu, preferred_element_type=jnp.float32)
    gate_part = gate_vals[:, :FF]
    up_part = gate_vals[:, FF:]
    hid_low = (jax.nn.silu(gate_part) * up_part).astype(jnp.bfloat16)
    mlp_out = jnp.dot(hid_low, f_down, preferred_element_type=jnp.float32)
    out_full = residual + mlp_out
    keep_rows = valid_mask.astype(jnp.float32)
    stat_local = jnp.stack(
        [
            jnp.sum(keep_rows * jnp.sum(out_full * out_full, axis=1)),
            jnp.sum(keep_rows * jnp.sum(mixed * mixed, axis=1)),
            jnp.sum(keep_rows * jnp.sum(mlp_out * mlp_out, axis=1)),
            jnp.sum(keep_rows),
        ]
    )
    back_weights = (
        lax.all_gather(in_proj, "shard", axis=0, tiled=True),
        lax.all_gather(qkv_proj, "shard", axis=0, tiled=True),
        lax.all_gather(ssm_out, "shard", axis=0, tiled=True),
        lax.all_gather(attn_out, "shard", axis=0, tiled=True),
        lax.all_gather(gate_up, "shard", axis=0, tiled=True),
        lax.all_gather(down_proj, "shard", axis=0, tiled=True),
    )
    b_in, b_attn, b_mo, b_ao, b_gu, b_down = back_weights
    grad_out = cotangent.astype(jnp.float32) * keep_rows[:, None]
    grad_mlp = grad_out.astype(jnp.bfloat16)
    g_down = jnp.dot(hid_low.T, grad_mlp, preferred_element_type=jnp.float32)
    grad_hid = jnp.dot(grad_mlp, b_down.T, preferred_element_type=jnp.float32)
    grad_gu = jnp.concatenate(
        [grad_hid * up_part * dsilu(gate_part), grad_hid * jax.nn.silu(gate_part)], axis=1
    ).astype(jnp.bfloat16)
    g_gu = jnp.dot(h2_low.T, grad_gu, preferred_element_type=jnp.float32)
    grad_h2 = jnp.dot(grad_gu, b_gu.T, preferred_element_type=jnp.float32)
    grad_res_n, g_norm_two = norm_back(grad_h2, residual, r_two, norm_two)
    grad_res = grad_out + grad_res_n
    grad_mix = grad_res.astype(jnp.bfloat16)
    g_mo = jnp.dot(normed_low.T, grad_mix, preferred_element_type=jnp.float32)
    g_ao = jnp.dot(attn_low.T, grad_mix, preferred_element_type=jnp.float32)
    grad_normed = jnp.dot(grad_mix, b_mo.T, preferred_element_type=jnp.float32)
    grad_attn = (
        jnp.dot(grad_mix, b_ao.T, preferred_element_type=jnp.float32)
        .astype(jnp.bfloat16)
        .reshape(tok_rows, KVH, q_per_kv, HD)
    )

    def delta_step(blk_index, acc_out):

        def delta_do_block(acc_out):
            k_blk, v_blk = block_keys(blk_index)
            prob_blk = probs_of(blk_index, k_blk)
            grad_prob = jnp.einsum(
                "tgqd,kgd->gqtk", grad_attn, v_blk, preferred_element_type=jnp.float32
            )
            return acc_out + jnp.sum(prob_blk * grad_prob, axis=-1)

        return lax.cond(needed(blk_index), delta_do_block, unchanged, acc_out)

    delta_row = lax.fori_loop(0, block_count, delta_step, jnp.zeros(row_shape, jnp.float32))

    def grad_step(blk_index, state_acc):

        def grad_do_block(state_acc):
            grad_query, grad_kv = state_acc
            k_blk, v_blk = block_keys(blk_index)
            prob_blk = probs_of(blk_index, k_blk)
            grad_prob = jnp.einsum(
                "tgqd,kgd->gqtk", grad_attn, v_blk, preferred_element_type=jnp.float32
            )
            grad_raw = (prob_blk * (grad_prob - delta_row[..., None]) * score_scale).astype(
                jnp.bfloat16
            )
            grad_query = grad_query + jnp.einsum(
                "gqtk,kgd->tgqd", grad_raw, k_blk, preferred_element_type=jnp.float32
            )
            grad_key = jnp.einsum(
                "gqtk,tgqd->kgd", grad_raw, q_low, preferred_element_type=jnp.float32
            )
            grad_value = jnp.einsum(
                "gqtk,tgqd->kgd",
                prob_blk.astype(jnp.bfloat16),
                grad_attn,
                preferred_element_type=jnp.float32,
            )
            kv_piece = jnp.concatenate(
                [grad_key.reshape(KBLK, KW), grad_value.reshape(KBLK, KW)], axis=1
            )
            grad_kv = lax.dynamic_update_slice_in_dim(grad_kv, kv_piece, blk_index * KBLK, 0)
            return (grad_query, grad_kv)

        return lax.cond(needed(blk_index), grad_do_block, unchanged, state_acc)

    grad_query, grad_kv = lax.fori_loop(
        0,
        block_count,
        grad_step,
        (
            jnp.zeros((tok_rows, KVH, q_per_kv, HD), jnp.float32),
            jnp.zeros((seq_len, 2 * KW), jnp.float32),
        ),
    )
    own_kv = lax.psum_scatter(grad_kv, "shard", scatter_dimension=0, tiled=True)
    neg_sines = -sines
    grad_q_raw = rotate(grad_query.reshape(tok_rows, QW), QH, cosines, neg_sines)
    grad_k_raw = rotate(own_kv[:, :KW], KVH, cosines, neg_sines)
    grad_qkv = jnp.concatenate([grad_q_raw, grad_k_raw, own_kv[:, KW:]], axis=1).astype(
        jnp.bfloat16
    )
    g_attn = jnp.dot(h_low.T, grad_qkv, preferred_element_type=jnp.float32)
    grad_h_attn = jnp.dot(grad_qkv, b_attn.T, preferred_element_type=jnp.float32)
    grad_gated, g_gated_gain = norm_back(grad_normed, gated, r_gate, gated_gain)
    grad_y = (grad_gated * silu_z).reshape(tok_rows, NH, HP)
    grad_z = grad_gated * ssm_y * dsilu(gate_z)

    def mamba_out(state_start, x_vals, b_vals, c_vals, dt_vals, la_vals, skip_vals):
        y_zero, state_local = ssd_spans(
            empty_state, x_vals, b_vals, c_vals, dt_vals, la_vals, skip_vals, seg_ids, before
        )
        fac_vals = carry_factor(la_vals)
        return (
            y_zero + carry_term(state_start, c_vals, fac_vals),
            state_local + state_start * fac_vals[-1][:, None, None],
        )

    unused_out, pull_back = jax.vjp(
        mamba_out, state_in, ssm_x, ssm_b, ssm_c, step_size, log_decay, skip_scale
    )
    first_pull = pull_back((grad_y, jnp.zeros_like(state_in)))
    later_state, unused_later = entering(
        (first_pull[0], dev_decay),
        "shard",
        combine_states,
        (jnp.zeros_like(state_in), jnp.ones_like(dev_decay)),
    )
    second = pull_back((jnp.zeros_like(grad_y), later_state))
    grad_x = first_pull[1] + second[1]
    grad_b = first_pull[2] + second[2]
    grad_c = first_pull[3] + second[3]
    grad_dt = first_pull[4] + second[4]
    grad_la = first_pull[5] + second[5]
    g_skip = first_pull[6] + second[6]
    g_a_log = jnp.sum(-grad_la * step_size * decay_rate, axis=0)
    grad_soft = (grad_dt - grad_la * decay_rate) * jax.nn.sigmoid(soft_in)
    g_dt_bias = jnp.sum(grad_soft, axis=0)
    grad_act = jnp.concatenate([grad_x.reshape(tok_rows, DS), grad_b, grad_c], axis=1)
    grad_conv = grad_act * dsilu(conv_pre)
    g_conv_bias = jnp.sum(grad_conv, axis=0)
    grad_padded = jnp.zeros((tok_rows + KC - 1, CONV_CH), jnp.float32)
    weight_cols = []
    for tap_index in range(KC):
        term_vals = grad_conv * tap_masks[tap_index]
        grad_padded = grad_padded + jnp.pad(
            term_vals * conv_weight[:, tap_index][None, :],
            ((tap_index, KC - 1 - tap_index), (0, 0)),
        )
        weight_cols.append(jnp.sum(term_vals * padded[tap_index : tap_index + tok_rows], axis=0))
    g_conv_weight = jnp.stack(weight_cols, axis=1)
    back_edge = from_behind(grad_padded[: KC - 1], "shard", -1)
    grad_xbc = grad_padded[KC - 1 :] + jnp.concatenate(
        [jnp.zeros((tok_rows - (KC - 1), CONV_CH), jnp.float32), back_edge], axis=0
    )
    grad_proj = jnp.concatenate([grad_z, grad_xbc, grad_soft], axis=1).astype(jnp.bfloat16)
    g_in = jnp.dot(h_low.T, grad_proj, preferred_element_type=jnp.float32)
    grad_h = jnp.dot(grad_proj, b_in.T, preferred_element_type=jnp.float32) + grad_h_attn
    grad_x_n, g_norm_one = norm_back(grad_h, x_full, r_one, norm_one)
    grad_input = grad_res + grad_x_n
    owned_grads = (
        lax.psum_scatter(g_in, "shard", scatter_dimension=0, tiled=True),
        lax.psum_scatter(g_attn, "shard", scatter_dimension=0, tiled=True),
        lax.psum_scatter(g_mo, "shard", scatter_dimension=0, tiled=True),
        lax.psum_scatter(g_ao, "shard", scatter_dimension=0, tiled=True),
        lax.psum_scatter(g_gu, "shard", scatter_dimension=0, tiled=True),
        lax.psum_scatter(g_down, "shard", scatter_dimension=0, tiled=True),
    )
    summed = lax.psum(
        (
            owned_grads[0],
            owned_grads[1],
            owned_grads[2],
            owned_grads[3],
            owned_grads[4],
            owned_grads[5],
        ),
        "replica",
    )
    small_sums = lax.psum(
        (
            g_norm_one,
            g_conv_weight,
            g_conv_bias,
            g_dt_bias,
            g_a_log,
            g_skip,
            g_gated_gain,
            g_norm_two,
            stat_local,
        ),
        ("replica", "shard"),
    )
    stat_sums = small_sums[8]
    rms_stats = jnp.sqrt(stat_sums[:3] / (stat_sums[3] * D))
    return (
        out_full.astype(jnp.bfloat16),
        grad_input,
        small_sums[0],
        summed[0],
        small_sums[1],
        small_sums[2],
        small_sums[3],
        small_sums[4],
        small_sums[5],
        small_sums[6],
        summed[1],
        summed[2],
        summed[3],
        small_sums[7],
        summed[4],
        summed[5],
        rms_stats,
    )


HEADS_AT = 6
XW = HEADS_AT * HP
LANES = 128
TB = 128
VMEM_BYTES = 20 * 1024 * 1024
AT_Y, AT_CORE, AT_BIT, AT_STARTS = 0, 1, {1: 2, 2: 3, 4: 4}, 5
Q_AT = XW
KV_AT = Q_AT + QW // 4
BC_AT = KV_AT + LANES
DT_AT = BC_AT + 2 * NS
W_FIRST = DT_AT + LANES
LOW = jnp.bfloat16
F32 = jnp.float32


def swap(block, bits):
    return lax.ppermute(block, "shard", [(i, i ^ bits) for i in range(lax.axis_size("shard"))])


def swap_far(block, bits):
    replicas, shards = lax.axis_size("replica"), lax.axis_size("shard")
    route = [
        (r * shards + s, (r ^ bits[s % 2]) * shards + s)
        for r in range(replicas)
        for s in range(shards)
    ]
    return lax.ppermute(block, ("replica", "shard"), route)


def after(value, other):
    return lax.optimization_barrier((value, other))[0]


def dot32(a, b):
    return jnp.dot(a, b, preferred_element_type=F32)


def dot_t(a, b):
    return lax.dot_general(a, b, (((1,), (1,)), ((), ())), preferred_element_type=F32)


def t_dot(a, b):
    return lax.dot_general(a, b, (((0,), (0,)), ((), ())), preferred_element_type=F32)


def rough(a, b, dims=((1,), (0,))):
    return lax.dot_general(
        a.astype(LOW), b.astype(LOW), (dims, ((), ())), preferred_element_type=F32
    )


def picked(a, b, dims=((1,), (0,)), terms=2):
    value, total = (b, 0.0) if a.dtype == LOW else (a, 0.0)
    for _ in range(terms):
        low = value.astype(LOW)
        pair = (a, low) if a.dtype == LOW else (low, b)
        total = total + lax.dot_general(*pair, (dims, ((), ())), preferred_element_type=F32)
        value = value - low.astype(F32)
    return total


def iota(shape, axis):
    return lax.broadcasted_iota(jnp.int32, shape, axis)


def count_starts(info, where):
    total = (info[AT_STARTS] <= where).astype(jnp.int32)
    for k in range(AT_STARTS + 1, info.shape[0]):
        total = total + (info[k] <= where).astype(jnp.int32)
    return total


def part(index, size):
    return pl.ds(pl.multiple_of(index * size, size), size)


def part_at(start, index, step, size):
    return pl.ds(pl.multiple_of(start + index * step, LANES), size)


def peers(info):
    y, c = info[AT_Y], info[AT_CORE]
    return (2 * y + c, 2 * y + 1 - c, 2 * (1 - y) + c, 2 * (1 - y) + 1 - c)


def bit_of(info, bits):
    return jnp.where(info[AT_CORE] == 0, info[AT_BIT[bits[0]]], info[AT_BIT[bits[1]]])


def f32_of(*shape):
    return jax.ShapeDtypeStruct(shape, F32)


def low_of(*shape):
    return jax.ShapeDtypeStruct(shape, LOW)


def call(kernel, outs, info, *operands, scratch=()):
    whole = pl.BlockSpec(memory_space=pltpu.VMEM)
    return pl.pallas_call(
        kernel,
        out_shape=outs,
        in_specs=[pl.BlockSpec(memory_space=pltpu.SMEM)] + [whole] * len(operands),
        out_specs=jax.tree.map(lambda _: whole, outs),
        scratch_shapes=scratch,
        compiler_params=pltpu.CompilerParams(vmem_limit_bytes=VMEM_BYTES),
    )(info, *operands)


def pack_in_kernel(info, w_in, w_qkv, own, core, far, z_own, z_core, z_far):
    y, places = info[AT_Y], peers(info)

    def shared(dst, chip):
        k, v = w_qkv[:, QW : QW + KW], w_qkv[:, QW + KW :]
        first = jnp.concatenate([k[:, :HD], v[:, :HD]], axis=1)
        second = jnp.concatenate([k[:, HD:], v[:, HD:]], axis=1)
        dst[KV_AT:BC_AT, :] = jnp.where(chip == 0, first, second).T
        dst[BC_AT:DT_AT, :] = w_in[2 * DS : 2 * DS + 2 * NS, :]
        dst[DT_AT:W_FIRST, :] = jnp.zeros((LANES, dst.shape[1]), LOW)
        dst[DT_AT : DT_AT + NH, :] = w_in[DS + CONV_CH :, :]

    for place, dst, at in zip(places, (own, core, far, far), (0, 0, W_FIRST, 0)):
        dst[at : at + XW, :] = w_in[part_at(DS, place, XW, XW), :]
        dst[at + XW : at + KV_AT, :] = w_qkv[:, part(place, QW // 4)].T
    for place, dst, at in zip(places, (z_own, z_core, z_far, z_far), (0, 0, XW, 0)):
        dst[at : at + XW, :] = w_in[part_at(0, place, XW, XW), :]
    shared(own, y)
    shared(core, y)
    shared(far, 1 - y)


def prepare_kernel(
    info, conv_weight, conv_bias, dt_bias, a_log, skip, gain, norm_one, norm_two, mask, cotangent,
    taps, bias, bias_own, rate, skip_wide, gain_own, gain_one, gain_two, keep, grad, turn, wide,
):
    place = peers(info)[0]
    for src, dst in ((conv_weight, taps), (conv_bias, bias)):
        dst[:, :XW] = src[:, part(place, XW)]
        dst[:, XW:] = src[:, DS:]
    gain_own[...] = gain[:, part(place, XW)]
    gain_one[...] = norm_one[...]
    gain_two[...] = norm_two[...]
    pick = own_heads_pick(info)
    wide[...] = jnp.zeros_like(wide)
    for k, src in enumerate((dt_bias, a_log, skip)):
        wide[k : k + 1, :NH] = src[...]
    own = picked(wide[...], pick, terms=3)
    bias_own[...] = own[0:1]
    rate[...] = jnp.exp(own[1:2])
    skip_wide[...] = picked(own, head_spread(), terms=3)[2:3]
    column = jnp.broadcast_to(mask[...].astype(F32), (LANES, LANES)).T
    keep[...] = column
    grad[...] = (cotangent[...].astype(F32) * column[:, :1]).astype(LOW)
    row, col, half = iota((LANES, LANES), 0), iota((LANES, LANES), 1), HD // 2
    down, up = (row == col + half).astype(F32), (row == col - half).astype(F32)
    turn[...] = jnp.where((col // half) % 2 == 0, -down, up).astype(LOW)


def total_kernel(info, a, b, out):
    out[...] = a[...] + b[...]


def pack_up_kernel(info, w_up, own, core, far):
    quarter, half = FF // 4, w_up.shape[0] // 2
    places = peers(info)
    for place, dst in zip(places, (own, core)):
        dst[:, :quarter] = w_up[:, part_at(0, place, quarter, quarter)]
        dst[:, quarter:] = w_up[:, part_at(FF, place, quarter, quarter)]
    mine = part(info[AT_BIT[1]], half)
    for k, place in enumerate(places[2:]):
        rows = slice(k * half, (k + 1) * half)
        far[rows, :quarter] = w_up[mine, part_at(0, place, quarter, quarter)]
        far[rows, quarter:] = w_up[mine, part_at(FF, place, quarter, quarter)]


def head_spread():
    row, col = iota((LANES, XW), 0), iota((LANES, XW), 1)
    return ((col >= row * HP) & (col < (row + 1) * HP)).astype(LOW)


def own_heads_pick(info):
    row, col = iota((LANES, LANES), 0), iota((LANES, LANES), 1)
    return ((row == col + peers(info)[0] * HEADS_AT) & (col < HEADS_AT)).astype(LOW)


def step_sizes(soft):
    real = iota(soft.shape, 1) < HEADS_AT
    return jnp.where(real, jnp.maximum(soft, 0.0) + jnp.log1p(jnp.exp(-jnp.abs(soft))), 0.0)


def span_parts(info, first, dt, la):
    shape = (SPAN, SPAN)
    row, col = iota(shape, 0), iota(shape, 1)
    seg_row = count_starts(info, row + first)
    seg_col = count_starts(info, col + first)
    seen = (seg_row == seg_col) & (row >= col)
    before = count_starts(info, first - 1)
    last = count_starts(info, first + SPAN - 1)
    total = picked((row >= col).astype(LOW), la, terms=3)
    carried = jnp.exp(total) * (seg_row == before).astype(F32)
    tail = jnp.exp(total[SPAN - 1 :] - total) * (seg_row == last).astype(F32)
    return seen, total, total.T, dt.T, carried, tail


def decay_of(seen, total, total_t, h):
    return jnp.exp(jnp.where(seen, total[:, h : h + 1] - total_t[h : h + 1, :], NEG))


def tap_masks(info, seg):
    seq = seg.shape[0] - 8
    seg[:8, :] = jnp.full((8, LANES), -1, jnp.int32)
    seg[8:, :] = count_starts(info, iota((seq, LANES), 0))
    here = seg[8:, :]
    return [
        (seg[8 - back : 8 - back + seq, :] == here).astype(F32) for back in range(KC - 1, 0, -1)
    ]


def forward_kernel(
    info, h_own, h_core, h_far, h_far_core, w_own, w_core, w_far, w_far_core,
    norm, taps, bias, dt_bias, rate, skip, cosines, sines, turn,
    h_low, w_full, xbc, conv_pre, soft, q_low, kv_low, y_out, states,
    padded, act, step, seg,
):
    seq = h_low.shape[0]
    places = peers(info)
    for place, ref in zip(places, (h_own, h_core, h_far, h_far_core)):
        x = ref[...].astype(F32)
        h_low[part(place, TB), :] = (x * rms_scale(x) * norm[...]).astype(LOW)
    depth = w_own.shape[1]
    for place, ref, at in zip(places, (w_own, w_core, w_far, w_far_core), (0, 0, W_FIRST, 0)):
        w_full[:KV_AT, part(place, depth)] = ref[at : at + KV_AT, :]
        w_full[KV_AT:, part(place, depth)] = ref[KV_AT:W_FIRST, :]
    h = h_low[...]
    xbc[:, :XW] = dot_t(h, w_full[:XW, :])
    xbc[:, XW:] = dot_t(h, w_full[BC_AT:DT_AT, :])
    rest = dot_t(h, w_full[Q_AT:BC_AT, :])
    q, kv = rest[:, :LANES], rest[:, LANES:]
    soft[...] = picked(dot_t(h, w_full[DT_AT:, :]), own_heads_pick(info), terms=3) + dt_bias[...]

    def turned(value):
        return value * cosines[...] + picked(value, turn[...]) * sines[...]

    q_low[...] = turned(q).astype(LOW)
    kv_low[...] = jnp.where(iota(kv.shape, 1) < HD, turned(kv), kv).astype(LOW)

    width = xbc.shape[1]
    padded[:8, :] = jnp.zeros((8, width), F32)
    padded[8:, :] = xbc[...]
    masks = tap_masks(info, seg)
    for block in range(0, width, LANES):
        lanes = slice(block, block + LANES)
        total = bias[:, lanes] + taps[KC - 1 : KC, lanes] * padded[8:, lanes]
        for j in range(KC - 1):
            start = 8 - (KC - 1 - j)
            total = total + taps[j : j + 1, lanes] * padded[start : start + seq, lanes] * masks[j]
        conv_pre[:, lanes] = total
        act[:, lanes] = total * jax.nn.sigmoid(total)

    step[...] = step_sizes(soft[...])
    spread = head_spread()
    state = jnp.zeros((NS, XW), F32)
    for k in range(seq // SPAN):
        rows = pl.ds(k * SPAN, SPAN)
        x = act[rows, :XW]
        b = act[rows, XW : XW + NS]
        c = act[rows, XW + NS :]
        dt = step[rows, :]
        seen, total, total_t, dt_t, carried, tail = span_parts(
            info, k * SPAN, dt, -dt * rate[...]
        )
        states[k] = state
        inner = rough(c, b, ((1,), (1,)))
        wide = picked(carried, spread)
        y = rough(c, state) * wide + x * skip[...]
        parts = []
        for h in range(HEADS_AT):
            mixing = decay_of(seen, total, total_t, h) * inner * dt_t[h : h + 1, :]
            parts.append(rough(mixing, x[:, h * HP : (h + 1) * HP]))
        y_out[rows, :] = y + jnp.concatenate(parts, axis=1)
        weighted = x * picked(tail * dt, spread)
        state = state * wide[SPAN - 1 :] + rough(b, weighted, ((0,), (0,)))


def gate_kernel(info, h_low, z_own, z_core, z_far, z_far_core, y, z_full, gate_z, square):
    depth = z_own.shape[1]
    for place, ref, at in zip(peers(info), (z_own, z_core, z_far, z_far_core), (0, 0, XW, 0)):
        z_full[:, part(place, depth)] = ref[at : at + XW, :]
    z = dot_t(h_low[...], z_full[...])
    gate_z[...] = z
    gated = y[...] * (z * jax.nn.sigmoid(z))
    square[...] = picked(jnp.ones((8, XW), LOW), gated * gated, ((1,), (1,)))


def column_of(row):
    return jnp.concatenate(
        [row[:, k : k + LANES].T[:, :1] for k in range(0, row.shape[1], LANES)], axis=0
    )


def output_kernel(
    info, sq_a, sq_b, y, gate_z, gain, attn, ssm_out, attn_out, given, kept, normed
):
    z = gate_z[...]
    scale = lax.rsqrt(column_of(sq_a[...] + sq_b[...]) / DS + EPS)
    normed[...] = (y[...] * (z * jax.nn.sigmoid(z)) * scale * gain[...]).astype(LOW)
    c = info[AT_CORE]
    for core, dst in ((1 - c, given), (c, kept)):
        for k in range(2):
            rows = part(2 * k + core, TB)
            dst[k] = dot32(normed[rows, :], ssm_out[...]) + dot32(attn[rows, :], attn_out[...])


def add_kernel(info, kept, moved, chip, low):
    total = kept[...] + moved[...]
    chip[...] = total
    low[...] = total.astype(LOW)


def add_split_kernel(info, kept, moved, mine, given):
    y = info[AT_Y]
    mine[...] = kept[y] + moved[y]
    given[...] = kept[1 - y] + moved[1 - y]


def pair_of(info, own, far, dst):
    y = info[AT_Y]
    dst[y] = own[...]
    dst[1 - y] = far[...]


def second_norm_kernel(
    info, chip, moved, h_own, h_far, norm, keep, residual, h2, mixed_sum, x_pair
):
    pair_of(info, h_own, h_far, x_pair)
    mixed = chip[...] + moved[...].astype(F32)
    total = x_pair[...].astype(F32) + mixed
    residual[...] = total
    h2[...] = (total * rms_scale(total) * norm[...]).astype(LOW)
    mine = (chip[info[AT_Y]] + moved[info[AT_Y]].astype(F32)) * keep[:, :1]
    mixed_sum[...] = jnp.sum(mine * mine, axis=0, keepdims=True)


def mlp_kernel(
    info, h2, h2_core, u_own, u_core, u_y, u_x, u_y_core, u_x_core, g_own, g_core, g_far, g_far_core, w_down,
    given, kept, hid, ggu, h2_cat, gmlp, u_full,
):
    y, quarter = info[AT_Y], FF // 4
    half = 2 * TB
    for k in range(2):
        h2_cat[k * TB : (k + 1) * TB, :] = h2[k]
        h2_cat[half + k * TB : half + (k + 1) * TB, :] = h2_core[k]
    for at, ref in ((y, g_own), (1 - y, g_far), (2 + y, g_core), (3 - y, g_far_core)):
        gmlp[part(at, TB), :] = ref[...]
    depth = u_own.shape[0]
    places, x, piece = peers(info), info[AT_BIT[1]], depth // 2
    u_full[part(places[0], depth), :] = u_own[...]
    u_full[part(places[1], depth), :] = u_core[...]
    for at, ref, ref_core in ((x, u_y, u_y_core), (1 - x, u_x, u_x_core)):
        u_full[part(2 * places[2] + at, piece), :] = ref[:piece, :]
        u_full[part(2 * places[3] + at, piece), :] = ref_core[piece:, :]
    tile = quarter // 2
    for t in range(0, quarter, tile):
        ghid = dot_t(gmlp[...], w_down[t : t + tile, :])
        gate = dot32(h2_cat[...], u_full[:, t : t + tile])
        up = dot32(h2_cat[...], u_full[:, quarter + t : quarter + t + tile])
        sig = jax.nn.sigmoid(gate)
        silu = gate * sig
        hid[:, t : t + tile] = (silu * up).astype(LOW)
        ggu[:, t : t + tile] = (ghid * up * (sig * (1.0 + gate * (1.0 - sig)))).astype(LOW)
        ggu[:, quarter + t : quarter + t + tile] = (ghid * silu).astype(LOW)
    for t in range(0, D, 2 * tile):
        cols = slice(t, t + 2 * tile)
        part_sum = dot_t(ggu[half:, :], u_full[cols, :])
        given[0, :, cols] = part_sum[:TB]
        given[1, :, cols] = part_sum[TB:]
        part_sum = dot_t(ggu[:half, :], u_full[cols, :])
        kept[0, :, cols] = part_sum[:TB]
        kept[1, :, cols] = part_sum[TB:]


def down_kernel(info, hid, w_down, given, kept):
    half = 2 * TB
    for k in range(2):
        given[k] = dot32(hid[half + k * TB : half + (k + 1) * TB, :], w_down[...])
        kept[k] = dot32(hid[k * TB : (k + 1) * TB, :], w_down[...])


def grad_rows_kernel(bit, info, left, right, given, kept):
    mine = bit_of(info, bit)
    half = left.shape[1] // 2
    given[...] = t_dot(left[:, part(1 - mine, half)], right[...]).astype(LOW)
    kept[...] = t_dot(left[:, part(mine, half)], right[...])


def grad_mid_kernel(bit, info, normed, attn, right, given, kept, left):
    left[:, :XW] = normed[...]
    left[:, XW:] = attn[...]
    grad_rows_kernel(bit, info, left, right, given, kept)


def grad_columns_kernel(bit, info, left, right, given, kept):
    mine = bit_of(info, bit)
    step = left.shape[1] // 4
    for k in range(4):
        other = left[:, part_at(k * step, 1 - mine, step // 2, step // 2)]
        given[k] = t_dot(other, right[...]).astype(LOW)
    for k in range(4):
        own = left[:, part_at(k * step, mine, step // 2, step // 2)]
        kept[k] = t_dot(own, right[...])


def norm_back_pair_kernel(info, chip, moved, residual, norm, g_own, g_far, gres, gmix, g_norm, gout):
    pair_of(info, g_own, g_far, gout)
    gh2 = chip[...] + moved[...].astype(F32)
    value = residual[...]
    scale = rms_scale(value)
    uu = gh2 * norm[...]
    mean = jnp.mean(uu * value, axis=-1, keepdims=True)
    grad = gout[...].astype(F32) + scale * uu - value * scale**3 * mean
    gres[...] = grad
    gmix[...] = grad.astype(LOW)
    y = info[AT_Y]
    mine = residual[y]
    g_norm[...] = jnp.sum(
        (chip[y] + moved[y].astype(F32)) * mine * rms_scale(mine), axis=0, keepdims=True
    )


def output_back_kernel(
    info, gmix, gmix_core, y, gate_z, gain, ssm_out, attn_out, gmix_all, gnormed, gattn, uv
):
    c = info[AT_CORE]
    for core, src in ((c, gmix), (1 - c, gmix_core)):
        for k in range(2):
            gmix_all[part(2 * k + core, TB), :] = src[k]
    grad = dot_t(gmix_all[...], ssm_out[...])
    gnormed[...] = grad
    z = gate_z[...]
    product = grad * gain[...] * (y[...] * (z * jax.nn.sigmoid(z)))
    uv[...] = picked(jnp.ones((8, XW), LOW), product, ((1,), (1,)))
    gattn[...] = dot_t(gmix_all[...], attn_out[...]).astype(LOW)


def conv_back(masks, gconv, pre, taps, inputs, gpad):
    seq = gconv.shape[0]
    gconv = gconv * dsilu(pre)
    gpad[seq:, :] = jnp.zeros((8, LANES), F32)
    total = taps[KC - 1] * gconv
    rows = []
    for j in range(KC - 1):
        back = KC - 1 - j
        term = gconv * masks[j]
        rows.append(jnp.sum(term * inputs(j), axis=0, keepdims=True))
        gpad[:seq, :] = term * taps[j]
        total = total + gpad[back : back + seq, :]
    rows.append(jnp.sum(gconv * inputs(KC - 1), axis=0, keepdims=True))
    rows.append(jnp.sum(gconv, axis=0, keepdims=True))
    return total, rows


def gate_back_kernel(
    info, sq_a, sq_b, uv_a, uv_b, gnormed, y, gate_z, gain, gq, gkv, early, gy, g_gain
):
    z = gate_z[...]
    sig = jax.nn.sigmoid(z)
    gated = y[...] * (z * sig)
    scale = lax.rsqrt(column_of(sq_a[...] + sq_b[...]) / DS + EPS)
    mean = column_of(uv_a[...] + uv_b[...]) / DS
    grad = gnormed[...]
    ggz = scale * (grad * gain[...]) - gated * scale**3 * mean
    gy[...] = ggz * (z * sig)
    early[:, :XW] = (ggz * y[...] * (sig * (1.0 + z * (1.0 - sig)))).astype(LOW)
    early[:, XW : XW + LANES] = gq[...]
    half = (iota(gkv.shape, 1) < HD) == (info[AT_CORE] == 0)
    early[:, XW + LANES :] = jnp.where(half, gkv[...], 0.0).astype(LOW)
    g_gain[...] = jnp.sum(grad * gated * scale, axis=0, keepdims=True)


def scan_back_kernel(
    info, xbc, conv_pre, soft, rate, skip, states, taps, gy,
    gx_low, gbc_given, gbc_kept, gdr, gsoft_low, g_taps, g_skip, g_heads,
    act, step, gact, gdt, gla, padded, gpad, seg,
):
    seq = gy.shape[0]
    pre = conv_pre[...]
    act[...] = pre * jax.nn.sigmoid(pre)
    step[...] = step_sizes(soft[...])
    spread = head_spread()
    shape = (SPAN, SPAN)
    row, col = iota(shape, 0), iota(shape, 1)
    upper = (col >= row).astype(LOW)
    later = jnp.zeros((NS, XW), F32)
    skip_sum = jnp.zeros((1, XW), F32)
    for k in reversed(range(seq // SPAN)):
        rows = pl.ds(k * SPAN, SPAN)
        x = act[rows, :XW]
        b = act[rows, XW : XW + NS]
        c = act[rows, XW + NS :]
        dt = step[rows, :]
        g = gy[rows, :]
        state = states[k]
        seen, total, total_t, dt_t, carried, tail = span_parts(
            info, k * SPAN, dt, -dt * rate[...]
        )
        inner = rough(c, b, ((1,), (1,)))
        wide = picked(carried, spread)
        tail_dt = tail * dt
        wide_tail = picked(tail_dt, spread)
        g_carried = g * wide
        ginner = jnp.zeros(shape, F32)
        out_sum = jnp.zeros(shape, F32)
        in_sum = jnp.zeros(shape, F32)
        parts = []
        for h in range(HEADS_AT):
            own = slice(h * HP, (h + 1) * HP)
            decay = decay_of(seen, total, total_t, h)
            product = rough(g[:, own], x[:, own], ((1,), (1,))) * decay
            scaled = product * dt_t[h : h + 1, :]
            ginner = ginner + scaled
            out_sum = out_sum + jnp.where(
                col == h, jnp.sum(scaled * inner, axis=1, keepdims=True), 0.0
            )
            in_sum = in_sum + jnp.where(
                row == h, jnp.sum(product * inner, axis=0, keepdims=True), 0.0
            )
            mixing = decay * inner * dt_t[h : h + 1, :]
            parts.append(rough(mixing, g[:, own], ((0,), (0,))))
        from_later = rough(b, later)
        gact[rows, :XW] = (
            jnp.concatenate(parts, axis=1) + from_later * wide_tail + g * skip[...]
        )
        gact[rows, XW : XW + NS] = rough(ginner, c, ((0,), (0,))) + rough(
            x * wide_tail, later, ((1,), (1,))
        )
        gact[rows, XW + NS :] = rough(ginner, b) + rough(g_carried, state, ((1,), (1,)))
        tail_in = picked(x * from_later, spread, ((1,), (1,)))
        state_out = picked(rough(c, state) * g_carried, spread, ((1,), (1,)))
        in_col = in_sum.T
        gdt[rows, :] = in_col + tail_in * tail
        moved = tail_in * tail_dt
        kept = picked(
            jnp.sum(state * later, axis=0, keepdims=True) * wide[SPAN - 1 :],
            spread,
            ((1,), (1,)),
        )
        at_end = jnp.sum(moved, axis=0, keepdims=True) + kept
        change = out_sum - in_col * dt + state_out - moved
        gla[rows, :] = picked(upper, change, terms=3) + at_end
        skip_sum = skip_sum + jnp.sum(g * x, axis=0, keepdims=True)
        later = later * wide[SPAN - 1 :] + rough(c, g_carried, ((0,), (0,)))
    g_skip[...] = skip_sum

    core = info[AT_CORE]
    gbc_given[...] = gact[:, part_at(XW, 1 - core, NS, NS)]
    gbc_kept[...] = gact[:, part_at(XW, core, NS, NS)]

    gsoft = (gdt[...] - gla[...] * rate[...]) * jax.nn.sigmoid(soft[...])
    gsoft = jnp.where(iota(gsoft.shape, 1) < HEADS_AT, gsoft, 0.0)
    gsoft_low[...] = gsoft.astype(LOW)
    gdr[...] = dot_t(gsoft.astype(LOW), own_heads_pick(info)).astype(LOW)
    g_heads[0:1, :] = jnp.sum(-gla[...] * step[...] * rate[...], axis=0, keepdims=True)
    g_heads[1:2, :] = jnp.sum(gsoft, axis=0, keepdims=True)
    g_heads[2:, :] = jnp.zeros((6, LANES), F32)

    padded[:8, :] = jnp.zeros((8, LANES), F32)
    masks = tap_masks(info, seg)
    g_taps[...] = jnp.zeros_like(g_taps)
    for block in range(0, XW, LANES):
        lanes = slice(block, block + LANES)
        padded[8:, :] = xbc[:, lanes]
        total, sums = conv_back(
            masks, gact[:, lanes], conv_pre[:, lanes],
            [taps[j : j + 1, lanes] for j in range(KC)],
            lambda j: padded[8 - (KC - 1 - j) : 8 - (KC - 1 - j) + seq, :], gpad,
        )
        gx_low[:, lanes] = total.astype(LOW)
        for j, value in enumerate(sums):
            g_taps[j : j + 1, lanes] = value


def late_kernel(
    bit, info, gbc_kept, gbc_moved, xbc, conv_pre, taps, gx_low, gsoft, h_low,
    given, kept, g_dt, gbc_low, g_taps, left, padded, gpad, seg,
):
    seq = gx_low.shape[0]
    lanes = part_at(XW, info[AT_CORE], NS, NS)
    padded[:8, :] = jnp.zeros((8, LANES), F32)
    padded[8:, :] = xbc[:, lanes]
    total, sums = conv_back(
        tap_masks(info, seg), gbc_kept[...] + gbc_moved[...], conv_pre[:, lanes],
        [taps[j : j + 1, lanes] for j in range(KC)],
        lambda j: padded[8 - (KC - 1 - j) : 8 - (KC - 1 - j) + seq, :], gpad,
    )
    g_taps[...] = jnp.zeros_like(g_taps)
    for j, value in enumerate(sums):
        g_taps[j : j + 1, :] = value
    gbc_low[...] = total.astype(LOW)
    left[:, :XW] = gx_low[...]
    left[:, XW:] = gbc_low[...]
    mine, half = bit_of(info, bit), left.shape[1] // 2
    given[0] = t_dot(left[:, part(1 - mine, half)], h_low[...]).astype(LOW)
    kept[0] = t_dot(left[:, part(mine, half)], h_low[...])
    g_dt[...] = t_dot(gsoft[...], h_low[...])[:8]


def early_kernel(bit, info, early, h_low, given, kept):
    mine = bit_of(info, bit)
    full = t_dot(early[...], h_low[...])
    half = full.shape[0] // 2
    first, second = full[:half], full[half:]
    given[0] = jnp.where(mine == 0, second, first).astype(LOW)
    kept[0] = jnp.where(mine == 0, first, second)


def inputs_back_kernel(
    info, gx_low, early, gbc_low, gdr, w_full, z_full, given, kept, back
):
    c = info[AT_CORE]
    gbc = gbc_low[...]
    nothing = jnp.zeros_like(gbc)
    back[:, :XW] = gx_low[...]
    back[:, Q_AT:BC_AT] = early[:, XW:]
    back[:, BC_AT : BC_AT + NS] = jnp.where(c == 0, gbc, nothing)
    back[:, BC_AT + NS : DT_AT] = jnp.where(c == 0, nothing, gbc)
    back[:, DT_AT:W_FIRST] = gdr[...]
    back[:, W_FIRST:] = early[:, :XW]
    for core, dst in ((1 - c, given), (c, kept)):
        for k in range(2):
            rows = part(2 * k + core, TB)
            dst[k] = dot32(back[rows, :W_FIRST], w_full[...]) + dot32(
                back[rows, W_FIRST:], z_full[...]
            )


def first_norm_back_kernel(info, mine, moved, hidden, norm, gres, out, g_norm):
    gh = mine[...] + moved[...]
    value = hidden[...].astype(F32)
    scale = rms_scale(value)
    uu = gh * norm[...]
    mean = jnp.mean(uu * value, axis=-1, keepdims=True)
    out[...] = gres[info[AT_Y]] + scale * uu - value * scale**3 * mean
    g_norm[...] = jnp.sum(gh * value * scale, axis=0, keepdims=True)


def result_kernel(info, mine, moved, residual, keep, out, sums):
    mlp = mine[...] + moved[...]
    full = residual[info[AT_Y]] + mlp
    out[...] = full.astype(LOW)
    full = full * keep[:, :1]
    mlp = mlp * keep[:, :1]
    sums[0:1, :] = jnp.sum(full * full, axis=0, keepdims=True)
    sums[1:2, :] = jnp.sum(mlp * mlp, axis=0, keepdims=True)
    sums[2:, :] = jnp.zeros((6, D), F32)


def attend_kernel(info, q_ref, kv_ref, out_ref, lse_ref):
    scale = 1.0 / math.sqrt(HD)
    heads = q_ref.shape[1] // HD
    for k in range(q_ref.shape[0] // SPAN):
        rows, reach = pl.ds(k * SPAN, SPAN), (k + 1) * SPAN
        keys, values = kv_ref[:reach, :HD], kv_ref[:reach, HD:]
        counted = counted_keys(info, k * SPAN, reach)
        outs, tops = [], []
        for h in range(heads):
            s = dot_t(q_ref[rows, h * HD : (h + 1) * HD], keys) * scale
            s = jnp.where(counted, s, NEG)
            top = jnp.max(s, axis=1, keepdims=True)
            lse = top + jnp.log(jnp.sum(jnp.exp(s - top), axis=1, keepdims=True))
            prob = jnp.exp(s - lse).astype(LOW)
            outs.append(dot32(prob, values))
            tops.append(lse)
        out_ref[rows, :] = jnp.concatenate(outs, axis=1).astype(LOW)
        lane = iota((SPAN, LANES), 1)
        lse_ref[rows, :] = sum(jnp.where(lane == h, t, 0.0) for h, t in enumerate(tops))


def counted_keys(info, first, reach):
    shape = (SPAN, reach)
    row, col = iota(shape, 0) + first, iota(shape, 1)
    return (col <= row) & (count_starts(info, row) == count_starts(info, col))


def attend_back_kernel(
    info, q_ref, kv_ref, lse_ref, gout_ref, cosines, sines, turn, gq_ref, gkv_ref, gq_rot
):
    scale = 1.0 / math.sqrt(HD)
    heads = q_ref.shape[1] // HD
    gkv_ref[...] = jnp.zeros_like(gkv_ref)
    for k in range(q_ref.shape[0] // SPAN):
        rows, reach = pl.ds(k * SPAN, SPAN), (k + 1) * SPAN
        keys, values = kv_ref[:reach, :HD], kv_ref[:reach, HD:]
        counted = counted_keys(info, k * SPAN, reach)
        outs, gkeys, gvalues = [], 0.0, 0.0
        for h in range(heads):
            own = slice(h * HD, (h + 1) * HD)
            q, gout = q_ref[rows, own], gout_ref[rows, own]
            s = dot_t(q, keys) * scale
            pe = jnp.exp(jnp.where(counted, s - lse_ref[rows, h : h + 1], NEG))
            gprob = dot_t(gout, values)
            delta = jnp.sum(pe * gprob, axis=1, keepdims=True)
            gs = (pe * (gprob - delta) * scale).astype(LOW)
            outs.append(dot32(gs, keys))
            gkeys = gkeys + t_dot(gs, q)
            gvalues = gvalues + t_dot(pe.astype(LOW), gout)
        gq_rot[rows, :] = jnp.concatenate(outs, axis=1)
        gkv_ref[:reach, :] += jnp.concatenate([gkeys, gvalues], axis=1)
    value = gq_rot[...]
    gq_ref[...] = (value * cosines[...] - picked(value, turn[...]) * sines[...]).astype(LOW)


def keys_back_kernel(info, own, moved, cosines, sines, turn, out):
    value = own[...] + moved[...]
    back = value * cosines[...] - picked(value, turn[...]) * sines[...]
    out[...] = jnp.where(iota(value.shape, 1) < HD, back, value)


def halve_kernel(bit, info, kept, moved, given_next, kept_next):
    mine = bit_of(info, bit)
    half = kept.shape[1] // 2
    own, other = part(mine, half), part(1 - mine, half)
    given_next[...] = (kept[:, other, :] + moved[:, other, :].astype(F32)).astype(LOW)
    kept_next[...] = kept[:, own, :] + moved[:, own, :].astype(F32)


def settle_kernel(info, kept, moved, out):
    out[...] = (kept[...] + moved[...].astype(F32)).astype(LOW)


def settle_columns_kernel(info, kept, moved, own, core, far, far_core):
    for place, dst in zip(peers(info), (own, core, far, far_core)):
        dst[...] = (kept[place] + moved[place].astype(F32)).astype(LOW)


def settle_lanes_kernel(info, kept, moved, own, core, far, far_core):
    for place, dst in zip(peers(info), (own, core, far, far_core)):
        lanes = part(place, dst.shape[1])
        dst[...] = (kept[0, :, lanes] + moved[0, :, lanes].astype(F32)).astype(LOW)


def gather_columns_kernel(info, own, core, far, far_core, out):
    for place, ref in zip(peers(info), (own, core, far, far_core)):
        out[place] = ref[...]


def join_kernel(bit, info, own, moved, out):
    mine, size = bit_of(info, bit), own.shape[1]
    out[:, part(mine, size), :] = own[...]
    out[:, part(1 - mine, size), :] = moved[...]


def sum_steps(info, given, kept, order, spread):
    moved = swap_far(given, order[0])
    for bit in order[1:]:
        moved = after(moved, (yield given))
        n, size, width = kept.shape
        given, kept = call(
            functools.partial(halve_kernel, bit),
            (low_of(n, size // 2, width), f32_of(n, size // 2, width)),
            info, kept, moved,
        )
        moved = swap_far(given, bit)
    moved = after(moved, (yield given))
    if spread:
        n, size, width = kept.shape
        if n == 4:
            kernel, block = settle_columns_kernel, (size, width)
        else:
            kernel, block = settle_lanes_kernel, (size, width // 4)
        blocks = call(kernel, (low_of(*block),) * 4, info, kept, moved)
        sent = [swap(blocks[bits], bits) for bits in (1, 2, 3)]
        sent = after(sent, (yield blocks))
        own = call(gather_columns_kernel, low_of(4, *block), info, blocks[0], *sent)
    else:
        own = call(settle_kernel, low_of(*kept.shape), info, kept, moved)
    for bit in order[:0:-1]:
        moved = swap_far(own, bit)
        moved = after(moved, (yield own))
        n, size, width = own.shape
        own = call(
            functools.partial(join_kernel, bit), low_of(n, 2 * size, width), info, own, moved
        )
    moved = swap_far(own, order[0])
    return own, after(moved, (yield own))


class Running:
    def __init__(self, *args):
        self.steps, self.result, self.done = sum_steps(*args), None, False
        self.sent = next(self.steps)

    def step(self, value):
        if not self.done:
            try:
                self.sent = self.steps.send(value)
            except StopIteration as end:
                self.result, self.done = end.value, True
        return self.sent


def each_part(bit, info, own, moved):
    mine = bit_of(info, bit)
    return ((mine, own), (1 - mine, moved))


def quarters(bit, info, own, moved, source):
    size = own.shape[1] // 2
    same = info[AT_CORE] == source % 2
    for at, ref in each_part(bit, info, own, moved):
        for j in range(2):
            yield jnp.where(same, 2 * at + j, 2 * j + at), ref, slice(j * size, (j + 1) * size)


def finish_up_kernel(bit, info, own, moved, out):
    quarter = FF // 4
    size = own.shape[1] // 2
    for k in range(4):
        for at, ref, rows in quarters(bit, info, own, moved, k):
            block = ref[k, rows, :].astype(F32)
            out[part(at, size), k * quarter : (k + 1) * quarter] = block[:, :quarter]
            out[part(at, size), FF + k * quarter : FF + (k + 1) * quarter] = block[:, quarter:]


def finish_in_kernel(
    bit, info, early, early_moved, late, late_moved, small, out, out_qkv, early_full, late_full
):
    for pair, full in (((early, early_moved), early_full), ((late, late_moved), late_full)):
        size = full.shape[1] // 4
        for k in range(4):
            for at, ref, rows in quarters(bit, info, *pair, k):
                full[k, part(at, size), :] = ref[k, rows, :]
    for k in range(4):
        out[k * XW : (k + 1) * XW, :] = early_full[k, :XW, :].astype(F32)
        out[DS + k * XW : DS + (k + 1) * XW, :] = late_full[k, :XW, :].astype(F32)
        q = early_full[k, XW : XW + LANES, :].astype(F32)
        out_qkv[:, k * LANES : (k + 1) * LANES] = q.T
    for k in range(2):
        first = late_full[k, XW:, :].astype(F32)
        second = late_full[k + 2, XW:, :].astype(F32)
        out[2 * DS + k * NS : 2 * DS + (k + 1) * NS, :] = first + second
    across, own = D // LANES, early.shape[2] // LANES
    for h in range(NH):
        for k in range(own):
            at = ROW_DT + h * across + peers(info)[0] * own + k
            out[DS + CONV_CH + h : DS + CONV_CH + h + 1, k * LANES : (k + 1) * LANES] = small[
                pl.ds(at, 1), :
            ]
    kv_at = XW + LANES
    for k in range(2):
        rows = slice(kv_at + k * HD, kv_at + (k + 1) * HD)
        pair = [early_full[k, rows, :], early_full[k + 2, rows, :]]
        both = jnp.concatenate(pair, axis=0).astype(F32)
        out_qkv[:, QW + k * KW : QW + (k + 1) * KW] = both.T


def finish_mid_kernel(bit, info, own, moved, out_a, out_b, full):
    size = own.shape[1]
    for at, ref in each_part(bit, info, own, moved):
        full[part(at, size), :] = ref[0].astype(F32)
    out_a[...] = full[:XW, :]
    out_b[...] = full[XW:, :]


def finish_rows_kernel(bit, info, own, moved, out):
    size = own.shape[1]
    for at, ref in each_part(bit, info, own, moved):
        out[part(at, size), :] = ref[0].astype(F32)


def sum_all(info, vector):
    whole = f32_of(*vector.shape)
    for bits in (1, 2):
        vector = call(total_kernel, whole, info, vector, swap(vector, bits))
    for bit in (1, 2, 4):
        vector = call(total_kernel, whole, info, vector, swap_far(vector, (bit, bit)))
    return vector


def unpack_kernel(info, small, one, conv, conv_bias, dt_bias, a_log, skip, gain, two, stats):
    for first, out in ((ROW_ONE, one), (ROW_TWO, two), (ROW_GAIN, gain)):
        for k in range(out.shape[1] // LANES):
            out[:, k * LANES : (k + 1) * LANES] = small[first + k : first + k + 1, :]
    for j in range(KC + 1):
        for k in range(CONV_ROWS):
            at = ROW_TAPS + j * CONV_ROWS + k
            dst, row = (conv, j) if j < KC else (conv_bias, 0)
            dst[row : row + 1, k * LANES : (k + 1) * LANES] = small[at : at + 1, :]
    for first, out in ((ROW_RATE, a_log), (ROW_BIAS, dt_bias)):
        pieces = [small[first + k : first + k + 1, :HEADS_AT] for k in range(4)]
        out[...] = jnp.concatenate(pieces, axis=1)
    lane = iota((1, LANES), 1)
    total = jnp.zeros((1, LANES), F32)
    for k in range(NH):
        at, first = ROW_SKIP + k * HP // LANES, k * HP % LANES
        value = jnp.sum(small[at : at + 1, first : first + HP], axis=1, keepdims=True)
        total = total + jnp.where(lane == k, value, 0.0)
    skip[...] = total[:, :NH]
    sums = [
        jnp.sum(small[ROW_STATS + k : ROW_STATS + k + 1, :], axis=1, keepdims=True)
        for k in range(4)
    ]
    total = jnp.zeros((1, LANES), F32)
    for k in range(3):
        total = total + jnp.where(lane == k, jnp.sqrt(sums[k] / (sums[3] * D)), 0.0)
    stats[...] = total[:, :3]


ROW_ONE, ROW_TWO, ROW_TAPS = 0, 8, 16
CONV_ROWS = CONV_CH // LANES
ROW_GAIN = ROW_TAPS + (KC + 1) * CONV_ROWS
ROW_SKIP = ROW_GAIN + DS // LANES
ROW_RATE = ROW_SKIP + DS // LANES
ROW_BIAS = ROW_RATE + 4
ROW_STATS = ROW_BIAS + 4
ROW_DT = 128
SMALL_ROWS = ROW_DT + NH * D // LANES


def small_kernel(
    info, one, two, taps_x, taps_bc, gain, skip, heads, dt, sums, mixed, keep, out
):
    out[...] = jnp.zeros_like(out)
    place, core = peers(info)[0], info[AT_CORE]
    for k in range(D // LANES):
        lanes = slice(k * LANES, (k + 1) * LANES)
        out[ROW_ONE + k : ROW_ONE + k + 1, :] = one[:, lanes]
        out[ROW_TWO + k : ROW_TWO + k + 1, :] = two[:, lanes]
    blocks = XW // LANES
    for k in range(blocks):
        lanes = slice(k * LANES, (k + 1) * LANES)
        at = place * blocks + k
        for j in range(KC + 1):
            out[pl.ds(ROW_TAPS + j * CONV_ROWS + at, 1), :] = taps_x[j : j + 1, lanes]
        out[pl.ds(ROW_GAIN + at, 1), :] = gain[:, lanes]
        out[pl.ds(ROW_SKIP + at, 1), :] = skip[:, lanes]
    for j in range(KC + 1):
        out[pl.ds(ROW_TAPS + j * CONV_ROWS + DS // LANES + core, 1), :] = taps_bc[j : j + 1, :]
    across = D // LANES
    for h in range(HEADS_AT):
        for k in range(across):
            at = ROW_DT + (place * HEADS_AT + h) * across + k
            out[pl.ds(at, 1), :] = dt[h : h + 1, k * LANES : (k + 1) * LANES]
    out[pl.ds(ROW_RATE + place, 1), :] = heads[0:1, :]
    out[pl.ds(ROW_BIAS + place, 1), :] = heads[1:2, :]
    for k, row in enumerate((sums[0:1, :], mixed[...], sums[1:2, :])):
        folded = row[:, :LANES]
        for j in range(1, D // LANES):
            folded = folded + row[:, j * LANES : (j + 1) * LANES]
        out[ROW_STATS + k : ROW_STATS + k + 1, :] = folded
    out[ROW_STATS + 3 : ROW_STATS + 4, :] = keep[...].T[:1]


def by_heads(
    hidden_in, cotangent, doc_starts, valid_mask, norm_one, in_proj, conv_weight, conv_bias,
    dt_bias, a_log, skip_scale, gated_gain, qkv_proj, ssm_out, attn_out, norm_two, gate_up,
    down_proj,
):
    place, far_place = lax.axis_index("shard"), lax.axis_index("replica")
    y, c = place // 2, place % 2
    rows = hidden_in.shape[0]
    seq, depth = 4 * rows, in_proj.shape[0]
    bits = [y, c, far_place % 2, far_place // 2 % 2, far_place // 4]
    info = jnp.concatenate([jnp.stack(bits).astype(jnp.int32), doc_starts[0]])
    pair = (2, rows, D)

    h_far = swap(hidden_in, 2)
    h_core = swap(hidden_in, 1)
    w_own, w_core, w_far, z_own, z_core, z_far = call(
        pack_in_kernel,
        (
            low_of(W_FIRST, depth), low_of(W_FIRST, depth), low_of(W_FIRST + KV_AT, depth),
            low_of(XW, depth), low_of(XW, depth), low_of(2 * XW, depth),
        ),
        info, in_proj.T, qkv_proj,
    )
    u_own, u_core, u_far = call(
        pack_up_kernel, (low_of(depth, FF // 2),) * 3, info, after(gate_up, w_own)
    )
    freqs = ROPE_BASE ** (-(jnp.arange(HD // 2).astype(F32) * 2.0) / HD)
    angles = jnp.arange(seq).astype(F32)[:, None] * jnp.tile(freqs, LANES // (HD // 2))[None, :]
    cosines, sines = jnp.cos(angles), jnp.sin(angles)
    taps, bias, bias_own, rate, skip, gain, gain_one, gain_two, keep, g_own, turn = call(
        prepare_kernel,
        (
            f32_of(KC, XW + 2 * NS), f32_of(1, XW + 2 * NS), f32_of(1, LANES), f32_of(1, LANES),
            f32_of(1, XW), f32_of(1, XW), f32_of(1, D), f32_of(1, D), f32_of(LANES, LANES),
            low_of(rows, D), low_of(LANES, LANES),
        ),
        info, conv_weight.T, conv_bias[None], dt_bias[None], a_log[None], skip_scale[None],
        gated_gain[None], norm_one[None], norm_two[None], valid_mask[None],
        after(cotangent, (cosines, sines)),
        scratch=(pltpu.VMEM((8, LANES), F32),),
    )
    w_far = swap(after(w_far, (u_own, g_own, h_far)), 2)
    w_core = swap(w_core, 1)
    h_far_core = swap(h_far, 1)
    w_far_core = swap(w_far, 1)
    z_far = swap(after(z_far, w_far), 2)

    h_low, w_full, xbc, conv_pre, soft, q_low, kv_low, ssm_y, states = call(
        forward_kernel,
        (
            low_of(seq, D), low_of(W_FIRST, D), f32_of(seq, XW + 2 * NS), f32_of(seq, XW + 2 * NS),
            f32_of(seq, LANES), low_of(seq, LANES), low_of(seq, LANES), f32_of(seq, XW),
            f32_of(seq // SPAN, NS, XW),
        ),
        info, hidden_in, h_core, h_far, h_far_core, w_own, w_core, w_far, w_far_core,
        gain_one, taps, bias, bias_own, rate, skip, cosines, sines, turn,
        scratch=(
            pltpu.VMEM((seq + 8, XW + 2 * NS), F32), pltpu.VMEM((seq, XW + 2 * NS), F32),
            pltpu.VMEM((seq, LANES), F32), pltpu.VMEM((seq + 8, LANES), jnp.int32),
        ),
    )
    z_far, z_core = after((z_far, z_core), h_low)
    z_core, z_far_core = swap(z_core, 1), swap(z_far, 1)
    u_far, u_core, g_out = after((u_far, u_core, g_own), z_far)
    u_y, g_far = swap(u_far, 2), swap(g_out, 2)
    z_full, gate_z, square = call(
        gate_kernel, (low_of(XW, D), f32_of(seq, XW), f32_of(8, seq)),
        info, h_low, z_own, z_core, z_far, z_far_core, ssm_y,
    )
    square = call(total_kernel, f32_of(8, seq), info, square, swap(square, 1))
    square_far = swap(square, 2)
    attn, lse = call(
        attend_kernel, (low_of(seq, LANES), f32_of(seq, LANES)), info, after(q_low, square), kv_low
    )

    given, kept, normed = call(
        output_kernel, (f32_of(*pair), f32_of(*pair), low_of(seq, XW)),
        info, square, square_far, ssm_y, gate_z, gain, after(attn, u_y), ssm_out, attn_out,
    )
    u_x = swap_far(after(u_y, given), (1, 1))
    u_y_core = swap(after(u_y, given), 1)
    chip, sent = call(add_kernel, (f32_of(*pair), low_of(*pair)), info, kept, swap(given, 1))
    u_core, g_core = swap(after(u_core, sent), 1), swap(after(g_out, sent), 1)
    g_far_core = swap(after(g_far, sent), 1)
    residual, h2, mixed_sum = call(
        second_norm_kernel, (f32_of(*pair), low_of(*pair), f32_of(1, D)),
        info, chip, swap(sent, 2), hidden_in, h_far, gain_two, keep,
        scratch=(pltpu.VMEM(pair, LOW),),
    )
    u_x_core = swap(u_x, 1)

    given, kept, hid, ggu, h2_cat, gmlp = call(
        mlp_kernel,
        (
            f32_of(*pair), f32_of(*pair), low_of(seq, FF // 4), low_of(seq, FF // 2),
            low_of(seq, D), low_of(seq, D),
        ),
        info, h2, swap(h2, 1), u_own, u_core, u_y, u_x, u_y_core, u_x_core,
        g_own, g_core, g_far, g_far_core, down_proj,
        scratch=(pltpu.VMEM((D, FF // 2), LOW),),
    )
    order = ((1, 2), (2, 1), (4, 4))
    moved = swap(given, 1)
    up_given, up_kept = call(
        functools.partial(grad_columns_kernel, order[0]),
        (low_of(4, D // 8, FF // 2), f32_of(4, D // 8, FF // 2)), info, h2_cat, ggu,
    )
    s_up = Running(info, up_given, up_kept, order, True)
    down_given, down_kept = call(
        functools.partial(grad_rows_kernel, order[0]),
        (low_of(FF // 8, D), f32_of(FF // 8, D)), info, hid, after(gmlp, up_given),
    )
    s_down = Running(info, down_given[None], down_kept[None], order, False)
    kept = after(kept, (up_given, down_given))
    chip, sent = call(add_kernel, (f32_of(*pair), low_of(*pair)), info, kept, moved)
    mlp_given, mlp_kept = call(
        down_kernel, (f32_of(*pair), f32_of(*pair)), info, after(hid, sent), down_proj
    )
    mlp_mine, mlp_given = call(
        add_split_kernel, (f32_of(rows, D),) * 2, info, mlp_kept, swap(mlp_given, 1)
    )
    gres, gmix, g_norm_two = call(
        norm_back_pair_kernel, (f32_of(*pair), low_of(*pair), f32_of(1, D)),
        info, after(chip, mlp_given), swap(sent, 2), residual, gain_two, g_own, g_far,
        scratch=(pltpu.VMEM(pair, LOW),),
    )

    moved = swap(gmix, 1)
    gmix_all, gnormed, gattn, uv = call(
        output_back_kernel,
        (low_of(seq, D), f32_of(seq, XW), low_of(seq, LANES), f32_of(8, seq)),
        info, gmix, moved, ssm_y, gate_z, gain, ssm_out, attn_out,
    )
    uv = call(total_kernel, f32_of(8, seq), info, uv, swap(uv, 1))
    uv_far = swap(uv, 2)
    gq, gkv_part = call(
        attend_back_kernel, (low_of(seq, LANES), f32_of(seq, LANES)),
        info, q_low, kv_low, lse, after(gattn, uv), cosines, sines, turn,
        scratch=(pltpu.VMEM((seq, LANES), F32),),
    )
    moved = swap(gkv_part, 1)
    gkv = call(
        keys_back_kernel, f32_of(seq, LANES),
        info, gkv_part, moved, cosines, sines, turn,
    )
    early, gy, g_gain = call(
        gate_back_kernel, (low_of(seq, XW + 2 * LANES), f32_of(seq, XW), f32_of(1, XW)),
        info, square, square_far, uv, uv_far, gnormed, ssm_y, gate_z, gain, gq, gkv,
    )
    sent = [one.step(gy) for one in (s_up, s_down)]
    mlp_moved = swap(after(mlp_given, gy), 2)

    gx_low, gbc_given, gbc_kept, gdr, gsoft, taps_x, g_skip, g_heads = call(
        scan_back_kernel,
        (
            low_of(seq, XW), f32_of(seq, NS), f32_of(seq, NS), low_of(seq, LANES),
            low_of(seq, LANES), f32_of(8, XW), f32_of(1, XW), f32_of(8, LANES),
        ),
        info, xbc, conv_pre, soft, rate, skip, states, taps, after(gy, sent),
        scratch=(
            pltpu.VMEM((seq, XW + 2 * NS), F32), pltpu.VMEM((seq, LANES), F32),
            pltpu.VMEM((seq, XW + 2 * NS), F32),
            pltpu.VMEM((seq, LANES), F32), pltpu.VMEM((seq, LANES), F32),
            pltpu.VMEM((seq + 8, LANES), F32), pltpu.VMEM((seq + 8, LANES), F32),
            pltpu.VMEM((seq + 8, LANES), jnp.int32),
        ),
    )
    moved = swap(gbc_given, 1)
    mid_given, mid_kept = call(
        functools.partial(grad_mid_kernel, order[0]),
        (low_of(XW - LANES, D), f32_of(XW - LANES, D)),
        info, normed, attn, after(gmix_all, gbc_given),
        scratch=(pltpu.VMEM((seq, XW + LANES), LOW),),
    )
    s_mid = Running(info, mid_given[None], mid_kept[None], order, False)
    half = early.shape[1] // 2
    early_given, early_kept = call(
        functools.partial(early_kernel, order[0]), (low_of(1, half, D), f32_of(1, half, D)),
        info, after(early, gbc_given), h_low,
    )
    s_early = Running(info, early_given, early_kept, order, True)
    half = (XW + NS) // 2
    late_given, late_kept, g_dt, gbc_low, taps_bc = call(
        functools.partial(late_kernel, order[0]),
        (
            low_of(1, half, D), f32_of(1, half, D), f32_of(8, D), low_of(seq, NS),
            f32_of(8, LANES),
        ),
        info, after(gbc_kept, (mid_given, early_given)), moved, xbc, conv_pre, taps, gx_low, gsoft, h_low,
        scratch=(
            pltpu.VMEM((seq, XW + NS), LOW), pltpu.VMEM((seq + 8, LANES), F32),
            pltpu.VMEM((seq + 8, LANES), F32), pltpu.VMEM((seq + 8, LANES), jnp.int32),
        ),
    )
    s_late = Running(info, late_given, late_kept, order, True)

    sent = [one.step(gbc_low) for one in (s_up, s_down)]

    given, kept = call(
        inputs_back_kernel, (f32_of(*pair), f32_of(*pair)),
        info, after(gx_low, (late_given, sent)), early, gbc_low, gdr, w_full, z_full,
        scratch=(pltpu.VMEM((seq, W_FIRST + XW), LOW),),
    )
    mine, given = call(add_split_kernel, (f32_of(rows, D),) * 2, info, kept, swap(given, 1))
    moved = swap(given, 2)
    running = (s_late, s_early, s_up, s_mid, s_down)
    for one in running:
        one.step(given)
    grad_input, g_norm_one = call(
        first_norm_back_kernel, (f32_of(rows, D), f32_of(1, D)),
        info, mine, moved, hidden_in, gain_one, gres,
    )
    output, sums = call(
        result_kernel, (low_of(rows, D), f32_of(8, D)),
        info, mlp_mine, mlp_moved, residual, keep,
    )
    small = call(
        small_kernel, f32_of(SMALL_ROWS, LANES),
        info, g_norm_one, g_norm_two, taps_x, taps_bc, g_gain, g_skip, g_heads, g_dt, sums,
        mixed_sum, keep,
    )
    while not all(one.done for one in running):
        for one in running:
            one.step(grad_input)
    small = sum_all(info, small)

    grad_in, grad_qkv = call(
        functools.partial(finish_in_kernel, order[0]),
        (f32_of(in_proj.shape[1], depth), f32_of(*qkv_proj.shape)),
        info, *s_early.result, *s_late.result, small,
        scratch=(
            pltpu.VMEM((4, XW + 2 * LANES, depth), LOW), pltpu.VMEM((4, XW + NS, depth), LOW)
        ),
    )
    grad_up = call(
        functools.partial(finish_up_kernel, order[0]), f32_of(*gate_up.shape), info, *s_up.result
    )
    grad_down = call(
        functools.partial(finish_rows_kernel, order[0]), f32_of(*down_proj.shape),
        info, *s_down.result,
    )
    grad_ssm, grad_attn = call(
        functools.partial(finish_mid_kernel, order[0]),
        (f32_of(*ssm_out.shape), f32_of(*attn_out.shape)), info, *s_mid.result,
        scratch=(pltpu.VMEM((XW + LANES, D), F32),),
    )

    one, conv, bias, dt, rate, skip, gain, two, stats = call(
        unpack_kernel,
        (
            f32_of(1, D), f32_of(KC, CONV_CH), f32_of(1, CONV_CH), f32_of(1, NH), f32_of(1, NH),
            f32_of(1, NH), f32_of(1, DS), f32_of(1, D), f32_of(1, 3),
        ),
        info, small,
    )
    return (
        output, grad_input, one[0], grad_in.T, conv.T, bias[0], dt[0], rate[0], skip[0], gain[0],
        grad_qkv, grad_ssm, grad_attn, two[0], grad_up, grad_down, stats[0],
    )


def on_any(*args):
    sizes = (lax.axis_size("replica"), lax.axis_size("shard"), args[0].shape[0])
    return (by_heads if sizes == (8, 4, TB) else on_device)(*args)


def solution(mesh):
    return jax.shard_map(
        on_any,
        mesh=mesh,
        in_specs=(
            P(("replica", "shard"), None),
            P(("replica", "shard"), None),
            P("replica", None),
            P(("replica", "shard")),
            P(),
            P("shard", None),
            P(),
            P(),
            P(),
            P(),
            P(),
            P(),
            P("shard", None),
            P("shard", None),
            P("shard", None),
            P(),
            P("shard", None),
            P("shard", None),
        ),
        out_specs=(
            P(("replica", "shard"), None),
            P(("replica", "shard"), None),
            P(),
            P("shard", None),
            P(),
            P(),
            P(),
            P(),
            P(),
            P(),
            P("shard", None),
            P("shard", None),
            P("shard", None),
            P(),
            P("shard", None),
            P("shard", None),
            P(),
        ),
        check_vma=False,
    )
```

```python
import functools
import math

import jax
import jax.numpy as jnp
from jax import lax
from jax.experimental import pallas as pl
from jax.experimental.pallas import tpu as pltpu
from jax.sharding import PartitionSpec as P

D = 1024
NH = 24
HP = 64
NS = 128
KC = 4
QH = 8
KVH = 2
HD = 64
FF = 2048
SPAN = 128
KBLK = 512
DS = 1536
QW = 512
KW = 128
CONV_CH = 1792


EPS = 1e-05
ROPE_BASE = 100000000000.0
NEG = -1e30
HIGH = lax.Precision.HIGHEST


def from_behind(block, axis, distance):
    devices = range(lax.axis_size(axis))
    route = [(i - distance, i) for i in devices if i - distance in devices]
    return lax.ppermute(block, axis, route)


def carried_in(part, axis, combine, identity):
    place = lax.axis_index(axis)
    gathered = jax.tree.map(lambda a: lax.all_gather(a, axis), part)
    state = jax.tree.map(lambda a, e: jnp.zeros_like(a) + jnp.asarray(e, a.dtype), part, identity)

    def one(step, state):
        return combine(
            state, jax.tree.map(lambda a: lax.dynamic_index_in_dim(a, step, 0, False), gathered)
        )

    return lax.fori_loop(0, place, one, state)


def entering(value, axis, combine, identity):
    size, mine = (lax.axis_size(axis), lax.axis_index(axis))
    everything = jax.tree.map(
        lambda part, kind: lax.all_gather(part.astype(kind), axis),
        value,
        jax.tree.map(lambda a: jnp.bfloat16 if a.dtype == jnp.float32 else a.dtype, value),
    )
    start = jax.tree.map(
        lambda part, zero: jnp.broadcast_to(jnp.asarray(zero, part.dtype), part.shape),
        value,
        identity,
    )

    def step(k, before):
        at = size - 1 - k
        reached = at > mine
        new = combine(
            before, jax.tree.map(lambda part, own: part[at].astype(own.dtype), everything, value)
        )
        return jax.tree.map(lambda a, b: jnp.where(reached, a, b), new, before)

    return lax.fori_loop(0, size, step, start)


def rms_scale(tensor):
    return lax.rsqrt(jnp.mean(tensor * tensor, axis=-1, keepdims=True) + EPS)


def rope_tables(positions):
    freqs = ROPE_BASE ** (-(jnp.arange(HD // 2).astype(jnp.float32) * 2.0) / HD)
    angles = positions.astype(jnp.float32)[:, None] * freqs[None, :]
    return (jnp.cos(angles), jnp.sin(angles))


def rotate(tensor, heads, cosines, sines):
    shaped = tensor.reshape(tensor.shape[0], heads, HD)
    first_half = shaped[:, :, : HD // 2]
    second_half = shaped[:, :, HD // 2 :]
    cos_b = cosines[:, None, :]
    sin_b = sines[:, None, :]
    turned = jnp.concatenate(
        [first_half * cos_b - second_half * sin_b, second_half * cos_b + first_half * sin_b],
        axis=-1,
    )
    return turned.reshape(tensor.shape[0], heads * HD)


def segment_of(positions, starts_row):
    return jnp.sum((starts_row[None, :] <= positions[:, None]).astype(jnp.int32), axis=1) - 1


def norm_back(grad_out, tensor, scale_rows, gain):
    scaled = grad_out * gain
    grad_in = scale_rows * scaled - tensor * scale_rows**3 * jnp.mean(
        scaled * tensor, axis=-1, keepdims=True
    )
    return (grad_in, jnp.sum(grad_out * tensor * scale_rows, axis=0))


def dsilu(tensor):
    sig_part = jax.nn.sigmoid(tensor)
    return sig_part * (1.0 + tensor * (1.0 - sig_part))


def combine_states(earlier, later):
    return (earlier[0] * later[1][:, None, None] + later[0], earlier[1] * later[1])


def ssd_spans(state, ssm_x, ssm_b, ssm_c, step_size, log_decay, skip_scale, seg_ids, before):
    count = ssm_x.shape[0] // SPAN
    prev_seg = jnp.concatenate([before.reshape(1), seg_ids[:-1]])

    def by_span(tensor):
        return tensor.reshape((count, SPAN) + tensor.shape[1:])

    def span_step(state_acc, pieces):
        x_c, b_c, c_c, dt_c, la_c, s_c, p_c = pieces
        cum_decay = jnp.cumsum(la_c, axis=0)
        order = jnp.arange(SPAN)
        same_mask = (s_c[:, None] == s_c[None, :]) & (order[:, None] >= order[None, :])
        differ = cum_decay.T[:, :, None] - cum_decay.T[:, None, :]
        decay_mat = jnp.exp(jnp.where(same_mask[None], differ, NEG))
        inner = jnp.dot(c_c, b_c.T, precision=HIGH)
        mixing = decay_mat * inner[None] * dt_c.T[:, None, :]
        y_inner = jnp.einsum("hpq,qhd->phd", mixing, x_c, precision=HIGH)
        alive = (s_c == p_c[0]).astype(jnp.float32)
        carried = jnp.exp(cum_decay) * alive[:, None]
        y_state = jnp.einsum("hdn,pn->phd", state_acc, c_c, precision=HIGH) * carried[:, :, None]
        y_span = y_inner + y_state + skip_scale[None, :, None] * x_c
        tail_w = (
            jnp.exp(cum_decay[-1][None, :] - cum_decay)
            * (s_c == s_c[-1]).astype(jnp.float32)[:, None]
            * dt_c
        )
        new_state = state_acc * carried[-1][:, None, None] + jnp.einsum(
            "qh,qhd,qn->hdn", tail_w, x_c, b_c, precision=HIGH
        )
        return (new_state, y_span)

    final_state, ys = lax.scan(
        span_step,
        state,
        (
            by_span(ssm_x),
            by_span(ssm_b),
            by_span(ssm_c),
            by_span(step_size),
            by_span(log_decay),
            by_span(seg_ids),
            by_span(prev_seg),
        ),
    )
    return (ys.reshape(ssm_x.shape), final_state)


def on_device(
    hidden_in,
    cotangent,
    doc_starts,
    valid_mask,
    norm_one,
    in_proj,
    conv_weight,
    conv_bias,
    dt_bias,
    a_log,
    skip_scale,
    gated_gain,
    qkv_proj,
    ssm_out,
    attn_out,
    norm_two,
    gate_up,
    down_proj,
):
    tok_rows = hidden_in.shape[0]
    shard_count = lax.axis_size("shard")
    offset = lax.axis_index("shard") * tok_rows
    seq_len = tok_rows * shard_count
    score_scale = 1.0 / math.sqrt(HD)
    q_per_kv = QH // KVH
    starts_row = doc_starts[0]
    positions = offset + jnp.arange(tok_rows, dtype=jnp.int32)
    seg_ids = segment_of(positions, starts_row)
    before = segment_of(positions[:1] - 1, starts_row)[0]
    first_start = jnp.max(jnp.where(starts_row <= positions[0], starts_row, 0))
    last_pos = positions[-1]
    full_weights = (
        lax.all_gather(in_proj, "shard", axis=0, tiled=True),
        lax.all_gather(qkv_proj, "shard", axis=0, tiled=True),
        lax.all_gather(ssm_out, "shard", axis=0, tiled=True),
        lax.all_gather(attn_out, "shard", axis=0, tiled=True),
        lax.all_gather(gate_up, "shard", axis=0, tiled=True),
        lax.all_gather(down_proj, "shard", axis=0, tiled=True),
    )
    f_in, f_attn, f_mo, f_ao, f_gu, f_down = full_weights
    x_full = hidden_in.astype(jnp.float32)
    r_one = rms_scale(x_full)
    h_low = (x_full * r_one * norm_one).astype(jnp.bfloat16)
    proj_out = jnp.dot(h_low, f_in, preferred_element_type=jnp.float32)
    gate_z = proj_out[:, :DS]
    xbc = proj_out[:, DS : DS + CONV_CH]
    dt_raw = proj_out[:, DS + CONV_CH :]
    edge_rows = from_behind(xbc[tok_rows - (KC - 1) :], "shard", 1)
    padded = jnp.concatenate([edge_rows, xbc], axis=0)
    pad_pos = positions[0] - (KC - 1) + jnp.arange(tok_rows + KC - 1, dtype=jnp.int32)
    pad_seg = segment_of(pad_pos, starts_row)
    tap_masks = [
        (pad_seg[tap_index : tap_index + tok_rows] == seg_ids).astype(jnp.float32)[:, None]
        for tap_index in range(KC)
    ]
    conv_pre = jnp.zeros((tok_rows, CONV_CH), jnp.float32) + conv_bias[None, :]
    for tap_index in range(KC):
        conv_pre = (
            conv_pre
            + conv_weight[:, tap_index][None, :]
            * padded[tap_index : tap_index + tok_rows]
            * tap_masks[tap_index]
        )
    conv_act = jax.nn.silu(conv_pre)
    ssm_x = conv_act[:, :DS].reshape(tok_rows, NH, HP)
    ssm_b = conv_act[:, DS : DS + NS]
    ssm_c = conv_act[:, DS + NS :]
    soft_in = dt_raw + dt_bias
    step_size = jax.nn.softplus(soft_in)
    decay_rate = jnp.exp(a_log)
    log_decay = -step_size * decay_rate
    empty_state = jnp.zeros((NH, HP, NS), jnp.float32)

    def carry_factor(log_vals):
        return (
            jnp.exp(jnp.cumsum(log_vals, axis=0)) * (seg_ids == before).astype(jnp.float32)[:, None]
        )

    def carry_term(state_in, c_vals, factor):
        return jnp.einsum("hdn,pn->phd", state_in, c_vals, precision=HIGH) * factor[:, :, None]

    ssm_zero, local_state = ssd_spans(
        empty_state, ssm_x, ssm_b, ssm_c, step_size, log_decay, skip_scale, seg_ids, before
    )
    factor = carry_factor(log_decay)
    dev_decay = factor[-1]
    state_in, unused_decay = carried_in(
        (local_state, dev_decay),
        "shard",
        combine_states,
        (jnp.zeros_like(local_state), jnp.ones_like(dev_decay)),
    )
    ssm_y = (ssm_zero + carry_term(state_in, ssm_c, factor)).reshape(tok_rows, DS)
    silu_z = jax.nn.silu(gate_z)
    gated = ssm_y * silu_z
    r_gate = rms_scale(gated)
    normed_low = (gated * r_gate * gated_gain).astype(jnp.bfloat16)
    qkv = jnp.dot(h_low, f_attn, preferred_element_type=jnp.float32)
    cosines, sines = rope_tables(positions)
    q_low = (
        rotate(qkv[:, :QW], QH, cosines, sines)
        .astype(jnp.bfloat16)
        .reshape(tok_rows, KVH, q_per_kv, HD)
    )
    k_low = rotate(qkv[:, QW : QW + KW], KVH, cosines, sines).astype(jnp.bfloat16)
    v_low = qkv[:, QW + KW :].astype(jnp.bfloat16)
    key_all, value_all = (
        lax.all_gather(k_low, "shard", axis=0, tiled=True),
        lax.all_gather(v_low, "shard", axis=0, tiled=True),
    )
    key_all = key_all.reshape(seq_len, KVH, HD)
    value_all = value_all.reshape(seq_len, KVH, HD)
    key_pos = jnp.arange(seq_len, dtype=jnp.int32)
    key_seg = segment_of(key_pos, starts_row)
    block_count = seq_len // KBLK
    row_shape = (KVH, q_per_kv, tok_rows)

    def needed(blk_index):
        low_edge = blk_index * KBLK
        return (low_edge <= last_pos) & (low_edge + KBLK > first_start)

    def block_keys(blk_index):
        return (
            lax.dynamic_slice_in_dim(key_all, blk_index * KBLK, KBLK, 0),
            lax.dynamic_slice_in_dim(value_all, blk_index * KBLK, KBLK, 0),
        )

    def block_scores(blk_index, k_blk):
        pos_blk = lax.dynamic_slice_in_dim(key_pos, blk_index * KBLK, KBLK, 0)
        seg_blk = lax.dynamic_slice_in_dim(key_seg, blk_index * KBLK, KBLK, 0)
        raw_scores = (
            jnp.einsum("tgqd,kgd->gqtk", q_low, k_blk, preferred_element_type=jnp.float32)
            * score_scale
        )
        key_mask = (pos_blk[None, :] <= positions[:, None]) & (seg_blk[None, :] == seg_ids[:, None])
        return (raw_scores, key_mask[None, None])

    def unchanged(passed):
        return passed

    def lse_step(blk_index, state_acc):

        def lse_do_block(state_acc):
            row_top, row_total = state_acc
            k_blk, v_blk = block_keys(blk_index)
            raw_scores, key_mask = block_scores(blk_index, k_blk)
            new_top = jnp.maximum(row_top, jnp.max(jnp.where(key_mask, raw_scores, NEG), axis=-1))
            row_total = row_total * jnp.exp(row_top - new_top) + jnp.sum(
                jnp.where(key_mask, jnp.exp(raw_scores - new_top[..., None]), 0.0), axis=-1
            )
            return (new_top, row_total)

        return lax.cond(needed(blk_index), lse_do_block, unchanged, state_acc)

    row_top, row_total = lax.fori_loop(
        0,
        block_count,
        lse_step,
        (jnp.full(row_shape, NEG, jnp.float32), jnp.zeros(row_shape, jnp.float32)),
    )
    log_total = row_top + jnp.log(row_total)

    def probs_of(blk_index, k_blk):
        raw_scores, key_mask = block_scores(blk_index, k_blk)
        return jnp.where(key_mask, jnp.exp(raw_scores - log_total[..., None]), 0.0)

    def out_step(blk_index, acc_out):

        def out_do_block(acc_out):
            k_blk, v_blk = block_keys(blk_index)
            prob_blk = probs_of(blk_index, k_blk).astype(jnp.bfloat16)
            return acc_out + jnp.einsum(
                "gqtk,kgd->tgqd", prob_blk, v_blk, preferred_element_type=jnp.float32
            )

        return lax.cond(needed(blk_index), out_do_block, unchanged, acc_out)

    attended = lax.fori_loop(
        0, block_count, out_step, jnp.zeros((tok_rows, KVH, q_per_kv, HD), jnp.float32)
    )
    attn_low = attended.reshape(tok_rows, QW).astype(jnp.bfloat16)
    mixed = jnp.dot(normed_low, f_mo, preferred_element_type=jnp.float32) + jnp.dot(
        attn_low, f_ao, preferred_element_type=jnp.float32
    )
    residual = x_full + mixed
    r_two = rms_scale(residual)
    h2_low = (residual * r_two * norm_two).astype(jnp.bfloat16)
    gate_vals = jnp.dot(h2_low, f_gu, preferred_element_type=jnp.float32)
    gate_part = gate_vals[:, :FF]
    up_part = gate_vals[:, FF:]
    hid_low = (jax.nn.silu(gate_part) * up_part).astype(jnp.bfloat16)
    mlp_out = jnp.dot(hid_low, f_down, preferred_element_type=jnp.float32)
    out_full = residual + mlp_out
    keep_rows = valid_mask.astype(jnp.float32)
    stat_local = jnp.stack(
        [
            jnp.sum(keep_rows * jnp.sum(out_full * out_full, axis=1)),
            jnp.sum(keep_rows * jnp.sum(mixed * mixed, axis=1)),
            jnp.sum(keep_rows * jnp.sum(mlp_out * mlp_out, axis=1)),
            jnp.sum(keep_rows),
        ]
    )
    back_weights = (
        lax.all_gather(in_proj, "shard", axis=0, tiled=True),
        lax.all_gather(qkv_proj, "shard", axis=0, tiled=True),
        lax.all_gather(ssm_out, "shard", axis=0, tiled=True),
        lax.all_gather(attn_out, "shard", axis=0, tiled=True),
        lax.all_gather(gate_up, "shard", axis=0, tiled=True),
        lax.all_gather(down_proj, "shard", axis=0, tiled=True),
    )
    b_in, b_attn, b_mo, b_ao, b_gu, b_down = back_weights
    grad_out = cotangent.astype(jnp.float32) * keep_rows[:, None]
    grad_mlp = grad_out.astype(jnp.bfloat16)
    g_down = jnp.dot(hid_low.T, grad_mlp, preferred_element_type=jnp.float32)
    grad_hid = jnp.dot(grad_mlp, b_down.T, preferred_element_type=jnp.float32)
    grad_gu = jnp.concatenate(
        [grad_hid * up_part * dsilu(gate_part), grad_hid * jax.nn.silu(gate_part)], axis=1
    ).astype(jnp.bfloat16)
    g_gu = jnp.dot(h2_low.T, grad_gu, preferred_element_type=jnp.float32)
    grad_h2 = jnp.dot(grad_gu, b_gu.T, preferred_element_type=jnp.float32)
    grad_res_n, g_norm_two = norm_back(grad_h2, residual, r_two, norm_two)
    grad_res = grad_out + grad_res_n
    grad_mix = grad_res.astype(jnp.bfloat16)
    g_mo = jnp.dot(normed_low.T, grad_mix, preferred_element_type=jnp.float32)
    g_ao = jnp.dot(attn_low.T, grad_mix, preferred_element_type=jnp.float32)
    grad_normed = jnp.dot(grad_mix, b_mo.T, preferred_element_type=jnp.float32)
    grad_attn = (
        jnp.dot(grad_mix, b_ao.T, preferred_element_type=jnp.float32)
        .astype(jnp.bfloat16)
        .reshape(tok_rows, KVH, q_per_kv, HD)
    )

    def delta_step(blk_index, acc_out):

        def delta_do_block(acc_out):
            k_blk, v_blk = block_keys(blk_index)
            prob_blk = probs_of(blk_index, k_blk)
            grad_prob = jnp.einsum(
                "tgqd,kgd->gqtk", grad_attn, v_blk, preferred_element_type=jnp.float32
            )
            return acc_out + jnp.sum(prob_blk * grad_prob, axis=-1)

        return lax.cond(needed(blk_index), delta_do_block, unchanged, acc_out)

    delta_row = lax.fori_loop(0, block_count, delta_step, jnp.zeros(row_shape, jnp.float32))

    def grad_step(blk_index, state_acc):

        def grad_do_block(state_acc):
            grad_query, grad_kv = state_acc
            k_blk, v_blk = block_keys(blk_index)
            prob_blk = probs_of(blk_index, k_blk)
            grad_prob = jnp.einsum(
                "tgqd,kgd->gqtk", grad_attn, v_blk, preferred_element_type=jnp.float32
            )
            grad_raw = (prob_blk * (grad_prob - delta_row[..., None]) * score_scale).astype(
                jnp.bfloat16
            )
            grad_query = grad_query + jnp.einsum(
                "gqtk,kgd->tgqd", grad_raw, k_blk, preferred_element_type=jnp.float32
            )
            grad_key = jnp.einsum(
                "gqtk,tgqd->kgd", grad_raw, q_low, preferred_element_type=jnp.float32
            )
            grad_value = jnp.einsum(
                "gqtk,tgqd->kgd",
                prob_blk.astype(jnp.bfloat16),
                grad_attn,
                preferred_element_type=jnp.float32,
            )
            kv_piece = jnp.concatenate(
                [grad_key.reshape(KBLK, KW), grad_value.reshape(KBLK, KW)], axis=1
            )
            grad_kv = lax.dynamic_update_slice_in_dim(grad_kv, kv_piece, blk_index * KBLK, 0)
            return (grad_query, grad_kv)

        return lax.cond(needed(blk_index), grad_do_block, unchanged, state_acc)

    grad_query, grad_kv = lax.fori_loop(
        0,
        block_count,
        grad_step,
        (
            jnp.zeros((tok_rows, KVH, q_per_kv, HD), jnp.float32),
            jnp.zeros((seq_len, 2 * KW), jnp.float32),
        ),
    )
    own_kv = lax.psum_scatter(grad_kv, "shard", scatter_dimension=0, tiled=True)
    neg_sines = -sines
    grad_q_raw = rotate(grad_query.reshape(tok_rows, QW), QH, cosines, neg_sines)
    grad_k_raw = rotate(own_kv[:, :KW], KVH, cosines, neg_sines)
    grad_qkv = jnp.concatenate([grad_q_raw, grad_k_raw, own_kv[:, KW:]], axis=1).astype(
        jnp.bfloat16
    )
    g_attn = jnp.dot(h_low.T, grad_qkv, preferred_element_type=jnp.float32)
    grad_h_attn = jnp.dot(grad_qkv, b_attn.T, preferred_element_type=jnp.float32)
    grad_gated, g_gated_gain = norm_back(grad_normed, gated, r_gate, gated_gain)
    grad_y = (grad_gated * silu_z).reshape(tok_rows, NH, HP)
    grad_z = grad_gated * ssm_y * dsilu(gate_z)

    def mamba_out(state_start, x_vals, b_vals, c_vals, dt_vals, la_vals, skip_vals):
        y_zero, state_local = ssd_spans(
            empty_state, x_vals, b_vals, c_vals, dt_vals, la_vals, skip_vals, seg_ids, before
        )
        fac_vals = carry_factor(la_vals)
        return (
            y_zero + carry_term(state_start, c_vals, fac_vals),
            state_local + state_start * fac_vals[-1][:, None, None],
        )

    unused_out, pull_back = jax.vjp(
        mamba_out, state_in, ssm_x, ssm_b, ssm_c, step_size, log_decay, skip_scale
    )
    first_pull = pull_back((grad_y, jnp.zeros_like(state_in)))
    later_state, unused_later = entering(
        (first_pull[0], dev_decay),
        "shard",
        combine_states,
        (jnp.zeros_like(state_in), jnp.ones_like(dev_decay)),
    )
    second = pull_back((jnp.zeros_like(grad_y), later_state))
    grad_x = first_pull[1] + second[1]
    grad_b = first_pull[2] + second[2]
    grad_c = first_pull[3] + second[3]
    grad_dt = first_pull[4] + second[4]
    grad_la = first_pull[5] + second[5]
    g_skip = first_pull[6] + second[6]
    g_a_log = jnp.sum(-grad_la * step_size * decay_rate, axis=0)
    grad_soft = (grad_dt - grad_la * decay_rate) * jax.nn.sigmoid(soft_in)
    g_dt_bias = jnp.sum(grad_soft, axis=0)
    grad_act = jnp.concatenate([grad_x.reshape(tok_rows, DS), grad_b, grad_c], axis=1)
    grad_conv = grad_act * dsilu(conv_pre)
    g_conv_bias = jnp.sum(grad_conv, axis=0)
    grad_padded = jnp.zeros((tok_rows + KC - 1, CONV_CH), jnp.float32)
    weight_cols = []
    for tap_index in range(KC):
        term_vals = grad_conv * tap_masks[tap_index]
        grad_padded = grad_padded + jnp.pad(
            term_vals * conv_weight[:, tap_index][None, :],
            ((tap_index, KC - 1 - tap_index), (0, 0)),
        )
        weight_cols.append(jnp.sum(term_vals * padded[tap_index : tap_index + tok_rows], axis=0))
    g_conv_weight = jnp.stack(weight_cols, axis=1)
    back_edge = from_behind(grad_padded[: KC - 1], "shard", -1)
    grad_xbc = grad_padded[KC - 1 :] + jnp.concatenate(
        [jnp.zeros((tok_rows - (KC - 1), CONV_CH), jnp.float32), back_edge], axis=0
    )
    grad_proj = jnp.concatenate([grad_z, grad_xbc, grad_soft], axis=1).astype(jnp.bfloat16)
    g_in = jnp.dot(h_low.T, grad_proj, preferred_element_type=jnp.float32)
    grad_h = jnp.dot(grad_proj, b_in.T, preferred_element_type=jnp.float32) + grad_h_attn
    grad_x_n, g_norm_one = norm_back(grad_h, x_full, r_one, norm_one)
    grad_input = grad_res + grad_x_n
    owned_grads = (
        lax.psum_scatter(g_in, "shard", scatter_dimension=0, tiled=True),
        lax.psum_scatter(g_attn, "shard", scatter_dimension=0, tiled=True),
        lax.psum_scatter(g_mo, "shard", scatter_dimension=0, tiled=True),
        lax.psum_scatter(g_ao, "shard", scatter_dimension=0, tiled=True),
        lax.psum_scatter(g_gu, "shard", scatter_dimension=0, tiled=True),
        lax.psum_scatter(g_down, "shard", scatter_dimension=0, tiled=True),
    )
    summed = lax.psum(
        (
            owned_grads[0],
            owned_grads[1],
            owned_grads[2],
            owned_grads[3],
            owned_grads[4],
            owned_grads[5],
        ),
        "replica",
    )
    small_sums = lax.psum(
        (
            g_norm_one,
            g_conv_weight,
            g_conv_bias,
            g_dt_bias,
            g_a_log,
            g_skip,
            g_gated_gain,
            g_norm_two,
            stat_local,
        ),
        ("replica", "shard"),
    )
    stat_sums = small_sums[8]
    rms_stats = jnp.sqrt(stat_sums[:3] / (stat_sums[3] * D))
    return (
        out_full.astype(jnp.bfloat16),
        grad_input,
        small_sums[0],
        summed[0],
        small_sums[1],
        small_sums[2],
        small_sums[3],
        small_sums[4],
        small_sums[5],
        small_sums[6],
        summed[1],
        summed[2],
        summed[3],
        small_sums[7],
        summed[4],
        summed[5],
        rms_stats,
    )


HEADS_AT = 6
XW = HEADS_AT * HP
LANES = 128
TB = 128
VMEM_BYTES = 20 * 1024 * 1024
AT_Y, AT_CORE, AT_BIT, AT_STARTS = 0, 1, {1: 2, 2: 3, 4: 4}, 5
Q_AT = XW
KV_AT = Q_AT + QW // 4
BC_AT = KV_AT + LANES
DT_AT = BC_AT + 2 * NS
W_FIRST = DT_AT + LANES
LOW = jnp.bfloat16
F32 = jnp.float32


def swap(block, bits):
    return lax.ppermute(block, "shard", [(i, i ^ bits) for i in range(lax.axis_size("shard"))])


def swap_far(block, bits):
    replicas, shards = lax.axis_size("replica"), lax.axis_size("shard")
    route = [
        (r * shards + s, (r ^ bits[s % 2]) * shards + s)
        for r in range(replicas)
        for s in range(shards)
    ]
    return lax.ppermute(block, ("replica", "shard"), route)


def after(value, other):
    return lax.optimization_barrier((value, other))[0]


def dot32(a, b):
    return jnp.dot(a, b, preferred_element_type=F32)


def dot_t(a, b):
    return lax.dot_general(a, b, (((1,), (1,)), ((), ())), preferred_element_type=F32)


def t_dot(a, b):
    return lax.dot_general(a, b, (((0,), (0,)), ((), ())), preferred_element_type=F32)


def rough(a, b, dims=((1,), (0,))):
    return lax.dot_general(
        a.astype(LOW), b.astype(LOW), (dims, ((), ())), preferred_element_type=F32
    )


def fair(a, b, dims=((1,), (0,))):
    a_high, b_high = a.astype(LOW), b.astype(LOW)
    a_low = (a - a_high.astype(F32)).astype(LOW)
    b_low = (b - b_high.astype(F32)).astype(LOW)

    def dot(x, y):
        return lax.dot_general(x, y, (dims, ((), ())), preferred_element_type=F32)

    return dot(a_high, b_high) + (dot(a_high, b_low) + dot(a_low, b_high))


def picked(a, b, dims=((1,), (0,)), terms=2):
    value, total = (b, 0.0) if a.dtype == LOW else (a, 0.0)
    for _ in range(terms):
        low = value.astype(LOW)
        pair = (a, low) if a.dtype == LOW else (low, b)
        total = total + lax.dot_general(*pair, (dims, ((), ())), preferred_element_type=F32)
        value = value - low.astype(F32)
    return total


def iota(shape, axis):
    return lax.broadcasted_iota(jnp.int32, shape, axis)


def count_starts(info, where):
    total = (info[AT_STARTS] <= where).astype(jnp.int32)
    for k in range(AT_STARTS + 1, info.shape[0]):
        total = total + (info[k] <= where).astype(jnp.int32)
    return total


def part(index, size):
    return pl.ds(pl.multiple_of(index * size, size), size)


def part_at(start, index, step, size):
    return pl.ds(pl.multiple_of(start + index * step, LANES), size)


def peers(info):
    y, c = info[AT_Y], info[AT_CORE]
    return (2 * y + c, 2 * y + 1 - c, 2 * (1 - y) + c, 2 * (1 - y) + 1 - c)


def bit_of(info, bits):
    return jnp.where(info[AT_CORE] == 0, info[AT_BIT[bits[0]]], info[AT_BIT[bits[1]]])


def f32_of(*shape):
    return jax.ShapeDtypeStruct(shape, F32)


def low_of(*shape):
    return jax.ShapeDtypeStruct(shape, LOW)


def call(kernel, outs, info, *operands, scratch=()):
    whole = pl.BlockSpec(memory_space=pltpu.VMEM)
    return pl.pallas_call(
        kernel,
        out_shape=outs,
        in_specs=[pl.BlockSpec(memory_space=pltpu.SMEM)] + [whole] * len(operands),
        out_specs=jax.tree.map(lambda _: whole, outs),
        scratch_shapes=scratch,
        compiler_params=pltpu.CompilerParams(vmem_limit_bytes=VMEM_BYTES),
    )(info, *operands)


def pack_in_kernel(info, w_in, w_qkv, own, core, far, z_own, z_core, z_far):
    y, places = info[AT_Y], peers(info)

    def shared(dst, chip):
        k, v = w_qkv[:, QW : QW + KW], w_qkv[:, QW + KW :]
        first = jnp.concatenate([k[:, :HD], v[:, :HD]], axis=1)
        second = jnp.concatenate([k[:, HD:], v[:, HD:]], axis=1)
        dst[KV_AT:BC_AT, :] = jnp.where(chip == 0, first, second).T
        dst[BC_AT:DT_AT, :] = w_in[2 * DS : 2 * DS + 2 * NS, :]
        dst[DT_AT:W_FIRST, :] = jnp.zeros((LANES, dst.shape[1]), LOW)
        dst[DT_AT : DT_AT + NH, :] = w_in[DS + CONV_CH :, :]

    for place, dst, at in zip(places, (own, core, far, far), (0, 0, W_FIRST, 0)):
        dst[at : at + XW, :] = w_in[part_at(DS, place, XW, XW), :]
        dst[at + XW : at + KV_AT, :] = w_qkv[:, part(place, QW // 4)].T
    for place, dst, at in zip(places, (z_own, z_core, z_far, z_far), (0, 0, XW, 0)):
        dst[at : at + XW, :] = w_in[part_at(0, place, XW, XW), :]
    shared(own, y)
    shared(core, y)
    shared(far, 1 - y)


def prepare_kernel(
    info, conv_weight, conv_bias, dt_bias, a_log, skip, gain, norm_one, norm_two, mask, cotangent,
    taps, bias, bias_own, rate, skip_wide, gain_own, gain_one, gain_two, keep, grad, turn, wide,
):
    place = peers(info)[0]
    for src, dst in ((conv_weight, taps), (conv_bias, bias)):
        dst[:, :XW] = src[:, part(place, XW)]
        dst[:, XW:] = src[:, DS:]
    gain_own[...] = gain[:, part(place, XW)]
    gain_one[...] = norm_one[...]
    gain_two[...] = norm_two[...]
    pick = own_heads_pick(info)
    wide[...] = jnp.zeros_like(wide)
    for k, src in enumerate((dt_bias, a_log, skip)):
        wide[k : k + 1, :NH] = src[...]
    own = picked(wide[...], pick, terms=3)
    bias_own[...] = own[0:1]
    rate[...] = jnp.exp(own[1:2])
    skip_wide[...] = picked(own, head_spread(), terms=3)[2:3]
    column = jnp.broadcast_to(mask[...].astype(F32), (LANES, LANES)).T
    keep[...] = column
    grad[...] = (cotangent[...].astype(F32) * column[:, :1]).astype(LOW)
    row, col, half = iota((LANES, LANES), 0), iota((LANES, LANES), 1), HD // 2
    down, up = (row == col + half).astype(F32), (row == col - half).astype(F32)
    turn[...] = jnp.where((col // half) % 2 == 0, -down, up).astype(LOW)


def total_kernel(info, a, b, out):
    out[...] = a[...] + b[...]


def pack_up_kernel(info, w_up, own, core, far):
    quarter, half = FF // 4, w_up.shape[0] // 2
    places = peers(info)
    for place, dst in zip(places, (own, core)):
        dst[:, :quarter] = w_up[:, part_at(0, place, quarter, quarter)]
        dst[:, quarter:] = w_up[:, part_at(FF, place, quarter, quarter)]
    mine = part(info[AT_BIT[1]], half)
    for k, place in enumerate(places[2:]):
        rows = slice(k * half, (k + 1) * half)
        far[rows, :quarter] = w_up[mine, part_at(0, place, quarter, quarter)]
        far[rows, quarter:] = w_up[mine, part_at(FF, place, quarter, quarter)]


def head_spread():
    row, col = iota((LANES, XW), 0), iota((LANES, XW), 1)
    return ((col >= row * HP) & (col < (row + 1) * HP)).astype(LOW)


def own_heads_pick(info):
    row, col = iota((LANES, LANES), 0), iota((LANES, LANES), 1)
    return ((row == col + peers(info)[0] * HEADS_AT) & (col < HEADS_AT)).astype(LOW)


def step_sizes(soft):
    real = iota(soft.shape, 1) < HEADS_AT
    return jnp.where(real, jnp.maximum(soft, 0.0) + jnp.log1p(jnp.exp(-jnp.abs(soft))), 0.0)


def span_parts(info, first, dt, la):
    shape = (SPAN, SPAN)
    row, col = iota(shape, 0), iota(shape, 1)
    seg_row = count_starts(info, row + first)
    seg_col = count_starts(info, col + first)
    seen = (seg_row == seg_col) & (row >= col)
    before = count_starts(info, first - 1)
    last = count_starts(info, first + SPAN - 1)
    total = picked((row >= col).astype(LOW), la, terms=3)
    carried = jnp.exp(total) * (seg_row == before).astype(F32)
    tail = jnp.exp(total[SPAN - 1 :] - total) * (seg_row == last).astype(F32)
    return seen, total, total.T, dt.T, carried, tail


def decay_of(seen, total, total_t, h):
    return jnp.exp(jnp.where(seen, total[:, h : h + 1] - total_t[h : h + 1, :], NEG))


def tap_masks(info, seg):
    seq = seg.shape[0] - 8
    seg[:8, :] = jnp.full((8, LANES), -1, jnp.int32)
    seg[8:, :] = count_starts(info, iota((seq, LANES), 0))
    here = seg[8:, :]
    return [
        (seg[8 - back : 8 - back + seq, :] == here).astype(F32) for back in range(KC - 1, 0, -1)
    ]


def forward_kernel(
    info, h_own, h_core, h_far, h_far_core, w_own, w_core, w_far, w_far_core,
    norm, taps, bias, dt_bias, rate, skip, cosines, sines, turn,
    h_low, w_full, xbc, conv_pre, soft, q_low, kv_low, y_out, states,
    padded, act, step, seg,
):
    seq = h_low.shape[0]
    places = peers(info)
    for place, ref in zip(places, (h_own, h_core, h_far, h_far_core)):
        x = ref[...].astype(F32)
        h_low[part(place, TB), :] = (x * rms_scale(x) * norm[...]).astype(LOW)
    depth = w_own.shape[1]
    for place, ref, at in zip(places, (w_own, w_core, w_far, w_far_core), (0, 0, W_FIRST, 0)):
        w_full[:KV_AT, part(place, depth)] = ref[at : at + KV_AT, :]
        w_full[KV_AT:, part(place, depth)] = ref[KV_AT:W_FIRST, :]
    h = h_low[...]
    xbc[:, :XW] = dot_t(h, w_full[:XW, :])
    xbc[:, XW:] = dot_t(h, w_full[BC_AT:DT_AT, :])
    rest = dot_t(h, w_full[Q_AT:BC_AT, :])
    q, kv = rest[:, :LANES], rest[:, LANES:]
    soft[...] = picked(dot_t(h, w_full[DT_AT:, :]), own_heads_pick(info), terms=3) + dt_bias[...]

    def turned(value):
        return value * cosines[...] + picked(value, turn[...]) * sines[...]

    q_low[...] = turned(q).astype(LOW)
    kv_low[...] = jnp.where(iota(kv.shape, 1) < HD, turned(kv), kv).astype(LOW)

    width = xbc.shape[1]
    padded[:8, :] = jnp.zeros((8, width), F32)
    padded[8:, :] = xbc[...]
    masks = tap_masks(info, seg)
    for block in range(0, width, LANES):
        lanes = slice(block, block + LANES)
        total = bias[:, lanes] + taps[KC - 1 : KC, lanes] * padded[8:, lanes]
        for j in range(KC - 1):
            start = 8 - (KC - 1 - j)
            total = total + taps[j : j + 1, lanes] * padded[start : start + seq, lanes] * masks[j]
        conv_pre[:, lanes] = total
        act[:, lanes] = total * jax.nn.sigmoid(total)

    step[...] = step_sizes(soft[...])
    spread = head_spread()
    state = jnp.zeros((NS, XW), F32)
    for k in range(seq // SPAN):
        rows = pl.ds(k * SPAN, SPAN)
        x = act[rows, :XW]
        b = act[rows, XW : XW + NS]
        c = act[rows, XW + NS :]
        dt = step[rows, :]
        seen, total, total_t, dt_t, carried, tail = span_parts(
            info, k * SPAN, dt, -dt * rate[...]
        )
        states[k] = state
        inner = fair(c, b, ((1,), (1,)))
        wide = picked(carried, spread)
        y = fair(c, state) * wide + x * skip[...]
        parts = []
        for h in range(HEADS_AT):
            mixing = decay_of(seen, total, total_t, h) * inner * dt_t[h : h + 1, :]
            parts.append(fair(mixing, x[:, h * HP : (h + 1) * HP]))
        y_out[rows, :] = y + jnp.concatenate(parts, axis=1)
        weighted = x * picked(tail * dt, spread)
        state = state * wide[SPAN - 1 :] + fair(b, weighted, ((0,), (0,)))


def gate_kernel(info, h_low, z_own, z_core, z_far, z_far_core, y, z_full, gate_z, square):
    depth = z_own.shape[1]
    for place, ref, at in zip(peers(info), (z_own, z_core, z_far, z_far_core), (0, 0, XW, 0)):
        z_full[:, part(place, depth)] = ref[at : at + XW, :]
    z = dot_t(h_low[...], z_full[...])
    gate_z[...] = z
    gated = y[...] * (z * jax.nn.sigmoid(z))
    square[...] = picked(jnp.ones((8, XW), LOW), gated * gated, ((1,), (1,)))


def column_of(row):
    return jnp.concatenate(
        [row[:, k : k + LANES].T[:, :1] for k in range(0, row.shape[1], LANES)], axis=0
    )


def output_kernel(
    info, sq_a, sq_b, y, gate_z, gain, attn, ssm_out, attn_out, given, kept, normed
):
    z = gate_z[...]
    scale = lax.rsqrt(column_of(sq_a[...] + sq_b[...]) / DS + EPS)
    normed[...] = (y[...] * (z * jax.nn.sigmoid(z)) * scale * gain[...]).astype(LOW)
    c = info[AT_CORE]
    for core, dst in ((1 - c, given), (c, kept)):
        for k in range(2):
            rows = part(2 * k + core, TB)
            dst[k] = dot32(normed[rows, :], ssm_out[...]) + dot32(attn[rows, :], attn_out[...])


def add_kernel(info, kept, moved, chip, low):
    total = kept[...] + moved[...]
    chip[...] = total
    low[...] = total.astype(LOW)


def add_split_kernel(info, kept, moved, mine, given):
    y = info[AT_Y]
    mine[...] = kept[y] + moved[y]
    given[...] = kept[1 - y] + moved[1 - y]


def pair_of(info, own, far, dst):
    y = info[AT_Y]
    dst[y] = own[...]
    dst[1 - y] = far[...]


def second_norm_kernel(
    info, chip, moved, h_own, h_far, norm, keep, residual, h2, mixed_sum, x_pair
):
    pair_of(info, h_own, h_far, x_pair)
    mixed = chip[...] + moved[...].astype(F32)
    total = x_pair[...].astype(F32) + mixed
    residual[...] = total
    h2[...] = (total * rms_scale(total) * norm[...]).astype(LOW)
    mine = (chip[info[AT_Y]] + moved[info[AT_Y]].astype(F32)) * keep[:, :1]
    mixed_sum[...] = jnp.sum(mine * mine, axis=0, keepdims=True)


def mlp_kernel(
    info, h2, h2_core, u_own, u_core, u_y, u_x, u_y_core, u_x_core, g_own, g_core, g_far, g_far_core, w_down,
    given, kept, hid, ggu, h2_cat, gmlp, u_full,
):
    y, quarter = info[AT_Y], FF // 4
    half = 2 * TB
    for k in range(2):
        h2_cat[k * TB : (k + 1) * TB, :] = h2[k]
        h2_cat[half + k * TB : half + (k + 1) * TB, :] = h2_core[k]
    for at, ref in ((y, g_own), (1 - y, g_far), (2 + y, g_core), (3 - y, g_far_core)):
        gmlp[part(at, TB), :] = ref[...]
    depth = u_own.shape[0]
    places, x, piece = peers(info), info[AT_BIT[1]], depth // 2
    u_full[part(places[0], depth), :] = u_own[...]
    u_full[part(places[1], depth), :] = u_core[...]
    for at, ref, ref_core in ((x, u_y, u_y_core), (1 - x, u_x, u_x_core)):
        u_full[part(2 * places[2] + at, piece), :] = ref[:piece, :]
        u_full[part(2 * places[3] + at, piece), :] = ref_core[piece:, :]
    tile = quarter // 2
    for t in range(0, quarter, tile):
        ghid = dot_t(gmlp[...], w_down[t : t + tile, :])
        gate = dot32(h2_cat[...], u_full[:, t : t + tile])
        up = dot32(h2_cat[...], u_full[:, quarter + t : quarter + t + tile])
        sig = jax.nn.sigmoid(gate)
        silu = gate * sig
        hid[:, t : t + tile] = (silu * up).astype(LOW)
        ggu[:, t : t + tile] = (ghid * up * (sig * (1.0 + gate * (1.0 - sig)))).astype(LOW)
        ggu[:, quarter + t : quarter + t + tile] = (ghid * silu).astype(LOW)
    for t in range(0, D, 2 * tile):
        cols = slice(t, t + 2 * tile)
        part_sum = dot_t(ggu[half:, :], u_full[cols, :])
        given[0, :, cols] = part_sum[:TB]
        given[1, :, cols] = part_sum[TB:]
        part_sum = dot_t(ggu[:half, :], u_full[cols, :])
        kept[0, :, cols] = part_sum[:TB]
        kept[1, :, cols] = part_sum[TB:]


def down_kernel(info, hid, w_down, given, kept):
    half = 2 * TB
    for k in range(2):
        given[k] = dot32(hid[half + k * TB : half + (k + 1) * TB, :], w_down[...])
        kept[k] = dot32(hid[k * TB : (k + 1) * TB, :], w_down[...])


def store_halves(mine, rows, first, given, kept):
    half = LANES // 2
    for k in range(rows.shape[0] // LANES):
        low, high = rows[k * LANES : k * LANES + half], rows[k * LANES + half : (k + 1) * LANES]
        given[first + k] = jnp.where(mine == 0, high, low).astype(LOW)
        kept[first + k] = jnp.where(mine == 0, low, high)


def grad_mlp_kernel(bits, info, h2, ggu, hid, gmlp, given, kept):
    mine, step = bit_of(info, bits), 2 * LANES
    for left, right, first in ((h2, ggu, 0), (hid, gmlp, D // LANES)):
        for at in range(0, left.shape[1], step):
            rows = t_dot(left[:, at : at + step], right[...])
            store_halves(mine, rows, first + at // LANES, given, kept)


def grad_mid_kernel(bits, info, normed, attn, gmix, given, kept):
    mine, first = bit_of(info, bits), 0
    for left, right in ((normed, gmix), (attn, gmix)):
        for at in range(0, left.shape[1], LANES):
            rows = t_dot(left[:, at : at + LANES], right[...])
            store_halves(mine, rows, first + at // LANES, given, kept)
        first += left.shape[1] // LANES


def norm_back_pair_kernel(info, chip, moved, residual, norm, g_own, g_far, gres, gmix, g_norm, gout):
    pair_of(info, g_own, g_far, gout)
    gh2 = chip[...] + moved[...].astype(F32)
    value = residual[...]
    scale = rms_scale(value)
    uu = gh2 * norm[...]
    mean = jnp.mean(uu * value, axis=-1, keepdims=True)
    grad = gout[...].astype(F32) + scale * uu - value * scale**3 * mean
    gres[...] = grad
    gmix[...] = grad.astype(LOW)
    y = info[AT_Y]
    mine = residual[y]
    g_norm[...] = jnp.sum(
        (chip[y] + moved[y].astype(F32)) * mine * rms_scale(mine), axis=0, keepdims=True
    )


def output_back_kernel(
    info, gmix, gmix_core, y, gate_z, gain, ssm_out, attn_out, gmix_all, gnormed, gattn, uv
):
    c = info[AT_CORE]
    for core, src in ((c, gmix), (1 - c, gmix_core)):
        for k in range(2):
            gmix_all[part(2 * k + core, TB), :] = src[k]
    grad = dot_t(gmix_all[...], ssm_out[...])
    gnormed[...] = grad
    z = gate_z[...]
    product = grad * gain[...] * (y[...] * (z * jax.nn.sigmoid(z)))
    uv[...] = picked(jnp.ones((8, XW), LOW), product, ((1,), (1,)))
    gattn[...] = dot_t(gmix_all[...], attn_out[...]).astype(LOW)


def conv_back(masks, gconv, slope, taps, inputs, gpad):
    seq = gconv.shape[0]
    gconv = gconv * slope
    gpad[seq:, :] = jnp.zeros((8, LANES), F32)
    total = taps[KC - 1] * gconv
    rows = []
    for j in range(KC - 1):
        back = KC - 1 - j
        term = gconv * masks[j]
        rows.append(jnp.sum(term * inputs(j), axis=0, keepdims=True))
        gpad[:seq, :] = term * taps[j]
        total = total + gpad[back : back + seq, :]
    rows.append(jnp.sum(gconv * inputs(KC - 1), axis=0, keepdims=True))
    rows.append(jnp.sum(gconv, axis=0, keepdims=True))
    return total, rows


def gate_back_kernel(
    info, sq_a, sq_b, uv_a, uv_b, gnormed, y, gate_z, gain, gzz, gy, g_gain
):
    z = gate_z[...]
    sig = jax.nn.sigmoid(z)
    gated = y[...] * (z * sig)
    scale = lax.rsqrt(column_of(sq_a[...] + sq_b[...]) / DS + EPS)
    mean = column_of(uv_a[...] + uv_b[...]) / DS
    grad = gnormed[...]
    ggz = scale * (grad * gain[...]) - gated * scale**3 * mean
    gy[...] = ggz * (z * sig)
    gzz[...] = (ggz * y[...] * (sig * (1.0 + z * (1.0 - sig)))).astype(LOW)
    g_gain[...] = jnp.sum(grad * gated * scale, axis=0, keepdims=True)


def scan_prepare_kernel(
    info, conv_pre, soft, rate, states,
    decay_dt, decay_in, act, slope, from_state, wide, wide_tail, tail_out, step,
):
    pre = conv_pre[...]
    sig = jax.nn.sigmoid(pre)
    act[...] = pre * sig
    slope[...] = sig * (1.0 + pre * (1.0 - sig))
    step[...] = step_sizes(soft[...])
    spread = head_spread()
    for k in range(states.shape[0]):
        rows = pl.ds(k * SPAN, SPAN)
        b = act[rows, XW : XW + NS]
        c = act[rows, XW + NS :]
        dt = step[rows, :]
        seen, total, total_t, dt_t, carried, tail = span_parts(
            info, k * SPAN, dt, -dt * rate[...]
        )
        inner = fair(c, b, ((1,), (1,)))
        for h in range(HEADS_AT):
            decay = decay_of(seen, total, total_t, h)
            decay_dt[k * HEADS_AT + h] = decay * dt_t[h : h + 1, :]
            decay_in[k * HEADS_AT + h] = decay * inner
        from_state[rows, :] = fair(c, states[k])
        wide[rows, :] = picked(carried, spread)
        wide_tail[rows, :] = picked(tail * dt, spread)
        tail_out[rows, :] = tail


def scan_back_kernel(
    info, xbc, soft, rate, skip, states, taps, gy,
    decay_dt, decay_in, act, slope, from_state, wide_all, wide_tail_all, tail_all, step,
    gx_low, gbc_given, gbc_kept, gdr, gsoft_low, g_taps, g_skip, g_heads,
    gact, gdt, gla, padded, gpad, seg,
):
    seq = gy.shape[0]
    spread = head_spread()
    shape = (SPAN, SPAN)
    row, col = iota(shape, 0), iota(shape, 1)
    upper = (col >= row).astype(LOW)
    later = jnp.zeros((NS, XW), F32)
    skip_sum = jnp.zeros((1, XW), F32)
    for k in reversed(range(seq // SPAN)):
        rows = pl.ds(k * SPAN, SPAN)
        x = act[rows, :XW]
        b = act[rows, XW : XW + NS]
        c = act[rows, XW + NS :]
        dt = step[rows, :]
        dt_t = dt.T
        g = gy[rows, :]
        state = states[k]
        wide, wide_tail, tail = wide_all[rows, :], wide_tail_all[rows, :], tail_all[rows, :]
        g_carried = g * wide
        ginner = jnp.zeros(shape, F32)
        out_sum = jnp.zeros(shape, F32)
        in_sum = jnp.zeros(shape, F32)
        parts = []
        for h in range(HEADS_AT):
            own = slice(h * HP, (h + 1) * HP)
            inner = decay_in[k * HEADS_AT + h]
            product = fair(g[:, own], x[:, own], ((1,), (1,)))
            ginner = ginner + product * decay_dt[k * HEADS_AT + h]
            both = product * inner
            out_sum = out_sum + jnp.where(
                col == h, jnp.sum(both * dt_t[h : h + 1, :], axis=1, keepdims=True), 0.0
            )
            in_sum = in_sum + jnp.where(row == h, jnp.sum(both, axis=0, keepdims=True), 0.0)
            parts.append(rough(inner, g[:, own], ((0,), (0,))) * dt[:, h : h + 1])
        from_later = fair(b, later)
        gact[rows, :XW] = (
            jnp.concatenate(parts, axis=1) + from_later * wide_tail + g * skip[...]
        )
        gact[rows, XW : XW + NS] = rough(ginner, c, ((0,), (0,))) + rough(
            x * wide_tail, later, ((1,), (1,))
        )
        gact[rows, XW + NS :] = rough(ginner, b) + rough(g_carried, state, ((1,), (1,)))
        tail_in = picked(x * from_later, spread, ((1,), (1,)))
        state_out = picked(from_state[rows, :] * g_carried, spread, ((1,), (1,)))
        in_col = in_sum.T
        gdt[rows, :] = in_col + tail_in * tail
        moved = tail_in * tail * dt
        kept = picked(
            jnp.sum(state * later, axis=0, keepdims=True) * wide[SPAN - 1 :],
            spread,
            ((1,), (1,)),
        )
        at_end = jnp.sum(moved, axis=0, keepdims=True) + kept
        change = out_sum - in_col * dt + state_out - moved
        gla[rows, :] = picked(upper, change, terms=3) + at_end
        skip_sum = skip_sum + jnp.sum(g * x, axis=0, keepdims=True)
        later = later * wide[SPAN - 1 :] + fair(c, g_carried, ((0,), (0,)))
    g_skip[...] = skip_sum

    core = info[AT_CORE]
    gbc_given[...] = gact[:, part_at(XW, 1 - core, NS, NS)]
    gbc_kept[...] = gact[:, part_at(XW, core, NS, NS)]

    gsoft = (gdt[...] - gla[...] * rate[...]) * jax.nn.sigmoid(soft[...])
    gsoft = jnp.where(iota(gsoft.shape, 1) < HEADS_AT, gsoft, 0.0)
    gsoft_low[...] = gsoft.astype(LOW)
    gdr[...] = dot_t(gsoft.astype(LOW), own_heads_pick(info)).astype(LOW)
    g_heads[0:1, :] = jnp.sum(-gla[...] * step[...] * rate[...], axis=0, keepdims=True)
    g_heads[1:2, :] = jnp.sum(gsoft, axis=0, keepdims=True)
    g_heads[2:, :] = jnp.zeros((6, LANES), F32)

    padded[:8, :] = jnp.zeros((8, LANES), F32)
    masks = tap_masks(info, seg)
    g_taps[...] = jnp.zeros_like(g_taps)
    for block in range(0, XW, LANES):
        lanes = slice(block, block + LANES)
        padded[8:, :] = xbc[:, lanes]
        total, sums = conv_back(
            masks, gact[:, lanes], slope[:, lanes],
            [taps[j : j + 1, lanes] for j in range(KC)],
            lambda j: padded[8 - (KC - 1 - j) : 8 - (KC - 1 - j) + seq, :], gpad,
        )
        gx_low[:, lanes] = total.astype(LOW)
        for j, value in enumerate(sums):
            g_taps[j : j + 1, lanes] = value


def shared_back_kernel(
    info, gbc_kept, gbc_moved, xbc, slope, taps, gbc_low, g_taps, padded, gpad, seg
):
    seq = gbc_low.shape[0]
    lanes = part_at(XW, info[AT_CORE], NS, NS)
    padded[:8, :] = jnp.zeros((8, LANES), F32)
    padded[8:, :] = xbc[:, lanes]
    total, sums = conv_back(
        tap_masks(info, seg), gbc_kept[...] + gbc_moved[...], slope[:, lanes],
        [taps[j : j + 1, lanes] for j in range(KC)],
        lambda j: padded[8 - (KC - 1 - j) : 8 - (KC - 1 - j) + seq, :], gpad,
    )
    g_taps[...] = jnp.zeros_like(g_taps)
    for j, value in enumerate(sums):
        g_taps[j : j + 1, :] = value
    gbc_low[...] = total.astype(LOW)


def late_kernel(bits, info, gzz, gq, gkv, gx_low, gbc_low, gsoft, h_low, given, kept, left):
    mine, core = bit_of(info, bits), info[AT_CORE]
    own = gsoft[...]
    other = jnp.concatenate([own[:, HD:], own[:, :HD]], axis=1)
    is_own = (iota(own.shape, 1) < HD) == (core == 0)
    left[...] = jnp.where(is_own, gkv[...], jnp.where(core == 0, other, own))
    first = 0
    for value in (gzz, gq, left, gx_low, gbc_low):
        for at in range(0, value.shape[1], LANES):
            rows = t_dot(value[:, at : at + LANES], h_low[...])
            store_halves(mine, rows, first + at // LANES, given, kept)
        first += value.shape[1] // LANES


def inputs_back_kernel(
    info, gx_low, gzz, gq, gkv, gbc_low, gdr, w_full, z_full, given, kept, back
):
    c = info[AT_CORE]
    gbc = gbc_low[...]
    nothing = jnp.zeros_like(gbc)
    back[:, :XW] = gx_low[...]
    back[:, Q_AT:KV_AT] = gq[...]
    back[:, KV_AT:BC_AT] = gkv[...]
    back[:, BC_AT : BC_AT + NS] = jnp.where(c == 0, gbc, nothing)
    back[:, BC_AT + NS : DT_AT] = jnp.where(c == 0, nothing, gbc)
    back[:, DT_AT:W_FIRST] = gdr[...]
    back[:, W_FIRST:] = gzz[...]
    for core, dst in ((1 - c, given), (c, kept)):
        for k in range(2):
            rows = part(2 * k + core, TB)
            dst[k] = dot32(back[rows, :W_FIRST], w_full[...]) + dot32(
                back[rows, W_FIRST:], z_full[...]
            )


def first_norm_back_kernel(info, mine, moved, hidden, norm, gres, out, g_norm):
    gh = mine[...] + moved[...]
    value = hidden[...].astype(F32)
    scale = rms_scale(value)
    uu = gh * norm[...]
    mean = jnp.mean(uu * value, axis=-1, keepdims=True)
    out[...] = gres[info[AT_Y]] + scale * uu - value * scale**3 * mean
    g_norm[...] = jnp.sum(gh * value * scale, axis=0, keepdims=True)


def result_kernel(info, mine, moved, residual, keep, out, sums):
    mlp = mine[...] + moved[...]
    full = residual[info[AT_Y]] + mlp
    out[...] = full.astype(LOW)
    full = full * keep[:, :1]
    mlp = mlp * keep[:, :1]
    sums[0:1, :] = jnp.sum(full * full, axis=0, keepdims=True)
    sums[1:2, :] = jnp.sum(mlp * mlp, axis=0, keepdims=True)
    sums[2:, :] = jnp.zeros((6, D), F32)


def attend_kernel(info, q_ref, kv_ref, out_ref, lse_ref):
    scale = 1.0 / math.sqrt(HD)
    heads = q_ref.shape[1] // HD
    for k in range(q_ref.shape[0] // SPAN):
        rows, reach = pl.ds(k * SPAN, SPAN), (k + 1) * SPAN
        keys, values = kv_ref[:reach, :HD], kv_ref[:reach, HD:]
        counted = counted_keys(info, k * SPAN, reach)
        outs, tops = [], []
        for h in range(heads):
            s = dot_t(q_ref[rows, h * HD : (h + 1) * HD], keys) * scale
            s = jnp.where(counted, s, NEG)
            top = jnp.max(s, axis=1, keepdims=True)
            lse = top + jnp.log(jnp.sum(jnp.exp(s - top), axis=1, keepdims=True))
            prob = jnp.exp(s - lse).astype(LOW)
            outs.append(dot32(prob, values))
            tops.append(lse)
        out_ref[rows, :] = jnp.concatenate(outs, axis=1).astype(LOW)
        lane = iota((SPAN, LANES), 1)
        lse_ref[rows, :] = sum(jnp.where(lane == h, t, 0.0) for h, t in enumerate(tops))


def counted_keys(info, first, reach):
    shape = (SPAN, reach)
    row, col = iota(shape, 0) + first, iota(shape, 1)
    return (col <= row) & (count_starts(info, row) == count_starts(info, col))


def attend_back_kernel(
    info, q_ref, kv_ref, lse_ref, gout_ref, cosines, sines, turn, gq_ref, gkv_ref, gq_rot
):
    scale = 1.0 / math.sqrt(HD)
    heads = q_ref.shape[1] // HD
    gkv_ref[...] = jnp.zeros_like(gkv_ref)
    for k in range(q_ref.shape[0] // SPAN):
        rows, reach = pl.ds(k * SPAN, SPAN), (k + 1) * SPAN
        keys, values = kv_ref[:reach, :HD], kv_ref[:reach, HD:]
        counted = counted_keys(info, k * SPAN, reach)
        outs, gkeys, gvalues = [], 0.0, 0.0
        for h in range(heads):
            own = slice(h * HD, (h + 1) * HD)
            q, gout = q_ref[rows, own], gout_ref[rows, own]
            s = dot_t(q, keys) * scale
            pe = jnp.exp(jnp.where(counted, s - lse_ref[rows, h : h + 1], NEG))
            gprob = dot_t(gout, values)
            delta = jnp.sum(pe * gprob, axis=1, keepdims=True)
            gs = (pe * (gprob - delta) * scale).astype(LOW)
            outs.append(dot32(gs, keys))
            gkeys = gkeys + t_dot(gs, q)
            gvalues = gvalues + t_dot(pe.astype(LOW), gout)
        gq_rot[rows, :] = jnp.concatenate(outs, axis=1)
        gkv_ref[:reach, :] += jnp.concatenate([gkeys, gvalues], axis=1)
    value = gq_rot[...]
    gq_ref[...] = (value * cosines[...] - picked(value, turn[...]) * sines[...]).astype(LOW)


def keys_back_kernel(info, own, moved, cosines, sines, turn, out):
    value = own[...] + moved[...]
    back = value * cosines[...] - picked(value, turn[...]) * sines[...]
    is_key = iota(value.shape, 1) < HD
    mine = is_key == (info[AT_CORE] == 0)
    out[...] = jnp.where(mine, jnp.where(is_key, back, value), 0.0).astype(LOW)


def halve_kernel(bits, info, kept, moved, given_next, kept_next):
    mine = bit_of(info, bits)
    half = kept.shape[1] // 2
    own, other = part(mine, half), part(1 - mine, half)
    given_next[...] = (kept[:, other, :] + moved[:, other, :].astype(F32)).astype(LOW)
    kept_next[...] = kept[:, own, :] + moved[:, own, :].astype(F32)


def settle_kernel(by_rows, info, kept, moved, total, core, far, far_core):
    total[...] = (kept[...] + moved[...].astype(F32)).astype(LOW)
    for place, dst in zip(peers(info)[1:], (core, far, far_core)):
        if by_rows:
            count = by_rows // 4
            dst[...] = total[pl.ds(count * place, count)]
        else:
            dst[...] = total[:, :, part(place, dst.shape[2])]


def total_low_kernel(info, kept, moved, out):
    out[...] = (kept[...] + moved[...].astype(F32)).astype(LOW)


def spread_kernel(by_rows, info, total, core, far, far_core, out):
    places = peers(info)
    out[...] = total[...]
    for place, ref in zip(places[1:], (core, far, far_core)):
        if by_rows:
            count = by_rows // 4
            out[pl.ds(count * place, count)] = ref[...]
        else:
            out[:, :, part(place, ref.shape[2])] = ref[...]


def join_kernel(bits, info, own, moved, out):
    mine, size = bit_of(info, bits), own.shape[1]
    out[:, part(mine, size), :] = own[...]
    out[:, part(1 - mine, size), :] = moved[...]


def sum_steps(info, given, kept, order, by_rows):
    moved = swap_far(given, order[0])
    for bits in order[1:]:
        moved = after(moved, (yield given))
        n, size, width = kept.shape
        given, kept = call(
            functools.partial(halve_kernel, bits),
            (low_of(n, size // 2, width), f32_of(n, size // 2, width)),
            info, kept, moved,
        )
        moved = swap_far(given, bits)
    moved = after(moved, (yield given))
    n, size, width = kept.shape
    if by_rows is None:
        own = call(total_low_kernel, low_of(n, size, width), info, kept, moved)
    else:
        block = (by_rows // 4, size, width) if by_rows else (n, size, width // 4)
        total, *blocks = call(
            functools.partial(settle_kernel, by_rows),
            (low_of(n, size, width),) + (low_of(*block),) * 3,
            info, kept, moved,
        )
        sent = [swap(block, bits) for block, bits in zip(blocks, (1, 2, 3))]
        sent = after(sent, (yield blocks))
        own = call(
            functools.partial(spread_kernel, by_rows), low_of(n, size, width), info, total, *sent
        )
    for bits in order[:0:-1]:
        moved = swap_far(own, bits)
        moved = after(moved, (yield own))
        n, size, width = own.shape
        own = call(
            functools.partial(join_kernel, bits), low_of(n, 2 * size, width), info, own, moved
        )
    moved = swap_far(own, order[0])
    return own, after(moved, (yield own))


class Running:
    def __init__(self, steps):
        self.steps, self.result = steps, None
        self.sent = next(steps)

    def step(self, value):
        if self.result is not None:
            return value
        try:
            self.sent = self.steps.send(value)
        except StopIteration as end:
            self.result = self.sent = end.value
        return self.sent


def quarters(bits, info, own, moved, source=None):
    mine, size = bit_of(info, bits), own.shape[1] // 2
    same = True if source is None else info[AT_CORE] == source % 2
    for at, ref in ((mine, own), (1 - mine, moved)):
        for j in range(2):
            yield jnp.where(same, 2 * at + j, 2 * j + at), ref, slice(j * size, (j + 1) * size)


def finish_mlp_kernel(bits, info, own, moved, out_up, out_down):
    quarter, size, blocks = FF // 4, own.shape[1] // 2, D // LANES
    each = blocks // 4
    for k in range(4):
        for at, ref, rows in quarters(bits, info, own, moved, k):
            for j in range(each):
                block = ref[each * k + j, rows, :].astype(F32)
                where = part(4 * j + at, size)
                out_up[where, k * quarter : (k + 1) * quarter] = block[:, :quarter]
                out_up[where, FF + k * quarter : FF + (k + 1) * quarter] = block[:, quarter:]
    for at, ref, rows in quarters(bits, info, own, moved):
        for j in range(out_down.shape[0] // LANES):
            out_down[part(4 * j + at, size), :] = ref[blocks + j, rows, :].astype(F32)


def finish_mid_kernel(bits, info, own, moved, out_ssm, out_attn):
    size, scan = own.shape[1] // 2, XW // LANES
    for at, ref, rows in quarters(bits, info, own, moved):
        for j in range(scan):
            out_ssm[part(4 * j + at, size), :] = ref[j, rows, :].astype(F32)
        out_attn[part(at, size), :] = ref[scan, rows, :].astype(F32)


def finish_in_kernel(bits, info, own, moved, out, out_qkv, blocks_q, blocks_kv, shared):
    size, wide, scan = own.shape[1] // 2, out.shape[1], XW // LANES
    q_at, x_at = scan, scan + 2
    for k in range(4):
        lanes = slice(k * wide, (k + 1) * wide)
        for at, ref, rows in quarters(bits, info, own, moved, k):
            for j in range(scan):
                for first, block in ((0, j), (DS, x_at + j)):
                    start = first + (k * scan + j) * LANES + at * size
                    out[pl.ds(pl.multiple_of(start, size), size), :] = ref[
                        block, rows, lanes
                    ].astype(F32)
            blocks_q[k, part(at, size), :] = ref[q_at, rows, lanes].astype(F32)
            blocks_kv[k, part(at, size), :] = ref[q_at + 1, rows, lanes].astype(F32)
            shared[k, part(at, size), :] = ref[x_at + scan, rows, lanes].astype(F32)
    for k in range(4):
        out_qkv[:, k * LANES : (k + 1) * LANES] = blocks_q[k].T
    for k in range(2):
        rows = slice(k * HD, (k + 1) * HD)
        both = jnp.concatenate([blocks_kv[k, rows, :], blocks_kv[k + 2, rows, :]], axis=0)
        out_qkv[:, QW + k * KW : QW + (k + 1) * KW] = both.T
        out[2 * DS + k * NS : 2 * DS + (k + 1) * NS, :] = shared[k] + shared[k + 2]
    steps = [
        blocks_kv[k, (1 - k % 2) * HD : (1 - k % 2) * HD + HEADS_AT, :] for k in range(4)
    ]
    out[DS + CONV_CH :, :] = jnp.concatenate(steps, axis=0)


def small_steps(info, vector):
    for bits in (1, 2, (1, 1), (2, 2), (4, 4)):
        moved = swap_far(vector, bits) if isinstance(bits, tuple) else swap(vector, bits)
        moved = after(moved, (yield vector))
        vector = call(total_kernel, f32_of(*vector.shape), info, vector, moved)
    return vector


def unpack_kernel(info, small, one, conv, conv_bias, dt_bias, a_log, skip, gain, two, stats):
    for first, out in ((ROW_ONE, one), (ROW_TWO, two), (ROW_GAIN, gain)):
        for k in range(out.shape[1] // LANES):
            out[:, k * LANES : (k + 1) * LANES] = small[first + k : first + k + 1, :]
    for j in range(KC + 1):
        for k in range(CONV_ROWS):
            at = ROW_TAPS + j * CONV_ROWS + k
            dst, row = (conv, j) if j < KC else (conv_bias, 0)
            dst[row : row + 1, k * LANES : (k + 1) * LANES] = small[at : at + 1, :]
    for first, out in ((ROW_RATE, a_log), (ROW_BIAS, dt_bias)):
        pieces = [small[first + k : first + k + 1, :HEADS_AT] for k in range(4)]
        out[...] = jnp.concatenate(pieces, axis=1)
    lane = iota((1, LANES), 1)
    total = jnp.zeros((1, LANES), F32)
    for k in range(NH):
        at, first = ROW_SKIP + k * HP // LANES, k * HP % LANES
        value = jnp.sum(small[at : at + 1, first : first + HP], axis=1, keepdims=True)
        total = total + jnp.where(lane == k, value, 0.0)
    skip[...] = total[:, :NH]
    sums = [
        jnp.sum(small[ROW_STATS + k : ROW_STATS + k + 1, :], axis=1, keepdims=True)
        for k in range(4)
    ]
    total = jnp.zeros((1, LANES), F32)
    for k in range(3):
        total = total + jnp.where(lane == k, jnp.sqrt(sums[k] / (sums[3] * D)), 0.0)
    stats[...] = total[:, :3]


ROW_ONE, ROW_TWO, ROW_TAPS = 0, 8, 16
CONV_ROWS = CONV_CH // LANES
ROW_GAIN = ROW_TAPS + (KC + 1) * CONV_ROWS
ROW_SKIP = ROW_GAIN + DS // LANES
ROW_RATE = ROW_SKIP + DS // LANES
ROW_BIAS = ROW_RATE + 4
ROW_STATS = ROW_BIAS + 4
SMALL_ROWS = 128


def small_kernel(
    info, one, two, taps_x, taps_bc, gain, skip, heads, sums, mixed, keep, out
):
    out[...] = jnp.zeros_like(out)
    place, core = peers(info)[0], info[AT_CORE]
    for k in range(D // LANES):
        lanes = slice(k * LANES, (k + 1) * LANES)
        out[ROW_ONE + k : ROW_ONE + k + 1, :] = one[:, lanes]
        out[ROW_TWO + k : ROW_TWO + k + 1, :] = two[:, lanes]
    blocks = XW // LANES
    for k in range(blocks):
        lanes = slice(k * LANES, (k + 1) * LANES)
        at = place * blocks + k
        for j in range(KC + 1):
            out[pl.ds(ROW_TAPS + j * CONV_ROWS + at, 1), :] = taps_x[j : j + 1, lanes]
        out[pl.ds(ROW_GAIN + at, 1), :] = gain[:, lanes]
        out[pl.ds(ROW_SKIP + at, 1), :] = skip[:, lanes]
    for j in range(KC + 1):
        out[pl.ds(ROW_TAPS + j * CONV_ROWS + DS // LANES + core, 1), :] = taps_bc[j : j + 1, :]
    out[pl.ds(ROW_RATE + place, 1), :] = heads[0:1, :]
    out[pl.ds(ROW_BIAS + place, 1), :] = heads[1:2, :]
    for k, row in enumerate((sums[0:1, :], mixed[...], sums[1:2, :])):
        folded = row[:, :LANES]
        for j in range(1, D // LANES):
            folded = folded + row[:, j * LANES : (j + 1) * LANES]
        out[ROW_STATS + k : ROW_STATS + k + 1, :] = folded
    out[ROW_STATS + 3 : ROW_STATS + 4, :] = keep[...].T[:1]


def by_heads(
    hidden_in, cotangent, doc_starts, valid_mask, norm_one, in_proj, conv_weight, conv_bias,
    dt_bias, a_log, skip_scale, gated_gain, qkv_proj, ssm_out, attn_out, norm_two, gate_up,
    down_proj,
):
    place, far_place = lax.axis_index("shard"), lax.axis_index("replica")
    y, c = place // 2, place % 2
    rows = hidden_in.shape[0]
    seq, depth = 4 * rows, in_proj.shape[0]
    bits = [y, c, far_place % 2, far_place // 2 % 2, far_place // 4]
    info = jnp.concatenate([jnp.stack(bits).astype(jnp.int32), doc_starts[0]])
    pair = (2, rows, D)

    h_far = swap(hidden_in, 2)
    h_core = swap(hidden_in, 1)
    w_own, w_core, w_far, z_own, z_core, z_far = call(
        pack_in_kernel,
        (
            low_of(W_FIRST, depth), low_of(W_FIRST, depth), low_of(W_FIRST + KV_AT, depth),
            low_of(XW, depth), low_of(XW, depth), low_of(2 * XW, depth),
        ),
        info, in_proj.T, qkv_proj,
    )
    u_own, u_core, u_far = call(
        pack_up_kernel, (low_of(depth, FF // 2),) * 3, info, after(gate_up, w_own)
    )
    freqs = ROPE_BASE ** (-(jnp.arange(HD // 2).astype(F32) * 2.0) / HD)
    angles = jnp.arange(seq).astype(F32)[:, None] * jnp.tile(freqs, LANES // (HD // 2))[None, :]
    cosines, sines = jnp.cos(angles), jnp.sin(angles)
    taps, bias, bias_own, rate, skip, gain, gain_one, gain_two, keep, g_own, turn = call(
        prepare_kernel,
        (
            f32_of(KC, XW + 2 * NS), f32_of(1, XW + 2 * NS), f32_of(1, LANES), f32_of(1, LANES),
            f32_of(1, XW), f32_of(1, XW), f32_of(1, D), f32_of(1, D), f32_of(LANES, LANES),
            low_of(rows, D), low_of(LANES, LANES),
        ),
        info, conv_weight.T, conv_bias[None], dt_bias[None], a_log[None], skip_scale[None],
        gated_gain[None], norm_one[None], norm_two[None], valid_mask[None],
        after(cotangent, (cosines, sines)),
        scratch=(pltpu.VMEM((8, LANES), F32),),
    )
    w_far = swap(after(w_far, (u_own, g_own, h_far)), 2)
    w_core = swap(w_core, 1)
    h_far_core = swap(h_far, 1)
    w_far_core = swap(w_far, 1)
    z_far = swap(after(z_far, w_far), 2)

    h_low, w_full, xbc, conv_pre, soft, q_low, kv_low, ssm_y, states = call(
        forward_kernel,
        (
            low_of(seq, D), low_of(W_FIRST, D), f32_of(seq, XW + 2 * NS), f32_of(seq, XW + 2 * NS),
            f32_of(seq, LANES), low_of(seq, LANES), low_of(seq, LANES), f32_of(seq, XW),
            f32_of(seq // SPAN, NS, XW),
        ),
        info, hidden_in, h_core, h_far, h_far_core, w_own, w_core, w_far, w_far_core,
        gain_one, taps, bias, bias_own, rate, skip, cosines, sines, turn,
        scratch=(
            pltpu.VMEM((seq + 8, XW + 2 * NS), F32), pltpu.VMEM((seq, XW + 2 * NS), F32),
            pltpu.VMEM((seq, LANES), F32), pltpu.VMEM((seq + 8, LANES), jnp.int32),
        ),
    )
    z_far, z_core = after((z_far, z_core), h_low)
    z_core, z_far_core = swap(z_core, 1), swap(z_far, 1)
    u_far, u_core, g_out = after((u_far, u_core, g_own), z_far)
    u_y, g_far = swap(u_far, 2), swap(g_out, 2)
    z_full, gate_z, square = call(
        gate_kernel, (low_of(XW, D), f32_of(seq, XW), f32_of(8, seq)),
        info, h_low, z_own, z_core, z_far, z_far_core, ssm_y,
    )
    square = call(total_kernel, f32_of(8, seq), info, square, swap(square, 1))
    square_far = swap(square, 2)
    attn, lse = call(
        attend_kernel, (low_of(seq, LANES), f32_of(seq, LANES)), info, after(q_low, square), kv_low
    )

    given, kept, normed = call(
        output_kernel, (f32_of(*pair), f32_of(*pair), low_of(seq, XW)),
        info, square, square_far, ssm_y, gate_z, gain, after(attn, u_y), ssm_out, attn_out,
    )
    u_x = swap_far(after(u_y, given), (1, 1))
    u_y_core = swap(after(u_y, given), 1)
    chip, sent = call(add_kernel, (f32_of(*pair), low_of(*pair)), info, kept, swap(given, 1))
    u_core, g_core = swap(after(u_core, sent), 1), swap(after(g_out, sent), 1)
    g_far_core = swap(after(g_far, sent), 1)
    residual, h2, mixed_sum = call(
        second_norm_kernel, (f32_of(*pair), low_of(*pair), f32_of(1, D)),
        info, chip, swap(sent, 2), hidden_in, h_far, gain_two, keep,
        scratch=(pltpu.VMEM(pair, LOW),),
    )
    u_x_core = swap(u_x, 1)

    given, kept, hid, ggu, h2_cat, gmlp = call(
        mlp_kernel,
        (
            f32_of(*pair), f32_of(*pair), low_of(seq, FF // 4), low_of(seq, FF // 2),
            low_of(seq, D), low_of(seq, D),
        ),
        info, h2, swap(h2, 1), u_own, u_core, u_y, u_x, u_y_core, u_x_core,
        g_own, g_core, g_far, g_far_core, down_proj,
        scratch=(pltpu.VMEM((D, FF // 2), LOW),),
    )
    order = ((1, 2), (2, 1), (4, 4))
    moved = swap(given, 1)
    half = LANES // 2
    blocks = (D + FF // 4) // LANES
    up_given, up_kept = call(
        functools.partial(grad_mlp_kernel, order[0]),
        (low_of(blocks, half, D), f32_of(blocks, half, D)), info, h2_cat, ggu, hid, gmlp,
    )
    s_up = Running(sum_steps(info, up_given, up_kept, order, D // LANES))
    kept = after(kept, up_given)
    chip, sent = call(add_kernel, (f32_of(*pair), low_of(*pair)), info, kept, moved)
    prepared = call(
        scan_prepare_kernel,
        (
            f32_of(seq // SPAN * HEADS_AT, SPAN, SPAN), f32_of(seq // SPAN * HEADS_AT, SPAN, SPAN),
            f32_of(seq, XW + 2 * NS), f32_of(seq, XW + 2 * NS), f32_of(seq, XW), f32_of(seq, XW),
            f32_of(seq, XW), f32_of(seq, LANES), f32_of(seq, LANES),
        ),
        info, after(conv_pre, sent), soft, rate, states,
    )
    gres, gmix, g_norm_two = call(
        norm_back_pair_kernel, (f32_of(*pair), low_of(*pair), f32_of(1, D)),
        info, after(chip, prepared), swap(sent, 2), residual, gain_two, g_own, g_far,
        scratch=(pltpu.VMEM(pair, LOW),),
    )

    moved = swap(gmix, 1)
    mlp_given, mlp_kept = call(
        down_kernel, (f32_of(*pair), f32_of(*pair)), info, after(hid, gmix), down_proj
    )
    mlp_mine, mlp_given = call(
        add_split_kernel, (f32_of(rows, D),) * 2, info, mlp_kept, swap(mlp_given, 1)
    )
    gmix_all, gnormed, gattn, uv = call(
        output_back_kernel,
        (low_of(seq, D), f32_of(seq, XW), low_of(seq, LANES), f32_of(8, seq)),
        info, gmix, moved, ssm_y, gate_z, gain, ssm_out, attn_out,
    )
    uv = call(total_kernel, f32_of(8, seq), info, uv, swap(uv, 1))
    uv_far = swap(uv, 2)
    gq, gkv_part = call(
        attend_back_kernel, (low_of(seq, LANES), f32_of(seq, LANES)),
        info, q_low, kv_low, lse, after(gattn, uv), cosines, sines, turn,
        scratch=(pltpu.VMEM((seq, LANES), F32),),
    )
    gzz, gy, g_gain = call(
        gate_back_kernel, (low_of(seq, XW), f32_of(seq, XW), f32_of(1, XW)),
        info, square, square_far, uv, uv_far, after(gnormed, gkv_part), ssm_y, gate_z, gain,
    )
    blocks = (XW + LANES) // LANES
    mid_given, mid_kept = call(
        functools.partial(grad_mid_kernel, order[0]),
        (low_of(blocks, half, D), f32_of(blocks, half, D)),
        info, normed, attn, after(gmix_all, gkv_part),
    )
    s_mid = Running(sum_steps(info, mid_given, mid_kept, order, None))

    gx_low, gbc_given, gbc_kept, gdr, gsoft, taps_x, g_skip, g_heads = call(
        scan_back_kernel,
        (
            low_of(seq, XW), f32_of(seq, NS), f32_of(seq, NS), low_of(seq, LANES),
            low_of(seq, LANES), f32_of(8, XW), f32_of(1, XW), f32_of(8, LANES),
        ),
        info, xbc, soft, rate, skip, states, taps, after(gy, (s_up.step(gy), mid_given)),
        *prepared,
        scratch=(
            pltpu.VMEM((seq, XW + 2 * NS), F32),
            pltpu.VMEM((seq, LANES), F32), pltpu.VMEM((seq, LANES), F32),
            pltpu.VMEM((seq + 8, LANES), F32), pltpu.VMEM((seq + 8, LANES), F32),
            pltpu.VMEM((seq + 8, LANES), jnp.int32),
        ),
    )
    gkv_part = after(gkv_part, gbc_given)
    moved = swap(gbc_given, 1)
    gkv = call(
        keys_back_kernel, low_of(seq, LANES),
        info, gkv_part, swap(gkv_part, 1), cosines, sines, turn,
    )
    gbc_low, taps_bc = call(
        shared_back_kernel, (low_of(seq, NS), f32_of(8, LANES)),
        info, after(gbc_kept, gkv), moved, xbc, prepared[3], taps,
        scratch=(
            pltpu.VMEM((seq + 8, LANES), F32), pltpu.VMEM((seq + 8, LANES), F32),
            pltpu.VMEM((seq + 8, LANES), jnp.int32),
        ),
    )

    blocks = (2 * XW + 3 * LANES) // LANES
    late_given, late_kept = call(
        functools.partial(late_kernel, order[0]),
        (low_of(blocks, half, D), f32_of(blocks, half, D)),
        info, gzz, gq, gkv, gx_low, gbc_low, gsoft, h_low,
        scratch=(pltpu.VMEM((seq, LANES), LOW),),
    )
    s_late = Running(sum_steps(info, late_given, late_kept, order, 0))

    given, kept = call(
        inputs_back_kernel, (f32_of(*pair), f32_of(*pair)),
        info, after(gx_low, (s_up.step(gbc_low), s_mid.step(gbc_low), late_given)), gzz, gq, gkv, gbc_low, gdr, w_full, z_full,
        scratch=(pltpu.VMEM((seq, W_FIRST + XW), LOW),),
    )
    moved = swap(given, 1)
    kept = after(kept, late_given)
    mine, given = call(add_split_kernel, (f32_of(rows, D),) * 2, info, kept, moved)
    moved = swap(given, 2)

    token = given

    def steps(*sums):
        nonlocal token
        for one in sums:
            token = one.step(token)

    steps(s_up, s_late, s_up)
    grad_input, g_norm_one = call(
        first_norm_back_kernel, (f32_of(rows, D), f32_of(1, D)),
        info, mine, after(moved, token), hidden_in, gain_one, gres,
    )
    mlp_moved = swap(after(mlp_given, g_norm_one), 2)
    token = g_norm_one
    steps(s_mid)
    output, sums = call(
        result_kernel, (low_of(rows, D), f32_of(8, D)),
        info, mlp_mine, after(mlp_moved, token), residual, keep,
    )
    small = call(
        small_kernel, f32_of(SMALL_ROWS, LANES),
        info, g_norm_one, g_norm_two, taps_x, taps_bc, g_gain, g_skip, g_heads, sums,
        mixed_sum, keep,
    )
    s_small = Running(small_steps(info, small))
    steps(s_late, s_mid, s_up, s_small, s_mid, s_small, s_late, s_up, s_late, s_mid, s_small, s_late, s_up, s_mid, s_small, s_late, s_small, s_late)
    small = s_small.result
    grad_up, grad_down = call(
        functools.partial(finish_mlp_kernel, order[0]),
        (f32_of(*gate_up.shape), f32_of(*down_proj.shape)), info, *s_up.result,
    )
    grad_ssm, grad_attn = call(
        functools.partial(finish_mid_kernel, order[0]),
        (f32_of(*ssm_out.shape), f32_of(*attn_out.shape)), info, *s_mid.result,
    )
    grad_in, grad_qkv = call(
        functools.partial(finish_in_kernel, order[0]),
        (f32_of(in_proj.shape[1], depth), f32_of(*qkv_proj.shape)), info, *s_late.result,
        scratch=(pltpu.VMEM((4, LANES, depth), F32),) * 3,
    )
    one, conv, bias, dt, rate, skip, gain, two, stats = call(
        unpack_kernel,
        (
            f32_of(1, D), f32_of(KC, CONV_CH), f32_of(1, CONV_CH), f32_of(1, NH), f32_of(1, NH),
            f32_of(1, NH), f32_of(1, DS), f32_of(1, D), f32_of(1, 3),
        ),
        info, small,
    )
    return (
        output, grad_input, one[0], grad_in.T, conv.T, bias[0], dt[0], rate[0], skip[0], gain[0],
        grad_qkv, grad_ssm, grad_attn, two[0], grad_up, grad_down, stats[0],
    )


def on_any(*args):
    sizes = (lax.axis_size("replica"), lax.axis_size("shard"), args[0].shape[0])
    return (by_heads if sizes == (8, 4, TB) else on_device)(*args)


def solution(mesh):
    return jax.shard_map(
        on_any,
        mesh=mesh,
        in_specs=(
            P(("replica", "shard"), None),
            P(("replica", "shard"), None),
            P("replica", None),
            P(("replica", "shard")),
            P(),
            P("shard", None),
            P(),
            P(),
            P(),
            P(),
            P(),
            P(),
            P("shard", None),
            P("shard", None),
            P("shard", None),
            P(),
            P("shard", None),
            P("shard", None),
        ),
        out_specs=(
            P(("replica", "shard"), None),
            P(("replica", "shard"), None),
            P(),
            P("shard", None),
            P(),
            P(),
            P(),
            P(),
            P(),
            P(),
            P("shard", None),
            P("shard", None),
            P("shard", None),
            P(),
            P("shard", None),
            P("shard", None),
            P(),
        ),
        check_vma=False,
    )
```

```python
import functools
import math

import jax
import jax.numpy as jnp
from jax import lax
from jax.experimental import pallas as pl
from jax.experimental.pallas import tpu as pltpu
from jax.sharding import PartitionSpec as P

D = 1024
NH = 24
HP = 64
NS = 128
KC = 4
QH = 8
KVH = 2
HD = 64
FF = 2048
SPAN = 128
KBLK = 512
DS = 1536
QW = 512
KW = 128
CONV_CH = 1792


EPS = 1e-05
ROPE_BASE = 100000000000.0
NEG = -1e30
HIGH = lax.Precision.HIGHEST


def from_behind(block, axis, distance):
    devices = range(lax.axis_size(axis))
    route = [(i - distance, i) for i in devices if i - distance in devices]
    return lax.ppermute(block, axis, route)


def carried_in(part, axis, combine, identity):
    place = lax.axis_index(axis)
    gathered = jax.tree.map(lambda a: lax.all_gather(a, axis), part)
    state = jax.tree.map(lambda a, e: jnp.zeros_like(a) + jnp.asarray(e, a.dtype), part, identity)

    def one(step, state):
        return combine(
            state, jax.tree.map(lambda a: lax.dynamic_index_in_dim(a, step, 0, False), gathered)
        )

    return lax.fori_loop(0, place, one, state)


def entering(value, axis, combine, identity):
    size, mine = (lax.axis_size(axis), lax.axis_index(axis))
    everything = jax.tree.map(
        lambda part, kind: lax.all_gather(part.astype(kind), axis),
        value,
        jax.tree.map(lambda a: jnp.bfloat16 if a.dtype == jnp.float32 else a.dtype, value),
    )
    start = jax.tree.map(
        lambda part, zero: jnp.broadcast_to(jnp.asarray(zero, part.dtype), part.shape),
        value,
        identity,
    )

    def step(k, before):
        at = size - 1 - k
        reached = at > mine
        new = combine(
            before, jax.tree.map(lambda part, own: part[at].astype(own.dtype), everything, value)
        )
        return jax.tree.map(lambda a, b: jnp.where(reached, a, b), new, before)

    return lax.fori_loop(0, size, step, start)


def rms_scale(tensor):
    return lax.rsqrt(jnp.mean(tensor * tensor, axis=-1, keepdims=True) + EPS)


def rope_tables(positions):
    freqs = ROPE_BASE ** (-(jnp.arange(HD // 2).astype(jnp.float32) * 2.0) / HD)
    angles = positions.astype(jnp.float32)[:, None] * freqs[None, :]
    return (jnp.cos(angles), jnp.sin(angles))


def rotate(tensor, heads, cosines, sines):
    shaped = tensor.reshape(tensor.shape[0], heads, HD)
    first_half = shaped[:, :, : HD // 2]
    second_half = shaped[:, :, HD // 2 :]
    cos_b = cosines[:, None, :]
    sin_b = sines[:, None, :]
    turned = jnp.concatenate(
        [first_half * cos_b - second_half * sin_b, second_half * cos_b + first_half * sin_b],
        axis=-1,
    )
    return turned.reshape(tensor.shape[0], heads * HD)


def segment_of(positions, starts_row):
    return jnp.sum((starts_row[None, :] <= positions[:, None]).astype(jnp.int32), axis=1) - 1


def norm_back(grad_out, tensor, scale_rows, gain):
    scaled = grad_out * gain
    grad_in = scale_rows * scaled - tensor * scale_rows**3 * jnp.mean(
        scaled * tensor, axis=-1, keepdims=True
    )
    return (grad_in, jnp.sum(grad_out * tensor * scale_rows, axis=0))


def dsilu(tensor):
    sig_part = jax.nn.sigmoid(tensor)
    return sig_part * (1.0 + tensor * (1.0 - sig_part))


def combine_states(earlier, later):
    return (earlier[0] * later[1][:, None, None] + later[0], earlier[1] * later[1])


def ssd_spans(state, ssm_x, ssm_b, ssm_c, step_size, log_decay, skip_scale, seg_ids, before):
    count = ssm_x.shape[0] // SPAN
    prev_seg = jnp.concatenate([before.reshape(1), seg_ids[:-1]])

    def by_span(tensor):
        return tensor.reshape((count, SPAN) + tensor.shape[1:])

    def span_step(state_acc, pieces):
        x_c, b_c, c_c, dt_c, la_c, s_c, p_c = pieces
        cum_decay = jnp.cumsum(la_c, axis=0)
        order = jnp.arange(SPAN)
        same_mask = (s_c[:, None] == s_c[None, :]) & (order[:, None] >= order[None, :])
        differ = cum_decay.T[:, :, None] - cum_decay.T[:, None, :]
        decay_mat = jnp.exp(jnp.where(same_mask[None], differ, NEG))
        inner = jnp.dot(c_c, b_c.T, precision=HIGH)
        mixing = decay_mat * inner[None] * dt_c.T[:, None, :]
        y_inner = jnp.einsum("hpq,qhd->phd", mixing, x_c, precision=HIGH)
        alive = (s_c == p_c[0]).astype(jnp.float32)
        carried = jnp.exp(cum_decay) * alive[:, None]
        y_state = jnp.einsum("hdn,pn->phd", state_acc, c_c, precision=HIGH) * carried[:, :, None]
        y_span = y_inner + y_state + skip_scale[None, :, None] * x_c
        tail_w = (
            jnp.exp(cum_decay[-1][None, :] - cum_decay)
            * (s_c == s_c[-1]).astype(jnp.float32)[:, None]
            * dt_c
        )
        new_state = state_acc * carried[-1][:, None, None] + jnp.einsum(
            "qh,qhd,qn->hdn", tail_w, x_c, b_c, precision=HIGH
        )
        return (new_state, y_span)

    final_state, ys = lax.scan(
        span_step,
        state,
        (
            by_span(ssm_x),
            by_span(ssm_b),
            by_span(ssm_c),
            by_span(step_size),
            by_span(log_decay),
            by_span(seg_ids),
            by_span(prev_seg),
        ),
    )
    return (ys.reshape(ssm_x.shape), final_state)


def on_device(
    hidden_in,
    cotangent,
    doc_starts,
    valid_mask,
    norm_one,
    in_proj,
    conv_weight,
    conv_bias,
    dt_bias,
    a_log,
    skip_scale,
    gated_gain,
    qkv_proj,
    ssm_out,
    attn_out,
    norm_two,
    gate_up,
    down_proj,
):
    tok_rows = hidden_in.shape[0]
    shard_count = lax.axis_size("shard")
    offset = lax.axis_index("shard") * tok_rows
    seq_len = tok_rows * shard_count
    score_scale = 1.0 / math.sqrt(HD)
    q_per_kv = QH // KVH
    starts_row = doc_starts[0]
    positions = offset + jnp.arange(tok_rows, dtype=jnp.int32)
    seg_ids = segment_of(positions, starts_row)
    before = segment_of(positions[:1] - 1, starts_row)[0]
    first_start = jnp.max(jnp.where(starts_row <= positions[0], starts_row, 0))
    last_pos = positions[-1]
    full_weights = (
        lax.all_gather(in_proj, "shard", axis=0, tiled=True),
        lax.all_gather(qkv_proj, "shard", axis=0, tiled=True),
        lax.all_gather(ssm_out, "shard", axis=0, tiled=True),
        lax.all_gather(attn_out, "shard", axis=0, tiled=True),
        lax.all_gather(gate_up, "shard", axis=0, tiled=True),
        lax.all_gather(down_proj, "shard", axis=0, tiled=True),
    )
    f_in, f_attn, f_mo, f_ao, f_gu, f_down = full_weights
    x_full = hidden_in.astype(jnp.float32)
    r_one = rms_scale(x_full)
    h_low = (x_full * r_one * norm_one).astype(jnp.bfloat16)
    proj_out = jnp.dot(h_low, f_in, preferred_element_type=jnp.float32)
    gate_z = proj_out[:, :DS]
    xbc = proj_out[:, DS : DS + CONV_CH]
    dt_raw = proj_out[:, DS + CONV_CH :]
    edge_rows = from_behind(xbc[tok_rows - (KC - 1) :], "shard", 1)
    padded = jnp.concatenate([edge_rows, xbc], axis=0)
    pad_pos = positions[0] - (KC - 1) + jnp.arange(tok_rows + KC - 1, dtype=jnp.int32)
    pad_seg = segment_of(pad_pos, starts_row)
    tap_masks = [
        (pad_seg[tap_index : tap_index + tok_rows] == seg_ids).astype(jnp.float32)[:, None]
        for tap_index in range(KC)
    ]
    conv_pre = jnp.zeros((tok_rows, CONV_CH), jnp.float32) + conv_bias[None, :]
    for tap_index in range(KC):
        conv_pre = (
            conv_pre
            + conv_weight[:, tap_index][None, :]
            * padded[tap_index : tap_index + tok_rows]
            * tap_masks[tap_index]
        )
    conv_act = jax.nn.silu(conv_pre)
    ssm_x = conv_act[:, :DS].reshape(tok_rows, NH, HP)
    ssm_b = conv_act[:, DS : DS + NS]
    ssm_c = conv_act[:, DS + NS :]
    soft_in = dt_raw + dt_bias
    step_size = jax.nn.softplus(soft_in)
    decay_rate = jnp.exp(a_log)
    log_decay = -step_size * decay_rate
    empty_state = jnp.zeros((NH, HP, NS), jnp.float32)

    def carry_factor(log_vals):
        return (
            jnp.exp(jnp.cumsum(log_vals, axis=0)) * (seg_ids == before).astype(jnp.float32)[:, None]
        )

    def carry_term(state_in, c_vals, factor):
        return jnp.einsum("hdn,pn->phd", state_in, c_vals, precision=HIGH) * factor[:, :, None]

    ssm_zero, local_state = ssd_spans(
        empty_state, ssm_x, ssm_b, ssm_c, step_size, log_decay, skip_scale, seg_ids, before
    )
    factor = carry_factor(log_decay)
    dev_decay = factor[-1]
    state_in, unused_decay = carried_in(
        (local_state, dev_decay),
        "shard",
        combine_states,
        (jnp.zeros_like(local_state), jnp.ones_like(dev_decay)),
    )
    ssm_y = (ssm_zero + carry_term(state_in, ssm_c, factor)).reshape(tok_rows, DS)
    silu_z = jax.nn.silu(gate_z)
    gated = ssm_y * silu_z
    r_gate = rms_scale(gated)
    normed_low = (gated * r_gate * gated_gain).astype(jnp.bfloat16)
    qkv = jnp.dot(h_low, f_attn, preferred_element_type=jnp.float32)
    cosines, sines = rope_tables(positions)
    q_low = (
        rotate(qkv[:, :QW], QH, cosines, sines)
        .astype(jnp.bfloat16)
        .reshape(tok_rows, KVH, q_per_kv, HD)
    )
    k_low = rotate(qkv[:, QW : QW + KW], KVH, cosines, sines).astype(jnp.bfloat16)
    v_low = qkv[:, QW + KW :].astype(jnp.bfloat16)
    key_all, value_all = (
        lax.all_gather(k_low, "shard", axis=0, tiled=True),
        lax.all_gather(v_low, "shard", axis=0, tiled=True),
    )
    key_all = key_all.reshape(seq_len, KVH, HD)
    value_all = value_all.reshape(seq_len, KVH, HD)
    key_pos = jnp.arange(seq_len, dtype=jnp.int32)
    key_seg = segment_of(key_pos, starts_row)
    block_count = seq_len // KBLK
    row_shape = (KVH, q_per_kv, tok_rows)

    def needed(blk_index):
        low_edge = blk_index * KBLK
        return (low_edge <= last_pos) & (low_edge + KBLK > first_start)

    def block_keys(blk_index):
        return (
            lax.dynamic_slice_in_dim(key_all, blk_index * KBLK, KBLK, 0),
            lax.dynamic_slice_in_dim(value_all, blk_index * KBLK, KBLK, 0),
        )

    def block_scores(blk_index, k_blk):
        pos_blk = lax.dynamic_slice_in_dim(key_pos, blk_index * KBLK, KBLK, 0)
        seg_blk = lax.dynamic_slice_in_dim(key_seg, blk_index * KBLK, KBLK, 0)
        raw_scores = (
            jnp.einsum("tgqd,kgd->gqtk", q_low, k_blk, preferred_element_type=jnp.float32)
            * score_scale
        )
        key_mask = (pos_blk[None, :] <= positions[:, None]) & (seg_blk[None, :] == seg_ids[:, None])
        return (raw_scores, key_mask[None, None])

    def unchanged(passed):
        return passed

    def lse_step(blk_index, state_acc):

        def lse_do_block(state_acc):
            row_top, row_total = state_acc
            k_blk, v_blk = block_keys(blk_index)
            raw_scores, key_mask = block_scores(blk_index, k_blk)
            new_top = jnp.maximum(row_top, jnp.max(jnp.where(key_mask, raw_scores, NEG), axis=-1))
            row_total = row_total * jnp.exp(row_top - new_top) + jnp.sum(
                jnp.where(key_mask, jnp.exp(raw_scores - new_top[..., None]), 0.0), axis=-1
            )
            return (new_top, row_total)

        return lax.cond(needed(blk_index), lse_do_block, unchanged, state_acc)

    row_top, row_total = lax.fori_loop(
        0,
        block_count,
        lse_step,
        (jnp.full(row_shape, NEG, jnp.float32), jnp.zeros(row_shape, jnp.float32)),
    )
    log_total = row_top + jnp.log(row_total)

    def probs_of(blk_index, k_blk):
        raw_scores, key_mask = block_scores(blk_index, k_blk)
        return jnp.where(key_mask, jnp.exp(raw_scores - log_total[..., None]), 0.0)

    def out_step(blk_index, acc_out):

        def out_do_block(acc_out):
            k_blk, v_blk = block_keys(blk_index)
            prob_blk = probs_of(blk_index, k_blk).astype(jnp.bfloat16)
            return acc_out + jnp.einsum(
                "gqtk,kgd->tgqd", prob_blk, v_blk, preferred_element_type=jnp.float32
            )

        return lax.cond(needed(blk_index), out_do_block, unchanged, acc_out)

    attended = lax.fori_loop(
        0, block_count, out_step, jnp.zeros((tok_rows, KVH, q_per_kv, HD), jnp.float32)
    )
    attn_low = attended.reshape(tok_rows, QW).astype(jnp.bfloat16)
    mixed = jnp.dot(normed_low, f_mo, preferred_element_type=jnp.float32) + jnp.dot(
        attn_low, f_ao, preferred_element_type=jnp.float32
    )
    residual = x_full + mixed
    r_two = rms_scale(residual)
    h2_low = (residual * r_two * norm_two).astype(jnp.bfloat16)
    gate_vals = jnp.dot(h2_low, f_gu, preferred_element_type=jnp.float32)
    gate_part = gate_vals[:, :FF]
    up_part = gate_vals[:, FF:]
    hid_low = (jax.nn.silu(gate_part) * up_part).astype(jnp.bfloat16)
    mlp_out = jnp.dot(hid_low, f_down, preferred_element_type=jnp.float32)
    out_full = residual + mlp_out
    keep_rows = valid_mask.astype(jnp.float32)
    stat_local = jnp.stack(
        [
            jnp.sum(keep_rows * jnp.sum(out_full * out_full, axis=1)),
            jnp.sum(keep_rows * jnp.sum(mixed * mixed, axis=1)),
            jnp.sum(keep_rows * jnp.sum(mlp_out * mlp_out, axis=1)),
            jnp.sum(keep_rows),
        ]
    )
    back_weights = (
        lax.all_gather(in_proj, "shard", axis=0, tiled=True),
        lax.all_gather(qkv_proj, "shard", axis=0, tiled=True),
        lax.all_gather(ssm_out, "shard", axis=0, tiled=True),
        lax.all_gather(attn_out, "shard", axis=0, tiled=True),
        lax.all_gather(gate_up, "shard", axis=0, tiled=True),
        lax.all_gather(down_proj, "shard", axis=0, tiled=True),
    )
    b_in, b_attn, b_mo, b_ao, b_gu, b_down = back_weights
    grad_out = cotangent.astype(jnp.float32) * keep_rows[:, None]
    grad_mlp = grad_out.astype(jnp.bfloat16)
    g_down = jnp.dot(hid_low.T, grad_mlp, preferred_element_type=jnp.float32)
    grad_hid = jnp.dot(grad_mlp, b_down.T, preferred_element_type=jnp.float32)
    grad_gu = jnp.concatenate(
        [grad_hid * up_part * dsilu(gate_part), grad_hid * jax.nn.silu(gate_part)], axis=1
    ).astype(jnp.bfloat16)
    g_gu = jnp.dot(h2_low.T, grad_gu, preferred_element_type=jnp.float32)
    grad_h2 = jnp.dot(grad_gu, b_gu.T, preferred_element_type=jnp.float32)
    grad_res_n, g_norm_two = norm_back(grad_h2, residual, r_two, norm_two)
    grad_res = grad_out + grad_res_n
    grad_mix = grad_res.astype(jnp.bfloat16)
    g_mo = jnp.dot(normed_low.T, grad_mix, preferred_element_type=jnp.float32)
    g_ao = jnp.dot(attn_low.T, grad_mix, preferred_element_type=jnp.float32)
    grad_normed = jnp.dot(grad_mix, b_mo.T, preferred_element_type=jnp.float32)
    grad_attn = (
        jnp.dot(grad_mix, b_ao.T, preferred_element_type=jnp.float32)
        .astype(jnp.bfloat16)
        .reshape(tok_rows, KVH, q_per_kv, HD)
    )

    def delta_step(blk_index, acc_out):

        def delta_do_block(acc_out):
            k_blk, v_blk = block_keys(blk_index)
            prob_blk = probs_of(blk_index, k_blk)
            grad_prob = jnp.einsum(
                "tgqd,kgd->gqtk", grad_attn, v_blk, preferred_element_type=jnp.float32
            )
            return acc_out + jnp.sum(prob_blk * grad_prob, axis=-1)

        return lax.cond(needed(blk_index), delta_do_block, unchanged, acc_out)

    delta_row = lax.fori_loop(0, block_count, delta_step, jnp.zeros(row_shape, jnp.float32))

    def grad_step(blk_index, state_acc):

        def grad_do_block(state_acc):
            grad_query, grad_kv = state_acc
            k_blk, v_blk = block_keys(blk_index)
            prob_blk = probs_of(blk_index, k_blk)
            grad_prob = jnp.einsum(
                "tgqd,kgd->gqtk", grad_attn, v_blk, preferred_element_type=jnp.float32
            )
            grad_raw = (prob_blk * (grad_prob - delta_row[..., None]) * score_scale).astype(
                jnp.bfloat16
            )
            grad_query = grad_query + jnp.einsum(
                "gqtk,kgd->tgqd", grad_raw, k_blk, preferred_element_type=jnp.float32
            )
            grad_key = jnp.einsum(
                "gqtk,tgqd->kgd", grad_raw, q_low, preferred_element_type=jnp.float32
            )
            grad_value = jnp.einsum(
                "gqtk,tgqd->kgd",
                prob_blk.astype(jnp.bfloat16),
                grad_attn,
                preferred_element_type=jnp.float32,
            )
            kv_piece = jnp.concatenate(
                [grad_key.reshape(KBLK, KW), grad_value.reshape(KBLK, KW)], axis=1
            )
            grad_kv = lax.dynamic_update_slice_in_dim(grad_kv, kv_piece, blk_index * KBLK, 0)
            return (grad_query, grad_kv)

        return lax.cond(needed(blk_index), grad_do_block, unchanged, state_acc)

    grad_query, grad_kv = lax.fori_loop(
        0,
        block_count,
        grad_step,
        (
            jnp.zeros((tok_rows, KVH, q_per_kv, HD), jnp.float32),
            jnp.zeros((seq_len, 2 * KW), jnp.float32),
        ),
    )
    own_kv = lax.psum_scatter(grad_kv, "shard", scatter_dimension=0, tiled=True)
    neg_sines = -sines
    grad_q_raw = rotate(grad_query.reshape(tok_rows, QW), QH, cosines, neg_sines)
    grad_k_raw = rotate(own_kv[:, :KW], KVH, cosines, neg_sines)
    grad_qkv = jnp.concatenate([grad_q_raw, grad_k_raw, own_kv[:, KW:]], axis=1).astype(
        jnp.bfloat16
    )
    g_attn = jnp.dot(h_low.T, grad_qkv, preferred_element_type=jnp.float32)
    grad_h_attn = jnp.dot(grad_qkv, b_attn.T, preferred_element_type=jnp.float32)
    grad_gated, g_gated_gain = norm_back(grad_normed, gated, r_gate, gated_gain)
    grad_y = (grad_gated * silu_z).reshape(tok_rows, NH, HP)
    grad_z = grad_gated * ssm_y * dsilu(gate_z)

    def mamba_out(state_start, x_vals, b_vals, c_vals, dt_vals, la_vals, skip_vals):
        y_zero, state_local = ssd_spans(
            empty_state, x_vals, b_vals, c_vals, dt_vals, la_vals, skip_vals, seg_ids, before
        )
        fac_vals = carry_factor(la_vals)
        return (
            y_zero + carry_term(state_start, c_vals, fac_vals),
            state_local + state_start * fac_vals[-1][:, None, None],
        )

    unused_out, pull_back = jax.vjp(
        mamba_out, state_in, ssm_x, ssm_b, ssm_c, step_size, log_decay, skip_scale
    )
    first_pull = pull_back((grad_y, jnp.zeros_like(state_in)))
    later_state, unused_later = entering(
        (first_pull[0], dev_decay),
        "shard",
        combine_states,
        (jnp.zeros_like(state_in), jnp.ones_like(dev_decay)),
    )
    second = pull_back((jnp.zeros_like(grad_y), later_state))
    grad_x = first_pull[1] + second[1]
    grad_b = first_pull[2] + second[2]
    grad_c = first_pull[3] + second[3]
    grad_dt = first_pull[4] + second[4]
    grad_la = first_pull[5] + second[5]
    g_skip = first_pull[6] + second[6]
    g_a_log = jnp.sum(-grad_la * step_size * decay_rate, axis=0)
    grad_soft = (grad_dt - grad_la * decay_rate) * jax.nn.sigmoid(soft_in)
    g_dt_bias = jnp.sum(grad_soft, axis=0)
    grad_act = jnp.concatenate([grad_x.reshape(tok_rows, DS), grad_b, grad_c], axis=1)
    grad_conv = grad_act * dsilu(conv_pre)
    g_conv_bias = jnp.sum(grad_conv, axis=0)
    grad_padded = jnp.zeros((tok_rows + KC - 1, CONV_CH), jnp.float32)
    weight_cols = []
    for tap_index in range(KC):
        term_vals = grad_conv * tap_masks[tap_index]
        grad_padded = grad_padded + jnp.pad(
            term_vals * conv_weight[:, tap_index][None, :],
            ((tap_index, KC - 1 - tap_index), (0, 0)),
        )
        weight_cols.append(jnp.sum(term_vals * padded[tap_index : tap_index + tok_rows], axis=0))
    g_conv_weight = jnp.stack(weight_cols, axis=1)
    back_edge = from_behind(grad_padded[: KC - 1], "shard", -1)
    grad_xbc = grad_padded[KC - 1 :] + jnp.concatenate(
        [jnp.zeros((tok_rows - (KC - 1), CONV_CH), jnp.float32), back_edge], axis=0
    )
    grad_proj = jnp.concatenate([grad_z, grad_xbc, grad_soft], axis=1).astype(jnp.bfloat16)
    g_in = jnp.dot(h_low.T, grad_proj, preferred_element_type=jnp.float32)
    grad_h = jnp.dot(grad_proj, b_in.T, preferred_element_type=jnp.float32) + grad_h_attn
    grad_x_n, g_norm_one = norm_back(grad_h, x_full, r_one, norm_one)
    grad_input = grad_res + grad_x_n
    owned_grads = (
        lax.psum_scatter(g_in, "shard", scatter_dimension=0, tiled=True),
        lax.psum_scatter(g_attn, "shard", scatter_dimension=0, tiled=True),
        lax.psum_scatter(g_mo, "shard", scatter_dimension=0, tiled=True),
        lax.psum_scatter(g_ao, "shard", scatter_dimension=0, tiled=True),
        lax.psum_scatter(g_gu, "shard", scatter_dimension=0, tiled=True),
        lax.psum_scatter(g_down, "shard", scatter_dimension=0, tiled=True),
    )
    summed = lax.psum(
        (
            owned_grads[0],
            owned_grads[1],
            owned_grads[2],
            owned_grads[3],
            owned_grads[4],
            owned_grads[5],
        ),
        "replica",
    )
    small_sums = lax.psum(
        (
            g_norm_one,
            g_conv_weight,
            g_conv_bias,
            g_dt_bias,
            g_a_log,
            g_skip,
            g_gated_gain,
            g_norm_two,
            stat_local,
        ),
        ("replica", "shard"),
    )
    stat_sums = small_sums[8]
    rms_stats = jnp.sqrt(stat_sums[:3] / (stat_sums[3] * D))
    return (
        out_full.astype(jnp.bfloat16),
        grad_input,
        small_sums[0],
        summed[0],
        small_sums[1],
        small_sums[2],
        small_sums[3],
        small_sums[4],
        small_sums[5],
        small_sums[6],
        summed[1],
        summed[2],
        summed[3],
        small_sums[7],
        summed[4],
        summed[5],
        rms_stats,
    )


HEADS_AT = 6
XW = HEADS_AT * HP
LANES = 128
TB = 128
VMEM_BYTES = 20 * 1024 * 1024
AT_Y, AT_CORE, AT_BIT, AT_STARTS = 0, 1, {1: 2, 2: 3, 4: 4}, 5
Q_AT = XW
KV_AT = Q_AT + QW // 4
BC_AT = KV_AT + LANES
DT_AT = BC_AT + 2 * NS
W_FIRST = DT_AT + LANES
LOW = jnp.bfloat16
F32 = jnp.float32


def swap(block, bits):
    return lax.ppermute(block, "shard", [(i, i ^ bits) for i in range(lax.axis_size("shard"))])


def swap_far(block, bits):
    replicas, shards = lax.axis_size("replica"), lax.axis_size("shard")
    route = [
        (r * shards + s, (r ^ bits[s % 2]) * shards + s)
        for r in range(replicas)
        for s in range(shards)
    ]
    return lax.ppermute(block, ("replica", "shard"), route)


def after(value, other):
    return lax.optimization_barrier((value, other))[0]


def dot32(a, b):
    return jnp.dot(a, b, preferred_element_type=F32)


def dot_t(a, b):
    return lax.dot_general(a, b, (((1,), (1,)), ((), ())), preferred_element_type=F32)


def t_dot(a, b):
    return lax.dot_general(a, b, (((0,), (0,)), ((), ())), preferred_element_type=F32)


def rough(a, b, dims=((1,), (0,))):
    return lax.dot_general(
        a.astype(LOW), b.astype(LOW), (dims, ((), ())), preferred_element_type=F32
    )


def fair(a, b, dims=((1,), (0,))):
    a_high, b_high = a.astype(LOW), b.astype(LOW)
    a_low = (a - a_high.astype(F32)).astype(LOW)
    b_low = (b - b_high.astype(F32)).astype(LOW)

    def dot(x, y):
        return lax.dot_general(x, y, (dims, ((), ())), preferred_element_type=F32)

    return dot(a_high, b_high) + (dot(a_high, b_low) + dot(a_low, b_high))


def picked(a, b, dims=((1,), (0,)), terms=2):
    value, total = (b, 0.0) if a.dtype == LOW else (a, 0.0)
    for _ in range(terms):
        low = value.astype(LOW)
        pair = (a, low) if a.dtype == LOW else (low, b)
        total = total + lax.dot_general(*pair, (dims, ((), ())), preferred_element_type=F32)
        value = value - low.astype(F32)
    return total


def iota(shape, axis):
    return lax.broadcasted_iota(jnp.int32, shape, axis)


def count_starts(info, where):
    total = (info[AT_STARTS] <= where).astype(jnp.int32)
    for k in range(AT_STARTS + 1, info.shape[0]):
        total = total + (info[k] <= where).astype(jnp.int32)
    return total


def part(index, size):
    return pl.ds(pl.multiple_of(index * size, size), size)


def part_at(start, index, step, size):
    return pl.ds(pl.multiple_of(start + index * step, LANES), size)


def peers(info):
    y, c = info[AT_Y], info[AT_CORE]
    return (2 * y + c, 2 * y + 1 - c, 2 * (1 - y) + c, 2 * (1 - y) + 1 - c)


def bit_of(info, bits):
    return jnp.where(info[AT_CORE] == 0, info[AT_BIT[bits[0]]], info[AT_BIT[bits[1]]])


def f32_of(*shape):
    return jax.ShapeDtypeStruct(shape, F32)


def low_of(*shape):
    return jax.ShapeDtypeStruct(shape, LOW)


def call(kernel, outs, info, *operands, scratch=()):
    whole = pl.BlockSpec(memory_space=pltpu.VMEM)
    return pl.pallas_call(
        kernel,
        out_shape=outs,
        in_specs=[pl.BlockSpec(memory_space=pltpu.SMEM)] + [whole] * len(operands),
        out_specs=jax.tree.map(lambda _: whole, outs),
        scratch_shapes=scratch,
        compiler_params=pltpu.CompilerParams(vmem_limit_bytes=VMEM_BYTES),
    )(info, *operands)


def pack_in_kernel(info, w_in, w_qkv, own, core, far, z_own, z_core, z_far):
    y, places = info[AT_Y], peers(info)

    def shared(dst, chip):
        k, v = w_qkv[:, QW : QW + KW], w_qkv[:, QW + KW :]
        first = jnp.concatenate([k[:, :HD], v[:, :HD]], axis=1)
        second = jnp.concatenate([k[:, HD:], v[:, HD:]], axis=1)
        dst[KV_AT:BC_AT, :] = jnp.where(chip == 0, first, second).T
        dst[BC_AT:DT_AT, :] = w_in[2 * DS : 2 * DS + 2 * NS, :]
        dst[DT_AT:W_FIRST, :] = jnp.zeros((LANES, dst.shape[1]), LOW)
        dst[DT_AT : DT_AT + NH, :] = w_in[DS + CONV_CH :, :]

    for place, dst, at in zip(places, (own, core, far, far), (0, 0, W_FIRST, 0)):
        dst[at : at + XW, :] = w_in[part_at(DS, place, XW, XW), :]
        dst[at + XW : at + KV_AT, :] = w_qkv[:, part(place, QW // 4)].T
    for place, dst, at in zip(places, (z_own, z_core, z_far, z_far), (0, 0, XW, 0)):
        dst[at : at + XW, :] = w_in[part_at(0, place, XW, XW), :]
    shared(own, y)
    shared(core, y)
    shared(far, 1 - y)


def prepare_kernel(
    info, conv_weight, conv_bias, dt_bias, a_log, skip, gain, norm_one, norm_two, mask, cotangent,
    taps, bias, bias_own, rate, skip_wide, gain_own, gain_one, gain_two, keep, grad, turn, wide,
):
    place = peers(info)[0]
    for src, dst in ((conv_weight, taps), (conv_bias, bias)):
        dst[:, :XW] = src[:, part(place, XW)]
        dst[:, XW:] = src[:, DS:]
    gain_own[...] = gain[:, part(place, XW)]
    gain_one[...] = norm_one[...]
    gain_two[...] = norm_two[...]
    pick = own_heads_pick(info)
    wide[...] = jnp.zeros_like(wide)
    for k, src in enumerate((dt_bias, a_log, skip)):
        wide[k : k + 1, :NH] = src[...]
    own = picked(wide[...], pick, terms=3)
    bias_own[...] = own[0:1]
    rate[...] = jnp.exp(own[1:2])
    skip_wide[...] = picked(own, head_spread(), terms=3)[2:3]
    column = jnp.broadcast_to(mask[...].astype(F32), (LANES, LANES)).T
    keep[...] = column
    grad[...] = (cotangent[...].astype(F32) * column[:, :1]).astype(LOW)
    row, col, half = iota((LANES, LANES), 0), iota((LANES, LANES), 1), HD // 2
    down, up = (row == col + half).astype(F32), (row == col - half).astype(F32)
    turn[...] = jnp.where((col // half) % 2 == 0, -down, up).astype(LOW)


def total_kernel(info, a, b, out):
    out[...] = a[...] + b[...]


def pack_up_kernel(info, w_up, own, core, far):
    quarter, half = FF // 4, w_up.shape[0] // 2
    places = peers(info)
    for place, dst in zip(places, (own, core)):
        dst[:, :quarter] = w_up[:, part_at(0, place, quarter, quarter)]
        dst[:, quarter:] = w_up[:, part_at(FF, place, quarter, quarter)]
    mine = part(info[AT_BIT[1]], half)
    for k, place in enumerate(places[2:]):
        rows = slice(k * half, (k + 1) * half)
        far[rows, :quarter] = w_up[mine, part_at(0, place, quarter, quarter)]
        far[rows, quarter:] = w_up[mine, part_at(FF, place, quarter, quarter)]


def head_spread():
    row, col = iota((LANES, XW), 0), iota((LANES, XW), 1)
    return ((col >= row * HP) & (col < (row + 1) * HP)).astype(LOW)


def own_heads_pick(info):
    row, col = iota((LANES, LANES), 0), iota((LANES, LANES), 1)
    return ((row == col + peers(info)[0] * HEADS_AT) & (col < HEADS_AT)).astype(LOW)


def step_sizes(soft):
    real = iota(soft.shape, 1) < HEADS_AT
    return jnp.where(real, jnp.maximum(soft, 0.0) + jnp.log1p(jnp.exp(-jnp.abs(soft))), 0.0)


def span_parts(info, first, dt, la):
    shape = (SPAN, SPAN)
    row, col = iota(shape, 0), iota(shape, 1)
    seg_row = count_starts(info, row + first)
    seg_col = count_starts(info, col + first)
    seen = (seg_row == seg_col) & (row >= col)
    before = count_starts(info, first - 1)
    last = count_starts(info, first + SPAN - 1)
    total = picked((row >= col).astype(LOW), la, terms=3)
    carried = jnp.exp(total) * (seg_row == before).astype(F32)
    tail = jnp.exp(total[SPAN - 1 :] - total) * (seg_row == last).astype(F32)
    return seen, total, total.T, dt.T, carried, tail


def decay_of(seen, total, total_t, h):
    return jnp.exp(jnp.where(seen, total[:, h : h + 1] - total_t[h : h + 1, :], NEG))


def tap_masks(info, seg):
    seq = seg.shape[0] - 8
    seg[:8, :] = jnp.full((8, LANES), -1, jnp.int32)
    seg[8:, :] = count_starts(info, iota((seq, LANES), 0))
    here = seg[8:, :]
    return [
        (seg[8 - back : 8 - back + seq, :] == here).astype(F32) for back in range(KC - 1, 0, -1)
    ]


def forward_kernel(
    info, h_own, h_core, h_far, h_far_core, w_own, w_core, w_far, w_far_core,
    norm, taps, bias, dt_bias, rate, skip, cosines, sines, turn,
    h_low, w_full, xbc, conv_pre, soft, q_low, kv_low, y_out, states,
    padded, act, step, seg,
):
    seq = h_low.shape[0]
    places = peers(info)
    for place, ref in zip(places, (h_own, h_core, h_far, h_far_core)):
        x = ref[...].astype(F32)
        h_low[part(place, TB), :] = (x * rms_scale(x) * norm[...]).astype(LOW)
    depth = w_own.shape[1]
    for place, ref, at in zip(places, (w_own, w_core, w_far, w_far_core), (0, 0, W_FIRST, 0)):
        w_full[:KV_AT, part(place, depth)] = ref[at : at + KV_AT, :]
        w_full[KV_AT:, part(place, depth)] = ref[KV_AT:W_FIRST, :]
    h = h_low[...]
    xbc[:, :XW] = dot_t(h, w_full[:XW, :])
    xbc[:, XW:] = dot_t(h, w_full[BC_AT:DT_AT, :])
    rest = dot_t(h, w_full[Q_AT:BC_AT, :])
    q, kv = rest[:, :LANES], rest[:, LANES:]
    soft[...] = picked(dot_t(h, w_full[DT_AT:, :]), own_heads_pick(info), terms=3) + dt_bias[...]

    def turned(value):
        return value * cosines[...] + picked(value, turn[...]) * sines[...]

    q_low[...] = turned(q).astype(LOW)
    kv_low[...] = jnp.where(iota(kv.shape, 1) < HD, turned(kv), kv).astype(LOW)

    width = xbc.shape[1]
    padded[:8, :] = jnp.zeros((8, width), F32)
    padded[8:, :] = xbc[...]
    masks = tap_masks(info, seg)
    for block in range(0, width, LANES):
        lanes = slice(block, block + LANES)
        total = bias[:, lanes] + taps[KC - 1 : KC, lanes] * padded[8:, lanes]
        for j in range(KC - 1):
            start = 8 - (KC - 1 - j)
            total = total + taps[j : j + 1, lanes] * padded[start : start + seq, lanes] * masks[j]
        conv_pre[:, lanes] = total
        act[:, lanes] = total * jax.nn.sigmoid(total)

    step[...] = step_sizes(soft[...])
    spread = head_spread()
    state = jnp.zeros((NS, XW), F32)
    for k in range(seq // SPAN):
        rows = pl.ds(k * SPAN, SPAN)
        x = act[rows, :XW]
        b = act[rows, XW : XW + NS]
        c = act[rows, XW + NS :]
        dt = step[rows, :]
        seen, total, total_t, dt_t, carried, tail = span_parts(
            info, k * SPAN, dt, -dt * rate[...]
        )
        states[k] = state
        inner = fair(c, b, ((1,), (1,)))
        wide = picked(carried, spread)
        y = fair(c, state) * wide + x * skip[...]
        parts = []
        for h in range(HEADS_AT):
            mixing = decay_of(seen, total, total_t, h) * inner * dt_t[h : h + 1, :]
            parts.append(fair(mixing, x[:, h * HP : (h + 1) * HP]))
        y_out[rows, :] = y + jnp.concatenate(parts, axis=1)
        weighted = x * picked(tail * dt, spread)
        state = state * wide[SPAN - 1 :] + fair(b, weighted, ((0,), (0,)))


def gate_kernel(info, h_low, z_own, z_core, z_far, z_far_core, y, z_full, gate_z, square):
    depth = z_own.shape[1]
    for place, ref, at in zip(peers(info), (z_own, z_core, z_far, z_far_core), (0, 0, XW, 0)):
        z_full[:, part(place, depth)] = ref[at : at + XW, :]
    z = dot_t(h_low[...], z_full[...])
    gate_z[...] = z
    gated = y[...] * (z * jax.nn.sigmoid(z))
    square[...] = picked(jnp.ones((8, XW), LOW), gated * gated, ((1,), (1,)))


def column_of(row):
    return jnp.concatenate(
        [row[:, k : k + LANES].T[:, :1] for k in range(0, row.shape[1], LANES)], axis=0
    )


def output_kernel(
    info, sq_a, sq_b, y, gate_z, gain, attn, ssm_out, attn_out, given, kept, normed
):
    z = gate_z[...]
    scale = lax.rsqrt(column_of(sq_a[...] + sq_b[...]) / DS + EPS)
    normed[...] = (y[...] * (z * jax.nn.sigmoid(z)) * scale * gain[...]).astype(LOW)
    c = info[AT_CORE]
    for core, dst in ((1 - c, given), (c, kept)):
        for k in range(2):
            rows = part(2 * k + core, TB)
            dst[k] = dot32(normed[rows, :], ssm_out[...]) + dot32(attn[rows, :], attn_out[...])


def add_kernel(info, kept, moved, chip, low):
    total = kept[...] + moved[...]
    chip[...] = total
    low[...] = total.astype(LOW)


def add_split_kernel(info, kept, moved, mine, given):
    y = info[AT_Y]
    mine[...] = kept[y] + moved[y]
    given[...] = kept[1 - y] + moved[1 - y]


def pair_of(info, own, far, dst):
    y = info[AT_Y]
    dst[y] = own[...]
    dst[1 - y] = far[...]


def second_norm_kernel(
    info, chip, moved, h_own, h_far, norm, keep, residual, h2, mixed_sum, x_pair
):
    pair_of(info, h_own, h_far, x_pair)
    mixed = chip[...] + moved[...].astype(F32)
    total = x_pair[...].astype(F32) + mixed
    residual[...] = total
    h2[...] = (total * rms_scale(total) * norm[...]).astype(LOW)
    mine = (chip[info[AT_Y]] + moved[info[AT_Y]].astype(F32)) * keep[:, :1]
    mixed_sum[...] = jnp.sum(mine * mine, axis=0, keepdims=True)


def mlp_kernel(
    info, h2, h2_core, u_own, u_core, u_y, u_x, u_y_core, u_x_core, g_own, g_core, g_far, g_far_core, w_down,
    given, kept, hid, ggu, h2_cat, gmlp, u_full,
):
    y, quarter = info[AT_Y], FF // 4
    half = 2 * TB
    for k in range(2):
        h2_cat[k * TB : (k + 1) * TB, :] = h2[k]
        h2_cat[half + k * TB : half + (k + 1) * TB, :] = h2_core[k]
    for at, ref in ((y, g_own), (1 - y, g_far), (2 + y, g_core), (3 - y, g_far_core)):
        gmlp[part(at, TB), :] = ref[...]
    depth = u_own.shape[0]
    places, x, piece = peers(info), info[AT_BIT[1]], depth // 2
    u_full[part(places[0], depth), :] = u_own[...]
    u_full[part(places[1], depth), :] = u_core[...]
    for at, ref, ref_core in ((x, u_y, u_y_core), (1 - x, u_x, u_x_core)):
        u_full[part(2 * places[2] + at, piece), :] = ref[:piece, :]
        u_full[part(2 * places[3] + at, piece), :] = ref_core[piece:, :]
    tile = quarter // 2
    for t in range(0, quarter, tile):
        ghid = dot_t(gmlp[...], w_down[t : t + tile, :])
        gate = dot32(h2_cat[...], u_full[:, t : t + tile])
        up = dot32(h2_cat[...], u_full[:, quarter + t : quarter + t + tile])
        sig = jax.nn.sigmoid(gate)
        silu = gate * sig
        hid[:, t : t + tile] = (silu * up).astype(LOW)
        ggu[:, t : t + tile] = (ghid * up * (sig * (1.0 + gate * (1.0 - sig)))).astype(LOW)
        ggu[:, quarter + t : quarter + t + tile] = (ghid * silu).astype(LOW)
    for t in range(0, D, 2 * tile):
        cols = slice(t, t + 2 * tile)
        part_sum = dot_t(ggu[half:, :], u_full[cols, :])
        given[0, :, cols] = part_sum[:TB]
        given[1, :, cols] = part_sum[TB:]
        part_sum = dot_t(ggu[:half, :], u_full[cols, :])
        kept[0, :, cols] = part_sum[:TB]
        kept[1, :, cols] = part_sum[TB:]


def down_kernel(info, hid, w_down, given, kept):
    half = 2 * TB
    for k in range(2):
        given[k] = dot32(hid[half + k * TB : half + (k + 1) * TB, :], w_down[...])
        kept[k] = dot32(hid[k * TB : (k + 1) * TB, :], w_down[...])


def store_halves(mine, rows, first, given, kept):
    half = LANES // 2
    for k in range(rows.shape[0] // LANES):
        low, high = rows[k * LANES : k * LANES + half], rows[k * LANES + half : (k + 1) * LANES]
        given[first + k] = jnp.where(mine == 0, high, low).astype(LOW)
        kept[first + k] = jnp.where(mine == 0, low, high)


def grad_mlp_kernel(bits, info, h2, ggu, hid, gmlp, given, kept):
    mine, step = bit_of(info, bits), 2 * LANES
    for left, right, first in ((h2, ggu, 0), (hid, gmlp, D // LANES)):
        for at in range(0, left.shape[1], step):
            rows = t_dot(left[:, at : at + step], right[...])
            store_halves(mine, rows, first + at // LANES, given, kept)


def grad_mid_kernel(bits, info, normed, attn, gmix, given, kept):
    mine, first = bit_of(info, bits), 0
    for left, right in ((normed, gmix), (attn, gmix)):
        for at in range(0, left.shape[1], LANES):
            rows = t_dot(left[:, at : at + LANES], right[...])
            store_halves(mine, rows, first + at // LANES, given, kept)
        first += left.shape[1] // LANES


def norm_back_pair_kernel(info, chip, moved, residual, norm, g_own, g_far, gres, gmix, g_norm, gout):
    pair_of(info, g_own, g_far, gout)
    gh2 = chip[...] + moved[...].astype(F32)
    value = residual[...]
    scale = rms_scale(value)
    uu = gh2 * norm[...]
    mean = jnp.mean(uu * value, axis=-1, keepdims=True)
    grad = gout[...].astype(F32) + scale * uu - value * scale**3 * mean
    gres[...] = grad
    gmix[...] = grad.astype(LOW)
    y = info[AT_Y]
    mine = residual[y]
    g_norm[...] = jnp.sum(
        (chip[y] + moved[y].astype(F32)) * mine * rms_scale(mine), axis=0, keepdims=True
    )


def output_back_kernel(
    info, gmix, gmix_core, y, gate_z, gain, ssm_out, attn_out, gmix_all, gnormed, gattn, uv
):
    c = info[AT_CORE]
    for core, src in ((c, gmix), (1 - c, gmix_core)):
        for k in range(2):
            gmix_all[part(2 * k + core, TB), :] = src[k]
    grad = dot_t(gmix_all[...], ssm_out[...])
    gnormed[...] = grad
    z = gate_z[...]
    product = grad * gain[...] * (y[...] * (z * jax.nn.sigmoid(z)))
    uv[...] = picked(jnp.ones((8, XW), LOW), product, ((1,), (1,)))
    gattn[...] = dot_t(gmix_all[...], attn_out[...]).astype(LOW)


def conv_back(masks, gconv, slope, taps, inputs, gpad):
    seq = gconv.shape[0]
    gconv = gconv * slope
    gpad[seq:, :] = jnp.zeros((8, LANES), F32)
    total = taps[KC - 1] * gconv
    rows = []
    for j in range(KC - 1):
        back = KC - 1 - j
        term = gconv * masks[j]
        rows.append(jnp.sum(term * inputs(j), axis=0, keepdims=True))
        gpad[:seq, :] = term * taps[j]
        total = total + gpad[back : back + seq, :]
    rows.append(jnp.sum(gconv * inputs(KC - 1), axis=0, keepdims=True))
    rows.append(jnp.sum(gconv, axis=0, keepdims=True))
    return total, rows


def gate_back_kernel(
    info, sq_a, sq_b, uv_a, uv_b, gnormed, y, gate_z, gain, gzz, gy, g_gain
):
    z = gate_z[...]
    sig = jax.nn.sigmoid(z)
    gated = y[...] * (z * sig)
    scale = lax.rsqrt(column_of(sq_a[...] + sq_b[...]) / DS + EPS)
    mean = column_of(uv_a[...] + uv_b[...]) / DS
    grad = gnormed[...]
    ggz = scale * (grad * gain[...]) - gated * scale**3 * mean
    gy[...] = ggz * (z * sig)
    gzz[...] = (ggz * y[...] * (sig * (1.0 + z * (1.0 - sig)))).astype(LOW)
    g_gain[...] = jnp.sum(grad * gated * scale, axis=0, keepdims=True)


def scan_prepare_kernel(
    info, conv_pre, soft, rate, states,
    decay_dt, decay_in, act, slope, from_state, wide, wide_tail, tail_out, step,
):
    pre = conv_pre[...]
    sig = jax.nn.sigmoid(pre)
    act[...] = pre * sig
    slope[...] = sig * (1.0 + pre * (1.0 - sig))
    step[...] = step_sizes(soft[...])
    spread = head_spread()
    for k in range(states.shape[0]):
        rows = pl.ds(k * SPAN, SPAN)
        b = act[rows, XW : XW + NS]
        c = act[rows, XW + NS :]
        dt = step[rows, :]
        seen, total, total_t, dt_t, carried, tail = span_parts(
            info, k * SPAN, dt, -dt * rate[...]
        )
        inner = fair(c, b, ((1,), (1,)))
        for h in range(HEADS_AT):
            decay = decay_of(seen, total, total_t, h)
            decay_dt[k * HEADS_AT + h] = decay * dt_t[h : h + 1, :]
            decay_in[k * HEADS_AT + h] = decay * inner
        from_state[rows, :] = fair(c, states[k])
        wide[rows, :] = picked(carried, spread)
        wide_tail[rows, :] = picked(tail * dt, spread)
        tail_out[rows, :] = tail


def scan_back_kernel(
    info, xbc, soft, rate, skip, states, taps, gy,
    decay_dt, decay_in, act, slope, from_state, wide_all, wide_tail_all, tail_all, step,
    gx_low, gbc_given, gbc_kept, gdr, gsoft_low, g_taps, g_skip, g_heads,
    gact, gdt, gla, padded, gpad, seg,
):
    seq = gy.shape[0]
    spread = head_spread()
    shape = (SPAN, SPAN)
    row, col = iota(shape, 0), iota(shape, 1)
    upper = (col >= row).astype(LOW)
    later = jnp.zeros((NS, XW), F32)
    skip_sum = jnp.zeros((1, XW), F32)
    for k in reversed(range(seq // SPAN)):
        rows = pl.ds(k * SPAN, SPAN)
        x = act[rows, :XW]
        b = act[rows, XW : XW + NS]
        c = act[rows, XW + NS :]
        dt = step[rows, :]
        dt_t = dt.T
        g = gy[rows, :]
        state = states[k]
        wide, wide_tail, tail = wide_all[rows, :], wide_tail_all[rows, :], tail_all[rows, :]
        g_carried = g * wide
        ginner = jnp.zeros(shape, F32)
        out_sum = jnp.zeros(shape, F32)
        in_sum = jnp.zeros(shape, F32)
        parts = []
        for h in range(HEADS_AT):
            own = slice(h * HP, (h + 1) * HP)
            inner = decay_in[k * HEADS_AT + h]
            product = fair(g[:, own], x[:, own], ((1,), (1,)))
            ginner = ginner + product * decay_dt[k * HEADS_AT + h]
            both = product * inner
            out_sum = out_sum + jnp.where(
                col == h, jnp.sum(both * dt_t[h : h + 1, :], axis=1, keepdims=True), 0.0
            )
            in_sum = in_sum + jnp.where(row == h, jnp.sum(both, axis=0, keepdims=True), 0.0)
            parts.append(rough(inner, g[:, own], ((0,), (0,))) * dt[:, h : h + 1])
        from_later = fair(b, later)
        gact[rows, :XW] = (
            jnp.concatenate(parts, axis=1) + from_later * wide_tail + g * skip[...]
        )
        gact[rows, XW : XW + NS] = rough(ginner, c, ((0,), (0,))) + rough(
            x * wide_tail, later, ((1,), (1,))
        )
        gact[rows, XW + NS :] = rough(ginner, b) + rough(g_carried, state, ((1,), (1,)))
        tail_in = picked(x * from_later, spread, ((1,), (1,)))
        state_out = picked(from_state[rows, :] * g_carried, spread, ((1,), (1,)))
        in_col = in_sum.T
        gdt[rows, :] = in_col + tail_in * tail
        moved = tail_in * tail * dt
        kept = picked(
            jnp.sum(state * later, axis=0, keepdims=True) * wide[SPAN - 1 :],
            spread,
            ((1,), (1,)),
        )
        at_end = jnp.sum(moved, axis=0, keepdims=True) + kept
        change = out_sum - in_col * dt + state_out - moved
        gla[rows, :] = picked(upper, change, terms=3) + at_end
        skip_sum = skip_sum + jnp.sum(g * x, axis=0, keepdims=True)
        later = later * wide[SPAN - 1 :] + fair(c, g_carried, ((0,), (0,)))
    g_skip[...] = skip_sum

    core = info[AT_CORE]
    gbc_given[...] = gact[:, part_at(XW, 1 - core, NS, NS)]
    gbc_kept[...] = gact[:, part_at(XW, core, NS, NS)]

    gsoft = (gdt[...] - gla[...] * rate[...]) * jax.nn.sigmoid(soft[...])
    gsoft = jnp.where(iota(gsoft.shape, 1) < HEADS_AT, gsoft, 0.0)
    gsoft_low[...] = gsoft.astype(LOW)
    gdr[...] = dot_t(gsoft.astype(LOW), own_heads_pick(info)).astype(LOW)
    g_heads[0:1, :] = jnp.sum(-gla[...] * step[...] * rate[...], axis=0, keepdims=True)
    g_heads[1:2, :] = jnp.sum(gsoft, axis=0, keepdims=True)
    g_heads[2:, :] = jnp.zeros((6, LANES), F32)

    padded[:8, :] = jnp.zeros((8, LANES), F32)
    masks = tap_masks(info, seg)
    g_taps[...] = jnp.zeros_like(g_taps)
    for block in range(0, XW, LANES):
        lanes = slice(block, block + LANES)
        padded[8:, :] = xbc[:, lanes]
        total, sums = conv_back(
            masks, gact[:, lanes], slope[:, lanes],
            [taps[j : j + 1, lanes] for j in range(KC)],
            lambda j: padded[8 - (KC - 1 - j) : 8 - (KC - 1 - j) + seq, :], gpad,
        )
        gx_low[:, lanes] = total.astype(LOW)
        for j, value in enumerate(sums):
            g_taps[j : j + 1, lanes] = value


def shared_back_kernel(
    info, gbc_kept, gbc_moved, xbc, slope, taps, gbc_low, g_taps, padded, gpad, seg
):
    seq = gbc_low.shape[0]
    lanes = part_at(XW, info[AT_CORE], NS, NS)
    padded[:8, :] = jnp.zeros((8, LANES), F32)
    padded[8:, :] = xbc[:, lanes]
    total, sums = conv_back(
        tap_masks(info, seg), gbc_kept[...] + gbc_moved[...], slope[:, lanes],
        [taps[j : j + 1, lanes] for j in range(KC)],
        lambda j: padded[8 - (KC - 1 - j) : 8 - (KC - 1 - j) + seq, :], gpad,
    )
    g_taps[...] = jnp.zeros_like(g_taps)
    for j, value in enumerate(sums):
        g_taps[j : j + 1, :] = value
    gbc_low[...] = total.astype(LOW)


def late_kernel(bits, info, gzz, gq, gkv, gx_low, gbc_low, gsoft, h_low, given, kept, left):
    mine, core = bit_of(info, bits), info[AT_CORE]
    own = gsoft[...]
    other = jnp.concatenate([own[:, HD:], own[:, :HD]], axis=1)
    is_own = (iota(own.shape, 1) < HD) == (core == 0)
    left[...] = jnp.where(is_own, gkv[...], jnp.where(core == 0, other, own))
    first = 0
    for value in (gzz, gq, left, gx_low, gbc_low):
        for at in range(0, value.shape[1], LANES):
            rows = t_dot(value[:, at : at + LANES], h_low[...])
            store_halves(mine, rows, first + at // LANES, given, kept)
        first += value.shape[1] // LANES


def inputs_back_kernel(
    info, gx_low, gzz, gq, gkv, gbc_low, gdr, w_full, z_full, given, kept, back
):
    c = info[AT_CORE]
    gbc = gbc_low[...]
    nothing = jnp.zeros_like(gbc)
    back[:, :XW] = gx_low[...]
    back[:, Q_AT:KV_AT] = gq[...]
    back[:, KV_AT:BC_AT] = gkv[...]
    back[:, BC_AT : BC_AT + NS] = jnp.where(c == 0, gbc, nothing)
    back[:, BC_AT + NS : DT_AT] = jnp.where(c == 0, nothing, gbc)
    back[:, DT_AT:W_FIRST] = gdr[...]
    back[:, W_FIRST:] = gzz[...]
    for core, dst in ((1 - c, given), (c, kept)):
        for k in range(2):
            rows = part(2 * k + core, TB)
            dst[k] = dot32(back[rows, :W_FIRST], w_full[...]) + dot32(
                back[rows, W_FIRST:], z_full[...]
            )


def first_norm_back_kernel(info, mine, moved, hidden, norm, gres, out, g_norm):
    gh = mine[...] + moved[...]
    value = hidden[...].astype(F32)
    scale = rms_scale(value)
    uu = gh * norm[...]
    mean = jnp.mean(uu * value, axis=-1, keepdims=True)
    out[...] = gres[info[AT_Y]] + scale * uu - value * scale**3 * mean
    g_norm[...] = jnp.sum(gh * value * scale, axis=0, keepdims=True)


def result_kernel(info, mine, moved, residual, keep, out, sums):
    mlp = mine[...] + moved[...]
    full = residual[info[AT_Y]] + mlp
    out[...] = full.astype(LOW)
    full = full * keep[:, :1]
    mlp = mlp * keep[:, :1]
    sums[0:1, :] = jnp.sum(full * full, axis=0, keepdims=True)
    sums[1:2, :] = jnp.sum(mlp * mlp, axis=0, keepdims=True)
    sums[2:, :] = jnp.zeros((6, D), F32)


def attend_kernel(info, q_ref, kv_ref, out_ref, lse_ref):
    scale = 1.0 / math.sqrt(HD)
    heads = q_ref.shape[1] // HD
    for k in range(q_ref.shape[0] // SPAN):
        rows, reach = pl.ds(k * SPAN, SPAN), (k + 1) * SPAN
        keys, values = kv_ref[:reach, :HD], kv_ref[:reach, HD:]
        counted = counted_keys(info, k * SPAN, reach)
        outs, tops = [], []
        for h in range(heads):
            s = dot_t(q_ref[rows, h * HD : (h + 1) * HD], keys) * scale
            s = jnp.where(counted, s, NEG)
            top = jnp.max(s, axis=1, keepdims=True)
            lse = top + jnp.log(jnp.sum(jnp.exp(s - top), axis=1, keepdims=True))
            prob = jnp.exp(s - lse).astype(LOW)
            outs.append(dot32(prob, values))
            tops.append(lse)
        out_ref[rows, :] = jnp.concatenate(outs, axis=1).astype(LOW)
        lane = iota((SPAN, LANES), 1)
        lse_ref[rows, :] = sum(jnp.where(lane == h, t, 0.0) for h, t in enumerate(tops))


def counted_keys(info, first, reach):
    shape = (SPAN, reach)
    row, col = iota(shape, 0) + first, iota(shape, 1)
    return (col <= row) & (count_starts(info, row) == count_starts(info, col))


def attend_back_kernel(
    info, q_ref, kv_ref, lse_ref, gout_ref, cosines, sines, turn, gq_ref, gkv_ref, gq_rot
):
    scale = 1.0 / math.sqrt(HD)
    heads = q_ref.shape[1] // HD
    gkv_ref[...] = jnp.zeros_like(gkv_ref)
    for k in range(q_ref.shape[0] // SPAN):
        rows, reach = pl.ds(k * SPAN, SPAN), (k + 1) * SPAN
        keys, values = kv_ref[:reach, :HD], kv_ref[:reach, HD:]
        counted = counted_keys(info, k * SPAN, reach)
        outs, gkeys, gvalues = [], 0.0, 0.0
        for h in range(heads):
            own = slice(h * HD, (h + 1) * HD)
            q, gout = q_ref[rows, own], gout_ref[rows, own]
            s = dot_t(q, keys) * scale
            pe = jnp.exp(jnp.where(counted, s - lse_ref[rows, h : h + 1], NEG))
            gprob = dot_t(gout, values)
            delta = jnp.sum(pe * gprob, axis=1, keepdims=True)
            gs = (pe * (gprob - delta) * scale).astype(LOW)
            outs.append(dot32(gs, keys))
            gkeys = gkeys + t_dot(gs, q)
            gvalues = gvalues + t_dot(pe.astype(LOW), gout)
        gq_rot[rows, :] = jnp.concatenate(outs, axis=1)
        gkv_ref[:reach, :] += jnp.concatenate([gkeys, gvalues], axis=1)
    value = gq_rot[...]
    gq_ref[...] = (value * cosines[...] - picked(value, turn[...]) * sines[...]).astype(LOW)


def keys_back_kernel(info, own, moved, cosines, sines, turn, out):
    value = own[...] + moved[...]
    back = value * cosines[...] - picked(value, turn[...]) * sines[...]
    is_key = iota(value.shape, 1) < HD
    mine = is_key == (info[AT_CORE] == 0)
    out[...] = jnp.where(mine, jnp.where(is_key, back, value), 0.0).astype(LOW)


def halve_kernel(bits, info, kept, moved, given_next, kept_next):
    mine = bit_of(info, bits)
    half = kept.shape[1] // 2
    own, other = part(mine, half), part(1 - mine, half)
    given_next[...] = (kept[:, other, :] + moved[:, other, :].astype(F32)).astype(LOW)
    kept_next[...] = kept[:, own, :] + moved[:, own, :].astype(F32)


def settle_kernel(by_rows, info, kept, moved, total, core, far, far_core):
    total[...] = (kept[...] + moved[...].astype(F32)).astype(LOW)
    for place, dst in zip(peers(info)[1:], (core, far, far_core)):
        if by_rows:
            count = by_rows // 4
            dst[...] = total[pl.ds(count * place, count)]
        else:
            dst[...] = total[:, :, part(place, dst.shape[2])]


def total_low_kernel(info, kept, moved, out):
    out[...] = (kept[...] + moved[...].astype(F32)).astype(LOW)


def spread_kernel(by_rows, info, total, core, far, far_core, out):
    places = peers(info)
    out[...] = total[...]
    for place, ref in zip(places[1:], (core, far, far_core)):
        if by_rows:
            count = by_rows // 4
            out[pl.ds(count * place, count)] = ref[...]
        else:
            out[:, :, part(place, ref.shape[2])] = ref[...]


def join_kernel(bits, info, own, moved, out):
    mine, size = bit_of(info, bits), own.shape[1]
    out[:, part(mine, size), :] = own[...]
    out[:, part(1 - mine, size), :] = moved[...]


def sum_steps(info, given, kept, order, by_rows):
    moved = swap_far(given, order[0])
    for bits in order[1:]:
        moved = after(moved, (yield given))
        n, size, width = kept.shape
        given, kept = call(
            functools.partial(halve_kernel, bits),
            (low_of(n, size // 2, width), f32_of(n, size // 2, width)),
            info, kept, moved,
        )
        moved = swap_far(given, bits)
    moved = after(moved, (yield given))
    n, size, width = kept.shape
    if by_rows is None:
        own = call(total_low_kernel, low_of(n, size, width), info, kept, moved)
    else:
        block = (by_rows // 4, size, width) if by_rows else (n, size, width // 4)
        total, *blocks = call(
            functools.partial(settle_kernel, by_rows),
            (low_of(n, size, width),) + (low_of(*block),) * 3,
            info, kept, moved,
        )
        sent = [swap(block, bits) for block, bits in zip(blocks, (1, 2, 3))]
        sent = after(sent, (yield blocks))
        own = call(
            functools.partial(spread_kernel, by_rows), low_of(n, size, width), info, total, *sent
        )
    for bits in order[:0:-1]:
        moved = swap_far(own, bits)
        moved = after(moved, (yield own))
        n, size, width = own.shape
        own = call(
            functools.partial(join_kernel, bits), low_of(n, 2 * size, width), info, own, moved
        )
    moved = swap_far(own, order[0])
    return own, after(moved, (yield own))


class Running:
    def __init__(self, steps):
        self.steps, self.result = steps, None
        self.sent = next(steps)

    def step(self, value):
        if self.result is not None:
            return value
        try:
            self.sent = self.steps.send(value)
        except StopIteration as end:
            self.result = self.sent = end.value
        return self.sent


def quarters(bits, info, own, moved, source=None):
    mine, size = bit_of(info, bits), own.shape[1] // 2
    same = True if source is None else info[AT_CORE] == source % 2
    for at, ref in ((mine, own), (1 - mine, moved)):
        for j in range(2):
            yield jnp.where(same, 2 * at + j, 2 * j + at), ref, slice(j * size, (j + 1) * size)


def finish_mlp_kernel(bits, info, own, moved, out_up, out_down):
    quarter, size, blocks = FF // 4, own.shape[1] // 2, D // LANES
    each = blocks // 4
    for k in range(4):
        for at, ref, rows in quarters(bits, info, own, moved, k):
            for j in range(each):
                block = ref[each * k + j, rows, :].astype(F32)
                where = part(4 * j + at, size)
                out_up[where, k * quarter : (k + 1) * quarter] = block[:, :quarter]
                out_up[where, FF + k * quarter : FF + (k + 1) * quarter] = block[:, quarter:]
    for at, ref, rows in quarters(bits, info, own, moved):
        for j in range(out_down.shape[0] // LANES):
            out_down[part(4 * j + at, size), :] = ref[blocks + j, rows, :].astype(F32)


def finish_mid_kernel(bits, info, own, moved, out_ssm, out_attn):
    size, scan = own.shape[1] // 2, XW // LANES
    for at, ref, rows in quarters(bits, info, own, moved):
        for j in range(scan):
            out_ssm[part(4 * j + at, size), :] = ref[j, rows, :].astype(F32)
        out_attn[part(at, size), :] = ref[scan, rows, :].astype(F32)


def finish_in_kernel(bits, info, own, moved, out, out_qkv, blocks_q, blocks_kv, shared):
    size, wide, scan = own.shape[1] // 2, out.shape[1], XW // LANES
    q_at, x_at = scan, scan + 2
    for k in range(4):
        lanes = slice(k * wide, (k + 1) * wide)
        for at, ref, rows in quarters(bits, info, own, moved, k):
            for j in range(scan):
                for first, block in ((0, j), (DS, x_at + j)):
                    start = first + (k * scan + j) * LANES + at * size
                    out[pl.ds(pl.multiple_of(start, size), size), :] = ref[
                        block, rows, lanes
                    ].astype(F32)
            blocks_q[k, part(at, size), :] = ref[q_at, rows, lanes].astype(F32)
            blocks_kv[k, part(at, size), :] = ref[q_at + 1, rows, lanes].astype(F32)
            shared[k, part(at, size), :] = ref[x_at + scan, rows, lanes].astype(F32)
    for k in range(4):
        out_qkv[:, k * LANES : (k + 1) * LANES] = blocks_q[k].T
    for k in range(2):
        rows = slice(k * HD, (k + 1) * HD)
        both = jnp.concatenate([blocks_kv[k, rows, :], blocks_kv[k + 2, rows, :]], axis=0)
        out_qkv[:, QW + k * KW : QW + (k + 1) * KW] = both.T
        out[2 * DS + k * NS : 2 * DS + (k + 1) * NS, :] = shared[k] + shared[k + 2]
    steps = [
        blocks_kv[k, (1 - k % 2) * HD : (1 - k % 2) * HD + HEADS_AT, :] for k in range(4)
    ]
    out[DS + CONV_CH :, :] = jnp.concatenate(steps, axis=0)


def small_steps(info, vector):
    for bits in (1, 2, (1, 1), (2, 2), (4, 4)):
        moved = swap_far(vector, bits) if isinstance(bits, tuple) else swap(vector, bits)
        moved = after(moved, (yield vector))
        vector = call(total_kernel, f32_of(*vector.shape), info, vector, moved)
    return vector


def unpack_kernel(info, small, one, conv, conv_bias, dt_bias, a_log, skip, gain, two, stats):
    for first, out in ((ROW_ONE, one), (ROW_TWO, two), (ROW_GAIN, gain)):
        for k in range(out.shape[1] // LANES):
            out[:, k * LANES : (k + 1) * LANES] = small[first + k : first + k + 1, :]
    for j in range(KC + 1):
        for k in range(CONV_ROWS):
            at = ROW_TAPS + j * CONV_ROWS + k
            dst, row = (conv, j) if j < KC else (conv_bias, 0)
            dst[row : row + 1, k * LANES : (k + 1) * LANES] = small[at : at + 1, :]
    for first, out in ((ROW_RATE, a_log), (ROW_BIAS, dt_bias)):
        pieces = [small[first + k : first + k + 1, :HEADS_AT] for k in range(4)]
        out[...] = jnp.concatenate(pieces, axis=1)
    lane = iota((1, LANES), 1)
    total = jnp.zeros((1, LANES), F32)
    for k in range(NH):
        at, first = ROW_SKIP + k * HP // LANES, k * HP % LANES
        value = jnp.sum(small[at : at + 1, first : first + HP], axis=1, keepdims=True)
        total = total + jnp.where(lane == k, value, 0.0)
    skip[...] = total[:, :NH]
    sums = [
        jnp.sum(small[ROW_STATS + k : ROW_STATS + k + 1, :], axis=1, keepdims=True)
        for k in range(4)
    ]
    total = jnp.zeros((1, LANES), F32)
    for k in range(3):
        total = total + jnp.where(lane == k, jnp.sqrt(sums[k] / (sums[3] * D)), 0.0)
    stats[...] = total[:, :3]


ROW_ONE, ROW_TWO, ROW_TAPS = 0, 8, 16
CONV_ROWS = CONV_CH // LANES
ROW_GAIN = ROW_TAPS + (KC + 1) * CONV_ROWS
ROW_SKIP = ROW_GAIN + DS // LANES
ROW_RATE = ROW_SKIP + DS // LANES
ROW_BIAS = ROW_RATE + 4
ROW_STATS = ROW_BIAS + 4
SMALL_ROWS = 128


def small_kernel(
    info, one, two, taps_x, taps_bc, gain, skip, heads, sums, mixed, keep, out
):
    out[...] = jnp.zeros_like(out)
    place, core = peers(info)[0], info[AT_CORE]
    for k in range(D // LANES):
        lanes = slice(k * LANES, (k + 1) * LANES)
        out[ROW_ONE + k : ROW_ONE + k + 1, :] = one[:, lanes]
        out[ROW_TWO + k : ROW_TWO + k + 1, :] = two[:, lanes]
    blocks = XW // LANES
    for k in range(blocks):
        lanes = slice(k * LANES, (k + 1) * LANES)
        at = place * blocks + k
        for j in range(KC + 1):
            out[pl.ds(ROW_TAPS + j * CONV_ROWS + at, 1), :] = taps_x[j : j + 1, lanes]
        out[pl.ds(ROW_GAIN + at, 1), :] = gain[:, lanes]
        out[pl.ds(ROW_SKIP + at, 1), :] = skip[:, lanes]
    for j in range(KC + 1):
        out[pl.ds(ROW_TAPS + j * CONV_ROWS + DS // LANES + core, 1), :] = taps_bc[j : j + 1, :]
    out[pl.ds(ROW_RATE + place, 1), :] = heads[0:1, :]
    out[pl.ds(ROW_BIAS + place, 1), :] = heads[1:2, :]
    for k, row in enumerate((sums[0:1, :], mixed[...], sums[1:2, :])):
        folded = row[:, :LANES]
        for j in range(1, D // LANES):
            folded = folded + row[:, j * LANES : (j + 1) * LANES]
        out[ROW_STATS + k : ROW_STATS + k + 1, :] = folded
    out[ROW_STATS + 3 : ROW_STATS + 4, :] = keep[...].T[:1]


def by_heads(
    hidden_in, cotangent, doc_starts, valid_mask, norm_one, in_proj, conv_weight, conv_bias,
    dt_bias, a_log, skip_scale, gated_gain, qkv_proj, ssm_out, attn_out, norm_two, gate_up,
    down_proj,
):
    place, far_place = lax.axis_index("shard"), lax.axis_index("replica")
    y, c = place // 2, place % 2
    rows = hidden_in.shape[0]
    seq, depth = 4 * rows, in_proj.shape[0]
    bits = [y, c, far_place % 2, far_place // 2 % 2, far_place // 4]
    info = jnp.concatenate([jnp.stack(bits).astype(jnp.int32), doc_starts[0]])
    pair = (2, rows, D)

    h_far = swap(hidden_in, 2)
    h_core = swap(hidden_in, 1)
    w_own, w_core, w_far, z_own, z_core, z_far = call(
        pack_in_kernel,
        (
            low_of(W_FIRST, depth), low_of(W_FIRST, depth), low_of(W_FIRST + KV_AT, depth),
            low_of(XW, depth), low_of(XW, depth), low_of(2 * XW, depth),
        ),
        info, in_proj.T, qkv_proj,
    )
    u_own, u_core, u_far = call(
        pack_up_kernel, (low_of(depth, FF // 2),) * 3, info, after(gate_up, w_own)
    )
    freqs = ROPE_BASE ** (-(jnp.arange(HD // 2).astype(F32) * 2.0) / HD)
    angles = jnp.arange(seq).astype(F32)[:, None] * jnp.tile(freqs, LANES // (HD // 2))[None, :]
    cosines, sines = jnp.cos(angles), jnp.sin(angles)
    taps, bias, bias_own, rate, skip, gain, gain_one, gain_two, keep, g_own, turn = call(
        prepare_kernel,
        (
            f32_of(KC, XW + 2 * NS), f32_of(1, XW + 2 * NS), f32_of(1, LANES), f32_of(1, LANES),
            f32_of(1, XW), f32_of(1, XW), f32_of(1, D), f32_of(1, D), f32_of(LANES, LANES),
            low_of(rows, D), low_of(LANES, LANES),
        ),
        info, conv_weight.T, conv_bias[None], dt_bias[None], a_log[None], skip_scale[None],
        gated_gain[None], norm_one[None], norm_two[None], valid_mask[None],
        after(cotangent, (cosines, sines)),
        scratch=(pltpu.VMEM((8, LANES), F32),),
    )
    w_far = swap(after(w_far, (u_own, g_own, h_far)), 2)
    w_core = swap(w_core, 1)
    h_far_core = swap(h_far, 1)
    w_far_core = swap(w_far, 1)
    z_far = swap(after(z_far, w_far), 2)

    h_low, w_full, xbc, conv_pre, soft, q_low, kv_low, ssm_y, states = call(
        forward_kernel,
        (
            low_of(seq, D), low_of(W_FIRST, D), f32_of(seq, XW + 2 * NS), f32_of(seq, XW + 2 * NS),
            f32_of(seq, LANES), low_of(seq, LANES), low_of(seq, LANES), f32_of(seq, XW),
            f32_of(seq // SPAN, NS, XW),
        ),
        info, hidden_in, h_core, h_far, h_far_core, w_own, w_core, w_far, w_far_core,
        gain_one, taps, bias, bias_own, rate, skip, cosines, sines, turn,
        scratch=(
            pltpu.VMEM((seq + 8, XW + 2 * NS), F32), pltpu.VMEM((seq, XW + 2 * NS), F32),
            pltpu.VMEM((seq, LANES), F32), pltpu.VMEM((seq + 8, LANES), jnp.int32),
        ),
    )
    z_far, z_core = after((z_far, z_core), h_low)
    z_core, z_far_core = swap(z_core, 1), swap(z_far, 1)
    u_far, u_core, g_out = after((u_far, u_core, g_own), z_far)
    u_y, g_far = swap(u_far, 2), swap(g_out, 2)
    z_full, gate_z, square = call(
        gate_kernel, (low_of(XW, D), f32_of(seq, XW), f32_of(8, seq)),
        info, h_low, z_own, z_core, z_far, z_far_core, ssm_y,
    )
    square = call(total_kernel, f32_of(8, seq), info, square, swap(square, 1))
    square_far = swap(square, 2)
    attn, lse = call(
        attend_kernel, (low_of(seq, LANES), f32_of(seq, LANES)), info, after(q_low, square), kv_low
    )

    given, kept, normed = call(
        output_kernel, (f32_of(*pair), f32_of(*pair), low_of(seq, XW)),
        info, square, square_far, ssm_y, gate_z, gain, after(attn, u_y), ssm_out, attn_out,
    )
    u_x = swap_far(after(u_y, given), (1, 1))
    u_y_core = swap(after(u_y, given), 1)
    chip, sent = call(add_kernel, (f32_of(*pair), low_of(*pair)), info, kept, swap(given, 1))
    u_core, g_core = swap(after(u_core, sent), 1), swap(after(g_out, sent), 1)
    g_far_core = swap(after(g_far, sent), 1)
    residual, h2, mixed_sum = call(
        second_norm_kernel, (f32_of(*pair), low_of(*pair), f32_of(1, D)),
        info, chip, swap(sent, 2), hidden_in, h_far, gain_two, keep,
        scratch=(pltpu.VMEM(pair, LOW),),
    )
    u_x_core = swap(u_x, 1)

    given, kept, hid, ggu, h2_cat, gmlp = call(
        mlp_kernel,
        (
            f32_of(*pair), f32_of(*pair), low_of(seq, FF // 4), low_of(seq, FF // 2),
            low_of(seq, D), low_of(seq, D),
        ),
        info, h2, swap(h2, 1), u_own, u_core, u_y, u_x, u_y_core, u_x_core,
        g_own, g_core, g_far, g_far_core, down_proj,
        scratch=(pltpu.VMEM((D, FF // 2), LOW),),
    )
    order = ((1, 2), (2, 1), (4, 4))
    moved = swap(given, 1)
    half = LANES // 2
    blocks = (D + FF // 4) // LANES
    up_given, up_kept = call(
        functools.partial(grad_mlp_kernel, order[0]),
        (low_of(blocks, half, D), f32_of(blocks, half, D)), info, h2_cat, ggu, hid, gmlp,
    )
    s_up = Running(sum_steps(info, up_given, up_kept, order, D // LANES))
    kept = after(kept, up_given)
    chip, sent = call(add_kernel, (f32_of(*pair), low_of(*pair)), info, kept, moved)
    prepared = call(
        scan_prepare_kernel,
        (
            f32_of(seq // SPAN * HEADS_AT, SPAN, SPAN), f32_of(seq // SPAN * HEADS_AT, SPAN, SPAN),
            f32_of(seq, XW + 2 * NS), f32_of(seq, XW + 2 * NS), f32_of(seq, XW), f32_of(seq, XW),
            f32_of(seq, XW), f32_of(seq, LANES), f32_of(seq, LANES),
        ),
        info, after(conv_pre, sent), soft, rate, states,
    )
    gres, gmix, g_norm_two = call(
        norm_back_pair_kernel, (f32_of(*pair), low_of(*pair), f32_of(1, D)),
        info, after(chip, prepared), swap(sent, 2), residual, gain_two, g_own, g_far,
        scratch=(pltpu.VMEM(pair, LOW),),
    )

    moved = swap(gmix, 1)
    mlp_given, mlp_kept = call(
        down_kernel, (f32_of(*pair), f32_of(*pair)), info, after(hid, gmix), down_proj
    )
    mlp_mine, mlp_given = call(
        add_split_kernel, (f32_of(rows, D),) * 2, info, mlp_kept, swap(mlp_given, 1)
    )
    gmix_all, gnormed, gattn, uv = call(
        output_back_kernel,
        (low_of(seq, D), f32_of(seq, XW), low_of(seq, LANES), f32_of(8, seq)),
        info, gmix, moved, ssm_y, gate_z, gain, ssm_out, attn_out,
    )
    uv = call(total_kernel, f32_of(8, seq), info, uv, swap(uv, 1))
    uv_far = swap(uv, 2)
    gq, gkv_part = call(
        attend_back_kernel, (low_of(seq, LANES), f32_of(seq, LANES)),
        info, q_low, kv_low, lse, after(gattn, uv), cosines, sines, turn,
        scratch=(pltpu.VMEM((seq, LANES), F32),),
    )
    gzz, gy, g_gain = call(
        gate_back_kernel, (low_of(seq, XW), f32_of(seq, XW), f32_of(1, XW)),
        info, square, square_far, uv, uv_far, after(gnormed, gkv_part), ssm_y, gate_z, gain,
    )
    blocks = (XW + LANES) // LANES
    mid_given, mid_kept = call(
        functools.partial(grad_mid_kernel, order[0]),
        (low_of(blocks, half, D), f32_of(blocks, half, D)),
        info, normed, attn, after(gmix_all, gkv_part),
    )
    s_mid = Running(sum_steps(info, mid_given, mid_kept, order, None))

    gx_low, gbc_given, gbc_kept, gdr, gsoft, taps_x, g_skip, g_heads = call(
        scan_back_kernel,
        (
            low_of(seq, XW), f32_of(seq, NS), f32_of(seq, NS), low_of(seq, LANES),
            low_of(seq, LANES), f32_of(8, XW), f32_of(1, XW), f32_of(8, LANES),
        ),
        info, xbc, soft, rate, skip, states, taps, after(gy, (s_up.step(gy), mid_given)),
        *prepared,
        scratch=(
            pltpu.VMEM((seq, XW + 2 * NS), F32),
            pltpu.VMEM((seq, LANES), F32), pltpu.VMEM((seq, LANES), F32),
            pltpu.VMEM((seq + 8, LANES), F32), pltpu.VMEM((seq + 8, LANES), F32),
            pltpu.VMEM((seq + 8, LANES), jnp.int32),
        ),
    )
    gkv_part = after(gkv_part, gbc_given)
    moved = swap(gbc_given, 1)
    gkv = call(
        keys_back_kernel, low_of(seq, LANES),
        info, gkv_part, swap(gkv_part, 1), cosines, sines, turn,
    )
    gbc_low, taps_bc = call(
        shared_back_kernel, (low_of(seq, NS), f32_of(8, LANES)),
        info, after(gbc_kept, gkv), moved, xbc, prepared[3], taps,
        scratch=(
            pltpu.VMEM((seq + 8, LANES), F32), pltpu.VMEM((seq + 8, LANES), F32),
            pltpu.VMEM((seq + 8, LANES), jnp.int32),
        ),
    )

    blocks = (2 * XW + 3 * LANES) // LANES
    late_given, late_kept = call(
        functools.partial(late_kernel, order[0]),
        (low_of(blocks, half, D), f32_of(blocks, half, D)),
        info, gzz, gq, gkv, gx_low, gbc_low, gsoft, h_low,
        scratch=(pltpu.VMEM((seq, LANES), LOW),),
    )
    s_late = Running(sum_steps(info, late_given, late_kept, order, 0))

    given, kept = call(
        inputs_back_kernel, (f32_of(*pair), f32_of(*pair)),
        info, after(gx_low, (s_up.step(gbc_low), s_mid.step(gbc_low), late_given)), gzz, gq, gkv, gbc_low, gdr, w_full, z_full,
        scratch=(pltpu.VMEM((seq, W_FIRST + XW), LOW),),
    )
    moved = swap(given, 1)
    kept = after(kept, late_given)
    mine, given = call(add_split_kernel, (f32_of(rows, D),) * 2, info, kept, moved)
    moved = swap(given, 2)

    token = given

    def steps(*sums):
        nonlocal token
        for one in sums:
            token = one.step(token)

    steps(s_late, s_up, s_up)
    grad_input, g_norm_one = call(
        first_norm_back_kernel, (f32_of(rows, D), f32_of(1, D)),
        info, mine, after(moved, token), hidden_in, gain_one, gres,
    )
    mlp_moved = swap(after(mlp_given, g_norm_one), 2)
    token = g_norm_one
    steps(s_mid, s_late, s_mid)
    output, sums = call(
        result_kernel, (low_of(rows, D), f32_of(8, D)),
        info, mlp_mine, after(mlp_moved, token), residual, keep,
    )
    small = call(
        small_kernel, f32_of(SMALL_ROWS, LANES),
        info, g_norm_one, g_norm_two, taps_x, taps_bc, g_gain, g_skip, g_heads, sums,
        mixed_sum, keep,
    )
    s_small = Running(small_steps(info, small))
    steps(s_up, s_small, s_mid, s_small, s_late, s_up, s_mid, s_late, s_small, s_up, s_late, s_mid, s_small, s_late, s_small, s_late)
    small = s_small.result
    grad_up, grad_down = call(
        functools.partial(finish_mlp_kernel, order[0]),
        (f32_of(*gate_up.shape), f32_of(*down_proj.shape)), info, *s_up.result,
    )
    grad_ssm, grad_attn = call(
        functools.partial(finish_mid_kernel, order[0]),
        (f32_of(*ssm_out.shape), f32_of(*attn_out.shape)), info, *s_mid.result,
    )
    grad_in, grad_qkv = call(
        functools.partial(finish_in_kernel, order[0]),
        (f32_of(in_proj.shape[1], depth), f32_of(*qkv_proj.shape)), info, *s_late.result,
        scratch=(pltpu.VMEM((4, LANES, depth), F32),) * 3,
    )
    one, conv, bias, dt, rate, skip, gain, two, stats = call(
        unpack_kernel,
        (
            f32_of(1, D), f32_of(KC, CONV_CH), f32_of(1, CONV_CH), f32_of(1, NH), f32_of(1, NH),
            f32_of(1, NH), f32_of(1, DS), f32_of(1, D), f32_of(1, 3),
        ),
        info, small,
    )
    return (
        output, grad_input, one[0], grad_in.T, conv.T, bias[0], dt[0], rate[0], skip[0], gain[0],
        grad_qkv, grad_ssm, grad_attn, two[0], grad_up, grad_down, stats[0],
    )


def on_any(*args):
    sizes = (lax.axis_size("replica"), lax.axis_size("shard"), args[0].shape[0])
    return (by_heads if sizes == (8, 4, TB) else on_device)(*args)


def solution(mesh):
    return jax.shard_map(
        on_any,
        mesh=mesh,
        in_specs=(
            P(("replica", "shard"), None),
            P(("replica", "shard"), None),
            P("replica", None),
            P(("replica", "shard")),
            P(),
            P("shard", None),
            P(),
            P(),
            P(),
            P(),
            P(),
            P(),
            P("shard", None),
            P("shard", None),
            P("shard", None),
            P(),
            P("shard", None),
            P("shard", None),
        ),
        out_specs=(
            P(("replica", "shard"), None),
            P(("replica", "shard"), None),
            P(),
            P("shard", None),
            P(),
            P(),
            P(),
            P(),
            P(),
            P(),
            P("shard", None),
            P("shard", None),
            P("shard", None),
            P(),
            P("shard", None),
            P("shard", None),
            P(),
        ),
        check_vma=False,
    )
```

```python
import functools
import math

import jax
import jax.numpy as jnp
from jax import lax
from jax.experimental import pallas as pl
from jax.experimental.pallas import tpu as pltpu
from jax.sharding import PartitionSpec as P

D = 1024
NH = 24
HP = 64
NS = 128
KC = 4
QH = 8
KVH = 2
HD = 64
FF = 2048
SPAN = 128
KBLK = 512
DS = 1536
QW = 512
KW = 128
CONV_CH = 1792


EPS = 1e-05
ROPE_BASE = 100000000000.0
NEG = -1e30
HIGH = lax.Precision.HIGHEST


def from_behind(block, axis, distance):
    devices = range(lax.axis_size(axis))
    route = [(i - distance, i) for i in devices if i - distance in devices]
    return lax.ppermute(block, axis, route)


def carried_in(part, axis, combine, identity):
    place = lax.axis_index(axis)
    gathered = jax.tree.map(lambda a: lax.all_gather(a, axis), part)
    state = jax.tree.map(lambda a, e: jnp.zeros_like(a) + jnp.asarray(e, a.dtype), part, identity)

    def one(step, state):
        return combine(
            state, jax.tree.map(lambda a: lax.dynamic_index_in_dim(a, step, 0, False), gathered)
        )

    return lax.fori_loop(0, place, one, state)


def entering(value, axis, combine, identity):
    size, mine = (lax.axis_size(axis), lax.axis_index(axis))
    everything = jax.tree.map(
        lambda part, kind: lax.all_gather(part.astype(kind), axis),
        value,
        jax.tree.map(lambda a: jnp.bfloat16 if a.dtype == jnp.float32 else a.dtype, value),
    )
    start = jax.tree.map(
        lambda part, zero: jnp.broadcast_to(jnp.asarray(zero, part.dtype), part.shape),
        value,
        identity,
    )

    def step(k, before):
        at = size - 1 - k
        reached = at > mine
        new = combine(
            before, jax.tree.map(lambda part, own: part[at].astype(own.dtype), everything, value)
        )
        return jax.tree.map(lambda a, b: jnp.where(reached, a, b), new, before)

    return lax.fori_loop(0, size, step, start)


def rms_scale(tensor):
    return lax.rsqrt(jnp.mean(tensor * tensor, axis=-1, keepdims=True) + EPS)


def rope_tables(positions):
    freqs = ROPE_BASE ** (-(jnp.arange(HD // 2).astype(jnp.float32) * 2.0) / HD)
    angles = positions.astype(jnp.float32)[:, None] * freqs[None, :]
    return (jnp.cos(angles), jnp.sin(angles))


def rotate(tensor, heads, cosines, sines):
    shaped = tensor.reshape(tensor.shape[0], heads, HD)
    first_half = shaped[:, :, : HD // 2]
    second_half = shaped[:, :, HD // 2 :]
    cos_b = cosines[:, None, :]
    sin_b = sines[:, None, :]
    turned = jnp.concatenate(
        [first_half * cos_b - second_half * sin_b, second_half * cos_b + first_half * sin_b],
        axis=-1,
    )
    return turned.reshape(tensor.shape[0], heads * HD)


def segment_of(positions, starts_row):
    return jnp.sum((starts_row[None, :] <= positions[:, None]).astype(jnp.int32), axis=1) - 1


def norm_back(grad_out, tensor, scale_rows, gain):
    scaled = grad_out * gain
    grad_in = scale_rows * scaled - tensor * scale_rows**3 * jnp.mean(
        scaled * tensor, axis=-1, keepdims=True
    )
    return (grad_in, jnp.sum(grad_out * tensor * scale_rows, axis=0))


def dsilu(tensor):
    sig_part = jax.nn.sigmoid(tensor)
    return sig_part * (1.0 + tensor * (1.0 - sig_part))


def combine_states(earlier, later):
    return (earlier[0] * later[1][:, None, None] + later[0], earlier[1] * later[1])


def ssd_spans(state, ssm_x, ssm_b, ssm_c, step_size, log_decay, skip_scale, seg_ids, before):
    count = ssm_x.shape[0] // SPAN
    prev_seg = jnp.concatenate([before.reshape(1), seg_ids[:-1]])

    def by_span(tensor):
        return tensor.reshape((count, SPAN) + tensor.shape[1:])

    def span_step(state_acc, pieces):
        x_c, b_c, c_c, dt_c, la_c, s_c, p_c = pieces
        cum_decay = jnp.cumsum(la_c, axis=0)
        order = jnp.arange(SPAN)
        same_mask = (s_c[:, None] == s_c[None, :]) & (order[:, None] >= order[None, :])
        differ = cum_decay.T[:, :, None] - cum_decay.T[:, None, :]
        decay_mat = jnp.exp(jnp.where(same_mask[None], differ, NEG))
        inner = jnp.dot(c_c, b_c.T, precision=HIGH)
        mixing = decay_mat * inner[None] * dt_c.T[:, None, :]
        y_inner = jnp.einsum("hpq,qhd->phd", mixing, x_c, precision=HIGH)
        alive = (s_c == p_c[0]).astype(jnp.float32)
        carried = jnp.exp(cum_decay) * alive[:, None]
        y_state = jnp.einsum("hdn,pn->phd", state_acc, c_c, precision=HIGH) * carried[:, :, None]
        y_span = y_inner + y_state + skip_scale[None, :, None] * x_c
        tail_w = (
            jnp.exp(cum_decay[-1][None, :] - cum_decay)
            * (s_c == s_c[-1]).astype(jnp.float32)[:, None]
            * dt_c
        )
        new_state = state_acc * carried[-1][:, None, None] + jnp.einsum(
            "qh,qhd,qn->hdn", tail_w, x_c, b_c, precision=HIGH
        )
        return (new_state, y_span)

    final_state, ys = lax.scan(
        span_step,
        state,
        (
            by_span(ssm_x),
            by_span(ssm_b),
            by_span(ssm_c),
            by_span(step_size),
            by_span(log_decay),
            by_span(seg_ids),
            by_span(prev_seg),
        ),
    )
    return (ys.reshape(ssm_x.shape), final_state)


def on_device(
    hidden_in,
    cotangent,
    doc_starts,
    valid_mask,
    norm_one,
    in_proj,
    conv_weight,
    conv_bias,
    dt_bias,
    a_log,
    skip_scale,
    gated_gain,
    qkv_proj,
    ssm_out,
    attn_out,
    norm_two,
    gate_up,
    down_proj,
):
    tok_rows = hidden_in.shape[0]
    shard_count = lax.axis_size("shard")
    offset = lax.axis_index("shard") * tok_rows
    seq_len = tok_rows * shard_count
    score_scale = 1.0 / math.sqrt(HD)
    q_per_kv = QH // KVH
    starts_row = doc_starts[0]
    positions = offset + jnp.arange(tok_rows, dtype=jnp.int32)
    seg_ids = segment_of(positions, starts_row)
    before = segment_of(positions[:1] - 1, starts_row)[0]
    first_start = jnp.max(jnp.where(starts_row <= positions[0], starts_row, 0))
    last_pos = positions[-1]
    full_weights = (
        lax.all_gather(in_proj, "shard", axis=0, tiled=True),
        lax.all_gather(qkv_proj, "shard", axis=0, tiled=True),
        lax.all_gather(ssm_out, "shard", axis=0, tiled=True),
        lax.all_gather(attn_out, "shard", axis=0, tiled=True),
        lax.all_gather(gate_up, "shard", axis=0, tiled=True),
        lax.all_gather(down_proj, "shard", axis=0, tiled=True),
    )
    f_in, f_attn, f_mo, f_ao, f_gu, f_down = full_weights
    x_full = hidden_in.astype(jnp.float32)
    r_one = rms_scale(x_full)
    h_low = (x_full * r_one * norm_one).astype(jnp.bfloat16)
    proj_out = jnp.dot(h_low, f_in, preferred_element_type=jnp.float32)
    gate_z = proj_out[:, :DS]
    xbc = proj_out[:, DS : DS + CONV_CH]
    dt_raw = proj_out[:, DS + CONV_CH :]
    edge_rows = from_behind(xbc[tok_rows - (KC - 1) :], "shard", 1)
    padded = jnp.concatenate([edge_rows, xbc], axis=0)
    pad_pos = positions[0] - (KC - 1) + jnp.arange(tok_rows + KC - 1, dtype=jnp.int32)
    pad_seg = segment_of(pad_pos, starts_row)
    tap_masks = [
        (pad_seg[tap_index : tap_index + tok_rows] == seg_ids).astype(jnp.float32)[:, None]
        for tap_index in range(KC)
    ]
    conv_pre = jnp.zeros((tok_rows, CONV_CH), jnp.float32) + conv_bias[None, :]
    for tap_index in range(KC):
        conv_pre = (
            conv_pre
            + conv_weight[:, tap_index][None, :]
            * padded[tap_index : tap_index + tok_rows]
            * tap_masks[tap_index]
        )
    conv_act = jax.nn.silu(conv_pre)
    ssm_x = conv_act[:, :DS].reshape(tok_rows, NH, HP)
    ssm_b = conv_act[:, DS : DS + NS]
    ssm_c = conv_act[:, DS + NS :]
    soft_in = dt_raw + dt_bias
    step_size = jax.nn.softplus(soft_in)
    decay_rate = jnp.exp(a_log)
    log_decay = -step_size * decay_rate
    empty_state = jnp.zeros((NH, HP, NS), jnp.float32)

    def carry_factor(log_vals):
        return (
            jnp.exp(jnp.cumsum(log_vals, axis=0)) * (seg_ids == before).astype(jnp.float32)[:, None]
        )

    def carry_term(state_in, c_vals, factor):
        return jnp.einsum("hdn,pn->phd", state_in, c_vals, precision=HIGH) * factor[:, :, None]

    ssm_zero, local_state = ssd_spans(
        empty_state, ssm_x, ssm_b, ssm_c, step_size, log_decay, skip_scale, seg_ids, before
    )
    factor = carry_factor(log_decay)
    dev_decay = factor[-1]
    state_in, unused_decay = carried_in(
        (local_state, dev_decay),
        "shard",
        combine_states,
        (jnp.zeros_like(local_state), jnp.ones_like(dev_decay)),
    )
    ssm_y = (ssm_zero + carry_term(state_in, ssm_c, factor)).reshape(tok_rows, DS)
    silu_z = jax.nn.silu(gate_z)
    gated = ssm_y * silu_z
    r_gate = rms_scale(gated)
    normed_low = (gated * r_gate * gated_gain).astype(jnp.bfloat16)
    qkv = jnp.dot(h_low, f_attn, preferred_element_type=jnp.float32)
    cosines, sines = rope_tables(positions)
    q_low = (
        rotate(qkv[:, :QW], QH, cosines, sines)
        .astype(jnp.bfloat16)
        .reshape(tok_rows, KVH, q_per_kv, HD)
    )
    k_low = rotate(qkv[:, QW : QW + KW], KVH, cosines, sines).astype(jnp.bfloat16)
    v_low = qkv[:, QW + KW :].astype(jnp.bfloat16)
    key_all, value_all = (
        lax.all_gather(k_low, "shard", axis=0, tiled=True),
        lax.all_gather(v_low, "shard", axis=0, tiled=True),
    )
    key_all = key_all.reshape(seq_len, KVH, HD)
    value_all = value_all.reshape(seq_len, KVH, HD)
    key_pos = jnp.arange(seq_len, dtype=jnp.int32)
    key_seg = segment_of(key_pos, starts_row)
    block_count = seq_len // KBLK
    row_shape = (KVH, q_per_kv, tok_rows)

    def needed(blk_index):
        low_edge = blk_index * KBLK
        return (low_edge <= last_pos) & (low_edge + KBLK > first_start)

    def block_keys(blk_index):
        return (
            lax.dynamic_slice_in_dim(key_all, blk_index * KBLK, KBLK, 0),
            lax.dynamic_slice_in_dim(value_all, blk_index * KBLK, KBLK, 0),
        )

    def block_scores(blk_index, k_blk):
        pos_blk = lax.dynamic_slice_in_dim(key_pos, blk_index * KBLK, KBLK, 0)
        seg_blk = lax.dynamic_slice_in_dim(key_seg, blk_index * KBLK, KBLK, 0)
        raw_scores = (
            jnp.einsum("tgqd,kgd->gqtk", q_low, k_blk, preferred_element_type=jnp.float32)
            * score_scale
        )
        key_mask = (pos_blk[None, :] <= positions[:, None]) & (seg_blk[None, :] == seg_ids[:, None])
        return (raw_scores, key_mask[None, None])

    def unchanged(passed):
        return passed

    def lse_step(blk_index, state_acc):

        def lse_do_block(state_acc):
            row_top, row_total = state_acc
            k_blk, v_blk = block_keys(blk_index)
            raw_scores, key_mask = block_scores(blk_index, k_blk)
            new_top = jnp.maximum(row_top, jnp.max(jnp.where(key_mask, raw_scores, NEG), axis=-1))
            row_total = row_total * jnp.exp(row_top - new_top) + jnp.sum(
                jnp.where(key_mask, jnp.exp(raw_scores - new_top[..., None]), 0.0), axis=-1
            )
            return (new_top, row_total)

        return lax.cond(needed(blk_index), lse_do_block, unchanged, state_acc)

    row_top, row_total = lax.fori_loop(
        0,
        block_count,
        lse_step,
        (jnp.full(row_shape, NEG, jnp.float32), jnp.zeros(row_shape, jnp.float32)),
    )
    log_total = row_top + jnp.log(row_total)

    def probs_of(blk_index, k_blk):
        raw_scores, key_mask = block_scores(blk_index, k_blk)
        return jnp.where(key_mask, jnp.exp(raw_scores - log_total[..., None]), 0.0)

    def out_step(blk_index, acc_out):

        def out_do_block(acc_out):
            k_blk, v_blk = block_keys(blk_index)
            prob_blk = probs_of(blk_index, k_blk).astype(jnp.bfloat16)
            return acc_out + jnp.einsum(
                "gqtk,kgd->tgqd", prob_blk, v_blk, preferred_element_type=jnp.float32
            )

        return lax.cond(needed(blk_index), out_do_block, unchanged, acc_out)

    attended = lax.fori_loop(
        0, block_count, out_step, jnp.zeros((tok_rows, KVH, q_per_kv, HD), jnp.float32)
    )
    attn_low = attended.reshape(tok_rows, QW).astype(jnp.bfloat16)
    mixed = jnp.dot(normed_low, f_mo, preferred_element_type=jnp.float32) + jnp.dot(
        attn_low, f_ao, preferred_element_type=jnp.float32
    )
    residual = x_full + mixed
    r_two = rms_scale(residual)
    h2_low = (residual * r_two * norm_two).astype(jnp.bfloat16)
    gate_vals = jnp.dot(h2_low, f_gu, preferred_element_type=jnp.float32)
    gate_part = gate_vals[:, :FF]
    up_part = gate_vals[:, FF:]
    hid_low = (jax.nn.silu(gate_part) * up_part).astype(jnp.bfloat16)
    mlp_out = jnp.dot(hid_low, f_down, preferred_element_type=jnp.float32)
    out_full = residual + mlp_out
    keep_rows = valid_mask.astype(jnp.float32)
    stat_local = jnp.stack(
        [
            jnp.sum(keep_rows * jnp.sum(out_full * out_full, axis=1)),
            jnp.sum(keep_rows * jnp.sum(mixed * mixed, axis=1)),
            jnp.sum(keep_rows * jnp.sum(mlp_out * mlp_out, axis=1)),
            jnp.sum(keep_rows),
        ]
    )
    back_weights = (
        lax.all_gather(in_proj, "shard", axis=0, tiled=True),
        lax.all_gather(qkv_proj, "shard", axis=0, tiled=True),
        lax.all_gather(ssm_out, "shard", axis=0, tiled=True),
        lax.all_gather(attn_out, "shard", axis=0, tiled=True),
        lax.all_gather(gate_up, "shard", axis=0, tiled=True),
        lax.all_gather(down_proj, "shard", axis=0, tiled=True),
    )
    b_in, b_attn, b_mo, b_ao, b_gu, b_down = back_weights
    grad_out = cotangent.astype(jnp.float32) * keep_rows[:, None]
    grad_mlp = grad_out.astype(jnp.bfloat16)
    g_down = jnp.dot(hid_low.T, grad_mlp, preferred_element_type=jnp.float32)
    grad_hid = jnp.dot(grad_mlp, b_down.T, preferred_element_type=jnp.float32)
    grad_gu = jnp.concatenate(
        [grad_hid * up_part * dsilu(gate_part), grad_hid * jax.nn.silu(gate_part)], axis=1
    ).astype(jnp.bfloat16)
    g_gu = jnp.dot(h2_low.T, grad_gu, preferred_element_type=jnp.float32)
    grad_h2 = jnp.dot(grad_gu, b_gu.T, preferred_element_type=jnp.float32)
    grad_res_n, g_norm_two = norm_back(grad_h2, residual, r_two, norm_two)
    grad_res = grad_out + grad_res_n
    grad_mix = grad_res.astype(jnp.bfloat16)
    g_mo = jnp.dot(normed_low.T, grad_mix, preferred_element_type=jnp.float32)
    g_ao = jnp.dot(attn_low.T, grad_mix, preferred_element_type=jnp.float32)
    grad_normed = jnp.dot(grad_mix, b_mo.T, preferred_element_type=jnp.float32)
    grad_attn = (
        jnp.dot(grad_mix, b_ao.T, preferred_element_type=jnp.float32)
        .astype(jnp.bfloat16)
        .reshape(tok_rows, KVH, q_per_kv, HD)
    )

    def delta_step(blk_index, acc_out):

        def delta_do_block(acc_out):
            k_blk, v_blk = block_keys(blk_index)
            prob_blk = probs_of(blk_index, k_blk)
            grad_prob = jnp.einsum(
                "tgqd,kgd->gqtk", grad_attn, v_blk, preferred_element_type=jnp.float32
            )
            return acc_out + jnp.sum(prob_blk * grad_prob, axis=-1)

        return lax.cond(needed(blk_index), delta_do_block, unchanged, acc_out)

    delta_row = lax.fori_loop(0, block_count, delta_step, jnp.zeros(row_shape, jnp.float32))

    def grad_step(blk_index, state_acc):

        def grad_do_block(state_acc):
            grad_query, grad_kv = state_acc
            k_blk, v_blk = block_keys(blk_index)
            prob_blk = probs_of(blk_index, k_blk)
            grad_prob = jnp.einsum(
                "tgqd,kgd->gqtk", grad_attn, v_blk, preferred_element_type=jnp.float32
            )
            grad_raw = (prob_blk * (grad_prob - delta_row[..., None]) * score_scale).astype(
                jnp.bfloat16
            )
            grad_query = grad_query + jnp.einsum(
                "gqtk,kgd->tgqd", grad_raw, k_blk, preferred_element_type=jnp.float32
            )
            grad_key = jnp.einsum(
                "gqtk,tgqd->kgd", grad_raw, q_low, preferred_element_type=jnp.float32
            )
            grad_value = jnp.einsum(
                "gqtk,tgqd->kgd",
                prob_blk.astype(jnp.bfloat16),
                grad_attn,
                preferred_element_type=jnp.float32,
            )
            kv_piece = jnp.concatenate(
                [grad_key.reshape(KBLK, KW), grad_value.reshape(KBLK, KW)], axis=1
            )
            grad_kv = lax.dynamic_update_slice_in_dim(grad_kv, kv_piece, blk_index * KBLK, 0)
            return (grad_query, grad_kv)

        return lax.cond(needed(blk_index), grad_do_block, unchanged, state_acc)

    grad_query, grad_kv = lax.fori_loop(
        0,
        block_count,
        grad_step,
        (
            jnp.zeros((tok_rows, KVH, q_per_kv, HD), jnp.float32),
            jnp.zeros((seq_len, 2 * KW), jnp.float32),
        ),
    )
    own_kv = lax.psum_scatter(grad_kv, "shard", scatter_dimension=0, tiled=True)
    neg_sines = -sines
    grad_q_raw = rotate(grad_query.reshape(tok_rows, QW), QH, cosines, neg_sines)
    grad_k_raw = rotate(own_kv[:, :KW], KVH, cosines, neg_sines)
    grad_qkv = jnp.concatenate([grad_q_raw, grad_k_raw, own_kv[:, KW:]], axis=1).astype(
        jnp.bfloat16
    )
    g_attn = jnp.dot(h_low.T, grad_qkv, preferred_element_type=jnp.float32)
    grad_h_attn = jnp.dot(grad_qkv, b_attn.T, preferred_element_type=jnp.float32)
    grad_gated, g_gated_gain = norm_back(grad_normed, gated, r_gate, gated_gain)
    grad_y = (grad_gated * silu_z).reshape(tok_rows, NH, HP)
    grad_z = grad_gated * ssm_y * dsilu(gate_z)

    def mamba_out(state_start, x_vals, b_vals, c_vals, dt_vals, la_vals, skip_vals):
        y_zero, state_local = ssd_spans(
            empty_state, x_vals, b_vals, c_vals, dt_vals, la_vals, skip_vals, seg_ids, before
        )
        fac_vals = carry_factor(la_vals)
        return (
            y_zero + carry_term(state_start, c_vals, fac_vals),
            state_local + state_start * fac_vals[-1][:, None, None],
        )

    unused_out, pull_back = jax.vjp(
        mamba_out, state_in, ssm_x, ssm_b, ssm_c, step_size, log_decay, skip_scale
    )
    first_pull = pull_back((grad_y, jnp.zeros_like(state_in)))
    later_state, unused_later = entering(
        (first_pull[0], dev_decay),
        "shard",
        combine_states,
        (jnp.zeros_like(state_in), jnp.ones_like(dev_decay)),
    )
    second = pull_back((jnp.zeros_like(grad_y), later_state))
    grad_x = first_pull[1] + second[1]
    grad_b = first_pull[2] + second[2]
    grad_c = first_pull[3] + second[3]
    grad_dt = first_pull[4] + second[4]
    grad_la = first_pull[5] + second[5]
    g_skip = first_pull[6] + second[6]
    g_a_log = jnp.sum(-grad_la * step_size * decay_rate, axis=0)
    grad_soft = (grad_dt - grad_la * decay_rate) * jax.nn.sigmoid(soft_in)
    g_dt_bias = jnp.sum(grad_soft, axis=0)
    grad_act = jnp.concatenate([grad_x.reshape(tok_rows, DS), grad_b, grad_c], axis=1)
    grad_conv = grad_act * dsilu(conv_pre)
    g_conv_bias = jnp.sum(grad_conv, axis=0)
    grad_padded = jnp.zeros((tok_rows + KC - 1, CONV_CH), jnp.float32)
    weight_cols = []
    for tap_index in range(KC):
        term_vals = grad_conv * tap_masks[tap_index]
        grad_padded = grad_padded + jnp.pad(
            term_vals * conv_weight[:, tap_index][None, :],
            ((tap_index, KC - 1 - tap_index), (0, 0)),
        )
        weight_cols.append(jnp.sum(term_vals * padded[tap_index : tap_index + tok_rows], axis=0))
    g_conv_weight = jnp.stack(weight_cols, axis=1)
    back_edge = from_behind(grad_padded[: KC - 1], "shard", -1)
    grad_xbc = grad_padded[KC - 1 :] + jnp.concatenate(
        [jnp.zeros((tok_rows - (KC - 1), CONV_CH), jnp.float32), back_edge], axis=0
    )
    grad_proj = jnp.concatenate([grad_z, grad_xbc, grad_soft], axis=1).astype(jnp.bfloat16)
    g_in = jnp.dot(h_low.T, grad_proj, preferred_element_type=jnp.float32)
    grad_h = jnp.dot(grad_proj, b_in.T, preferred_element_type=jnp.float32) + grad_h_attn
    grad_x_n, g_norm_one = norm_back(grad_h, x_full, r_one, norm_one)
    grad_input = grad_res + grad_x_n
    owned_grads = (
        lax.psum_scatter(g_in, "shard", scatter_dimension=0, tiled=True),
        lax.psum_scatter(g_attn, "shard", scatter_dimension=0, tiled=True),
        lax.psum_scatter(g_mo, "shard", scatter_dimension=0, tiled=True),
        lax.psum_scatter(g_ao, "shard", scatter_dimension=0, tiled=True),
        lax.psum_scatter(g_gu, "shard", scatter_dimension=0, tiled=True),
        lax.psum_scatter(g_down, "shard", scatter_dimension=0, tiled=True),
    )
    summed = lax.psum(
        (
            owned_grads[0],
            owned_grads[1],
            owned_grads[2],
            owned_grads[3],
            owned_grads[4],
            owned_grads[5],
        ),
        "replica",
    )
    small_sums = lax.psum(
        (
            g_norm_one,
            g_conv_weight,
            g_conv_bias,
            g_dt_bias,
            g_a_log,
            g_skip,
            g_gated_gain,
            g_norm_two,
            stat_local,
        ),
        ("replica", "shard"),
    )
    stat_sums = small_sums[8]
    rms_stats = jnp.sqrt(stat_sums[:3] / (stat_sums[3] * D))
    return (
        out_full.astype(jnp.bfloat16),
        grad_input,
        small_sums[0],
        summed[0],
        small_sums[1],
        small_sums[2],
        small_sums[3],
        small_sums[4],
        small_sums[5],
        small_sums[6],
        summed[1],
        summed[2],
        summed[3],
        small_sums[7],
        summed[4],
        summed[5],
        rms_stats,
    )


HEADS_AT = 6
XW = HEADS_AT * HP
LANES = 128
TB = 128
VMEM_BYTES = 20 * 1024 * 1024
AT_Y, AT_CORE, AT_BIT, AT_STARTS = 0, 1, {1: 2, 2: 3, 4: 4}, 5
Q_AT = XW
KV_AT = Q_AT + QW // 4
BC_AT = KV_AT + LANES
DT_AT = BC_AT + 2 * NS
W_FIRST = DT_AT + LANES
W_SENT = DT_AT + 32
LOW = jnp.bfloat16
F32 = jnp.float32


def swap(block, bits):
    return lax.ppermute(block, "shard", [(i, i ^ bits) for i in range(lax.axis_size("shard"))])


def swap_far(block, bits):
    replicas, shards = lax.axis_size("replica"), lax.axis_size("shard")
    route = [
        (r * shards + s, (r ^ bits[s % 2]) * shards + s)
        for r in range(replicas)
        for s in range(shards)
    ]
    return lax.ppermute(block, ("replica", "shard"), route)


def after(value, other):
    return lax.optimization_barrier((value, other))[0]


def dot32(a, b):
    return jnp.dot(a, b, preferred_element_type=F32)


def dot_t(a, b):
    return lax.dot_general(a, b, (((1,), (1,)), ((), ())), preferred_element_type=F32)


def t_dot(a, b):
    return lax.dot_general(a, b, (((0,), (0,)), ((), ())), preferred_element_type=F32)


def rough(a, b, dims=((1,), (0,))):
    return lax.dot_general(
        a.astype(LOW), b.astype(LOW), (dims, ((), ())), preferred_element_type=F32
    )


def fair(a, b, dims=((1,), (0,))):
    a_high, b_high = a.astype(LOW), b.astype(LOW)
    a_low = (a - a_high.astype(F32)).astype(LOW)
    b_low = (b - b_high.astype(F32)).astype(LOW)

    def dot(x, y):
        return lax.dot_general(x, y, (dims, ((), ())), preferred_element_type=F32)

    return dot(a_high, b_high) + (dot(a_high, b_low) + dot(a_low, b_high))


def picked(a, b, dims=((1,), (0,)), terms=2):
    value, total = (b, 0.0) if a.dtype == LOW else (a, 0.0)
    for _ in range(terms):
        low = value.astype(LOW)
        pair = (a, low) if a.dtype == LOW else (low, b)
        total = total + lax.dot_general(*pair, (dims, ((), ())), preferred_element_type=F32)
        value = value - low.astype(F32)
    return total


def iota(shape, axis):
    return lax.broadcasted_iota(jnp.int32, shape, axis)


def count_starts(info, where):
    total = (info[AT_STARTS] <= where).astype(jnp.int32)
    for k in range(AT_STARTS + 1, info.shape[0]):
        total = total + (info[k] <= where).astype(jnp.int32)
    return total


def part(index, size):
    return pl.ds(pl.multiple_of(index * size, size), size)


def part_at(start, index, step, size):
    return pl.ds(pl.multiple_of(start + index * step, LANES), size)


def peers(info):
    y, c = info[AT_Y], info[AT_CORE]
    return (2 * y + c, 2 * y + 1 - c, 2 * (1 - y) + c, 2 * (1 - y) + 1 - c)


def bit_of(info, bits):
    return jnp.where(info[AT_CORE] == 0, info[AT_BIT[bits[0]]], info[AT_BIT[bits[1]]])


def f32_of(*shape):
    return jax.ShapeDtypeStruct(shape, F32)


def low_of(*shape):
    return jax.ShapeDtypeStruct(shape, LOW)


def call(kernel, outs, info, *operands, scratch=()):
    whole = pl.BlockSpec(memory_space=pltpu.VMEM)
    return pl.pallas_call(
        kernel,
        out_shape=outs,
        in_specs=[pl.BlockSpec(memory_space=pltpu.SMEM)] + [whole] * len(operands),
        out_specs=jax.tree.map(lambda _: whole, outs),
        scratch_shapes=scratch,
        compiler_params=pltpu.CompilerParams(vmem_limit_bytes=VMEM_BYTES),
    )(info, *operands)


def pack_in_kernel(info, w_in, w_qkv, own, core, far, z_own, z_core, z_far):
    y, places = info[AT_Y], peers(info)

    def shared(dst, chip):
        k, v = w_qkv[:, QW : QW + KW], w_qkv[:, QW + KW :]
        first = jnp.concatenate([k[:, :HD], v[:, :HD]], axis=1)
        second = jnp.concatenate([k[:, HD:], v[:, HD:]], axis=1)
        dst[KV_AT:BC_AT, :] = jnp.where(chip == 0, first, second).T
        dst[BC_AT:DT_AT, :] = w_in[2 * DS : 2 * DS + 2 * NS, :]
        dst[DT_AT:W_SENT, :] = jnp.zeros((W_SENT - DT_AT, dst.shape[1]), LOW)
        dst[DT_AT : DT_AT + NH, :] = w_in[DS + CONV_CH :, :]

    for place, dst, at in zip(places, (own, core, far, far), (0, 0, W_SENT, 0)):
        dst[at : at + XW, :] = w_in[part_at(DS, place, XW, XW), :]
        dst[at + XW : at + KV_AT, :] = w_qkv[:, part(place, QW // 4)].T
    for place, dst, at in zip(places, (z_own, z_core, z_far, z_far), (0, 0, XW, 0)):
        dst[at : at + XW, :] = w_in[part_at(0, place, XW, XW), :]
    shared(own, y)
    shared(core, y)
    shared(far, 1 - y)


def prepare_kernel(
    info, conv_weight, conv_bias, dt_bias, a_log, skip, gain, norm_one, norm_two, mask, cotangent,
    taps, bias, bias_own, rate, skip_wide, gain_own, gain_one, gain_two, keep, grad, turn, wide,
):
    place = peers(info)[0]
    for src, dst in ((conv_weight, taps), (conv_bias, bias)):
        dst[:, :XW] = src[:, part(place, XW)]
        dst[:, XW:] = src[:, DS:]
    gain_own[...] = gain[:, part(place, XW)]
    gain_one[...] = norm_one[...]
    gain_two[...] = norm_two[...]
    pick = own_heads_pick(info)
    wide[...] = jnp.zeros_like(wide)
    for k, src in enumerate((dt_bias, a_log, skip)):
        wide[k : k + 1, :NH] = src[...]
    own = picked(wide[...], pick, terms=3)
    bias_own[...] = own[0:1]
    rate[...] = jnp.exp(own[1:2])
    skip_wide[...] = picked(own, head_spread(), terms=3)[2:3]
    column = jnp.broadcast_to(mask[...].astype(F32), (LANES, LANES)).T
    keep[...] = column
    grad[...] = (cotangent[...].astype(F32) * column[:, :1]).astype(LOW)
    row, col, half = iota((LANES, LANES), 0), iota((LANES, LANES), 1), HD // 2
    down, up = (row == col + half).astype(F32), (row == col - half).astype(F32)
    turn[...] = jnp.where((col // half) % 2 == 0, -down, up).astype(LOW)


def total_kernel(info, a, b, out):
    out[...] = a[...] + b[...]


def pack_up_kernel(info, w_up, own, core, far):
    quarter, half = FF // 4, w_up.shape[0] // 2
    places = peers(info)
    for place, dst in zip(places, (own, core)):
        dst[:, :quarter] = w_up[:, part_at(0, place, quarter, quarter)]
        dst[:, quarter:] = w_up[:, part_at(FF, place, quarter, quarter)]
    mine = part(info[AT_BIT[1]], half)
    for k, place in enumerate(places[2:]):
        rows = slice(k * half, (k + 1) * half)
        far[rows, :quarter] = w_up[mine, part_at(0, place, quarter, quarter)]
        far[rows, quarter:] = w_up[mine, part_at(FF, place, quarter, quarter)]


def head_spread():
    row, col = iota((LANES, XW), 0), iota((LANES, XW), 1)
    return ((col >= row * HP) & (col < (row + 1) * HP)).astype(LOW)


def own_heads_pick(info):
    row, col = iota((LANES, LANES), 0), iota((LANES, LANES), 1)
    return ((row == col + peers(info)[0] * HEADS_AT) & (col < HEADS_AT)).astype(LOW)


def step_sizes(soft):
    real = iota(soft.shape, 1) < HEADS_AT
    return jnp.where(real, jnp.maximum(soft, 0.0) + jnp.log1p(jnp.exp(-jnp.abs(soft))), 0.0)


def span_parts(info, first, dt, la):
    shape = (SPAN, SPAN)
    row, col = iota(shape, 0), iota(shape, 1)
    seg_row = count_starts(info, row + first)
    seg_col = count_starts(info, col + first)
    seen = (seg_row == seg_col) & (row >= col)
    before = count_starts(info, first - 1)
    last = count_starts(info, first + SPAN - 1)
    total = picked((row >= col).astype(LOW), la, terms=3)
    carried = jnp.exp(total) * (seg_row == before).astype(F32)
    tail = jnp.exp(total[SPAN - 1 :] - total) * (seg_row == last).astype(F32)
    return seen, total, total.T, dt.T, carried, tail


def decay_of(seen, total, total_t, h):
    return jnp.exp(jnp.where(seen, total[:, h : h + 1] - total_t[h : h + 1, :], NEG))


def tap_masks(info, seg):
    seq = seg.shape[0] - 8
    seg[:8, :] = jnp.full((8, LANES), -1, jnp.int32)
    seg[8:, :] = count_starts(info, iota((seq, LANES), 0))
    here = seg[8:, :]
    return [
        (seg[8 - back : 8 - back + seq, :] == here).astype(F32) for back in range(KC - 1, 0, -1)
    ]


def forward_kernel(
    info, h_own, h_core, h_far, h_far_core, w_own, w_core, w_far, w_far_core,
    norm, taps, bias, dt_bias, rate, skip, cosines, sines, turn,
    h_low, w_full, xbc, conv_pre, soft, q_low, kv_low, y_out, states,
    padded, act, step, seg,
):
    seq = h_low.shape[0]
    places = peers(info)
    for place, ref in zip(places, (h_own, h_core, h_far, h_far_core)):
        x = ref[...].astype(F32)
        h_low[part(place, TB), :] = (x * rms_scale(x) * norm[...]).astype(LOW)
    depth = w_own.shape[1]
    for place, ref, at in zip(places, (w_own, w_core, w_far, w_far_core), (0, 0, W_SENT, 0)):
        w_full[:KV_AT, part(place, depth)] = ref[at : at + KV_AT, :]
        w_full[KV_AT:W_SENT, part(place, depth)] = ref[KV_AT:W_SENT, :]
    w_full[W_SENT:, :] = jnp.zeros((W_FIRST - W_SENT, w_full.shape[1]), LOW)
    h = h_low[...]
    xbc[:, :XW] = dot_t(h, w_full[:XW, :])
    xbc[:, XW:] = dot_t(h, w_full[BC_AT:DT_AT, :])
    rest = dot_t(h, w_full[Q_AT:BC_AT, :])
    q, kv = rest[:, :LANES], rest[:, LANES:]
    soft[...] = picked(dot_t(h, w_full[DT_AT:, :]), own_heads_pick(info), terms=3) + dt_bias[...]

    def turned(value):
        return value * cosines[...] + picked(value, turn[...]) * sines[...]

    q_low[...] = turned(q).astype(LOW)
    kv_low[...] = jnp.where(iota(kv.shape, 1) < HD, turned(kv), kv).astype(LOW)

    width = xbc.shape[1]
    padded[:8, :] = jnp.zeros((8, width), F32)
    padded[8:, :] = xbc[...]
    masks = tap_masks(info, seg)
    for block in range(0, width, LANES):
        lanes = slice(block, block + LANES)
        total = bias[:, lanes] + taps[KC - 1 : KC, lanes] * padded[8:, lanes]
        for j in range(KC - 1):
            start = 8 - (KC - 1 - j)
            total = total + taps[j : j + 1, lanes] * padded[start : start + seq, lanes] * masks[j]
        conv_pre[:, lanes] = total
        act[:, lanes] = total * jax.nn.sigmoid(total)

    step[...] = step_sizes(soft[...])
    spread = head_spread()
    state = jnp.zeros((NS, XW), F32)
    for k in range(seq // SPAN):
        rows = pl.ds(k * SPAN, SPAN)
        x = act[rows, :XW]
        b = act[rows, XW : XW + NS]
        c = act[rows, XW + NS :]
        dt = step[rows, :]
        seen, total, total_t, dt_t, carried, tail = span_parts(
            info, k * SPAN, dt, -dt * rate[...]
        )
        states[k] = state
        inner = fair(c, b, ((1,), (1,)))
        wide = picked(carried, spread)
        y = fair(c, state) * wide + x * skip[...]
        parts = []
        for h in range(HEADS_AT):
            mixing = decay_of(seen, total, total_t, h) * inner * dt_t[h : h + 1, :]
            parts.append(fair(mixing, x[:, h * HP : (h + 1) * HP]))
        y_out[rows, :] = y + jnp.concatenate(parts, axis=1)
        weighted = x * picked(tail * dt, spread)
        state = state * wide[SPAN - 1 :] + fair(b, weighted, ((0,), (0,)))


def gate_kernel(info, h_low, z_own, z_core, z_far, z_far_core, y, z_full, gate_z, square):
    depth = z_own.shape[1]
    for place, ref, at in zip(peers(info), (z_own, z_core, z_far, z_far_core), (0, 0, XW, 0)):
        z_full[:, part(place, depth)] = ref[at : at + XW, :]
    z = dot_t(h_low[...], z_full[...])
    gate_z[...] = z
    gated = y[...] * (z * jax.nn.sigmoid(z))
    square[...] = picked(jnp.ones((8, XW), LOW), gated * gated, ((1,), (1,)))


def column_of(row):
    return jnp.concatenate(
        [row[:, k : k + LANES].T[:, :1] for k in range(0, row.shape[1], LANES)], axis=0
    )


def output_kernel(
    info, sq_a, sq_b, y, gate_z, gain, attn, ssm_out, attn_out, given, kept, normed
):
    z = gate_z[...]
    scale = lax.rsqrt(column_of(sq_a[...] + sq_b[...]) / DS + EPS)
    normed[...] = (y[...] * (z * jax.nn.sigmoid(z)) * scale * gain[...]).astype(LOW)
    c = info[AT_CORE]
    for core, dst in ((1 - c, given), (c, kept)):
        for k in range(2):
            rows = part(2 * k + core, TB)
            dst[k] = dot32(normed[rows, :], ssm_out[...]) + dot32(attn[rows, :], attn_out[...])


def add_kernel(info, kept, moved, chip, low):
    total = kept[...] + moved[...]
    chip[...] = total
    low[...] = total.astype(LOW)


def add_split_kernel(info, kept, moved, mine, given):
    y = info[AT_Y]
    mine[...] = kept[y] + moved[y]
    given[...] = kept[1 - y] + moved[1 - y]


def pair_of(info, own, far, dst):
    y = info[AT_Y]
    dst[y] = own[...]
    dst[1 - y] = far[...]


def second_norm_kernel(
    info, chip, moved, h_own, h_far, norm, keep, residual, h2, mixed_sum, x_pair
):
    pair_of(info, h_own, h_far, x_pair)
    mixed = chip[...] + moved[...].astype(F32)
    total = x_pair[...].astype(F32) + mixed
    residual[...] = total
    h2[...] = (total * rms_scale(total) * norm[...]).astype(LOW)
    mine = (chip[info[AT_Y]] + moved[info[AT_Y]].astype(F32)) * keep[:, :1]
    mixed_sum[...] = jnp.sum(mine * mine, axis=0, keepdims=True)


def mlp_kernel(
    info, h2, h2_core, u_own, u_core, u_y, u_x, u_y_core, u_x_core, g_own, g_core, g_far, g_far_core, w_down,
    given, kept, hid, ggu, h2_cat, gmlp, u_full,
):
    y, quarter = info[AT_Y], FF // 4
    half = 2 * TB
    for k in range(2):
        h2_cat[k * TB : (k + 1) * TB, :] = h2[k]
        h2_cat[half + k * TB : half + (k + 1) * TB, :] = h2_core[k]
    for at, ref in ((y, g_own), (1 - y, g_far), (2 + y, g_core), (3 - y, g_far_core)):
        gmlp[part(at, TB), :] = ref[...]
    depth = u_own.shape[0]
    places, x, piece = peers(info), info[AT_BIT[1]], depth // 2
    u_full[part(places[0], depth), :] = u_own[...]
    u_full[part(places[1], depth), :] = u_core[...]
    for at, ref, ref_core in ((x, u_y, u_y_core), (1 - x, u_x, u_x_core)):
        u_full[part(2 * places[2] + at, piece), :] = ref[:piece, :]
        u_full[part(2 * places[3] + at, piece), :] = ref_core[piece:, :]
    tile = quarter // 2
    for t in range(0, quarter, tile):
        ghid = dot_t(gmlp[...], w_down[t : t + tile, :])
        gate = dot32(h2_cat[...], u_full[:, t : t + tile])
        up = dot32(h2_cat[...], u_full[:, quarter + t : quarter + t + tile])
        sig = jax.nn.sigmoid(gate)
        silu = gate * sig
        hid[:, t : t + tile] = (silu * up).astype(LOW)
        ggu[:, t : t + tile] = (ghid * up * (sig * (1.0 + gate * (1.0 - sig)))).astype(LOW)
        ggu[:, quarter + t : quarter + t + tile] = (ghid * silu).astype(LOW)
    for t in range(0, D, 2 * tile):
        cols = slice(t, t + 2 * tile)
        part_sum = dot_t(ggu[half:, :], u_full[cols, :])
        given[0, :, cols] = part_sum[:TB]
        given[1, :, cols] = part_sum[TB:]
        part_sum = dot_t(ggu[:half, :], u_full[cols, :])
        kept[0, :, cols] = part_sum[:TB]
        kept[1, :, cols] = part_sum[TB:]


def down_kernel(info, hid, w_down, given, kept):
    half = 2 * TB
    for k in range(2):
        given[k] = dot32(hid[half + k * TB : half + (k + 1) * TB, :], w_down[...])
        kept[k] = dot32(hid[k * TB : (k + 1) * TB, :], w_down[...])


def store_halves(mine, rows, first, given, kept):
    half = LANES // 2
    for k in range(rows.shape[0] // LANES):
        low, high = rows[k * LANES : k * LANES + half], rows[k * LANES + half : (k + 1) * LANES]
        given[first + k] = jnp.where(mine == 0, high, low).astype(LOW)
        kept[first + k] = jnp.where(mine == 0, low, high)


def grad_mlp_kernel(bits, info, h2, ggu, hid, gmlp, given, kept):
    mine, step = bit_of(info, bits), 2 * LANES
    for left, right, first in ((h2, ggu, 0), (hid, gmlp, D // LANES)):
        for at in range(0, left.shape[1], step):
            rows = t_dot(left[:, at : at + step], right[...])
            store_halves(mine, rows, first + at // LANES, given, kept)


def grad_mid_kernel(bits, info, normed, attn, gmix, given, kept):
    mine, first = bit_of(info, bits), 0
    for left, right in ((normed, gmix), (attn, gmix)):
        for at in range(0, left.shape[1], LANES):
            rows = t_dot(left[:, at : at + LANES], right[...])
            store_halves(mine, rows, first + at // LANES, given, kept)
        first += left.shape[1] // LANES


def norm_back_pair_kernel(info, chip, moved, residual, norm, g_own, g_far, gres, gmix, g_norm, gout):
    pair_of(info, g_own, g_far, gout)
    gh2 = chip[...] + moved[...].astype(F32)
    value = residual[...]
    scale = rms_scale(value)
    uu = gh2 * norm[...]
    mean = jnp.mean(uu * value, axis=-1, keepdims=True)
    grad = gout[...].astype(F32) + scale * uu - value * scale**3 * mean
    gres[...] = grad
    gmix[...] = grad.astype(LOW)
    y = info[AT_Y]
    mine = residual[y]
    g_norm[...] = jnp.sum(
        (chip[y] + moved[y].astype(F32)) * mine * rms_scale(mine), axis=0, keepdims=True
    )


def output_back_kernel(
    info, gmix, gmix_core, y, gate_z, gain, ssm_out, attn_out, gmix_all, gnormed, gattn, uv
):
    c = info[AT_CORE]
    for core, src in ((c, gmix), (1 - c, gmix_core)):
        for k in range(2):
            gmix_all[part(2 * k + core, TB), :] = src[k]
    grad = dot_t(gmix_all[...], ssm_out[...])
    gnormed[...] = grad
    z = gate_z[...]
    product = grad * gain[...] * (y[...] * (z * jax.nn.sigmoid(z)))
    uv[...] = picked(jnp.ones((8, XW), LOW), product, ((1,), (1,)))
    gattn[...] = dot_t(gmix_all[...], attn_out[...]).astype(LOW)


def conv_back(masks, gconv, slope, taps, inputs, gpad):
    seq = gconv.shape[0]
    gconv = gconv * slope
    gpad[seq:, :] = jnp.zeros((8, LANES), F32)
    total = taps[KC - 1] * gconv
    rows = []
    for j in range(KC - 1):
        back = KC - 1 - j
        term = gconv * masks[j]
        rows.append(jnp.sum(term * inputs(j), axis=0, keepdims=True))
        gpad[:seq, :] = term * taps[j]
        total = total + gpad[back : back + seq, :]
    rows.append(jnp.sum(gconv * inputs(KC - 1), axis=0, keepdims=True))
    rows.append(jnp.sum(gconv, axis=0, keepdims=True))
    return total, rows


def gate_back_kernel(
    info, sq_a, sq_b, uv_a, uv_b, gnormed, y, gate_z, gain, gzz, gy, g_gain
):
    z = gate_z[...]
    sig = jax.nn.sigmoid(z)
    gated = y[...] * (z * sig)
    scale = lax.rsqrt(column_of(sq_a[...] + sq_b[...]) / DS + EPS)
    mean = column_of(uv_a[...] + uv_b[...]) / DS
    grad = gnormed[...]
    ggz = scale * (grad * gain[...]) - gated * scale**3 * mean
    gy[...] = ggz * (z * sig)
    gzz[...] = (ggz * y[...] * (sig * (1.0 + z * (1.0 - sig)))).astype(LOW)
    g_gain[...] = jnp.sum(grad * gated * scale, axis=0, keepdims=True)


def scan_prepare_kernel(
    info, conv_pre, soft, rate, states,
    decay_dt, decay_in, act, slope, from_state, wide, wide_tail, tail_out, step,
):
    pre = conv_pre[...]
    sig = jax.nn.sigmoid(pre)
    act[...] = pre * sig
    slope[...] = sig * (1.0 + pre * (1.0 - sig))
    step[...] = step_sizes(soft[...])
    spread = head_spread()
    for k in range(states.shape[0]):
        rows = pl.ds(k * SPAN, SPAN)
        b = act[rows, XW : XW + NS]
        c = act[rows, XW + NS :]
        dt = step[rows, :]
        seen, total, total_t, dt_t, carried, tail = span_parts(
            info, k * SPAN, dt, -dt * rate[...]
        )
        inner = fair(c, b, ((1,), (1,)))
        for h in range(HEADS_AT):
            decay = decay_of(seen, total, total_t, h)
            decay_dt[k * HEADS_AT + h] = decay * dt_t[h : h + 1, :]
            decay_in[k * HEADS_AT + h] = decay * inner
        from_state[rows, :] = fair(c, states[k])
        wide[rows, :] = picked(carried, spread)
        wide_tail[rows, :] = picked(tail * dt, spread)
        tail_out[rows, :] = tail


def scan_back_kernel(
    info, xbc, soft, rate, skip, states, taps, gy,
    decay_dt, decay_in, act, slope, from_state, wide_all, wide_tail_all, tail_all, step,
    gx_low, gbc_given, gbc_kept, gdr, gsoft_low, g_taps, g_skip, g_heads,
    gact, gdt, gla, padded, gpad, seg,
):
    seq = gy.shape[0]
    spread = head_spread()
    shape = (SPAN, SPAN)
    row, col = iota(shape, 0), iota(shape, 1)
    upper = (col >= row).astype(LOW)
    later = jnp.zeros((NS, XW), F32)
    skip_sum = jnp.zeros((1, XW), F32)
    for k in reversed(range(seq // SPAN)):
        rows = pl.ds(k * SPAN, SPAN)
        x = act[rows, :XW]
        b = act[rows, XW : XW + NS]
        c = act[rows, XW + NS :]
        dt = step[rows, :]
        dt_t = dt.T
        g = gy[rows, :]
        state = states[k]
        wide, wide_tail, tail = wide_all[rows, :], wide_tail_all[rows, :], tail_all[rows, :]
        g_carried = g * wide
        ginner = jnp.zeros(shape, F32)
        out_sum = jnp.zeros(shape, F32)
        in_sum = jnp.zeros(shape, F32)
        parts = []
        for h in range(HEADS_AT):
            own = slice(h * HP, (h + 1) * HP)
            inner = decay_in[k * HEADS_AT + h]
            product = fair(g[:, own], x[:, own], ((1,), (1,)))
            ginner = ginner + product * decay_dt[k * HEADS_AT + h]
            both = product * inner
            out_sum = out_sum + jnp.where(
                col == h, jnp.sum(both * dt_t[h : h + 1, :], axis=1, keepdims=True), 0.0
            )
            in_sum = in_sum + jnp.where(row == h, jnp.sum(both, axis=0, keepdims=True), 0.0)
            parts.append(rough(inner, g[:, own], ((0,), (0,))) * dt[:, h : h + 1])
        from_later = fair(b, later)
        gact[rows, :XW] = (
            jnp.concatenate(parts, axis=1) + from_later * wide_tail + g * skip[...]
        )
        gact[rows, XW : XW + NS] = rough(ginner, c, ((0,), (0,))) + rough(
            x * wide_tail, later, ((1,), (1,))
        )
        gact[rows, XW + NS :] = rough(ginner, b) + rough(g_carried, state, ((1,), (1,)))
        tail_in = picked(x * from_later, spread, ((1,), (1,)))
        state_out = picked(from_state[rows, :] * g_carried, spread, ((1,), (1,)))
        in_col = in_sum.T
        gdt[rows, :] = in_col + tail_in * tail
        moved = tail_in * tail * dt
        kept = picked(
            jnp.sum(state * later, axis=0, keepdims=True) * wide[SPAN - 1 :],
            spread,
            ((1,), (1,)),
        )
        at_end = jnp.sum(moved, axis=0, keepdims=True) + kept
        change = out_sum - in_col * dt + state_out - moved
        gla[rows, :] = picked(upper, change, terms=3) + at_end
        skip_sum = skip_sum + jnp.sum(g * x, axis=0, keepdims=True)
        later = later * wide[SPAN - 1 :] + fair(c, g_carried, ((0,), (0,)))
    g_skip[...] = skip_sum

    core = info[AT_CORE]
    gbc_given[...] = gact[:, part_at(XW, 1 - core, NS, NS)]
    gbc_kept[...] = gact[:, part_at(XW, core, NS, NS)]

    gsoft = (gdt[...] - gla[...] * rate[...]) * jax.nn.sigmoid(soft[...])
    gsoft = jnp.where(iota(gsoft.shape, 1) < HEADS_AT, gsoft, 0.0)
    gsoft_low[...] = gsoft.astype(LOW)
    gdr[...] = dot_t(gsoft.astype(LOW), own_heads_pick(info)).astype(LOW)
    g_heads[0:1, :] = jnp.sum(-gla[...] * step[...] * rate[...], axis=0, keepdims=True)
    g_heads[1:2, :] = jnp.sum(gsoft, axis=0, keepdims=True)
    g_heads[2:, :] = jnp.zeros((6, LANES), F32)

    padded[:8, :] = jnp.zeros((8, LANES), F32)
    masks = tap_masks(info, seg)
    g_taps[...] = jnp.zeros_like(g_taps)
    for block in range(0, XW, LANES):
        lanes = slice(block, block + LANES)
        padded[8:, :] = xbc[:, lanes]
        total, sums = conv_back(
            masks, gact[:, lanes], slope[:, lanes],
            [taps[j : j + 1, lanes] for j in range(KC)],
            lambda j: padded[8 - (KC - 1 - j) : 8 - (KC - 1 - j) + seq, :], gpad,
        )
        gx_low[:, lanes] = total.astype(LOW)
        for j, value in enumerate(sums):
            g_taps[j : j + 1, lanes] = value


def shared_back_kernel(
    info, gbc_kept, gbc_moved, xbc, slope, taps, gbc_low, g_taps, padded, gpad, seg
):
    seq = gbc_low.shape[0]
    lanes = part_at(XW, info[AT_CORE], NS, NS)
    padded[:8, :] = jnp.zeros((8, LANES), F32)
    padded[8:, :] = xbc[:, lanes]
    total, sums = conv_back(
        tap_masks(info, seg), gbc_kept[...] + gbc_moved[...], slope[:, lanes],
        [taps[j : j + 1, lanes] for j in range(KC)],
        lambda j: padded[8 - (KC - 1 - j) : 8 - (KC - 1 - j) + seq, :], gpad,
    )
    g_taps[...] = jnp.zeros_like(g_taps)
    for j, value in enumerate(sums):
        g_taps[j : j + 1, :] = value
    gbc_low[...] = total.astype(LOW)


def late_kernel(bits, info, gzz, gq, gkv, gx_low, gbc_low, gsoft, h_low, given, kept, left):
    mine, core = bit_of(info, bits), info[AT_CORE]
    own = gsoft[...]
    other = jnp.concatenate([own[:, HD:], own[:, :HD]], axis=1)
    is_own = (iota(own.shape, 1) < HD) == (core == 0)
    left[...] = jnp.where(is_own, gkv[...], jnp.where(core == 0, other, own))
    first = 0
    for value in (gzz, gq, left, gx_low, gbc_low):
        for at in range(0, value.shape[1], LANES):
            rows = t_dot(value[:, at : at + LANES], h_low[...])
            store_halves(mine, rows, first + at // LANES, given, kept)
        first += value.shape[1] // LANES


def inputs_back_kernel(
    info, gx_low, gzz, gq, gkv, gbc_low, gdr, w_full, z_full, given, kept, back
):
    c = info[AT_CORE]
    gbc = gbc_low[...]
    nothing = jnp.zeros_like(gbc)
    back[:, :XW] = gx_low[...]
    back[:, Q_AT:KV_AT] = gq[...]
    back[:, KV_AT:BC_AT] = gkv[...]
    back[:, BC_AT : BC_AT + NS] = jnp.where(c == 0, gbc, nothing)
    back[:, BC_AT + NS : DT_AT] = jnp.where(c == 0, nothing, gbc)
    back[:, DT_AT:W_FIRST] = gdr[...]
    back[:, W_FIRST:] = gzz[...]
    for core, dst in ((1 - c, given), (c, kept)):
        for k in range(2):
            rows = part(2 * k + core, TB)
            dst[k] = dot32(back[rows, :W_FIRST], w_full[...]) + dot32(
                back[rows, W_FIRST:], z_full[...]
            )


def first_norm_back_kernel(info, mine, moved, hidden, norm, gres, out, g_norm):
    gh = mine[...] + moved[...]
    value = hidden[...].astype(F32)
    scale = rms_scale(value)
    uu = gh * norm[...]
    mean = jnp.mean(uu * value, axis=-1, keepdims=True)
    out[...] = gres[info[AT_Y]] + scale * uu - value * scale**3 * mean
    g_norm[...] = jnp.sum(gh * value * scale, axis=0, keepdims=True)


def result_kernel(info, mine, moved, residual, keep, out, sums):
    mlp = mine[...] + moved[...]
    full = residual[info[AT_Y]] + mlp
    out[...] = full.astype(LOW)
    full = full * keep[:, :1]
    mlp = mlp * keep[:, :1]
    sums[0:1, :] = jnp.sum(full * full, axis=0, keepdims=True)
    sums[1:2, :] = jnp.sum(mlp * mlp, axis=0, keepdims=True)
    sums[2:, :] = jnp.zeros((6, D), F32)


def attend_kernel(info, q_ref, kv_ref, out_ref, lse_ref):
    scale = 1.0 / math.sqrt(HD)
    heads = q_ref.shape[1] // HD
    for k in range(q_ref.shape[0] // SPAN):
        rows, reach = pl.ds(k * SPAN, SPAN), (k + 1) * SPAN
        keys, values = kv_ref[:reach, :HD], kv_ref[:reach, HD:]
        counted = counted_keys(info, k * SPAN, reach)
        outs, tops = [], []
        for h in range(heads):
            s = dot_t(q_ref[rows, h * HD : (h + 1) * HD], keys) * scale
            s = jnp.where(counted, s, NEG)
            top = jnp.max(s, axis=1, keepdims=True)
            lse = top + jnp.log(jnp.sum(jnp.exp(s - top), axis=1, keepdims=True))
            prob = jnp.exp(s - lse).astype(LOW)
            outs.append(dot32(prob, values))
            tops.append(lse)
        out_ref[rows, :] = jnp.concatenate(outs, axis=1).astype(LOW)
        lane = iota((SPAN, LANES), 1)
        lse_ref[rows, :] = sum(jnp.where(lane == h, t, 0.0) for h, t in enumerate(tops))


def counted_keys(info, first, reach):
    shape = (SPAN, reach)
    row, col = iota(shape, 0) + first, iota(shape, 1)
    return (col <= row) & (count_starts(info, row) == count_starts(info, col))


def attend_back_kernel(
    info, q_ref, kv_ref, lse_ref, gout_ref, cosines, sines, turn, gq_ref, gkv_ref, gq_rot
):
    scale = 1.0 / math.sqrt(HD)
    heads = q_ref.shape[1] // HD
    gkv_ref[...] = jnp.zeros_like(gkv_ref)
    for k in range(q_ref.shape[0] // SPAN):
        rows, reach = pl.ds(k * SPAN, SPAN), (k + 1) * SPAN
        keys, values = kv_ref[:reach, :HD], kv_ref[:reach, HD:]
        counted = counted_keys(info, k * SPAN, reach)
        outs, gkeys, gvalues = [], 0.0, 0.0
        for h in range(heads):
            own = slice(h * HD, (h + 1) * HD)
            q, gout = q_ref[rows, own], gout_ref[rows, own]
            s = dot_t(q, keys) * scale
            pe = jnp.exp(jnp.where(counted, s - lse_ref[rows, h : h + 1], NEG))
            gprob = dot_t(gout, values)
            delta = jnp.sum(pe * gprob, axis=1, keepdims=True)
            gs = (pe * (gprob - delta) * scale).astype(LOW)
            outs.append(dot32(gs, keys))
            gkeys = gkeys + t_dot(gs, q)
            gvalues = gvalues + t_dot(pe.astype(LOW), gout)
        gq_rot[rows, :] = jnp.concatenate(outs, axis=1)
        gkv_ref[:reach, :] += jnp.concatenate([gkeys, gvalues], axis=1)
    value = gq_rot[...]
    gq_ref[...] = (value * cosines[...] - picked(value, turn[...]) * sines[...]).astype(LOW)


def keys_back_kernel(info, own, moved, cosines, sines, turn, out):
    value = own[...] + moved[...]
    back = value * cosines[...] - picked(value, turn[...]) * sines[...]
    is_key = iota(value.shape, 1) < HD
    mine = is_key == (info[AT_CORE] == 0)
    out[...] = jnp.where(mine, jnp.where(is_key, back, value), 0.0).astype(LOW)


def halve_kernel(bits, info, kept, moved, given_next, kept_next):
    mine = bit_of(info, bits)
    half = kept.shape[1] // 2
    own, other = part(mine, half), part(1 - mine, half)
    given_next[...] = (kept[:, other, :] + moved[:, other, :].astype(F32)).astype(LOW)
    kept_next[...] = kept[:, own, :] + moved[:, own, :].astype(F32)


def settle_kernel(by_rows, info, kept, moved, total, core, far, far_core):
    total[...] = (kept[...] + moved[...].astype(F32)).astype(LOW)
    for place, dst in zip(peers(info)[1:], (core, far, far_core)):
        if by_rows:
            count = by_rows // 4
            dst[...] = total[pl.ds(count * place, count)]
        else:
            dst[...] = total[:, :, part(place, dst.shape[2])]


def total_low_kernel(info, kept, moved, out):
    out[...] = (kept[...] + moved[...].astype(F32)).astype(LOW)


def spread_kernel(by_rows, info, total, core, far, far_core, out):
    places = peers(info)
    out[...] = total[...]
    for place, ref in zip(places[1:], (core, far, far_core)):
        if by_rows:
            count = by_rows // 4
            out[pl.ds(count * place, count)] = ref[...]
        else:
            out[:, :, part(place, ref.shape[2])] = ref[...]


def join_kernel(bits, info, own, moved, out):
    mine, size = bit_of(info, bits), own.shape[1]
    out[:, part(mine, size), :] = own[...]
    out[:, part(1 - mine, size), :] = moved[...]


def sum_steps(info, given, kept, order, by_rows):
    moved = swap_far(given, order[0])
    for bits in order[1:]:
        moved = after(moved, (yield given))
        n, size, width = kept.shape
        given, kept = call(
            functools.partial(halve_kernel, bits),
            (low_of(n, size // 2, width), f32_of(n, size // 2, width)),
            info, kept, moved,
        )
        moved = swap_far(given, bits)
    moved = after(moved, (yield given))
    n, size, width = kept.shape
    if by_rows is None:
        own = call(total_low_kernel, low_of(n, size, width), info, kept, moved)
    else:
        block = (by_rows // 4, size, width) if by_rows else (n, size, width // 4)
        total, *blocks = call(
            functools.partial(settle_kernel, by_rows),
            (low_of(n, size, width),) + (low_of(*block),) * 3,
            info, kept, moved,
        )
        sent = [swap(block, bits) for block, bits in zip(blocks, (1, 2, 3))]
        sent = after(sent, (yield blocks))
        own = call(
            functools.partial(spread_kernel, by_rows), low_of(n, size, width), info, total, *sent
        )
    for bits in order[:0:-1]:
        moved = swap_far(own, bits)
        moved = after(moved, (yield own))
        n, size, width = own.shape
        own = call(
            functools.partial(join_kernel, bits), low_of(n, 2 * size, width), info, own, moved
        )
    moved = swap_far(own, order[0])
    return own, after(moved, (yield own))


class Running:
    def __init__(self, steps):
        self.steps, self.result = steps, None
        self.sent = next(steps)

    def step(self, value):
        if self.result is not None:
            return value
        try:
            self.sent = self.steps.send(value)
        except StopIteration as end:
            self.result = self.sent = end.value
        return self.sent


def quarters(bits, info, own, moved, source=None):
    mine, size = bit_of(info, bits), own.shape[1] // 2
    same = True if source is None else info[AT_CORE] == source % 2
    for at, ref in ((mine, own), (1 - mine, moved)):
        for j in range(2):
            yield jnp.where(same, 2 * at + j, 2 * j + at), ref, slice(j * size, (j + 1) * size)


def finish_mlp_kernel(bits, info, own, moved, out_up, out_down):
    quarter, size, blocks = FF // 4, own.shape[1] // 2, D // LANES
    each = blocks // 4
    for k in range(4):
        for at, ref, rows in quarters(bits, info, own, moved, k):
            for j in range(each):
                block = ref[each * k + j, rows, :].astype(F32)
                where = part(4 * j + at, size)
                out_up[where, k * quarter : (k + 1) * quarter] = block[:, :quarter]
                out_up[where, FF + k * quarter : FF + (k + 1) * quarter] = block[:, quarter:]
    for at, ref, rows in quarters(bits, info, own, moved):
        for j in range(out_down.shape[0] // LANES):
            out_down[part(4 * j + at, size), :] = ref[blocks + j, rows, :].astype(F32)


def finish_mid_kernel(bits, info, own, moved, out_ssm, out_attn):
    size, scan = own.shape[1] // 2, XW // LANES
    for at, ref, rows in quarters(bits, info, own, moved):
        for j in range(scan):
            out_ssm[part(4 * j + at, size), :] = ref[j, rows, :].astype(F32)
        out_attn[part(at, size), :] = ref[scan, rows, :].astype(F32)


def finish_in_kernel(bits, info, own, moved, out, out_qkv, blocks_q, blocks_kv, shared):
    size, wide, scan = own.shape[1] // 2, out.shape[1], XW // LANES
    q_at, x_at = scan, scan + 2
    for k in range(4):
        lanes = slice(k * wide, (k + 1) * wide)
        for at, ref, rows in quarters(bits, info, own, moved, k):
            for j in range(scan):
                for first, block in ((0, j), (DS, x_at + j)):
                    start = first + (k * scan + j) * LANES + at * size
                    out[pl.ds(pl.multiple_of(start, size), size), :] = ref[
                        block, rows, lanes
                    ].astype(F32)
            blocks_q[k, part(at, size), :] = ref[q_at, rows, lanes].astype(F32)
            blocks_kv[k, part(at, size), :] = ref[q_at + 1, rows, lanes].astype(F32)
            shared[k, part(at, size), :] = ref[x_at + scan, rows, lanes].astype(F32)
    for k in range(4):
        out_qkv[:, k * LANES : (k + 1) * LANES] = blocks_q[k].T
    for k in range(2):
        rows = slice(k * HD, (k + 1) * HD)
        both = jnp.concatenate([blocks_kv[k, rows, :], blocks_kv[k + 2, rows, :]], axis=0)
        out_qkv[:, QW + k * KW : QW + (k + 1) * KW] = both.T
        out[2 * DS + k * NS : 2 * DS + (k + 1) * NS, :] = shared[k] + shared[k + 2]
    steps = [
        blocks_kv[k, (1 - k % 2) * HD : (1 - k % 2) * HD + HEADS_AT, :] for k in range(4)
    ]
    out[DS + CONV_CH :, :] = jnp.concatenate(steps, axis=0)


def small_steps(info, vector):
    for bits in (1, 2, (1, 1), (2, 2), (4, 4)):
        moved = swap_far(vector, bits) if isinstance(bits, tuple) else swap(vector, bits)
        moved = after(moved, (yield vector))
        vector = call(total_kernel, f32_of(*vector.shape), info, vector, moved)
    return vector


def unpack_kernel(info, small, one, conv, conv_bias, dt_bias, a_log, skip, gain, two, stats):
    for first, out in ((ROW_ONE, one), (ROW_TWO, two), (ROW_GAIN, gain)):
        for k in range(out.shape[1] // LANES):
            out[:, k * LANES : (k + 1) * LANES] = small[first + k : first + k + 1, :]
    for j in range(KC + 1):
        for k in range(CONV_ROWS):
            at = ROW_TAPS + j * CONV_ROWS + k
            dst, row = (conv, j) if j < KC else (conv_bias, 0)
            dst[row : row + 1, k * LANES : (k + 1) * LANES] = small[at : at + 1, :]
    for first, out in ((ROW_RATE, a_log), (ROW_BIAS, dt_bias)):
        pieces = [small[first + k : first + k + 1, :HEADS_AT] for k in range(4)]
        out[...] = jnp.concatenate(pieces, axis=1)
    lane = iota((1, LANES), 1)
    total = jnp.zeros((1, LANES), F32)
    for k in range(NH):
        at, first = ROW_SKIP + k * HP // LANES, k * HP % LANES
        value = jnp.sum(small[at : at + 1, first : first + HP], axis=1, keepdims=True)
        total = total + jnp.where(lane == k, value, 0.0)
    skip[...] = total[:, :NH]
    sums = [
        jnp.sum(small[ROW_STATS + k : ROW_STATS + k + 1, :], axis=1, keepdims=True)
        for k in range(4)
    ]
    total = jnp.zeros((1, LANES), F32)
    for k in range(3):
        total = total + jnp.where(lane == k, jnp.sqrt(sums[k] / (sums[3] * D)), 0.0)
    stats[...] = total[:, :3]


ROW_ONE, ROW_TWO, ROW_TAPS = 0, 8, 16
CONV_ROWS = CONV_CH // LANES
ROW_GAIN = ROW_TAPS + (KC + 1) * CONV_ROWS
ROW_SKIP = ROW_GAIN + DS // LANES
ROW_RATE = ROW_SKIP + DS // LANES
ROW_BIAS = ROW_RATE + 4
ROW_STATS = ROW_BIAS + 4
SMALL_ROWS = 128


def small_kernel(
    info, one, two, taps_x, taps_bc, gain, skip, heads, sums, mixed, keep, out
):
    out[...] = jnp.zeros_like(out)
    place, core = peers(info)[0], info[AT_CORE]
    for k in range(D // LANES):
        lanes = slice(k * LANES, (k + 1) * LANES)
        out[ROW_ONE + k : ROW_ONE + k + 1, :] = one[:, lanes]
        out[ROW_TWO + k : ROW_TWO + k + 1, :] = two[:, lanes]
    blocks = XW // LANES
    for k in range(blocks):
        lanes = slice(k * LANES, (k + 1) * LANES)
        at = place * blocks + k
        for j in range(KC + 1):
            out[pl.ds(ROW_TAPS + j * CONV_ROWS + at, 1), :] = taps_x[j : j + 1, lanes]
        out[pl.ds(ROW_GAIN + at, 1), :] = gain[:, lanes]
        out[pl.ds(ROW_SKIP + at, 1), :] = skip[:, lanes]
    for j in range(KC + 1):
        out[pl.ds(ROW_TAPS + j * CONV_ROWS + DS // LANES + core, 1), :] = taps_bc[j : j + 1, :]
    out[pl.ds(ROW_RATE + place, 1), :] = heads[0:1, :]
    out[pl.ds(ROW_BIAS + place, 1), :] = heads[1:2, :]
    for k, row in enumerate((sums[0:1, :], mixed[...], sums[1:2, :])):
        folded = row[:, :LANES]
        for j in range(1, D // LANES):
            folded = folded + row[:, j * LANES : (j + 1) * LANES]
        out[ROW_STATS + k : ROW_STATS + k + 1, :] = folded
    out[ROW_STATS + 3 : ROW_STATS + 4, :] = keep[...].T[:1]


def by_heads(
    hidden_in, cotangent, doc_starts, valid_mask, norm_one, in_proj, conv_weight, conv_bias,
    dt_bias, a_log, skip_scale, gated_gain, qkv_proj, ssm_out, attn_out, norm_two, gate_up,
    down_proj,
):
    place, far_place = lax.axis_index("shard"), lax.axis_index("replica")
    y, c = place // 2, place % 2
    rows = hidden_in.shape[0]
    seq, depth = 4 * rows, in_proj.shape[0]
    bits = [y, c, far_place % 2, far_place // 2 % 2, far_place // 4]
    info = jnp.concatenate([jnp.stack(bits).astype(jnp.int32), doc_starts[0]])
    pair = (2, rows, D)

    h_far = swap(hidden_in, 2)
    h_core = swap(hidden_in, 1)
    w_own, w_core, w_far, z_own, z_core, z_far = call(
        pack_in_kernel,
        (
            low_of(W_SENT, depth), low_of(W_SENT, depth), low_of(W_SENT + KV_AT, depth),
            low_of(XW, depth), low_of(XW, depth), low_of(2 * XW, depth),
        ),
        info, in_proj.T, qkv_proj,
    )
    u_own, u_core, u_far = call(
        pack_up_kernel, (low_of(depth, FF // 2),) * 3, info, after(gate_up, w_own)
    )
    freqs = ROPE_BASE ** (-(jnp.arange(HD // 2).astype(F32) * 2.0) / HD)
    angles = jnp.arange(seq).astype(F32)[:, None] * jnp.tile(freqs, LANES // (HD // 2))[None, :]
    cosines, sines = jnp.cos(angles), jnp.sin(angles)
    taps, bias, bias_own, rate, skip, gain, gain_one, gain_two, keep, g_own, turn = call(
        prepare_kernel,
        (
            f32_of(KC, XW + 2 * NS), f32_of(1, XW + 2 * NS), f32_of(1, LANES), f32_of(1, LANES),
            f32_of(1, XW), f32_of(1, XW), f32_of(1, D), f32_of(1, D), f32_of(LANES, LANES),
            low_of(rows, D), low_of(LANES, LANES),
        ),
        info, conv_weight.T, conv_bias[None], dt_bias[None], a_log[None], skip_scale[None],
        gated_gain[None], norm_one[None], norm_two[None], valid_mask[None],
        after(cotangent, (cosines, sines)),
        scratch=(pltpu.VMEM((8, LANES), F32),),
    )
    w_far = swap(after(w_far, (u_own, g_own, h_far)), 2)
    w_core = swap(w_core, 1)
    h_far_core = swap(h_far, 1)
    w_far_core = swap(w_far, 1)
    z_far = swap(after(z_far, w_far), 2)

    h_low, w_full, xbc, conv_pre, soft, q_low, kv_low, ssm_y, states = call(
        forward_kernel,
        (
            low_of(seq, D), low_of(W_FIRST, D), f32_of(seq, XW + 2 * NS), f32_of(seq, XW + 2 * NS),
            f32_of(seq, LANES), low_of(seq, LANES), low_of(seq, LANES), f32_of(seq, XW),
            f32_of(seq // SPAN, NS, XW),
        ),
        info, hidden_in, h_core, h_far, h_far_core, w_own, w_core, w_far, w_far_core,
        gain_one, taps, bias, bias_own, rate, skip, cosines, sines, turn,
        scratch=(
            pltpu.VMEM((seq + 8, XW + 2 * NS), F32), pltpu.VMEM((seq, XW + 2 * NS), F32),
            pltpu.VMEM((seq, LANES), F32), pltpu.VMEM((seq + 8, LANES), jnp.int32),
        ),
    )
    z_far, z_core = after((z_far, z_core), h_low)
    z_core, z_far_core = swap(z_core, 1), swap(z_far, 1)
    u_far, u_core, g_out = after((u_far, u_core, g_own), z_far)
    u_y, g_far = swap(u_far, 2), swap(g_out, 2)
    z_full, gate_z, square = call(
        gate_kernel, (low_of(XW, D), f32_of(seq, XW), f32_of(8, seq)),
        info, h_low, z_own, z_core, z_far, z_far_core, ssm_y,
    )
    square = call(total_kernel, f32_of(8, seq), info, square, swap(square, 1))
    square_far = swap(square, 2)
    attn, lse = call(
        attend_kernel, (low_of(seq, LANES), f32_of(seq, LANES)), info, after(q_low, square), kv_low
    )

    given, kept, normed = call(
        output_kernel, (f32_of(*pair), f32_of(*pair), low_of(seq, XW)),
        info, square, square_far, ssm_y, gate_z, gain, after(attn, u_y), ssm_out, attn_out,
    )
    u_x = swap_far(after(u_y, given), (1, 1))
    u_y_core = swap(after(u_y, given), 1)
    chip, sent = call(add_kernel, (f32_of(*pair), low_of(*pair)), info, kept, swap(given, 1))
    u_core, g_core = swap(after(u_core, sent), 1), swap(after(g_out, sent), 1)
    g_far_core = swap(after(g_far, sent), 1)
    residual, h2, mixed_sum = call(
        second_norm_kernel, (f32_of(*pair), low_of(*pair), f32_of(1, D)),
        info, chip, swap(sent, 2), hidden_in, h_far, gain_two, keep,
        scratch=(pltpu.VMEM(pair, LOW),),
    )
    u_x_core = swap(u_x, 1)

    given, kept, hid, ggu, h2_cat, gmlp = call(
        mlp_kernel,
        (
            f32_of(*pair), f32_of(*pair), low_of(seq, FF // 4), low_of(seq, FF // 2),
            low_of(seq, D), low_of(seq, D),
        ),
        info, h2, swap(h2, 1), u_own, u_core, u_y, u_x, u_y_core, u_x_core,
        g_own, g_core, g_far, g_far_core, down_proj,
        scratch=(pltpu.VMEM((D, FF // 2), LOW),),
    )
    order = ((1, 2), (2, 1), (4, 4))
    moved = swap(given, 1)
    half = LANES // 2
    blocks = (D + FF // 4) // LANES
    up_given, up_kept = call(
        functools.partial(grad_mlp_kernel, order[0]),
        (low_of(blocks, half, D), f32_of(blocks, half, D)), info, h2_cat, ggu, hid, gmlp,
    )
    s_up = Running(sum_steps(info, up_given, up_kept, order, D // LANES))
    kept = after(kept, up_given)
    chip, sent = call(add_kernel, (f32_of(*pair), low_of(*pair)), info, kept, moved)
    prepared = call(
        scan_prepare_kernel,
        (
            f32_of(seq // SPAN * HEADS_AT, SPAN, SPAN), f32_of(seq // SPAN * HEADS_AT, SPAN, SPAN),
            f32_of(seq, XW + 2 * NS), f32_of(seq, XW + 2 * NS), f32_of(seq, XW), f32_of(seq, XW),
            f32_of(seq, XW), f32_of(seq, LANES), f32_of(seq, LANES),
        ),
        info, after(conv_pre, sent), soft, rate, states,
    )
    gres, gmix, g_norm_two = call(
        norm_back_pair_kernel, (f32_of(*pair), low_of(*pair), f32_of(1, D)),
        info, after(chip, prepared), swap(sent, 2), residual, gain_two, g_own, g_far,
        scratch=(pltpu.VMEM(pair, LOW),),
    )

    moved = swap(gmix, 1)
    mlp_given, mlp_kept = call(
        down_kernel, (f32_of(*pair), f32_of(*pair)), info, after(hid, gmix), down_proj
    )
    mlp_mine, mlp_given = call(
        add_split_kernel, (f32_of(rows, D),) * 2, info, mlp_kept, swap(mlp_given, 1)
    )
    gmix_all, gnormed, gattn, uv = call(
        output_back_kernel,
        (low_of(seq, D), f32_of(seq, XW), low_of(seq, LANES), f32_of(8, seq)),
        info, gmix, moved, ssm_y, gate_z, gain, ssm_out, attn_out,
    )
    uv = call(total_kernel, f32_of(8, seq), info, uv, swap(uv, 1))
    uv_far = swap(uv, 2)
    gq, gkv_part = call(
        attend_back_kernel, (low_of(seq, LANES), f32_of(seq, LANES)),
        info, q_low, kv_low, lse, after(gattn, uv), cosines, sines, turn,
        scratch=(pltpu.VMEM((seq, LANES), F32),),
    )
    gzz, gy, g_gain = call(
        gate_back_kernel, (low_of(seq, XW), f32_of(seq, XW), f32_of(1, XW)),
        info, square, square_far, uv, uv_far, after(gnormed, gkv_part), ssm_y, gate_z, gain,
    )
    blocks = (XW + LANES) // LANES
    mid_given, mid_kept = call(
        functools.partial(grad_mid_kernel, order[0]),
        (low_of(blocks, half, D), f32_of(blocks, half, D)),
        info, normed, attn, after(gmix_all, gkv_part),
    )
    s_mid = Running(sum_steps(info, mid_given, mid_kept, order, None))

    gx_low, gbc_given, gbc_kept, gdr, gsoft, taps_x, g_skip, g_heads = call(
        scan_back_kernel,
        (
            low_of(seq, XW), f32_of(seq, NS), f32_of(seq, NS), low_of(seq, LANES),
            low_of(seq, LANES), f32_of(8, XW), f32_of(1, XW), f32_of(8, LANES),
        ),
        info, xbc, soft, rate, skip, states, taps, after(gy, (s_up.step(gy), mid_given)),
        *prepared,
        scratch=(
            pltpu.VMEM((seq, XW + 2 * NS), F32),
            pltpu.VMEM((seq, LANES), F32), pltpu.VMEM((seq, LANES), F32),
            pltpu.VMEM((seq + 8, LANES), F32), pltpu.VMEM((seq + 8, LANES), F32),
            pltpu.VMEM((seq + 8, LANES), jnp.int32),
        ),
    )
    gkv_part = after(gkv_part, gbc_given)
    moved = swap(gbc_given, 1)
    gkv = call(
        keys_back_kernel, low_of(seq, LANES),
        info, gkv_part, swap(gkv_part, 1), cosines, sines, turn,
    )
    gbc_low, taps_bc = call(
        shared_back_kernel, (low_of(seq, NS), f32_of(8, LANES)),
        info, after(gbc_kept, gkv), moved, xbc, prepared[3], taps,
        scratch=(
            pltpu.VMEM((seq + 8, LANES), F32), pltpu.VMEM((seq + 8, LANES), F32),
            pltpu.VMEM((seq + 8, LANES), jnp.int32),
        ),
    )

    blocks = (2 * XW + 3 * LANES) // LANES
    late_given, late_kept = call(
        functools.partial(late_kernel, order[0]),
        (low_of(blocks, half, D), f32_of(blocks, half, D)),
        info, gzz, gq, gkv, gx_low, gbc_low, gsoft, h_low,
        scratch=(pltpu.VMEM((seq, LANES), LOW),),
    )
    s_late = Running(sum_steps(info, late_given, late_kept, order, 0))

    given, kept = call(
        inputs_back_kernel, (f32_of(*pair), f32_of(*pair)),
        info, after(gx_low, (s_up.step(gbc_low), s_mid.step(gbc_low), late_given)), gzz, gq, gkv, gbc_low, gdr, w_full, z_full,
        scratch=(pltpu.VMEM((seq, W_FIRST + XW), LOW),),
    )
    moved = swap(given, 1)
    kept = after(kept, late_given)
    mine, given = call(add_split_kernel, (f32_of(rows, D),) * 2, info, kept, moved)
    moved = swap(given, 2)

    token = given

    def steps(*sums):
        nonlocal token
        for one in sums:
            token = one.step(token)

    steps(s_late, s_up, s_up)
    grad_input, g_norm_one = call(
        first_norm_back_kernel, (f32_of(rows, D), f32_of(1, D)),
        info, mine, after(moved, token), hidden_in, gain_one, gres,
    )
    mlp_moved = swap(after(mlp_given, g_norm_one), 2)
    token = g_norm_one
    steps(s_mid, s_late, s_mid)
    output, sums = call(
        result_kernel, (low_of(rows, D), f32_of(8, D)),
        info, mlp_mine, after(mlp_moved, token), residual, keep,
    )
    small = call(
        small_kernel, f32_of(SMALL_ROWS, LANES),
        info, g_norm_one, g_norm_two, taps_x, taps_bc, g_gain, g_skip, g_heads, sums,
        mixed_sum, keep,
    )
    s_small = Running(small_steps(info, small))
    steps(s_up, s_small, s_mid, s_small, s_late, s_up, s_mid, s_late, s_small, s_up, s_late, s_mid, s_small, s_late, s_small, s_late)
    small = s_small.result
    grad_up, grad_down = call(
        functools.partial(finish_mlp_kernel, order[0]),
        (f32_of(*gate_up.shape), f32_of(*down_proj.shape)), info, *s_up.result,
    )
    grad_ssm, grad_attn = call(
        functools.partial(finish_mid_kernel, order[0]),
        (f32_of(*ssm_out.shape), f32_of(*attn_out.shape)), info, *s_mid.result,
    )
    grad_in, grad_qkv = call(
        functools.partial(finish_in_kernel, order[0]),
        (f32_of(in_proj.shape[1], depth), f32_of(*qkv_proj.shape)), info, *s_late.result,
        scratch=(pltpu.VMEM((4, LANES, depth), F32),) * 3,
    )
    one, conv, bias, dt, rate, skip, gain, two, stats = call(
        unpack_kernel,
        (
            f32_of(1, D), f32_of(KC, CONV_CH), f32_of(1, CONV_CH), f32_of(1, NH), f32_of(1, NH),
            f32_of(1, NH), f32_of(1, DS), f32_of(1, D), f32_of(1, 3),
        ),
        info, small,
    )
    return (
        output, grad_input, one[0], grad_in.T, conv.T, bias[0], dt[0], rate[0], skip[0], gain[0],
        grad_qkv, grad_ssm, grad_attn, two[0], grad_up, grad_down, stats[0],
    )


def on_any(*args):
    sizes = (lax.axis_size("replica"), lax.axis_size("shard"), args[0].shape[0])
    return (by_heads if sizes == (8, 4, TB) else on_device)(*args)


def solution(mesh):
    return jax.shard_map(
        on_any,
        mesh=mesh,
        in_specs=(
            P(("replica", "shard"), None),
            P(("replica", "shard"), None),
            P("replica", None),
            P(("replica", "shard")),
            P(),
            P("shard", None),
            P(),
            P(),
            P(),
            P(),
            P(),
            P(),
            P("shard", None),
            P("shard", None),
            P("shard", None),
            P(),
            P("shard", None),
            P("shard", None),
        ),
        out_specs=(
            P(("replica", "shard"), None),
            P(("replica", "shard"), None),
            P(),
            P("shard", None),
            P(),
            P(),
            P(),
            P(),
            P(),
            P(),
            P("shard", None),
            P("shard", None),
            P("shard", None),
            P(),
            P("shard", None),
            P("shard", None),
            P(),
        ),
        check_vma=False,
    )
```
